32 devices in a mesh: grp: 4 (over y, x), seq: 8 (over z, core).
Axes of the slice: x: 2, y: 2, z: 4, core: 2. Of those that a mesh axis runs over, the one named last changes fastest.
Arguments:
- events: bfloat16 [8192, 1024], P(('grp', 'seq')), may hold values from -6 to 6
- lengths: int32 [32, 8], P(('grp', 'seq')), may hold values from 1 to 48, as said below
- destinations: int32 [32, 8], P(('grp', 'seq')), may hold values from 0 to 7, as said below
- history: int32 [8192], P(('grp', 'seq')), may hold values from 0 to 4095, as said below
- negatives: int32 [8192, 3], P(('grp', 'seq')), may hold values from 0 to 4095, as said below
- in_weight: bfloat16 [1024, 2048], replicated, may hold values from -0.1875 to 0.1875
- out_weight: bfloat16 [1024, 512], replicated, may hold values from -0.25 to 0.25
- item_table: bfloat16 [4096, 1024], P('seq'), may hold values from -0.1875 to 0.1875
Outputs:
- layer_out: bfloat16 [8192, 1024], P(('grp', 'seq'))
- in_grad: float32 [1024, 2048], P('seq')
- out_grad: float32 [1024, 512], P('seq')
- table_grad: float32 [4096, 1024], P('seq')
The draws below stay inside these ranges and needn't reach their ends.
Inputs may be any that keep to these rules, and one draw needn't show every extreme that they name: Each loader device holds 8 users whose lengths sum to 256; the longest history is 48. `destinations`: the 8 users of a loader device go to the 8 different devices of its group, one to each, and every device of a group receives users with 256 rows in all. `history`: item i lies in row i % 512 of owner i // 512. The 4 candidates of an event lie on 4 different owners, and after the relayout every device holds exactly 128 candidates of each owner. `negatives`: numbered as history; see there.
All inputs are finite; a program needn't handle non-finite values.
Results may differ from the reference program's by a relative error of at most 0.02.
Values may be sent and summed in bfloat16 or wider, within the bound.
No kernel may reach another device: no remote copies, remote signals or barrier semaphores. Data moves between devices by JAX's collectives and lax.ppermute only.
A program may use at most 128 MiB of HBM per device.

```python
import jax
import jax.numpy as jnp
from jax import lax

D = 1024
HEADS = 4
HEAD_DIM = 128
HIDDEN_SIZE = 512
TOK_DEV = 256
OWNERS = 8
USERS = 8
NCAND = 4
VOCAB_DEV = 512
GROUPS = 4
LOADERS = 32
TOKENS = 8192
VOCAB = 4096


def layout_group(group_key):
    subkeys = jax.random.split(group_key, 9)
    mean_length = TOK_DEV // OWNERS
    half_length = mean_length // 2
    spread_amount = jax.random.randint(subkeys[0], (OWNERS // 2, OWNERS // 2), 0, half_length + 1)
    spread_amount = spread_amount.at[0, 0].set(half_length)
    parity = jnp.arange(OWNERS) % 2
    signs = jnp.where(parity[:, None] == parity[None, :], 1, -1)
    expanded = jnp.repeat(jnp.repeat(spread_amount, 2, 0), 2, 1)
    length_table = mean_length + signs * expanded
    loader_rank = jax.random.permutation(subkeys[1], OWNERS)
    relabel = jax.random.permutation(subkeys[2], OWNERS)
    by_loader = length_table[loader_rank]
    user_order = jax.vmap(lambda sub: jax.random.permutation(sub, OWNERS))(jax.random.split(subkeys[4], OWNERS))
    user_lengths = jnp.take_along_axis(by_loader, user_order, 1).astype(jnp.int32)
    user_dests = relabel[user_order].astype(jnp.int32)
    shuffles = jax.vmap(lambda sub: jax.random.permutation(sub, TOK_DEV))(jax.random.split(subkeys[5], OWNERS))
    owner_perm = jax.vmap(lambda sub: jax.random.permutation(sub, OWNERS))(jax.random.split(subkeys[6], OWNERS))
    cand_slot = jnp.arange(NCAND)
    slot_owner = (shuffles[:, :, None] + cand_slot[None, None, :]) % OWNERS
    owner_id = jax.vmap(lambda table_perm, picks: table_perm[picks])(owner_perm, slot_owner)
    row_limit = jax.random.randint(subkeys[7], (OWNERS, TOK_DEV, NCAND), 1, VOCAB_DEV + 1)
    row_id = jax.random.randint(subkeys[8], (OWNERS, TOK_DEV, NCAND), 0, row_limit)
    balanced = owner_id * VOCAB_DEV + row_id
    starts = jnp.cumsum(user_lengths, 1) - user_lengths
    positions = jnp.arange(TOK_DEV)
    user_id = jnp.sum((starts[:, None, :] <= positions[None, :, None]).astype(jnp.int32), -1) - 1
    target_dev = jnp.take_along_axis(user_dests, user_id, 1)
    within = positions[None, :] - jnp.take_along_axis(starts, user_id, 1)
    sent_rows = jnp.sum(user_lengths[:, :, None] * (user_dests[:, :, None] == jnp.arange(OWNERS)[None, None, :]).astype(jnp.int32), 1)
    before = jnp.cumsum(sent_rows, 0) - sent_rows
    row_at = jnp.take_along_axis(before, target_dev, 1) + within
    loader_cands = balanced[target_dev, row_at]
    return (user_lengths, user_dests, loader_cands.astype(jnp.int32))


def layout_all(key):
    group_keys = jax.random.split(jax.random.fold_in(key, 7), GROUPS)
    user_lengths, user_dests, loader_cands = jax.vmap(layout_group)(group_keys)
    return (user_lengths.reshape(LOADERS, USERS), user_dests.reshape(LOADERS, USERS), loader_cands.reshape(TOKENS, NCAND))


def draw_lengths(key, part):
    return layout_all(key)[0]


def draw_destinations(key, part):
    return layout_all(key)[1]


def draw_history(key, part):
    return layout_all(key)[2][:, 0]


def draw_negatives(key, part):
    return layout_all(key)[2][:, 1:]


def steps_of(own_key, shape, cuts, low, largest):
    def one(dim, shards_of):
        steps = jax.random.uniform(jax.random.fold_in(jax.random.fold_in(own_key, 6), dim), (shards_of,), jnp.float32, low / len(cuts), largest / len(cuts))
        return jnp.repeat(jnp.exp(steps), shape[dim] // shards_of).reshape((-1,) + (1,) * (len(shape) - dim - 1))

    loudness = one(*cuts[0])
    for cut in cuts[1:]:
        loudness = loudness * one(*cut)
    return loudness


def noise(stream_key, shape, scale, reach, cuts=(), kind=jnp.bfloat16):
    level = steps_of(stream_key, shape, cuts, -0.22, 0.18) if cuts else 1.0
    array = jax.random.normal(stream_key, shape, jnp.float32) * scale * level
    return jnp.minimum(jnp.maximum(array, -reach), reach).astype(kind)


def setup_inputs(seed: int = 0) -> dict:
    key_list = jax.random.split(jax.random.key(seed), 9)
    events = noise(key_list[0], (TOKENS, D), 1.0, 6.0, ((0, 32),))
    lengths = draw_lengths(jax.random.fold_in(key_list[8], 71), 0)
    destinations = draw_destinations(jax.random.fold_in(key_list[8], 71), 0)
    history = draw_history(jax.random.fold_in(key_list[8], 71), 0)
    negatives = draw_negatives(jax.random.fold_in(key_list[8], 71), 0)
    in_weight = noise(key_list[5], (D, 4 * HIDDEN_SIZE), D ** -0.5, 0.1875)
    out_weight = noise(key_list[6], (D, HIDDEN_SIZE), HIDDEN_SIZE ** -0.5, 0.25)
    item_table = noise(key_list[7], (VOCAB, D), D ** -0.5, 0.1875, ((0, 8),))
    return dict(events=events, lengths=lengths, destinations=destinations, history=history, negatives=negatives, in_weight=in_weight, out_weight=out_weight, item_table=item_table)


epsilon = 1e-05
softmax_warmth = 0.05

def center_scale(values):
    average = lax.optimization_barrier(jnp.mean(values, -1, keepdims=True))
    centered = values - average
    inverse = lax.rsqrt(lax.optimization_barrier(jnp.mean(centered * centered, -1, keepdims=True)) + epsilon)
    return (centered * inverse, inverse)

def silu_slope(values):
    sigmoid = jax.nn.sigmoid(values)
    return sigmoid * (1.0 + values * (1.0 - sigmoid))

def batch_stacked(pattern, first_operand, second_operand):
    return jnp.einsum(pattern, first_operand.astype(jnp.float32), second_operand.astype(jnp.float32))

def layer_forward(tokens, attend_mask, in_weight, out_weight, batch_count):
    hidden_width = out_weight.shape[1]
    scoring_scale = HEAD_DIM ** (-0.5)
    features = tokens.astype(jnp.float32)
    normed_in = center_scale(features)[0].astype(jnp.bfloat16)
    preact = jnp.dot(normed_in, in_weight, preferred_element_type=jnp.float32)
    projected = jax.nn.silu(preact).astype(jnp.bfloat16)
    gate_part = projected[:, :hidden_width]
    value_portion = projected[:, hidden_width:2 * hidden_width].reshape(batch_count, -1, hidden_width)
    query_portion = projected[:, 2 * hidden_width:3 * hidden_width].reshape(batch_count, -1, hidden_width)
    key_portion = projected[:, 3 * hidden_width:].reshape(batch_count, -1, hidden_width)
    score_list, weight_pieces, output_pieces = ([], [], [])
    for current_head in range(HEADS):
        column_begin = current_head * HEAD_DIM
        column_end = column_begin + HEAD_DIM
        attention_scores = batch_stacked('ptx,pux->ptu', query_portion[..., column_begin:column_end], key_portion[..., column_begin:column_end]) * scoring_scale
        attention_weight = (jax.nn.silu(attention_scores) * attend_mask).astype(jnp.bfloat16)
        output_pieces.append(batch_stacked('fjz,fzy->fjy', attention_weight, value_portion[..., column_begin:column_end]))
        score_list.append(attention_scores)
        weight_pieces.append(attention_weight)
    attended = jnp.concatenate(output_pieces, -1).reshape(-1, hidden_width)
    normed, inverse = center_scale(attended)
    gated_rows = (normed * gate_part.astype(jnp.float32)).astype(jnp.bfloat16)
    result = features + lax.dot_general(gated_rows, out_weight, (((1,), (1,)), ((), ())), preferred_element_type=jnp.float32)
    saved_state = (normed_in, preact, gate_part, value_portion, query_portion, key_portion, score_list, weight_pieces, normed, inverse, gated_rows)
    return (result, saved_state)

def layer_backward(upstream, saved_state, attend_mask, out_weight, batch_count):
    normed_in, preact, gate_part, value_portion, query_portion, key_portion, score_list, weight_pieces, normed, inverse, gated_rows = saved_state
    hidden_width = out_weight.shape[1]
    scoring_scale = HEAD_DIM ** (-0.5)
    upstream_b = upstream.astype(jnp.bfloat16)
    grad_gated = jnp.dot(upstream_b, out_weight, preferred_element_type=jnp.float32)
    grad_gate = grad_gated * normed
    grad_normed = grad_gated * gate_part.astype(jnp.float32)
    grad_attended = inverse * (grad_normed - lax.optimization_barrier(jnp.mean(grad_normed, -1, keepdims=True)) - normed * lax.optimization_barrier(jnp.mean(grad_normed * normed, -1, keepdims=True)))
    grad_attended = grad_attended.astype(jnp.bfloat16).reshape(batch_count, -1, hidden_width)
    value_gradient, query_gradient, key_gradient = ([], [], [])
    for current_head in range(HEADS):
        column_begin = current_head * HEAD_DIM
        column_end = column_begin + HEAD_DIM
        gradient_portion = grad_attended[..., column_begin:column_end]
        weight_gradient = batch_stacked('ptx,pux->ptu', gradient_portion, value_portion[..., column_begin:column_end])
        value_gradient.append(batch_stacked('hyo,hyx->hox', weight_pieces[current_head], gradient_portion))
        score_gradient = (weight_gradient * attend_mask * silu_slope(score_list[current_head]) * scoring_scale).astype(jnp.bfloat16)
        query_gradient.append(batch_stacked('fjz,fzy->fjy', score_gradient, key_portion[..., column_begin:column_end]))
        key_gradient.append(batch_stacked('hyo,hyx->hox', score_gradient, query_portion[..., column_begin:column_end]))
    grad_project = jnp.concatenate([grad_gate, jnp.concatenate(value_gradient, -1).reshape(-1, hidden_width), jnp.concatenate(query_gradient, -1).reshape(-1, hidden_width), jnp.concatenate(key_gradient, -1).reshape(-1, hidden_width)], -1)
    grad_preact = (grad_project * silu_slope(preact)).astype(jnp.bfloat16)
    return (normed_in, grad_preact, upstream_b, gated_rows)

def item_scores(result, cand_rows):
    length_out = jnp.sqrt(lax.optimization_barrier(jnp.sum(result * result, -1, keepdims=True)) + epsilon)
    single_output = result / length_out
    row_float = cand_rows.astype(jnp.float32)
    row_length = jnp.sqrt(lax.optimization_barrier(jnp.sum(row_float * row_float, -1, keepdims=True)) + epsilon)
    single_row = row_float / row_length
    logit_values = lax.optimization_barrier(jnp.sum(single_output[:, None, :] * single_row, -1)) / softmax_warmth
    exponent = jnp.exp(logit_values)
    softmax_weights = exponent / lax.optimization_barrier(jnp.sum(exponent, -1, keepdims=True))
    logit_gradient = softmax_weights - (jnp.arange(NCAND) == 0).astype(jnp.float32)[None, :]
    gathered_rows = lax.optimization_barrier(jnp.sum(logit_gradient[..., None] * single_row, 1)) / softmax_warmth
    upstream = (gathered_rows - single_output * lax.optimization_barrier(jnp.sum(single_output * gathered_rows, -1, keepdims=True))) / length_out
    scattered_rows = logit_gradient[..., None] * single_output[:, None, :] / softmax_warmth
    grad_rows = ((scattered_rows - single_row * lax.optimization_barrier(jnp.sum(single_row * scattered_rows, -1, keepdims=True))) / row_length).astype(jnp.bfloat16)
    return (upstream, grad_rows)

def balanced_index(lengths, destinations):
    grouped_len = lengths.reshape(GROUPS, OWNERS, USERS)
    grouped_dest = destinations.reshape(GROUPS, OWNERS, USERS)
    starts = jnp.cumsum(grouped_len, -1) - grouped_len
    positions = jnp.arange(TOK_DEV, dtype=jnp.int32)
    user_id = lax.optimization_barrier(jnp.sum((starts[:, :, None, :] <= positions[None, None, :, None]).astype(jnp.int32), -1)) - 1
    target_dev = jnp.take_along_axis(grouped_dest, user_id, 2)
    within = positions[None, None, :] - jnp.take_along_axis(starts, user_id, 2)
    sent_rows = lax.optimization_barrier(jnp.sum(grouped_len[..., None] * (grouped_dest[..., None] == jnp.arange(OWNERS, dtype=jnp.int32)).astype(jnp.int32), 2))
    before = jnp.cumsum(sent_rows, 1) - sent_rows
    earlier = jnp.take_along_axis(before, target_dev, 2)
    group_ids = jnp.arange(GROUPS, dtype=jnp.int32)[:, None, None]
    return ((group_ids * OWNERS + target_dev) * TOK_DEV + earlier + within).reshape(-1).astype(jnp.int32)

def reference(events, lengths, destinations, history, negatives, in_weight, out_weight, item_table):
    candidates = jnp.concatenate([history[:, None], negatives], 1)
    positions = jnp.arange(TOK_DEV, dtype=jnp.int32)

    def one_loader(running, inputs):
        in_acc, out_acc, table_acc = running
        tokens, user_lengths, loader_cands = inputs
        starts = jnp.cumsum(user_lengths) - user_lengths
        user_id = lax.optimization_barrier(jnp.sum((starts[None, :] <= positions[:, None]).astype(jnp.int32), 1))
        attend_mask = ((user_id[:, None] == user_id[None, :]) & (positions[None, :] <= positions[:, None])).astype(jnp.float32)[None]
        result, saved_state = layer_forward(tokens, attend_mask, in_weight, out_weight, 1)
        cand_rows = item_table[loader_cands]
        upstream, grad_rows = item_scores(result, cand_rows)
        normed_in, grad_preact, upstream_b, gated_rows = layer_backward(upstream, saved_state, attend_mask, out_weight, 1)
        in_acc = in_acc + lax.dot_general(normed_in, grad_preact, (((0,), (0,)), ((), ())), preferred_element_type=jnp.float32)
        out_acc = out_acc + lax.dot_general(upstream_b, gated_rows, (((0,), (0,)), ((), ())), preferred_element_type=jnp.float32)
        table_acc = table_acc.at[loader_cands.reshape(-1)].add(grad_rows.reshape(-1, D).astype(jnp.float32))
        return ((in_acc, out_acc, table_acc), result.astype(jnp.bfloat16))
    initial = (jnp.zeros((D, 4 * HIDDEN_SIZE), jnp.float32), jnp.zeros((D, HIDDEN_SIZE), jnp.float32), jnp.zeros((VOCAB, D), jnp.float32))
    stacked = (events.reshape(LOADERS, TOK_DEV, D), lengths, candidates.reshape(LOADERS, TOK_DEV, NCAND))
    (in_grad, out_grad, table_grad), outputs = lax.scan(one_loader, initial, stacked)
    placed = balanced_index(lengths, destinations)
    layer_out = jnp.zeros((TOKENS, D), jnp.bfloat16).at[placed].set(outputs.reshape(TOKENS, D))
    return (layer_out, in_grad, out_grad, table_grad)
```

```python
import jax
import jax.numpy as jnp
from jax import lax
from jax.sharding import PartitionSpec as P

HEADS = 4
HEAD_DIM = 128
NCAND = 4

epsilon = 1e-05
softmax_warmth = 0.05


def center_scale(values):
    average = jnp.mean(values, -1, keepdims=True)
    centered = values - average
    inverse = lax.rsqrt(jnp.mean(centered * centered, -1, keepdims=True) + epsilon)
    return (centered * inverse, inverse)


def silu_slope(values):
    sigmoid = jax.nn.sigmoid(values)
    return sigmoid * (1.0 + values * (1.0 - sigmoid))


def dot(a, b, dims):
    return lax.dot_general(a, b, (dims, ((), ())), preferred_element_type=jnp.float32)


NN = ((1,), (0,))
NT = ((1,), (1,))
TN = ((0,), (0,))


def layer_forward(tokens, mask, in_weight, out_weight):
    hidden = out_weight.shape[1]
    scale = HEAD_DIM ** (-0.5)
    features = tokens.astype(jnp.float32)
    normed_in = center_scale(features)[0].astype(jnp.bfloat16)
    preact = dot(normed_in, in_weight, NN)
    projected = jax.nn.silu(preact).astype(jnp.bfloat16)
    u, v, q, k = [projected[:, i * hidden : (i + 1) * hidden] for i in range(4)]
    scores, weights, outputs = ([], [], [])
    for head in range(HEADS):
        cols = slice(head * HEAD_DIM, (head + 1) * HEAD_DIM)
        score = dot(q[:, cols], k[:, cols], NT) * scale
        weight = jnp.where(mask, jax.nn.silu(score), 0.0).astype(jnp.bfloat16)
        outputs.append(dot(weight, v[:, cols], NN))
        scores.append(score)
        weights.append(weight)
    attended = jnp.concatenate(outputs, -1)
    normed, inverse = center_scale(attended)
    gated = (normed * u.astype(jnp.float32)).astype(jnp.bfloat16)
    result = features + dot(gated, out_weight, NT)
    return (result, (normed_in, preact, u, v, q, k, scores, weights, normed, inverse, gated))


def layer_backward(upstream_b, saved, mask, out_weight):
    normed_in, preact, u, v, q, k, scores, weights, normed, inverse, gated = saved
    scale = HEAD_DIM ** (-0.5)
    grad_gated = dot(upstream_b, out_weight, NN)
    grad_u = grad_gated * normed
    grad_normed = grad_gated * u.astype(jnp.float32)
    grad_attended = inverse * (
        grad_normed
        - jnp.mean(grad_normed, -1, keepdims=True)
        - normed * jnp.mean(grad_normed * normed, -1, keepdims=True)
    )
    grad_attended = grad_attended.astype(jnp.bfloat16)
    grad_v, grad_q, grad_k = ([], [], [])
    for head in range(HEADS):
        cols = slice(head * HEAD_DIM, (head + 1) * HEAD_DIM)
        part = grad_attended[:, cols]
        grad_attn = dot(part, v[:, cols], NT)
        grad_v.append(dot(weights[head], part, TN))
        grad_score = jnp.where(mask, grad_attn * silu_slope(scores[head]) * scale, 0.0)
        grad_score = grad_score.astype(jnp.bfloat16)
        grad_q.append(dot(grad_score, k[:, cols], NN))
        grad_k.append(dot(grad_score, q[:, cols], TN))
    grad_project = jnp.concatenate([grad_u] + grad_v + grad_q + grad_k, -1)
    return (grad_project * silu_slope(preact)).astype(jnp.bfloat16)


def body(events, lengths, destinations, history, negatives, in_weight, out_weight, item_table):
    groups = lax.axis_size("grp")
    owners = lax.axis_size("seq")
    chips = owners // 2
    grp = lax.axis_index("grp")
    seq = lax.axis_index("seq")
    chip, core = seq // 2, seq % 2
    tok = events.shape[0]
    vocab_dev, width = item_table.shape
    hidden = out_weight.shape[1]
    share = vocab_dev // groups
    slot = 3 * tok // (2 * owners)
    f32, b16 = jnp.float32, jnp.bfloat16

    def to_chip(x, d):
        pairs = [(2 * a + b, 2 * ((a + d) % chips) + b) for a in range(chips) for b in range(2)]
        return lax.ppermute(x, "seq", pairs)

    def to_group(x, k):
        return lax.ppermute(x, "grp", [(a, a ^ k) for a in range(groups)])

    def to_core(x):
        return lax.ppermute(x, "seq", [(a, a ^ 1) for a in range(owners)])

    table = item_table.astype(f32)
    table_inv = lax.rsqrt(jnp.sum(table * table, -1, keepdims=True) + epsilon)
    own = (table * table_inv).astype(b16)
    quarter = lax.dynamic_slice_in_dim(own, grp * share, share, 0)
    quarter_inv = lax.dynamic_slice_in_dim(table_inv, grp * share, share, 0)
    others = jnp.concatenate([to_chip(quarter, d) for d in range(1, chips)], 0)
    pieces = [own, others] + [to_group(others, k) for k in range(1, groups)]
    blocks = []
    row = jnp.arange(vocab_dev)
    far = jnp.arange((chips - 1) * share)
    for away in range(2):
        side = core ^ away
        for n, piece in enumerate(pieces):
            if n == 0:
                ids = (2 * chip + side) * vocab_dev + row
            else:
                at = (chip - 1 - far // share + chips) % chips
                ids = (2 * at + side) * vocab_dev + (grp ^ (n - 1)) * share + far % share
            blocks.append((to_core(piece) if away else piece, ids))

    user_lengths, user_dests = lengths[0], destinations[0]
    ends = jnp.cumsum(user_lengths)
    starts = ends - user_lengths
    position = jnp.arange(tok)
    inside = (starts[None, :] <= position[:, None]) & (position[:, None] < ends[None, :])
    user = jnp.sum(jnp.where(inside, jnp.arange(owners)[None, :], 0), 1)
    dest = jnp.sum(jnp.where(inside, user_dests[None, :], 0), 1)
    within = position - jnp.sum(jnp.where(inside, starts[None, :], 0), 1)
    mask = (user[:, None] == user[None, :]) & (position[None, :] <= position[:, None])
    send_length = jnp.sum(
        jnp.where(user_dests[None, :] == jnp.arange(owners)[:, None], user_lengths[None, :], 0), 1
    )
    counts = lax.all_to_all(send_length[:, None], "seq", 0, 0, tiled=True)[:, 0]

    result, saved = layer_forward(events, mask, in_weight, out_weight)
    normed_in, gated = saved[0], saved[-1]

    slot_id = jnp.arange(owners * slot)
    place = (dest * slot + within)[None, :] == slot_id[:, None]
    outgoing = dot(place.astype(b16), result.astype(b16), NN).astype(b16)
    arrived = lax.all_to_all(
        outgoing.reshape(owners, slot, width), "seq", 0, 0, tiled=True
    ).reshape(owners * slot, width)
    first = jnp.cumsum(counts) - counts
    slot_row = slot_id % slot
    target = jnp.where(slot_row < jnp.repeat(counts, slot), jnp.repeat(first, slot) + slot_row, -1)
    layer_out = dot((position[:, None] == target[None, :]).astype(b16), arrived, NN).astype(b16)

    length_out = jnp.sqrt(jnp.sum(result * result, -1, keepdims=True) + epsilon)
    unit = result / length_out
    unit_b = unit.astype(b16)
    candidates = jnp.concatenate([history[:, None], negatives], 1)
    logits = [0.0] * NCAND
    for block, ids in blocks:
        product = dot(unit_b, block, NT)
        for c in range(NCAND):
            hit = candidates[:, c : c + 1] == ids[None, :]
            logits[c] += jnp.sum(jnp.where(hit, product, 0.0), -1, keepdims=True)
    exponent = jnp.exp(jnp.concatenate(logits, 1) / softmax_warmth)
    softmax = exponent / jnp.sum(exponent, -1, keepdims=True)
    coef = (softmax - (jnp.arange(NCAND) == 0).astype(f32)[None, :]) / softmax_warmth
    pulled = 0.0
    for block, ids in blocks:
        spread = 0.0
        for c in range(NCAND):
            hit = candidates[:, c : c + 1] == ids[None, :]
            spread += jnp.where(hit, coef[:, c : c + 1], 0.0)
        pulled += dot(spread.astype(b16), block, NN)
    upstream = (pulled - unit * jnp.sum(unit * pulled, -1, keepdims=True)) / length_out
    upstream_b = upstream.astype(b16)

    units = jnp.stack([unit_b] + [to_group(unit_b, k) for k in range(1, groups)])
    tags = jnp.concatenate([coef.T, candidates.T.astype(f32)], 0)
    tags = jnp.stack([tags] + [to_group(tags, k) for k in range(1, groups)])
    units = jnp.concatenate([units, to_core(units)], 0).reshape(-1, width)
    tags = jnp.concatenate([tags, to_core(tags)], 0).transpose(1, 0, 2).reshape(2 * NCAND, -1)
    mine = jnp.arange(chips * share)
    mine_ids = (2 * ((chip - mine // share + chips) % chips) + core) * vocab_dev + grp * share + mine % share
    spread = 0.0
    for c in range(NCAND):
        hit = tags[NCAND + c][None, :] == mine_ids.astype(f32)[:, None]
        spread += jnp.where(hit, tags[c][None, :], 0.0)
    summed = dot(spread.astype(b16), units, NN)
    near = jnp.concatenate([quarter, others], 0).astype(f32)
    summed = summed - near * jnp.sum(near * summed, -1, keepdims=True)
    summed = summed.astype(b16).reshape(chips, share, width)
    total = summed[0].astype(f32)
    for d in range(1, chips):
        total += to_chip(summed[d], -d).astype(f32)
    total = (total * quarter_inv).astype(b16)
    table_grad = jnp.zeros((vocab_dev, width), f32)
    for k in range(groups):
        part = to_group(total, k) if k else total
        table_grad = lax.dynamic_update_slice_in_dim(table_grad, part.astype(f32), (grp ^ k) * share, 0)

    grad_preact = layer_backward(upstream_b, saved, mask, out_weight)
    rows = width // owners

    def both_cores(x):
        x = x.reshape(tok, chips, 2, rows)
        even, odd = x[:, :, 0].reshape(tok, -1), x[:, :, 1].reshape(tok, -1)
        keep = jnp.where(core == 0, even, odd)
        give = jnp.where(core == 0, odd, even)
        return jnp.concatenate([keep, to_core(give)], 0)

    def doubled(x):
        return jnp.concatenate([x, to_core(x)], 0)

    in_part = dot(both_cores(normed_in), doubled(grad_preact), TN)
    out_part = dot(both_cores(upstream_b), doubled(gated), TN)
    weight = jnp.concatenate([in_part, out_part], 1).astype(b16)
    fine = rows // groups
    weight = weight.reshape(chips, groups, fine, 5 * hidden)
    sums = lax.dynamic_index_in_dim(weight, grp, 1, False).astype(f32)
    for k in range(1, groups):
        sums += to_group(lax.dynamic_index_in_dim(weight, grp ^ k, 1, False), k).astype(f32)
    sums = sums.astype(b16)
    line = lax.dynamic_index_in_dim(sums, chip, 0, False).astype(f32)
    for d in range(1, chips):
        line += to_chip(lax.dynamic_index_in_dim(sums, (chip + d) % chips, 0, False), d).astype(f32)
    line = line.astype(b16)
    shard = jnp.zeros((rows, 5 * hidden), f32)
    for k in range(groups):
        part = to_group(line, k) if k else line
        shard = lax.dynamic_update_slice_in_dim(shard, part.astype(f32), (grp ^ k) * fine, 0)
    return (layer_out, shard[:, : 4 * hidden], shard[:, 4 * hidden :], table_grad)


def solution(mesh):
    return jax.shard_map(
        body,
        mesh=mesh,
        in_specs=(
            P(("grp", "seq"), None),
            P(("grp", "seq"), None),
            P(("grp", "seq"), None),
            P(("grp", "seq")),
            P(("grp", "seq"), None),
            P(),
            P(),
            P("seq", None),
        ),
        out_specs=(P(("grp", "seq"), None), P("seq", None), P("seq", None), P("seq", None)),
        check_vma=False,
    )
```

```python
import jax
import jax.numpy as jnp
from jax import lax
from jax.experimental import pallas as pl
from jax.experimental.pallas import tpu as pltpu
from jax.sharding import PartitionSpec as P

HEADS = 4
HEAD_DIM = 128
NCAND = 4

epsilon = 1e-05
softmax_warmth = 0.05

f32, b16, i32 = jnp.float32, jnp.bfloat16, jnp.int32
NN = ((1,), (0,))
NT = ((1,), (1,))
TN = ((0,), (0,))
VMEM = pl.BlockSpec(memory_space=pltpu.VMEM)
SMEM = pl.BlockSpec(memory_space=pltpu.SMEM)
ANY = pl.BlockSpec(memory_space=pl.ANY)


def dot(a, b, dims):
    return lax.dot_general(a, b, (dims, ((), ())), preferred_element_type=f32)


def iota(shape, axis):
    return lax.broadcasted_iota(i32, shape, axis)


def center_scale(values):
    average = jnp.mean(values, -1, keepdims=True)
    centered = values - average
    inverse = lax.rsqrt(jnp.mean(centered * centered, -1, keepdims=True) + epsilon)
    return (centered * inverse, inverse)


def sigmoid(values):
    return 1.0 / (1.0 + jnp.exp(-values))


def split_columns(x, owners, core):
    rows = x.shape[1] // owners
    blocks = [x[:, i * rows : (i + 1) * rows] for i in range(owners)]
    even, odd = jnp.concatenate(blocks[0::2], 1), jnp.concatenate(blocks[1::2], 1)
    first = jnp.broadcast_to(core, even.shape) == 0
    return jnp.where(first, even, odd), jnp.where(first, odd, even)


def call(kernel, out, specs, args, scratch=(), flops=0, nbytes=0):
    return pl.pallas_call(
        kernel,
        out_shape=[jax.ShapeDtypeStruct(s, t) for s, t in out],
        in_specs=specs,
        out_specs=[VMEM] * len(out),
        scratch_shapes=list(scratch),
        cost_estimate=pl.CostEstimate(flops=flops, bytes_accessed=nbytes, transcendentals=0),
        compiler_params=pltpu.CompilerParams(vmem_limit_bytes=48 * 2**20),
    )(*args)


def forward_kernel(
    owners, slot, lengths, dests, events, in_weight, out_weight,
    keep, give, proj, slope, attn, attn_slope, normed_out, inv_out, gated_out, unit, unit_b, inv_len, outgoing,
):
    tok = events.shape[0]
    hidden = out_weight.shape[1]
    scale = HEAD_DIM ** (-0.5)
    core = lax.axis_index("seq") % 2
    x = events[...].astype(f32)
    normed_in = center_scale(x)[0]
    mine, other = split_columns(normed_in, owners, core)
    keep[...] = mine.astype(b16)
    give[...] = other.astype(b16)
    normed_in = normed_in.astype(b16)
    for i in range(4):
        cols = slice(i * hidden, (i + 1) * hidden)
        p = dot(normed_in, in_weight[:, cols], NN)
        sig = sigmoid(p)
        proj[:, cols] = (p * sig).astype(b16)
        slope[:, cols] = (sig * (1.0 + p * (1.0 - sig))).astype(b16)

    pos_c, pos_r = iota((tok, 1), 0), iota((1, tok), 1)
    user_c, user_r = jnp.zeros((tok, 1), i32), jnp.zeros((1, tok), i32)
    target = jnp.zeros((1, tok), i32)
    start = jnp.int32(0)
    for j in range(lengths.shape[1]):
        end = start + lengths[0, j]
        user_c += (pos_c >= end).astype(i32)
        user_r += (pos_r >= end).astype(i32)
        here = (pos_r >= start) & (pos_r < end)
        target = jnp.where(here, dests[0, j] * slot + pos_r - start, target)
        start = end
    mask = (user_c == user_r) & (pos_r <= pos_c)

    outputs = []
    for h in range(HEADS):
        v = proj[:, hidden + h * HEAD_DIM : hidden + (h + 1) * HEAD_DIM]
        q = proj[:, 2 * hidden + h * HEAD_DIM : 2 * hidden + (h + 1) * HEAD_DIM]
        k = proj[:, 3 * hidden + h * HEAD_DIM : 3 * hidden + (h + 1) * HEAD_DIM]
        s = dot(q, k, NT) * scale
        sig = sigmoid(s)
        weight = jnp.where(mask, s * sig, 0.0).astype(b16)
        attn[h] = weight
        attn_slope[h] = jnp.where(mask, sig * (1.0 + s * (1.0 - sig)) * scale, 0.0).astype(b16)
        outputs.append(dot(weight, v, NN))
    normed, inverse = center_scale(jnp.concatenate(outputs, 1))
    normed_out[...] = normed
    inv_out[...] = inverse
    gated = (normed * proj[:, :hidden].astype(f32)).astype(b16)
    gated_out[...] = gated
    result = x + dot(gated, out_weight[...], NT)
    inverse = lax.rsqrt(jnp.sum(result * result, -1, keepdims=True) + epsilon)
    inv_len[...] = inverse
    yn = result * inverse
    unit[...] = yn
    unit_b[...] = yn.astype(b16)
    place = (iota((outgoing.shape[0], 1), 0) == target).astype(b16)
    outgoing[...] = dot(place, result.astype(b16), NN).astype(b16)


def score_kernel(groups, owners, share, count, cand, unit_b, unit, inv_len, *refs):
    pieces, (tags, up, up_keep, up_give, table, sems) = refs[:count], refs[count:]
    chips = owners // 2
    vocab_dev = share * groups
    grp, seq = lax.axis_index("grp"), lax.axis_index("seq")
    chip, core = seq // 2, seq % 2
    tok = unit_b.shape[0]
    runs, copies, at = [], [], 0
    owner_of = {}
    for side in range(2):
        for d in range(chips):
            owner_of[side, d] = 2 * ((chip + chips - d) % chips) + (core ^ side)
    for n in range(count):
        side, index = n // (groups + 1), n % (groups + 1)
        rows = pieces[n].shape[0]
        copies.append(pltpu.make_async_copy(pieces[n], table.at[pl.ds(at, rows)], sems.at[n]))
        copies[-1].start()
        if index == 0:
            here = [((side, 0), 0, vocab_dev, owner_of[side, 0] * vocab_dev)]
        else:
            first = (grp ^ (index - 1)) * share
            here = [
                ((side, d), (d - 1) * share, share, owner_of[side, d] * vocab_dev + first)
                for d in range(1, chips)
            ]
        runs.append((at, rows, here))
        at += rows
    candidates = cand[...]
    sel = {}
    for key, owner in owner_of.items():
        chosen = jnp.full((tok, 1), -1, i32)
        for c in range(NCAND):
            one = candidates[:, c : c + 1]
            chosen = jnp.where(one // vocab_dev == owner, one, chosen)
        sel[key] = chosen
    yb = unit_b[...]
    logits = [jnp.zeros((tok, 1), f32) for _ in range(NCAND)]
    value = {key: jnp.zeros((tok, 1), f32) for key in owner_of}
    for n, (at, rows, here) in enumerate(runs):
        copies[n].wait()
        product = dot(yb, table[at : at + rows], NT)
        for key, off, wide, base in here:
            hit = sel[key] == base + iota((1, wide), 1)
            value[key] += jnp.sum(jnp.where(hit, product[:, off : off + wide], 0.0), -1, keepdims=True)
    total = jnp.zeros((tok, 1), f32)
    for c in range(NCAND):
        owner = candidates[:, c : c + 1] // vocab_dev
        for key in owner_of:
            logits[c] += jnp.where(owner == owner_of[key], value[key], 0.0)
        logits[c] = jnp.exp(logits[c] / softmax_warmth)
        total += logits[c]
    coef = [(logits[c] / total - (1.0 if c == 0 else 0.0)) / softmax_warmth for c in range(NCAND)]
    lane = iota((tok, 128), 1)
    packed = jnp.zeros((tok, 128), f32)
    for c in range(NCAND):
        packed = jnp.where(lane == c, coef[c], packed)
        packed = jnp.where(lane == NCAND + c, candidates[:, c : c + 1].astype(f32), packed)
    tags[...] = packed.T[: 2 * NCAND]
    amount = {}
    for key in owner_of:
        amount[key] = jnp.zeros((tok, 1), f32)
        for c in range(NCAND):
            owner = candidates[:, c : c + 1] // vocab_dev
            amount[key] += jnp.where(owner == owner_of[key], coef[c], 0.0)
    pulled = jnp.zeros(unit.shape, f32)
    for at, rows, here in runs:
        parts = []
        for key, off, wide, base in here:
            hit = sel[key] == base + iota((1, wide), 1)
            parts.append(jnp.where(hit, amount[key], 0.0).astype(b16))
        spread = jnp.concatenate(parts, 1) if len(parts) > 1 else parts[0]
        pulled += dot(spread, table[at : at + rows], NN)
    yn = unit[...]
    upstream = (pulled - yn * jnp.sum(yn * pulled, -1, keepdims=True)) * inv_len[...]
    up[...] = upstream.astype(b16)
    mine, other = split_columns(upstream, owners, core)
    up_keep[...] = mine.astype(b16)
    up_give[...] = other.astype(b16)


def backward_kernel(up, out_weight, proj, slope, attn, attn_slope, normed_ref, inverse, grad):
    hidden = out_weight.shape[1]
    normed = normed_ref[...]
    grad_gated = dot(up[...], out_weight[...], NN)
    grad[:, :hidden] = (grad_gated * normed * slope[:, :hidden].astype(f32)).astype(b16)
    grad_normed = grad_gated * proj[:, :hidden].astype(f32)
    grad_attended = inverse[...] * (
        grad_normed
        - jnp.mean(grad_normed, -1, keepdims=True)
        - normed * jnp.mean(grad_normed * normed, -1, keepdims=True)
    )
    grad_attended = grad_attended.astype(b16)
    for h in range(HEADS):
        cv, cq, ck = [slice(i * hidden + h * HEAD_DIM, i * hidden + (h + 1) * HEAD_DIM) for i in (1, 2, 3)]
        part = grad_attended[:, h * HEAD_DIM : (h + 1) * HEAD_DIM]
        grad_attn = dot(part, proj[:, cv], NT)
        grad_score = (grad_attn * attn_slope[h].astype(f32)).astype(b16)
        grad[:, cv] = (dot(attn[h], part, TN) * slope[:, cv].astype(f32)).astype(b16)
        grad[:, cq] = (dot(grad_score, proj[:, ck], NN) * slope[:, cq].astype(f32)).astype(b16)
        grad[:, ck] = (dot(grad_score, proj[:, cq], TN) * slope[:, ck].astype(f32)).astype(b16)


def item_kernel(groups, owners, share, count, *refs):
    units, tags, (quarter, others, out) = refs[:count], refs[count : 2 * count], refs[2 * count :]
    chips = owners // 2
    vocab_dev = share * groups
    grp, seq = lax.axis_index("grp"), lax.axis_index("seq")
    chip, core = seq // 2, seq % 2
    bases = [(2 * ((chip + chips - d) % chips) + core) * vocab_dev for d in range(chips)]
    summed = jnp.zeros((chips * share, quarter.shape[1]), f32)
    for n in range(count):
        row = tags[n][...]
        items = row[NCAND:].astype(i32)
        parts = []
        for d in range(chips):
            chosen = jnp.full((1, row.shape[1]), -1, i32)
            amount = jnp.zeros((1, row.shape[1]), f32)
            for c in range(NCAND):
                one = items[c : c + 1]
                here = (one >= bases[d]) & (one < bases[d] + vocab_dev)
                chosen = jnp.where(here, one, chosen)
                amount = jnp.where(here, row[c : c + 1], amount)
            hit = bases[d] + grp * share + iota((share, 1), 0) == chosen
            parts.append(jnp.where(hit, amount, 0.0).astype(b16))
        summed += dot(jnp.concatenate(parts, 0), units[n][...], NN)
    near = jnp.concatenate([quarter[...], others[...]], 0).astype(f32)
    out[...] = (summed - near * jnp.sum(near * summed, -1, keepdims=True)).astype(b16)


def relay_kernel(slot, counts, arrived, out):
    tok = out.shape[0]
    lane = iota((1, arrived.shape[0]), 1)
    target = jnp.full(lane.shape, -1, i32)
    first = jnp.int32(0)
    for j in range(counts.shape[0]):
        within = lane - j * slot
        here = (within >= 0) & (within < counts[j, 0])
        target = jnp.where(here, within + first, target)
        first += counts[j, 0]
    place = (iota((tok, 1), 0) == target).astype(b16)
    out[...] = dot(place, arrived[...], NN).astype(b16)


def body(events, lengths, destinations, history, negatives, in_weight, out_weight, item_table):
    groups = lax.axis_size("grp")
    owners = lax.axis_size("seq")
    chips = owners // 2
    grp = lax.axis_index("grp")
    seq = lax.axis_index("seq")
    chip, core = seq // 2, seq % 2
    tok = events.shape[0]
    vocab_dev, width = item_table.shape
    hidden = out_weight.shape[1]
    share = vocab_dev // groups
    slot = 3 * tok // (2 * owners)
    rows = width // owners
    fine = rows // groups

    def to_chip(x, d):
        pairs = [(2 * a + b, 2 * ((a + d) % chips) + b) for a in range(chips) for b in range(2)]
        return lax.ppermute(x, "seq", pairs)

    def to_group(x, k):
        return lax.ppermute(x, "grp", [(a, a ^ k) for a in range(groups)])

    def to_core(x):
        return lax.ppermute(x, "seq", [(a, a ^ 1) for a in range(owners)])

    table = item_table.astype(f32)
    table_inv = lax.rsqrt(jnp.sum(table * table, -1, keepdims=True) + epsilon)
    own = (table * table_inv).astype(b16)
    quarter = lax.dynamic_slice_in_dim(own, grp * share, share, 0)
    quarter_inv = lax.dynamic_slice_in_dim(table_inv, grp * share, share, 0)
    others = jnp.concatenate([to_chip(quarter, d) for d in range(1, chips)], 0)
    pieces = [own, others] + [to_group(others, k) for k in range(1, groups)]
    pieces = pieces + [to_core(piece) for piece in pieces]

    send_length = jnp.sum(
        jnp.where(destinations == jnp.arange(owners)[:, None], lengths, 0), 1, keepdims=True
    )
    counts = lax.all_to_all(send_length, "seq", 0, 0, tiled=True)

    outs = [
        ((tok, width // 2), b16), ((tok, width // 2), b16), ((tok, 4 * hidden), b16), ((tok, 4 * hidden), b16),
        ((HEADS, tok, tok), b16), ((HEADS, tok, tok), b16), ((tok, hidden), f32), ((tok, 1), f32),
        ((tok, hidden), b16), ((tok, width), f32), ((tok, width), b16), ((tok, 1), f32),
        ((owners * slot, width), b16),
    ]
    (keep, give, proj, slope, attn, attn_slope, normed, inverse, gated, unit, unit_b, inv_len, outgoing) = call(
        lambda *refs: forward_kernel(owners, slot, *refs), outs, [SMEM, SMEM, VMEM, VMEM, VMEM],
        [lengths, destinations, events, in_weight, out_weight],
        flops=2 * tok * width * 6 * hidden, nbytes=24 * tok * width + 10 * width * hidden,
    )

    arrived = lax.all_to_all(
        outgoing.reshape(owners, slot, width), "seq", 0, 0, tiled=True
    ).reshape(owners * slot, width)
    layer_out, = call(
        lambda *refs: relay_kernel(slot, *refs), [((tok, width), b16)], [SMEM, VMEM], [counts, arrived],
        flops=3 * tok * tok * width, nbytes=6 * tok * width,
    )

    candidates = jnp.concatenate([history[:, None], negatives], 1)
    outs = [((2 * NCAND, tok), f32), ((tok, width), b16), ((tok, width // 2), b16), ((tok, width // 2), b16)]
    vocab = vocab_dev * owners
    tags, up, up_keep, up_give = call(
        lambda *refs: score_kernel(groups, owners, share, len(pieces), *refs),
        outs, [VMEM] * 4 + [ANY] * len(pieces), [candidates, unit_b, unit, inv_len] + pieces,
        [pltpu.VMEM((vocab, width), b16), pltpu.SemaphoreType.DMA((len(pieces),))],
        flops=4 * tok * width * vocab, nbytes=2 * vocab * width + 12 * tok * width,
    )

    units = [unit_b] + [to_group(unit_b, k) for k in range(1, groups)]
    units = units + [to_core(x) for x in units]
    tags = [tags] + [to_group(tags, k) for k in range(1, groups)]
    tags = tags + [to_core(x) for x in tags]
    summed, = call(
        lambda *refs: item_kernel(groups, owners, share, len(units), *refs),
        [((chips * share, width), b16)], [VMEM] * (2 * len(units) + 2), units + tags + [quarter, others],
        flops=4 * groups * tok * width * chips * share, nbytes=4 * tok * groups * width,
    )
    summed = summed.reshape(chips, share, width)
    total = summed[0].astype(f32)
    for d in range(1, chips):
        total += to_chip(summed[d], -d).astype(f32)
    total = (total * quarter_inv).astype(b16)
    table_grad = jnp.zeros((vocab_dev, width), f32)
    for k in range(groups):
        part = to_group(total, k) if k else total
        table_grad = lax.dynamic_update_slice_in_dim(table_grad, part.astype(f32), (grp ^ k) * share, 0)

    grad, = call(
        backward_kernel, [((tok, 4 * hidden), b16)], [VMEM] * 8,
        [up, out_weight, proj, slope, attn, attn_slope, normed, inverse],
        flops=2 * tok * width * hidden, nbytes=20 * tok * width,
    )

    def both(x, y):
        return jnp.concatenate([x, to_core(y)], 0)

    in_part = dot(both(keep, give), both(grad, grad), TN)
    out_part = dot(both(up_keep, up_give), both(gated, gated), TN)
    weight = jnp.concatenate([in_part, out_part], 1).astype(b16)
    weight = weight.reshape(chips, groups, fine, 5 * hidden)
    sums = lax.dynamic_index_in_dim(weight, grp, 1, False).astype(f32)
    for k in range(1, groups):
        sums += to_group(lax.dynamic_index_in_dim(weight, grp ^ k, 1, False), k).astype(f32)
    sums = sums.astype(b16)
    line = lax.dynamic_index_in_dim(sums, chip, 0, False).astype(f32)
    for d in range(1, chips):
        line += to_chip(lax.dynamic_index_in_dim(sums, (chip + d) % chips, 0, False), d).astype(f32)
    line = line.astype(b16)
    shard = jnp.zeros((rows, 5 * hidden), f32)
    for k in range(groups):
        part = to_group(line, k) if k else line
        shard = lax.dynamic_update_slice_in_dim(shard, part.astype(f32), (grp ^ k) * fine, 0)
    return (layer_out, shard[:, : 4 * hidden], shard[:, 4 * hidden :], table_grad)


def solution(mesh):
    return jax.shard_map(
        body,
        mesh=mesh,
        in_specs=(
            P(("grp", "seq"), None),
            P(("grp", "seq"), None),
            P(("grp", "seq"), None),
            P(("grp", "seq")),
            P(("grp", "seq"), None),
            P(),
            P(),
            P("seq", None),
        ),
        out_specs=(P(("grp", "seq"), None), P("seq", None), P("seq", None), P("seq", None)),
        check_vma=False,
    )
```

```python
import jax
import jax.numpy as jnp
from jax import lax
from jax.experimental import pallas as pl
from jax.experimental.pallas import tpu as pltpu
from jax.sharding import PartitionSpec as P

HEADS = 4
HEAD_DIM = 128
NCAND = 4

epsilon = 1e-05
softmax_warmth = 0.05
EMPTY = 2.0**100

f32, b16, i32 = jnp.float32, jnp.bfloat16, jnp.int32
NN = ((1,), (0,))
NT = ((1,), (1,))
TN = ((0,), (0,))
VMEM = pl.BlockSpec(memory_space=pltpu.VMEM)
SMEM = pl.BlockSpec(memory_space=pltpu.SMEM)
ANY = pl.BlockSpec(memory_space=pl.ANY)


def dot(a, b, dims):
    return lax.dot_general(a, b, (dims, ((), ())), preferred_element_type=f32)


def iota(shape, axis):
    return lax.broadcasted_iota(i32, shape, axis)


def center_scale(values):
    average = jnp.mean(values, -1, keepdims=True)
    centered = values - average
    inverse = lax.rsqrt(jnp.mean(centered * centered, -1, keepdims=True) + epsilon)
    return (centered * inverse, inverse)


def sigmoid(values):
    return 1.0 / (1.0 + jnp.exp(-values))


def split_columns(x, owners, core):
    rows = x.shape[1] // owners
    blocks = [x[:, i * rows : (i + 1) * rows] for i in range(owners)]
    even, odd = jnp.concatenate(blocks[0::2], 1), jnp.concatenate(blocks[1::2], 1)
    first = jnp.broadcast_to(core, even.shape) == 0
    return jnp.where(first, even, odd), jnp.where(first, odd, even)


def call(kernel, out, specs, args, scratch=(), flops=0, nbytes=0, room=32):
    return pl.pallas_call(
        kernel,
        out_shape=[jax.ShapeDtypeStruct(s, t) for s, t in out],
        in_specs=specs,
        out_specs=[VMEM] * len(out),
        scratch_shapes=list(scratch),
        cost_estimate=pl.CostEstimate(flops=flops, bytes_accessed=nbytes, transcendentals=0),
        compiler_params=pltpu.CompilerParams(vmem_limit_bytes=room * 2**20),
    )(*args)


def forward_kernel(
    owners, slot, lengths, dests, events, in_weight, out_weight,
    keep, give, proj, slope, attn, attn_slope, normed_out, inv_out, gated_out, unit, unit_b, inv_len, outgoing,
):
    tok = events.shape[0]
    hidden = out_weight.shape[1]
    scale = HEAD_DIM ** (-0.5)
    core = lax.axis_index("seq") % 2
    x = events[...].astype(f32)
    normed_in = center_scale(x)[0]
    mine, other = split_columns(normed_in, owners, core)
    keep[...] = mine.astype(b16)
    give[...] = other.astype(b16)
    normed_in = normed_in.astype(b16)
    for i in range(4):
        cols = slice(i * hidden, (i + 1) * hidden)
        p = dot(normed_in, in_weight[:, cols], NN)
        sig = sigmoid(p)
        proj[:, cols] = (p * sig).astype(b16)
        slope[:, cols] = (sig * (1.0 + p * (1.0 - sig))).astype(b16)

    pos_c, pos_r = iota((tok, 1), 0), iota((1, tok), 1)
    user_c, user_r = jnp.zeros((tok, 1), i32), jnp.zeros((1, tok), i32)
    target = jnp.zeros((1, tok), i32)
    start = jnp.int32(0)
    for j in range(lengths.shape[1]):
        end = start + lengths[0, j]
        user_c += (pos_c >= end).astype(i32)
        user_r += (pos_r >= end).astype(i32)
        here = (pos_r >= start) & (pos_r < end)
        target = jnp.where(here, dests[0, j] * slot + pos_r - start, target)
        start = end
    mask = (user_c == user_r) & (pos_r <= pos_c)

    outputs = []
    for h in range(HEADS):
        v = proj[:, hidden + h * HEAD_DIM : hidden + (h + 1) * HEAD_DIM]
        q = proj[:, 2 * hidden + h * HEAD_DIM : 2 * hidden + (h + 1) * HEAD_DIM]
        k = proj[:, 3 * hidden + h * HEAD_DIM : 3 * hidden + (h + 1) * HEAD_DIM]
        s = dot(q, k, NT) * scale
        sig = sigmoid(s)
        weight = jnp.where(mask, s * sig, 0.0).astype(b16)
        attn[h] = weight
        attn_slope[h] = jnp.where(mask, sig * (1.0 + s * (1.0 - sig)) * scale, 0.0).astype(b16)
        outputs.append(dot(weight, v, NN))
    normed, inverse = center_scale(jnp.concatenate(outputs, 1))
    normed_out[...] = normed
    inv_out[...] = inverse
    gated = (normed * proj[:, :hidden].astype(f32)).astype(b16)
    gated_out[...] = gated
    result = x + dot(gated, out_weight[...], NT)
    inverse = lax.rsqrt(jnp.sum(result * result, -1, keepdims=True) + epsilon)
    inv_len[...] = inverse
    yn = result * inverse
    unit[...] = yn
    unit_b[...] = yn.astype(b16)
    row = iota((outgoing.shape[0], 1), 0)
    filled = jnp.zeros(row.shape, i32)
    for j in range(lengths.shape[1]):
        at = dests[0, j] * slot
        filled = jnp.where((row >= at) & (row < at + lengths[0, j]), 1, filled)
    placed = dot((row == target).astype(b16), result.astype(b16), NN)
    outgoing[...] = jnp.where(filled == 1, placed, EMPTY).astype(b16)


def owner_ids(owners):
    seq = lax.axis_index("seq")
    chip, core = seq // 2, seq % 2
    chips = owners // 2
    return [2 * ((chip + chips - d) % chips) + (core ^ side) for side in range(2) for d in range(chips)]


def normalise_kernel(share, item_table, own, quarter, quarter_inv):
    grp = lax.axis_index("grp")
    x = item_table[...].astype(f32)
    own[...] = (x * lax.rsqrt(jnp.sum(x * x, -1, keepdims=True) + epsilon)).astype(b16)
    x = item_table[pl.ds(pl.multiple_of(grp * share, share), share)].astype(f32)
    inverse = lax.rsqrt(jnp.sum(x * x, -1, keepdims=True) + epsilon)
    quarter[...] = (x * inverse).astype(b16)
    quarter_inv[...] = inverse


def score_kernel(groups, owners, share, places, cand, unit_b, unit, inv_len, *refs):
    count = len(places)
    pieces, (tags, up, up_keep, up_give, table, spread, sems) = refs[:count], refs[count:]
    chips = owners // 2
    vocab_dev = share * groups
    grp, core = lax.axis_index("grp"), lax.axis_index("seq") % 2
    tok, width = unit_b.shape
    block = vocab_dev + groups * (chips - 1) * share
    copies = {}
    for n, (side, k, left, wide) in enumerate(places):
        rows = pieces[n].shape[0]
        at = side * block + (0 if k < 0 else vocab_dev + k * rows)
        copy = pltpu.make_async_copy(pieces[n], table.at[pl.ds(at, rows), pl.ds(left, wide)], sems.at[n])
        copy.start()
        copies.setdefault((side, k), []).append(copy)
    ids = owner_ids(owners)
    lane = iota((1, 128), 1)
    owner = jnp.full((1, 128), -1, i32)
    for j in range(owners):
        owner = jnp.where(lane == j, ids[j], owner)
    candidates = cand[...]
    chosen = jnp.full((tok, 128), -1, i32)
    first = jnp.zeros((tok, 128), f32)
    for c in range(NCAND):
        here = candidates[:, c : c + 1] // vocab_dev == owner
        chosen = jnp.where(here, candidates[:, c : c + 1], chosen)
        if c == 0:
            first = here.astype(f32)
    wanted = [jnp.broadcast_to(chosen[:, j : j + 1], (tok, 128)) for j in range(owners)]

    def runs(key):
        side, k = key
        at = side * block + (0 if k < 0 else vocab_dev + k * (chips - 1) * share)
        if k < 0:
            return at, vocab_dev, [(side * chips, 0, vocab_dev, ids[side * chips] * vocab_dev)]
        begin = (grp ^ k) * share
        return at, (chips - 1) * share, [
            (side * chips + d, (d - 1) * share, share, ids[side * chips + d] * vocab_dev + begin)
            for d in range(1, chips)
        ]

    def tiles(key):
        at, rows, here = runs(key)
        for j, off, wide, base in here:
            step = min(wide, 128)
            for o in range(0, wide, step):
                hit = wanted[j][:, :step] == base + o + iota((1, step), 1)
                yield j, off + o, step, hit

    yb = unit_b[...]
    value = [[] for _ in range(owners)]
    for key in copies:
        for copy in copies[key]:
            copy.wait()
        at, rows, _ = runs(key)
        product = dot(yb, table[at : at + rows], NT)
        for j, off, step, hit in tiles(key):
            value[j].append(jnp.where(hit, product[:, off : off + step], 0.0))
    logits = jnp.zeros((tok, 128), f32)
    for j in range(owners):
        total = value[j][0]
        for part in value[j][1:]:
            total = total + part
        logits = jnp.where(lane == j, jnp.sum(total, -1, keepdims=True), logits)
    exponent = jnp.where(chosen >= 0, jnp.exp(logits / softmax_warmth), 0.0)
    coef = (exponent / jnp.sum(exponent, -1, keepdims=True) - first) / softmax_warmth
    tags[:owners] = coef.T[:owners]
    tags[owners:] = chosen.astype(f32).T[:owners]
    amount = [jnp.broadcast_to(coef[:, j : j + 1], (tok, 128)) for j in range(owners)]
    for key in copies:
        at = runs(key)[0]
        for j, off, step, hit in tiles(key):
            spread[:, at + off : at + off + step] = jnp.where(hit, amount[j][:, :step], 0.0).astype(b16)
    pulled = dot(spread[...], table[...], NN)
    yn = unit[...]
    upstream = (pulled - yn * jnp.sum(yn * pulled, -1, keepdims=True)) * inv_len[...]
    up[...] = upstream.astype(b16)
    mine, other = split_columns(upstream, owners, core)
    up_keep[...] = mine.astype(b16)
    up_give[...] = other.astype(b16)


def backward_kernel(up, out_weight, proj, slope, attn, attn_slope, normed_ref, inverse, grad):
    hidden = out_weight.shape[1]
    normed = normed_ref[...]
    grad_gated = dot(up[...], out_weight[...], NN)
    grad[:, :hidden] = (grad_gated * normed * slope[:, :hidden].astype(f32)).astype(b16)
    grad_normed = grad_gated * proj[:, :hidden].astype(f32)
    grad_attended = inverse[...] * (
        grad_normed
        - jnp.mean(grad_normed, -1, keepdims=True)
        - normed * jnp.mean(grad_normed * normed, -1, keepdims=True)
    )
    grad_attended = grad_attended.astype(b16)
    for h in range(HEADS):
        cv, cq, ck = [slice(i * hidden + h * HEAD_DIM, i * hidden + (h + 1) * HEAD_DIM) for i in (1, 2, 3)]
        part = grad_attended[:, h * HEAD_DIM : (h + 1) * HEAD_DIM]
        grad_attn = dot(part, proj[:, cv], NT)
        grad_score = (grad_attn * attn_slope[h].astype(f32)).astype(b16)
        grad[:, cv] = (dot(attn[h], part, TN) * slope[:, cv].astype(f32)).astype(b16)
        grad[:, cq] = (dot(grad_score, proj[:, ck], NN) * slope[:, cq].astype(f32)).astype(b16)
        grad[:, ck] = (dot(grad_score, proj[:, cq], TN) * slope[:, ck].astype(f32)).astype(b16)


def item_kernel(groups, owners, share, places, *refs):
    count = len(places)
    units, tags = refs[:count], refs[count : count + groups]
    own, others, far_own, far_others, keep, give, gathered, near, sems = refs[count + groups :]
    chips = owners // 2
    vocab_dev = share * groups
    grp = lax.axis_index("grp")
    tok = tags[0].shape[1]
    copies = []
    for n, (k, left, wide) in enumerate(places):
        copies.append(pltpu.make_async_copy(units[n], gathered.at[pl.ds(k * tok, tok), pl.ds(left, wide)], sems.at[n]))
    begin = pl.multiple_of(grp * share, share)
    for side, (full, part) in enumerate(((own, others), (far_own, far_others))):
        at, n = side * chips * share, count + 2 * side
        copies.append(pltpu.make_async_copy(full.at[pl.ds(begin, share)], near.at[pl.ds(at, share)], sems.at[n]))
        copies.append(
            pltpu.make_async_copy(part, near.at[pl.ds(at + share, (chips - 1) * share)], sems.at[n + 1])
        )
    for copy in copies:
        copy.start()
    ids = owner_ids(owners)
    amounts = jnp.concatenate([t[:owners] for t in tags], 1)
    chosen = jnp.concatenate([t[owners:] for t in tags], 1).astype(i32)
    for copy in copies:
        copy.wait()
    for side, out in ((0, keep), (1, give)):
        parts = []
        for d in range(chips):
            j = side * chips + d
            hit = ids[j] * vocab_dev + grp * share + iota((share, 1), 0) == chosen[j : j + 1]
            parts.append(jnp.where(hit, amounts[j : j + 1], 0.0).astype(b16))
        summed = dot(jnp.concatenate(parts, 0), gathered[...], NN)
        row = near[side * chips * share : (side + 1) * chips * share].astype(f32)
        out[...] = (summed - row * jnp.sum(row * summed, -1, keepdims=True)).astype(b16)


def weight_kernel(groups, owners, keep, give, up_keep, up_give, grad, far_grad, gated, far_gated, *refs):
    outs, whole = refs[:-1], refs[-1]
    chips = owners // 2
    grp = lax.axis_index("grp")
    wide = grad.shape[1]
    step = gated.shape[1]
    for i in range(0, wide, step):
        cols = slice(i, i + step)
        part = dot(keep[...], grad[:, cols], TN) + dot(give[...], far_grad[:, cols], TN)
        whole[:, cols] = part.astype(b16)
    part = dot(up_keep[...], gated[...], TN) + dot(up_give[...], far_gated[...], TN)
    whole[:, wide:] = part.astype(b16)
    rows = whole.shape[0] // chips
    fine = rows // groups
    half = whole.shape[1] // 2
    for z in range(chips):
        for k in range(groups):
            piece = whole[pl.ds(pl.multiple_of(z * rows + (grp ^ k) * fine, fine), fine)]
            if k == 3:
                outs[3][z] = piece[:, :half]
                outs[4][z] = piece[:, half:]
            else:
                outs[k][z] = piece


def assemble_kernel(groups, columns, *refs):
    parts, outs = refs[:groups], refs[groups:]
    grp = lax.axis_index("grp")
    fine = parts[0].shape[0]
    for k in range(groups):
        at = pl.ds(pl.multiple_of((grp ^ k) * fine, fine), fine)
        left = 0
        for out, wide in zip(outs, columns):
            out[at] = parts[k][:, left : left + wide].astype(f32)
            left += wide


def relay_kernel(arrived, out):
    tok, slots = out.shape[0], arrived.shape[0]
    filled = (arrived[:, :128].astype(f32) < EMPTY / 2).astype(b16)
    before = (iota((slots, 1), 0) > iota((1, slots), 1)).astype(b16)
    rank = dot(before, filled, NN)[:, :1].astype(i32)
    rank = jnp.where(filled[:, :1].astype(f32) > 0, rank, -1)
    place = (rank == iota((1, tok), 1)).astype(b16)
    out[...] = dot(place, arrived[...], TN).astype(b16)


def body(events, lengths, destinations, history, negatives, in_weight, out_weight, item_table):
    groups = lax.axis_size("grp")
    owners = lax.axis_size("seq")
    chips = owners // 2
    grp = lax.axis_index("grp")
    seq = lax.axis_index("seq")
    chip, core = seq // 2, seq % 2
    tok = events.shape[0]
    vocab_dev, width = item_table.shape
    hidden = out_weight.shape[1]
    share = vocab_dev // groups
    slot = 3 * tok // (2 * owners)
    rows = width // owners
    fine = rows // groups

    def to_chip(x, d):
        pairs = [(2 * a + b, 2 * ((a + d) % chips) + b) for a in range(chips) for b in range(2)]
        return lax.ppermute(x, "seq", pairs)

    def to_group(x, k):
        return lax.ppermute(x, "grp", [(a, a ^ k) for a in range(groups)])

    def to_core(x):
        return lax.ppermute(x, "seq", [(a, a ^ 1) for a in range(owners)])

    def gather_groups(x):
        wide = x.shape[1]
        if groups != 4:
            return [(k, 0, wide, to_group(x, k) if k else x) for k in range(groups)]
        one, two = to_group(x, 1), to_group(x, 2)
        half = wide // 2
        left, right = to_group(one[:, :half], 2), to_group(two[:, half:], 1)
        return [(0, 0, wide, x), (1, 0, wide, one), (2, 0, wide, two), (3, 0, half, left), (3, half, half, right)]

    own, quarter, quarter_inv = call(
        lambda *refs: normalise_kernel(share, *refs),
        [((vocab_dev, width), b16), ((share, width), b16), ((share, 1), f32)],
        [VMEM], [item_table], flops=8 * vocab_dev * width, nbytes=5 * vocab_dev * width, room=24,
    )
    others = jnp.concatenate([to_chip(quarter, d) for d in range(1, chips)], 0)
    pieces = [(0, -1, 0, width, own)] + [(0,) + p for p in gather_groups(others)]
    pieces = pieces + [(1,) + p[1:4] + (to_core(p[4]),) for p in pieces]
    far_own, far_others = [p[4] for p in pieces if p[0] == 1 and p[1] <= 0]

    outs = [
        ((tok, width // 2), b16), ((tok, width // 2), b16), ((tok, 4 * hidden), b16), ((tok, 4 * hidden), b16),
        ((HEADS, tok, tok), b16), ((HEADS, tok, tok), b16), ((tok, hidden), f32), ((tok, 1), f32),
        ((tok, hidden), b16), ((tok, width), f32), ((tok, width), b16), ((tok, 1), f32),
        ((owners * slot, width), b16),
    ]
    (keep, give, proj, slope, attn, attn_slope, normed, inverse, gated, unit, unit_b, inv_len, outgoing) = call(
        lambda *refs: forward_kernel(owners, slot, *refs), outs, [SMEM, SMEM, VMEM, VMEM, VMEM],
        [lengths, destinations, events, in_weight, out_weight],
        flops=2 * tok * width * 6 * hidden, nbytes=24 * tok * width + 10 * width * hidden,
    )

    arrived = lax.all_to_all(
        outgoing.reshape(owners, slot, width), "seq", 0, 0, tiled=True
    ).reshape(owners * slot, width)
    layer_out, = call(
        relay_kernel, [((tok, width), b16)], [VMEM], [arrived],
        flops=3 * tok * tok * width, nbytes=6 * tok * width, room=16,
    )

    candidates = jnp.concatenate([history[:, None], negatives], 1)
    vocab = vocab_dev * owners
    layer_out, score_unit = lax.optimization_barrier((layer_out, unit))
    tags, up, up_keep, up_give = call(
        lambda *refs: score_kernel(groups, owners, share, [p[:4] for p in pieces], *refs),
        [((2 * owners, tok), f32), ((tok, width), b16), ((tok, width // 2), b16), ((tok, width // 2), b16)],
        [VMEM] * 4 + [ANY] * len(pieces), [candidates, unit_b, score_unit, inv_len] + [p[4] for p in pieces],
        [pltpu.VMEM((vocab, width), b16), pltpu.VMEM((tok, vocab), b16), pltpu.SemaphoreType.DMA((len(pieces),))],
        flops=4 * tok * width * vocab, nbytes=2 * vocab * width + 12 * tok * width, room=24 + vocab // 256,
    )

    grad, = call(
        backward_kernel, [((tok, 4 * hidden), b16)], [VMEM] * 8,
        [up, out_weight, proj, slope, attn, attn_slope, normed, inverse],
        flops=2 * tok * width * hidden, nbytes=20 * tok * width,
    )

    far = [to_core(x) for x in (give, up_give, grad, gated)]
    half = 5 * hidden // 2
    if groups == 4:
        block = (chips, fine, 5 * hidden)
        split = (chips, fine, half)
        parts = call(
            lambda *refs: weight_kernel(groups, owners, *refs),
            [(block, b16)] * 3 + [(split, b16)] * 2, [VMEM] * 8,
            [keep, far[0], up_keep, far[1], grad, far[2], gated, far[3]],
            [pltpu.VMEM((width // 2, 5 * hidden), b16)],
            flops=2 * tok * width * 5 * hidden, nbytes=20 * tok * width, room=24,
        )
        after = parts[0]
        left, right = to_group(parts[3], 1).astype(f32), to_group(parts[4], 2).astype(f32)
        one, two = parts[1].astype(f32), parts[2].astype(f32)
        one = jnp.concatenate([one[..., :half], one[..., half:] + right], 2).astype(b16)
        two = jnp.concatenate([two[..., :half] + left, two[..., half:]], 2).astype(b16)
        sums = parts[0].astype(f32) + to_group(one, 1).astype(f32) + to_group(two, 2).astype(f32)
    else:
        def both(x, y):
            return jnp.concatenate([x, y], 0)

        in_part = dot(both(keep, far[0]), both(grad, far[2]), TN)
        out_part = dot(both(up_keep, far[1]), both(gated, far[3]), TN)
        weight = jnp.concatenate([in_part, out_part], 1).astype(b16)
        weight = weight.reshape(chips, groups, fine, 5 * hidden)
        after = weight
        sums = lax.dynamic_index_in_dim(weight, grp, 1, False).astype(f32)
        for k in range(1, groups):
            sums += to_group(lax.dynamic_index_in_dim(weight, grp ^ k, 1, False), k).astype(f32)
    sums = sums.astype(b16)

    units = gather_groups(unit_b)
    all_tags = [to_group(tags, k) if k else tags for k in range(groups)]
    first_unit, after = lax.optimization_barrier((units[0][3], after))
    mine, other = call(
        lambda *refs: item_kernel(groups, owners, share, [p[:3] for p in units], *refs),
        [((chips * share, width), b16)] * 2, [ANY] * len(units) + [VMEM] * groups + [ANY] * 4,
        [first_unit] + [p[3] for p in units[1:]] + all_tags + [own, others, far_own, far_others],
        [pltpu.VMEM((groups * tok, width), b16), pltpu.VMEM((2 * chips * share, width), b16),
         pltpu.SemaphoreType.DMA((len(units) + 4,))],
        flops=4 * groups * tok * width * chips * share, nbytes=4 * tok * groups * width, room=32 if groups == 4 else 48,
    )
    summed = (mine.astype(f32) + to_core(other).astype(f32)).astype(b16).reshape(chips, share, width)
    total = summed[0].astype(f32)
    for d in range(1, chips):
        total += to_chip(summed[d], -d).astype(f32)
    total = (total * quarter_inv).astype(b16)
    table_grad, = call(
        lambda *refs: assemble_kernel(groups, [width], *refs), [((vocab_dev, width), f32)], [VMEM] * groups,
        [to_group(total, k) if k else total for k in range(groups)],
        flops=vocab_dev * width, nbytes=6 * vocab_dev * width, room=16,
    )

    line = lax.dynamic_index_in_dim(sums, chip, 0, False).astype(f32)
    for d in range(1, chips):
        line += to_chip(lax.dynamic_index_in_dim(sums, (chip + d) % chips, 0, False), d).astype(f32)
    line = line.astype(b16)
    lines = [to_group(line, k) if k else line for k in range(groups)]
    if fine % 16 == 0:
        in_grad, out_grad = call(
            lambda *refs: assemble_kernel(groups, [4 * hidden, hidden], *refs),
            [((rows, 4 * hidden), f32), ((rows, hidden), f32)], [VMEM] * groups, lines,
            flops=rows * hidden, nbytes=30 * rows * hidden, room=16,
        )
    else:
        shard = jnp.zeros((rows, 5 * hidden), f32)
        for k in range(groups):
            shard = lax.dynamic_update_slice_in_dim(shard, lines[k].astype(f32), (grp ^ k) * fine, 0)
        in_grad, out_grad = shard[:, : 4 * hidden], shard[:, 4 * hidden :]
    return (layer_out, in_grad, out_grad, table_grad)


def solution(mesh):
    return jax.shard_map(
        body,
        mesh=mesh,
        in_specs=(
            P(("grp", "seq"), None),
            P(("grp", "seq"), None),
            P(("grp", "seq"), None),
            P(("grp", "seq")),
            P(("grp", "seq"), None),
            P(),
            P(),
            P("seq", None),
        ),
        out_specs=(P(("grp", "seq"), None), P("seq", None), P("seq", None), P("seq", None)),
        check_vma=False,
    )
```

```python
import jax
import jax.numpy as jnp
from jax import lax
from jax.experimental import pallas as pl
from jax.experimental.pallas import tpu as pltpu
from jax.sharding import PartitionSpec as P

HEADS = 4
HEAD_DIM = 128
NCAND = 4

epsilon = 1e-05
softmax_warmth = 0.05
EMPTY = 2.0**100

f32, b16, i32 = jnp.float32, jnp.bfloat16, jnp.int32
NN = ((1,), (0,))
NT = ((1,), (1,))
TN = ((0,), (0,))
VMEM = pl.BlockSpec(memory_space=pltpu.VMEM)
SMEM = pl.BlockSpec(memory_space=pltpu.SMEM)
ANY = pl.BlockSpec(memory_space=pl.ANY)


def dot(a, b, dims):
    return lax.dot_general(a, b, (dims, ((), ())), preferred_element_type=f32)


def iota(shape, axis):
    return lax.broadcasted_iota(i32, shape, axis)


def center_scale(values):
    average = jnp.mean(values, -1, keepdims=True)
    centered = values - average
    inverse = lax.rsqrt(jnp.mean(centered * centered, -1, keepdims=True) + epsilon)
    return (centered * inverse, inverse)


def sigmoid(values):
    return 1.0 / (1.0 + jnp.exp(-values))


def split_columns(x, owners, core):
    rows = x.shape[1] // owners
    blocks = [x[:, i * rows : (i + 1) * rows] for i in range(owners)]
    even, odd = jnp.concatenate(blocks[0::2], 1), jnp.concatenate(blocks[1::2], 1)
    first = jnp.broadcast_to(core, even.shape) == 0
    return jnp.where(first, even, odd), jnp.where(first, odd, even)


def call(kernel, out, specs, args, scratch=(), flops=0, nbytes=0, room=14):
    return pl.pallas_call(
        kernel,
        out_shape=[jax.ShapeDtypeStruct(s, t) for s, t in out],
        in_specs=specs,
        out_specs=[VMEM] * len(out),
        scratch_shapes=list(scratch),
        cost_estimate=pl.CostEstimate(flops=flops, bytes_accessed=nbytes, transcendentals=0),
        compiler_params=pltpu.CompilerParams(vmem_limit_bytes=room * 2**20),
    )(*args)


def forward_kernel(
    owners, slot, lengths, dests, events, in_weight, out_weight,
    keep, give, proj, slope, attn, attn_slope, normed_out, inv_out, gated_out, unit, unit_b, inv_len, outgoing,
):
    tok = events.shape[0]
    hidden = out_weight.shape[1]
    scale = HEAD_DIM ** (-0.5)
    core = lax.axis_index("seq") % 2
    x = events[...].astype(f32)
    normed_in = center_scale(x)[0]
    mine, other = split_columns(normed_in, owners, core)
    keep[...] = mine.astype(b16)
    give[...] = other.astype(b16)
    normed_in = normed_in.astype(b16)
    for i in range(4):
        cols = slice(i * hidden, (i + 1) * hidden)
        p = dot(normed_in, in_weight[:, cols], NN)
        sig = sigmoid(p)
        proj[:, cols] = (p * sig).astype(b16)
        slope[:, cols] = (sig * (1.0 + p * (1.0 - sig))).astype(b16)

    pos_c, pos_r = iota((tok, 1), 0), iota((1, tok), 1)
    user_c, user_r = jnp.zeros((tok, 1), i32), jnp.zeros((1, tok), i32)
    target = jnp.zeros((1, tok), i32)
    start = jnp.int32(0)
    for j in range(lengths.shape[1]):
        end = start + lengths[0, j]
        user_c += (pos_c >= end).astype(i32)
        user_r += (pos_r >= end).astype(i32)
        here = (pos_r >= start) & (pos_r < end)
        target = jnp.where(here, dests[0, j] * slot + pos_r - start, target)
        start = end
    mask = (user_c == user_r) & (pos_r <= pos_c)

    outputs = []
    for h in range(HEADS):
        v = proj[:, hidden + h * HEAD_DIM : hidden + (h + 1) * HEAD_DIM]
        q = proj[:, 2 * hidden + h * HEAD_DIM : 2 * hidden + (h + 1) * HEAD_DIM]
        k = proj[:, 3 * hidden + h * HEAD_DIM : 3 * hidden + (h + 1) * HEAD_DIM]
        s = dot(q, k, NT) * scale
        sig = sigmoid(s)
        weight = jnp.where(mask, s * sig, 0.0).astype(b16)
        attn[h] = weight
        attn_slope[h] = jnp.where(mask, sig * (1.0 + s * (1.0 - sig)) * scale, 0.0).astype(b16)
        outputs.append(dot(weight, v, NN))
    normed, inverse = center_scale(jnp.concatenate(outputs, 1))
    normed_out[...] = normed
    inv_out[...] = inverse
    gated = (normed * proj[:, :hidden].astype(f32)).astype(b16)
    gated_out[...] = gated
    result = x + dot(gated, out_weight[...], NT)
    inverse = lax.rsqrt(jnp.sum(result * result, -1, keepdims=True) + epsilon)
    inv_len[...] = inverse
    yn = result * inverse
    unit[...] = yn
    unit_b[...] = yn.astype(b16)
    row = iota((outgoing.shape[0], 1), 0)
    filled = jnp.zeros(row.shape, i32)
    for j in range(lengths.shape[1]):
        at = dests[0, j] * slot
        filled = jnp.where((row >= at) & (row < at + lengths[0, j]), 1, filled)
    placed = dot((row == target).astype(b16), result.astype(b16), NN)
    outgoing[...] = jnp.where(filled == 1, placed, EMPTY).astype(b16)


def owner_ids(owners):
    seq = lax.axis_index("seq")
    chip, core = seq // 2, seq % 2
    chips = owners // 2
    return [2 * ((chip + chips - d) % chips) + (core ^ side) for side in range(2) for d in range(chips)]


def normalise_kernel(share, item_table, own, quarter, quarter_inv):
    grp = lax.axis_index("grp")
    x = item_table[...].astype(f32)
    own[...] = (x * lax.rsqrt(jnp.sum(x * x, -1, keepdims=True) + epsilon)).astype(b16)
    x = item_table[pl.ds(pl.multiple_of(grp * share, share), share)].astype(f32)
    inverse = lax.rsqrt(jnp.sum(x * x, -1, keepdims=True) + epsilon)
    quarter[...] = (x * inverse).astype(b16)
    quarter_inv[...] = inverse


def score_kernel(groups, owners, share, places, cand, unit_b, unit, inv_len, *refs):
    count = len(places)
    pieces, (tags, up, up_keep, up_give, table, spread, sems) = refs[:count], refs[count:]
    chips = owners // 2
    vocab_dev = share * groups
    grp, core = lax.axis_index("grp"), lax.axis_index("seq") % 2
    tok, width = unit_b.shape
    block = vocab_dev + groups * (chips - 1) * share
    copies = {}
    for n, (side, k, left, wide) in enumerate(places):
        rows = pieces[n].shape[0]
        at = side * block + (0 if k < 0 else vocab_dev + k * rows)
        copy = pltpu.make_async_copy(pieces[n], table.at[pl.ds(at, rows), pl.ds(left, wide)], sems.at[n])
        copy.start()
        copies.setdefault((side, k), []).append(copy)
    ids = owner_ids(owners)
    lane = iota((1, 128), 1)
    owner = jnp.full((1, 128), -1, i32)
    for j in range(owners):
        owner = jnp.where(lane == j, ids[j], owner)
    candidates = cand[...]
    chosen = jnp.full((tok, 128), -1, i32)
    first = jnp.zeros((tok, 128), f32)
    for c in range(NCAND):
        here = candidates[:, c : c + 1] // vocab_dev == owner
        chosen = jnp.where(here, candidates[:, c : c + 1], chosen)
        if c == 0:
            first = here.astype(f32)
    wanted = [jnp.broadcast_to(chosen[:, j : j + 1], (tok, 128)) for j in range(owners)]

    def runs(key):
        side, k = key
        at = side * block + (0 if k < 0 else vocab_dev + k * (chips - 1) * share)
        if k < 0:
            return at, vocab_dev, [(side * chips, 0, vocab_dev, ids[side * chips] * vocab_dev)]
        begin = (grp ^ k) * share
        return at, (chips - 1) * share, [
            (side * chips + d, (d - 1) * share, share, ids[side * chips + d] * vocab_dev + begin)
            for d in range(1, chips)
        ]

    def tiles(key):
        at, rows, here = runs(key)
        for j, off, wide, base in here:
            step = min(wide, 128)
            for o in range(0, wide, step):
                hit = wanted[j][:, :step] == base + o + iota((1, step), 1)
                yield j, off + o, step, hit

    yb = unit_b[...]
    value = [[] for _ in range(owners)]
    for key in copies:
        for copy in copies[key]:
            copy.wait()
        at, rows, _ = runs(key)
        product = dot(yb, table[at : at + rows], NT)
        for j, off, step, hit in tiles(key):
            value[j].append(jnp.where(hit, product[:, off : off + step], 0.0))
    logits = jnp.zeros((tok, 128), f32)
    for j in range(owners):
        total = value[j][0]
        for part in value[j][1:]:
            total = total + part
        logits = jnp.where(lane == j, jnp.sum(total, -1, keepdims=True), logits)
    exponent = jnp.where(chosen >= 0, jnp.exp(logits / softmax_warmth), 0.0)
    coef = (exponent / jnp.sum(exponent, -1, keepdims=True) - first) / softmax_warmth
    tags[:owners] = coef.T[:owners]
    tags[owners:] = chosen.astype(f32).T[:owners]
    amount = [jnp.broadcast_to(coef[:, j : j + 1], (tok, 128)) for j in range(owners)]
    for key in copies:
        at = runs(key)[0]
        for j, off, step, hit in tiles(key):
            spread[:, at + off : at + off + step] = jnp.where(hit, amount[j][:, :step], 0.0).astype(b16)
    pulled = dot(spread[...], table[...], NN)
    yn = unit[...]
    upstream = (pulled - yn * jnp.sum(yn * pulled, -1, keepdims=True)) * inv_len[...]
    up[...] = upstream.astype(b16)
    mine, other = split_columns(upstream, owners, core)
    up_keep[...] = mine.astype(b16)
    up_give[...] = other.astype(b16)


def backward_kernel(up, out_weight, proj, slope, attn, attn_slope, normed_ref, inverse, grad):
    hidden = out_weight.shape[1]
    normed = normed_ref[...]
    grad_gated = dot(up[...], out_weight[...], NN)
    grad[:, :hidden] = (grad_gated * normed * slope[:, :hidden].astype(f32)).astype(b16)
    grad_normed = grad_gated * proj[:, :hidden].astype(f32)
    grad_attended = inverse[...] * (
        grad_normed
        - jnp.mean(grad_normed, -1, keepdims=True)
        - normed * jnp.mean(grad_normed * normed, -1, keepdims=True)
    )
    grad_attended = grad_attended.astype(b16)
    for h in range(HEADS):
        cv, cq, ck = [slice(i * hidden + h * HEAD_DIM, i * hidden + (h + 1) * HEAD_DIM) for i in (1, 2, 3)]
        part = grad_attended[:, h * HEAD_DIM : (h + 1) * HEAD_DIM]
        grad_attn = dot(part, proj[:, cv], NT)
        grad_score = (grad_attn * attn_slope[h].astype(f32)).astype(b16)
        grad[:, cv] = (dot(attn[h], part, TN) * slope[:, cv].astype(f32)).astype(b16)
        grad[:, cq] = (dot(grad_score, proj[:, ck], NN) * slope[:, cq].astype(f32)).astype(b16)
        grad[:, ck] = (dot(grad_score, proj[:, cq], TN) * slope[:, ck].astype(f32)).astype(b16)


def item_kernel(groups, owners, share, places, *refs):
    count = len(places)
    units, tags = refs[:count], refs[count : count + groups]
    own, others, far_own, far_others, keep, give, gathered, near, sems = refs[count + groups :]
    chips = owners // 2
    vocab_dev = share * groups
    grp = lax.axis_index("grp")
    tok = tags[0].shape[1]
    copies = []
    for n, (k, left, wide) in enumerate(places):
        copies.append(pltpu.make_async_copy(units[n], gathered.at[pl.ds(k * tok, tok), pl.ds(left, wide)], sems.at[n]))
    begin = pl.multiple_of(grp * share, share)
    for side, (full, part) in enumerate(((own, others), (far_own, far_others))):
        at, n = side * chips * share, count + 2 * side
        copies.append(pltpu.make_async_copy(full.at[pl.ds(begin, share)], near.at[pl.ds(at, share)], sems.at[n]))
        copies.append(
            pltpu.make_async_copy(part, near.at[pl.ds(at + share, (chips - 1) * share)], sems.at[n + 1])
        )
    for copy in copies:
        copy.start()
    ids = owner_ids(owners)
    amounts = jnp.concatenate([t[:owners] for t in tags], 1)
    chosen = jnp.concatenate([t[owners:] for t in tags], 1).astype(i32)
    for copy in copies:
        copy.wait()
    for side, out in ((0, keep), (1, give)):
        parts = []
        for d in range(chips):
            j = side * chips + d
            hit = ids[j] * vocab_dev + grp * share + iota((share, 1), 0) == chosen[j : j + 1]
            parts.append(jnp.where(hit, amounts[j : j + 1], 0.0).astype(b16))
        summed = dot(jnp.concatenate(parts, 0), gathered[...], NN)
        row = near[side * chips * share : (side + 1) * chips * share].astype(f32)
        out[...] = (summed - row * jnp.sum(row * summed, -1, keepdims=True)).astype(b16)


def weight_kernel(groups, owners, keep, give, up_keep, up_give, grad, far_grad, gated, far_gated, *refs):
    outs, whole = refs[:-1], refs[-1]
    chips = owners // 2
    grp = lax.axis_index("grp")
    wide = grad.shape[1]
    step = gated.shape[1]
    for i in range(0, wide, step):
        cols = slice(i, i + step)
        part = dot(keep[...], grad[:, cols], TN) + dot(give[...], far_grad[:, cols], TN)
        whole[:, cols] = part.astype(b16)
    part = dot(up_keep[...], gated[...], TN) + dot(up_give[...], far_gated[...], TN)
    whole[:, wide:] = part.astype(b16)
    rows = whole.shape[0] // chips
    fine = rows // groups
    half = whole.shape[1] // 2
    for z in range(chips):
        for k in range(groups):
            piece = whole[pl.ds(pl.multiple_of(z * rows + (grp ^ k) * fine, fine), fine)]
            if k == 3:
                outs[3][z] = piece[:, :half]
                outs[4][z] = piece[:, half:]
            else:
                outs[k][z] = piece


def assemble_kernel(groups, columns, *refs):
    parts, outs = refs[:groups], refs[groups:]
    grp = lax.axis_index("grp")
    fine = parts[0].shape[0]
    for k in range(groups):
        at = pl.ds(pl.multiple_of((grp ^ k) * fine, fine), fine)
        left = 0
        for out, wide in zip(outs, columns):
            out[at] = parts[k][:, left : left + wide].astype(f32)
            left += wide


def relay_kernel(arrived, out):
    tok, slots = out.shape[0], arrived.shape[0]
    filled = (arrived[:, :128].astype(f32) < EMPTY / 2).astype(b16)
    before = (iota((slots, 1), 0) > iota((1, slots), 1)).astype(b16)
    rank = dot(before, filled, NN)[:, :1].astype(i32)
    rank = jnp.where(filled[:, :1].astype(f32) > 0, rank, -1)
    place = (rank == iota((1, tok), 1)).astype(b16)
    out[...] = dot(place, arrived[...], TN).astype(b16)


def body(events, lengths, destinations, history, negatives, in_weight, out_weight, item_table):
    groups = lax.axis_size("grp")
    owners = lax.axis_size("seq")
    chips = owners // 2
    grp = lax.axis_index("grp")
    seq = lax.axis_index("seq")
    chip, core = seq // 2, seq % 2
    tok = events.shape[0]
    vocab_dev, width = item_table.shape
    hidden = out_weight.shape[1]
    share = vocab_dev // groups
    slot = 3 * tok // (2 * owners)
    rows = width // owners
    fine = rows // groups

    def to_chip(x, d):
        pairs = [(2 * a + b, 2 * ((a + d) % chips) + b) for a in range(chips) for b in range(2)]
        return lax.ppermute(x, "seq", pairs)

    def to_group(x, k):
        return lax.ppermute(x, "grp", [(a, a ^ k) for a in range(groups)])

    def to_core(x):
        return lax.ppermute(x, "seq", [(a, a ^ 1) for a in range(owners)])

    def gather_groups(x):
        wide = x.shape[1]
        if groups != 4:
            return [(k, 0, wide, to_group(x, k) if k else x) for k in range(groups)]
        one, two = to_group(x, 1), to_group(x, 2)
        half = wide // 2
        left, right = to_group(one[:, :half], 2), to_group(two[:, half:], 1)
        return [(0, 0, wide, x), (1, 0, wide, one), (2, 0, wide, two), (3, 0, half, left), (3, half, half, right)]

    own, quarter, quarter_inv = call(
        lambda *refs: normalise_kernel(share, *refs),
        [((vocab_dev, width), b16), ((share, width), b16), ((share, 1), f32)],
        [VMEM], [item_table], flops=8 * vocab_dev * width, nbytes=5 * vocab_dev * width, room=8,
    )
    got = [to_chip(quarter, d) for d in range(1, chips)]
    far_own = to_core(own)

    outs = [
        ((tok, width // 2), b16), ((tok, width // 2), b16), ((tok, 4 * hidden), b16), ((tok, 4 * hidden), b16),
        ((HEADS, tok, tok), b16), ((HEADS, tok, tok), b16), ((tok, hidden), f32), ((tok, 1), f32),
        ((tok, hidden), b16), ((tok, width), f32), ((tok, width), b16), ((tok, 1), f32),
        ((owners * slot, width), b16),
    ]
    (keep, give, proj, slope, attn, attn_slope, normed, inverse, gated, unit, unit_b, inv_len, outgoing) = call(
        lambda *refs: forward_kernel(owners, slot, *refs), outs, [SMEM, SMEM, VMEM, VMEM, VMEM],
        [lengths, destinations, events, in_weight, out_weight],
        flops=2 * tok * width * 6 * hidden, nbytes=24 * tok * width + 10 * width * hidden, room=28,
    )

    got, far_own, unit_b = lax.optimization_barrier((got, far_own, unit_b))
    others = jnp.concatenate(got, 0)
    pieces = [(0, -1, 0, width, own)] + [(0,) + p for p in gather_groups(others)]
    pieces = pieces + [(1, -1, 0, width, far_own)] + [(1,) + p[1:4] + (to_core(p[4]),) for p in pieces[1:]]
    far_others = [p[4] for p in pieces if p[0] == 1 and p[1] == 0][0]
    sent_unit, _ = lax.optimization_barrier((unit_b, [p[4] for p in pieces if p[0] == 0]))
    unit_sent = gather_groups(sent_unit)
    outgoing, others = lax.optimization_barrier((outgoing, others))

    arrived = lax.all_to_all(
        outgoing.reshape(owners, slot, width), "seq", 0, 0, tiled=True
    ).reshape(owners * slot, width)
    layer_out, = call(
        relay_kernel, [((tok, width), b16)], [VMEM], [arrived],
        flops=3 * tok * tok * width, nbytes=6 * tok * width, room=8,
    )

    candidates = jnp.concatenate([history[:, None], negatives], 1)
    vocab = vocab_dev * owners
    layer_out, score_unit = lax.optimization_barrier((layer_out, unit))
    units = [p[3] for p in unit_sent]
    tags, up, up_keep, up_give = call(
        lambda *refs: score_kernel(groups, owners, share, [p[:4] for p in pieces], *refs),
        [((2 * owners, tok), f32), ((tok, width), b16), ((tok, width // 2), b16), ((tok, width // 2), b16)],
        [VMEM] * 4 + [ANY] * len(pieces), [candidates, unit_b, score_unit, inv_len] + [p[4] for p in pieces],
        [pltpu.VMEM((vocab, width), b16), pltpu.VMEM((tok, vocab), b16), pltpu.SemaphoreType.DMA((len(pieces),))],
        flops=4 * tok * width * vocab, nbytes=2 * vocab * width + 12 * tok * width, room=24 if groups == 4 else 58,
    )

    all_tags = [to_group(tags, k) if k else tags for k in range(groups)]
    mine, other = call(
        lambda *refs: item_kernel(groups, owners, share, [p[:3] for p in unit_sent], *refs),
        [((chips * share, width), b16)] * 2, [ANY] * len(units) + [VMEM] * groups + [ANY] * 4,
        units + all_tags + [own, others, far_own, far_others],
        [pltpu.VMEM((groups * tok, width), b16), pltpu.VMEM((2 * chips * share, width), b16),
         pltpu.SemaphoreType.DMA((len(units) + 4,))],
        flops=4 * groups * tok * width * chips * share, nbytes=4 * tok * groups * width, room=16 if groups == 4 else 48,
    )
    far_mine = to_core(other)

    up, _ = lax.optimization_barrier((up, [p[3] for p in unit_sent[1:3]]))

    grad, = call(
        backward_kernel, [((tok, 4 * hidden), b16)], [VMEM] * 8,
        [up, out_weight, proj, slope, attn, attn_slope, normed, inverse],
        flops=2 * tok * width * hidden, nbytes=20 * tok * width,
    )

    far = [to_core(x) for x in (give, up_give, grad, gated)]
    far, mine = lax.optimization_barrier((far, mine))
    half = 5 * hidden // 2
    if groups == 4:
        block = (chips, fine, 5 * hidden)
        split = (chips, fine, half)
        parts = call(
            lambda *refs: weight_kernel(groups, owners, *refs),
            [(block, b16)] * 3 + [(split, b16)] * 2, [VMEM] * 8,
            [keep, far[0], up_keep, far[1], grad, far[2], gated, far[3]],
            [pltpu.VMEM((width // 2, 5 * hidden), b16)],
            flops=2 * tok * width * 5 * hidden, nbytes=20 * tok * width, room=14,
        )
        left, right = to_group(parts[3], 1).astype(f32), to_group(parts[4], 2).astype(f32)
        one, two = parts[1].astype(f32), parts[2].astype(f32)
        one = jnp.concatenate([one[..., :half], one[..., half:] + right], 2).astype(b16)
        two = jnp.concatenate([two[..., :half] + left, two[..., half:]], 2).astype(b16)
        sums = parts[0].astype(f32) + to_group(one, 1).astype(f32) + to_group(two, 2).astype(f32)
    else:
        def both(x, y):
            return jnp.concatenate([x, y], 0)

        in_part = dot(both(keep, far[0]), both(grad, far[2]), TN)
        out_part = dot(both(up_keep, far[1]), both(gated, far[3]), TN)
        weight = jnp.concatenate([in_part, out_part], 1).astype(b16)
        weight = weight.reshape(chips, groups, fine, 5 * hidden)
        sums = lax.dynamic_index_in_dim(weight, grp, 1, False).astype(f32)
        for k in range(1, groups):
            sums += to_group(lax.dynamic_index_in_dim(weight, grp ^ k, 1, False), k).astype(f32)
    sums = sums.astype(b16)

    summed = (mine.astype(f32) + far_mine.astype(f32)).astype(b16).reshape(chips, share, width)
    total = summed[0].astype(f32)
    for d in range(1, chips):
        total += to_chip(summed[d], -d).astype(f32)
    total = (total * quarter_inv).astype(b16)
    table_grad, = call(
        lambda *refs: assemble_kernel(groups, [width], *refs), [((vocab_dev, width), f32)], [VMEM] * groups,
        [to_group(total, k) if k else total for k in range(groups)],
        flops=vocab_dev * width, nbytes=6 * vocab_dev * width, room=8,
    )

    line = lax.dynamic_index_in_dim(sums, chip, 0, False).astype(f32)
    for d in range(1, chips):
        line += to_chip(lax.dynamic_index_in_dim(sums, (chip + d) % chips, 0, False), d).astype(f32)
    line = line.astype(b16)
    lines = [to_group(line, k) if k else line for k in range(groups)]
    if fine % 16 == 0:
        in_grad, out_grad = call(
            lambda *refs: assemble_kernel(groups, [4 * hidden, hidden], *refs),
            [((rows, 4 * hidden), f32), ((rows, hidden), f32)], [VMEM] * groups, lines,
            flops=rows * hidden, nbytes=30 * rows * hidden, room=8,
        )
    else:
        shard = jnp.zeros((rows, 5 * hidden), f32)
        for k in range(groups):
            shard = lax.dynamic_update_slice_in_dim(shard, lines[k].astype(f32), (grp ^ k) * fine, 0)
        in_grad, out_grad = shard[:, : 4 * hidden], shard[:, 4 * hidden :]
    return (layer_out, in_grad, out_grad, table_grad)


def solution(mesh):
    return jax.shard_map(
        body,
        mesh=mesh,
        in_specs=(
            P(("grp", "seq"), None),
            P(("grp", "seq"), None),
            P(("grp", "seq"), None),
            P(("grp", "seq")),
            P(("grp", "seq"), None),
            P(),
            P(),
            P("seq", None),
        ),
        out_specs=(P(("grp", "seq"), None), P("seq", None), P("seq", None), P("seq", None)),
        check_vma=False,
    )
```

```python
import jax
import jax.numpy as jnp
from jax import lax
from jax.experimental import pallas as pl
from jax.experimental.pallas import tpu as pltpu
from jax.sharding import PartitionSpec as P

HEADS = 4
HEAD_DIM = 128
NCAND = 4

epsilon = 1e-05
softmax_warmth = 0.05
EMPTY = 2.0**100

f32, b16, i32 = jnp.float32, jnp.bfloat16, jnp.int32
NN = ((1,), (0,))
NT = ((1,), (1,))
TN = ((0,), (0,))
VMEM = pl.BlockSpec(memory_space=pltpu.VMEM)
SMEM = pl.BlockSpec(memory_space=pltpu.SMEM)
ANY = pl.BlockSpec(memory_space=pl.ANY)


def dot(a, b, dims):
    return lax.dot_general(a, b, (dims, ((), ())), preferred_element_type=f32)


def iota(shape, axis):
    return lax.broadcasted_iota(i32, shape, axis)


def center_scale(values):
    average = jnp.mean(values, -1, keepdims=True)
    centered = values - average
    inverse = lax.rsqrt(jnp.mean(centered * centered, -1, keepdims=True) + epsilon)
    return (centered * inverse, inverse)


def sigmoid(values):
    return 1.0 / (1.0 + jnp.exp(-values))


def split_columns(x, owners, core):
    rows = x.shape[1] // owners
    blocks = [x[:, i * rows : (i + 1) * rows] for i in range(owners)]
    even, odd = jnp.concatenate(blocks[0::2], 1), jnp.concatenate(blocks[1::2], 1)
    first = jnp.broadcast_to(core, even.shape) == 0
    return jnp.where(first, even, odd), jnp.where(first, odd, even)


def call(kernel, out, specs, args, scratch=(), flops=0, nbytes=0, room=14):
    return pl.pallas_call(
        kernel,
        out_shape=[jax.ShapeDtypeStruct(s, t) for s, t in out],
        in_specs=specs,
        out_specs=[VMEM] * len(out),
        scratch_shapes=list(scratch),
        cost_estimate=pl.CostEstimate(flops=flops, bytes_accessed=nbytes, transcendentals=0),
        compiler_params=pltpu.CompilerParams(vmem_limit_bytes=room * 2**20),
    )(*args)


def forward_kernel(
    owners, slot, lengths, dests, events, in_weight, out_weight,
    keep, give, proj, slope, attn, attn_slope, normed_out, inv_out, gated_out, unit, unit_b, inv_len, outgoing,
):
    tok = events.shape[0]
    hidden = out_weight.shape[1]
    scale = HEAD_DIM ** (-0.5)
    core = lax.axis_index("seq") % 2
    x = events[...].astype(f32)
    normed_in = center_scale(x)[0]
    mine, other = split_columns(normed_in, owners, core)
    keep[...] = mine.astype(b16)
    give[...] = other.astype(b16)
    normed_in = normed_in.astype(b16)
    for i in range(4):
        cols = slice(i * hidden, (i + 1) * hidden)
        p = dot(normed_in, in_weight[:, cols], NN)
        sig = sigmoid(p)
        proj[:, cols] = (p * sig).astype(b16)
        slope[:, cols] = (sig * (1.0 + p * (1.0 - sig))).astype(b16)

    pos_c, pos_r = iota((tok, 1), 0), iota((1, tok), 1)
    user_c, user_r = jnp.zeros((tok, 1), i32), jnp.zeros((1, tok), i32)
    target = jnp.zeros((1, tok), i32)
    start = jnp.int32(0)
    for j in range(lengths.shape[1]):
        end = start + lengths[0, j]
        user_c += (pos_c >= end).astype(i32)
        user_r += (pos_r >= end).astype(i32)
        here = (pos_r >= start) & (pos_r < end)
        target = jnp.where(here, dests[0, j] * slot + pos_r - start, target)
        start = end
    mask = (user_c == user_r) & (pos_r <= pos_c)

    outputs = []
    for h in range(HEADS):
        v = proj[:, hidden + h * HEAD_DIM : hidden + (h + 1) * HEAD_DIM]
        q = proj[:, 2 * hidden + h * HEAD_DIM : 2 * hidden + (h + 1) * HEAD_DIM]
        k = proj[:, 3 * hidden + h * HEAD_DIM : 3 * hidden + (h + 1) * HEAD_DIM]
        s = dot(q, k, NT) * scale
        sig = sigmoid(s)
        weight = jnp.where(mask, s * sig, 0.0).astype(b16)
        attn[h] = weight
        attn_slope[h] = jnp.where(mask, sig * (1.0 + s * (1.0 - sig)) * scale, 0.0).astype(b16)
        outputs.append(dot(weight, v, NN))
    normed, inverse = center_scale(jnp.concatenate(outputs, 1))
    normed_out[...] = normed
    inv_out[...] = inverse
    gated = (normed * proj[:, :hidden].astype(f32)).astype(b16)
    gated_out[...] = gated
    result = x + dot(gated, out_weight[...], NT)
    inverse = lax.rsqrt(jnp.sum(result * result, -1, keepdims=True) + epsilon)
    inv_len[...] = inverse
    yn = result * inverse
    unit[...] = yn
    unit_b[...] = yn.astype(b16)
    row = iota((outgoing.shape[0], 1), 0)
    filled = jnp.zeros(row.shape, i32)
    for j in range(lengths.shape[1]):
        at = dests[0, j] * slot
        filled = jnp.where((row >= at) & (row < at + lengths[0, j]), 1, filled)
    placed = dot((row == target).astype(b16), result.astype(b16), NN)
    outgoing[...] = jnp.where(filled == 1, placed, EMPTY).astype(b16)


def owner_ids(owners):
    seq = lax.axis_index("seq")
    chip, core = seq // 2, seq % 2
    chips = owners // 2
    return [2 * ((chip + chips - d) % chips) + (core ^ side) for side in range(2) for d in range(chips)]


def normalise_kernel(share, item_table, own, quarter, quarter_inv):
    grp = lax.axis_index("grp")
    x = item_table[...].astype(f32)
    own[...] = (x * lax.rsqrt(jnp.sum(x * x, -1, keepdims=True) + epsilon)).astype(b16)
    x = item_table[pl.ds(pl.multiple_of(grp * share, share), share)].astype(f32)
    inverse = lax.rsqrt(jnp.sum(x * x, -1, keepdims=True) + epsilon)
    quarter[...] = (x * inverse).astype(b16)
    quarter_inv[...] = inverse


def score_kernel(groups, owners, share, chunks, places, final, cand, unit_hbm, *refs):
    count = len(places)
    if final:
        inv_len, partial, yn_hbm, *refs = refs
        pieces, (tags, up, up_keep, up_give, table, unit_b, sems, spread, unit) = refs[:count], refs[count:]
    else:
        pieces, (partial_out, table, unit_b, sems) = refs[:count], refs[count:]
    chips = owners // 2
    vocab_dev = share * groups
    grp, core = lax.axis_index("grp"), lax.axis_index("seq") % 2
    tok = unit_b.shape[0]
    block = vocab_dev + groups * (chips - 1) * share

    def place(key):
        side, chunk, k = key
        if chunk < 0:
            return side * block, vocab_dev
        before = sum(len(ds) for ds in chunks[:chunk]) * groups * share
        rows = len(chunks[chunk]) * share
        return side * block + vocab_dev + before + k * rows, rows

    load_unit = pltpu.make_async_copy(unit_hbm, unit_b, sems.at[count])
    load_unit.start()
    copies = {}
    for n, (*key, left, wide) in enumerate(places):
        at, rows = place(key)
        copy = pltpu.make_async_copy(pieces[n], table.at[pl.ds(at, rows), pl.ds(left, wide)], sems.at[n])
        copy.start()
        copies.setdefault(tuple(key), []).append(copy)
    if final:
        load_yn = pltpu.make_async_copy(yn_hbm, unit, sems.at[count + 1])
        load_yn.start()
    ids = owner_ids(owners)
    lane = iota((1, 128), 1)
    owner = jnp.full((1, 128), -1, i32)
    for j in range(owners):
        owner = jnp.where(lane == j, ids[j], owner)
    candidates = cand[...]
    chosen = jnp.full((tok, 128), -1, i32)
    first = jnp.zeros((tok, 128), f32)
    for c in range(NCAND):
        here = candidates[:, c : c + 1] // vocab_dev == owner
        chosen = jnp.where(here, candidates[:, c : c + 1], chosen)
        if c == 0:
            first = here.astype(f32)
    wanted = [jnp.broadcast_to(chosen[:, j : j + 1], (tok, 128)) for j in range(owners)]

    def runs(key):
        side, chunk, k = key
        at, rows = place(key)
        if chunk < 0:
            return at, rows, [(side * chips, 0, vocab_dev, ids[side * chips] * vocab_dev)]
        begin = (grp ^ k) * share
        return at, rows, [
            (side * chips + d, i * share, share, ids[side * chips + d] * vocab_dev + begin)
            for i, d in enumerate(chunks[chunk])
        ]

    def tiles(key):
        at, rows, here = runs(key)
        for j, off, wide, base in here:
            step = min(wide, 128)
            for o in range(0, wide, step):
                hit = wanted[j][:, :step] == base + o + iota((1, step), 1)
                yield j, off + o, step, hit

    load_unit.wait()
    yb = unit_b[...]
    value = [[] for _ in range(owners)]
    for key in copies:
        for copy in copies[key]:
            copy.wait()
        if key[0] != int(final):
            continue
        at, rows, _ = runs(key)
        product = dot(yb, table[at : at + rows], NT)
        for j, off, step, hit in tiles(key):
            value[j].append(jnp.where(hit, product[:, off : off + step], 0.0))
    logits = partial[...] if final else jnp.zeros((tok, 128), f32)
    for j in range(owners):
        if not value[j]:
            continue
        total = value[j][0]
        for part in value[j][1:]:
            total = total + part
        logits = jnp.where(lane == j, jnp.sum(total, -1, keepdims=True), logits)
    if not final:
        partial_out[...] = logits
        return
    exponent = jnp.where(chosen >= 0, jnp.exp(logits / softmax_warmth), 0.0)
    coef = (exponent / jnp.sum(exponent, -1, keepdims=True) - first) / softmax_warmth
    tags[:owners] = coef.T[:owners]
    tags[owners:] = chosen.astype(f32).T[:owners]
    amount = [jnp.broadcast_to(coef[:, j : j + 1], (tok, 128)) for j in range(owners)]
    for key in copies:
        at = runs(key)[0]
        for j, off, step, hit in tiles(key):
            spread[:, at + off : at + off + step] = jnp.where(hit, amount[j][:, :step], 0.0).astype(b16)
    pulled = dot(spread[...], table[...], NN)
    load_yn.wait()
    yn = unit[...]
    upstream = (pulled - yn * jnp.sum(yn * pulled, -1, keepdims=True)) * inv_len[...]
    up[...] = upstream.astype(b16)
    mine, other = split_columns(upstream, owners, core)
    up_keep[...] = mine.astype(b16)
    up_give[...] = other.astype(b16)


def backward_kernel(up, out_weight, proj, slope, attn, attn_slope, normed_ref, inverse, grad):
    hidden = out_weight.shape[1]
    normed = normed_ref[...]
    grad_gated = dot(up[...], out_weight[...], NN)
    grad[:, :hidden] = (grad_gated * normed * slope[:, :hidden].astype(f32)).astype(b16)
    grad_normed = grad_gated * proj[:, :hidden].astype(f32)
    grad_attended = inverse[...] * (
        grad_normed
        - jnp.mean(grad_normed, -1, keepdims=True)
        - normed * jnp.mean(grad_normed * normed, -1, keepdims=True)
    )
    grad_attended = grad_attended.astype(b16)
    for h in range(HEADS):
        cv, cq, ck = [slice(i * hidden + h * HEAD_DIM, i * hidden + (h + 1) * HEAD_DIM) for i in (1, 2, 3)]
        part = grad_attended[:, h * HEAD_DIM : (h + 1) * HEAD_DIM]
        grad_attn = dot(part, proj[:, cv], NT)
        grad_score = (grad_attn * attn_slope[h].astype(f32)).astype(b16)
        grad[:, cv] = (dot(attn[h], part, TN) * slope[:, cv].astype(f32)).astype(b16)
        grad[:, cq] = (dot(grad_score, proj[:, ck], NN) * slope[:, cq].astype(f32)).astype(b16)
        grad[:, ck] = (dot(grad_score, proj[:, cq], TN) * slope[:, ck].astype(f32)).astype(b16)


def item_kernel(groups, owners, share, chunks, places, *refs):
    count = len(places)
    units, tags = refs[:count], refs[count : count + groups]
    parts, (keep, give, gathered, near, sems) = refs[count + groups : -5], refs[-5:]
    chips = owners // 2
    vocab_dev = share * groups
    grp = lax.axis_index("grp")
    tok = tags[0].shape[1]
    copies = []
    for n, (k, left, wide) in enumerate(places):
        copies.append(pltpu.make_async_copy(units[n], gathered.at[pl.ds(k * tok, tok), pl.ds(left, wide)], sems.at[n]))
    begin = pl.multiple_of(grp * share, share)
    for n, part in enumerate(parts):
        side, chunk = n // (len(chunks) + 1), n % (len(chunks) + 1) - 1
        for i, d in enumerate([0] if chunk < 0 else chunks[chunk]):
            rows = pl.ds(begin if chunk < 0 else i * share, share)
            at = pl.ds((side * chips + d) * share, share)
            copies.append(pltpu.make_async_copy(part.at[rows], near.at[at], sems.at[len(copies)]))
    for copy in copies:
        copy.start()
    ids = owner_ids(owners)
    amounts = jnp.concatenate([t[:owners] for t in tags], 1)
    chosen = jnp.concatenate([t[owners:] for t in tags], 1).astype(i32)
    for copy in copies:
        copy.wait()
    for side, out in ((0, keep), (1, give)):
        parts = []
        for d in range(chips):
            j = side * chips + d
            hit = ids[j] * vocab_dev + grp * share + iota((share, 1), 0) == chosen[j : j + 1]
            parts.append(jnp.where(hit, amounts[j : j + 1], 0.0).astype(b16))
        summed = dot(jnp.concatenate(parts, 0), gathered[...], NN)
        row = near[side * chips * share : (side + 1) * chips * share].astype(f32)
        out[...] = (summed - row * jnp.sum(row * summed, -1, keepdims=True)).astype(b16)


def weight_kernel(groups, owners, keep, give, up_keep, up_give, grad, far_grad, gated, far_gated, *refs):
    outs, whole = refs[:-1], refs[-1]
    chips = owners // 2
    grp = lax.axis_index("grp")
    wide = grad.shape[1]
    step = gated.shape[1]
    for i in range(0, wide, step):
        cols = slice(i, i + step)
        part = dot(keep[...], grad[:, cols], TN) + dot(give[...], far_grad[:, cols], TN)
        whole[:, cols] = part.astype(b16)
    part = dot(up_keep[...], gated[...], TN) + dot(up_give[...], far_gated[...], TN)
    whole[:, wide:] = part.astype(b16)
    rows = whole.shape[0] // chips
    fine = rows // groups
    half = whole.shape[1] // 2
    for z in range(chips):
        for k in range(groups):
            piece = whole[pl.ds(pl.multiple_of(z * rows + (grp ^ k) * fine, fine), fine)]
            if k == 0:
                outs[0][z] = piece
            else:
                outs[2 * k - 1][z] = piece[:, :half]
                outs[2 * k][z] = piece[:, half:]


def sum_kernel(halves, base, *refs):
    parts, outs = refs[: 2 * halves], refs[2 * halves :]
    chips = len(outs)
    chip = lax.axis_index("seq") // 2
    half = base.shape[2] // 2
    for d in range(chips):
        z = lax.rem(chip + d, chips)
        for i in range(2):
            cols = slice(i * half, (i + 1) * half)
            total = base[z][:, cols].astype(f32)
            for n in range(halves):
                total += parts[2 * n + i][z].astype(f32)
            outs[d][:, cols] = total.astype(b16)


def pair_kernel(x, y, *outs):
    rows = outs[0].shape[0]
    for d, out in enumerate(outs):
        at = slice(d * rows, (d + 1) * rows)
        out[...] = (x[at].astype(f32) + y[at].astype(f32)).astype(b16)


def assemble_kernel(groups, columns, *refs):
    parts, outs = refs[:groups], refs[groups:]
    grp = lax.axis_index("grp")
    fine = parts[0].shape[0]
    for k in range(groups):
        at = pl.ds(pl.multiple_of((grp ^ k) * fine, fine), fine)
        left = 0
        for out, wide in zip(outs, columns):
            out[at] = parts[k][:, left : left + wide].astype(f32)
            left += wide


def relay_kernel(arrived, out):
    tok, slots = out.shape[0], arrived.shape[0]
    filled = (arrived[:, :128].astype(f32) < EMPTY / 2).astype(b16)
    before = (iota((slots, 1), 0) > iota((1, slots), 1)).astype(b16)
    rank = dot(before, filled, NN)[:, :1].astype(i32)
    rank = jnp.where(filled[:, :1].astype(f32) > 0, rank, -1)
    place = (rank == iota((1, tok), 1)).astype(b16)
    out[...] = dot(place, arrived[...], TN).astype(b16)


def body(events, lengths, destinations, history, negatives, in_weight, out_weight, item_table):
    groups = lax.axis_size("grp")
    owners = lax.axis_size("seq")
    chips = owners // 2
    grp = lax.axis_index("grp")
    seq = lax.axis_index("seq")
    chip, core = seq // 2, seq % 2
    tok = events.shape[0]
    vocab_dev, width = item_table.shape
    hidden = out_weight.shape[1]
    share = vocab_dev // groups
    slot = 3 * tok // (2 * owners)
    rows = width // owners
    fine = rows // groups

    def to_chip(x, d):
        pairs = [(2 * a + b, 2 * ((a + d) % chips) + b) for a in range(chips) for b in range(2)]
        return lax.ppermute(x, "seq", pairs)

    def to_group(x, k):
        return lax.ppermute(x, "grp", [(a, a ^ k) for a in range(groups)])

    def to_core(x):
        return lax.ppermute(x, "seq", [(a, a ^ 1) for a in range(owners)])

    def gather_groups(x, near=None):
        wide = x.shape[1]
        if groups != 4:
            return [(k, 0, wide, to_group(x, k) if k else x) for k in range(groups)]
        one, two = near or [to_group(x, k) for k in (1, 2)]
        half = wide // 2
        left, right = to_group(one[:, :half], 2), to_group(two[:, half:], 1)
        return [(0, 0, wide, x), (1, 0, wide, one), (2, 0, wide, two), (3, 0, half, left), (3, half, half, right)]

    own, quarter, quarter_inv = call(
        lambda *refs: normalise_kernel(share, *refs),
        [((vocab_dev, width), b16), ((share, width), b16), ((share, 1), f32)],
        [VMEM], [item_table], flops=8 * vocab_dev * width, nbytes=5 * vocab_dev * width, room=8,
    )
    chunks = [[d for d in range(1, chips) if d % 2 == 0], [d for d in range(1, chips) if d % 2]]
    even = [to_chip(quarter, d) for d in chunks[0]]
    even, later = lax.optimization_barrier((even, quarter))
    odd = [to_chip(later, d) for d in chunks[1]]
    far_own = to_core(own)
    outs = [
        ((tok, width // 2), b16), ((tok, width // 2), b16), ((tok, 4 * hidden), b16), ((tok, 4 * hidden), b16),
        ((HEADS, tok, tok), b16), ((HEADS, tok, tok), b16), ((tok, hidden), f32), ((tok, 1), f32),
        ((tok, hidden), b16), ((tok, width), f32), ((tok, width), b16), ((tok, 1), f32),
        ((owners * slot, width), b16),
    ]
    (keep, give, proj, slope, attn, attn_slope, normed, inverse, gated, unit, unit_b, inv_len, outgoing) = call(
        lambda *refs: forward_kernel(owners, slot, *refs), outs, [SMEM, SMEM, VMEM, VMEM, VMEM],
        [lengths, destinations, events, in_weight, out_weight],
        flops=2 * tok * width * 6 * hidden, nbytes=24 * tok * width + 10 * width * hidden, room=28,
    )

    even = jnp.concatenate(even, 0) if len(even) > 1 else even[0]
    near = [to_group(even, k) for k in (1, 2)]
    odd, far_own, unit_b, near = lax.optimization_barrier((odd, far_own, unit_b, near))
    others = [even, jnp.concatenate(odd, 0)]
    pieces = [(0, -1, 0, 0, width, own)]
    for j, x in enumerate(others):
        pieces += [(0, j) + p for p in gather_groups(x, None if j else near)]
    pieces = pieces + [(1,) + p[1:5] + (to_core(p[5]) if p[1] >= 0 else far_own,) for p in pieces]
    near = [p[5] for p in pieces if p[2] == 0]
    outgoing, _ = lax.optimization_barrier((outgoing, others))

    arrived = lax.all_to_all(
        outgoing.reshape(owners, slot, width), "seq", 0, 0, tiled=True
    ).reshape(owners * slot, width)
    layer_out, = call(
        relay_kernel, [((tok, width), b16)], [VMEM], [arrived],
        flops=3 * tok * tok * width, nbytes=6 * tok * width, room=8,
    )

    candidates = jnp.concatenate([history[:, None], negatives], 1)
    vocab = vocab_dev * owners
    far_give, far_gated = to_core(give), to_core(gated)
    mine = [p for p in pieces if p[0] == 0]
    partial, = call(
        lambda *refs: score_kernel(groups, owners, share, chunks, [p[:5] for p in mine], False, *refs),
        [((tok, 128), f32)], [VMEM] + [ANY] * (len(mine) + 1), [candidates, unit_b] + [p[5] for p in mine],
        [pltpu.VMEM((vocab // 2, width), b16), pltpu.VMEM((tok, width), b16),
         pltpu.SemaphoreType.DMA((len(mine) + 1,))],
        flops=tok * width * vocab, nbytes=vocab * width + 2 * tok * width, room=14 if groups == 4 else 40,
    )
    sent_unit, _ = lax.optimization_barrier((unit_b, partial))
    unit_sent = gather_groups(sent_unit)
    layer_out, partial, far_give, far_gated = lax.optimization_barrier((layer_out, partial, far_give, far_gated))
    order = [p for p in pieces if p[0] == 1] + mine
    tags, up, up_keep, up_give = call(
        lambda *refs: score_kernel(groups, owners, share, chunks, [p[:5] for p in order], True, *refs),
        [((2 * owners, tok), f32), ((tok, width), b16), ((tok, width // 2), b16), ((tok, width // 2), b16)],
        [VMEM, ANY, VMEM, VMEM] + [ANY] * (len(order) + 1),
        [candidates, unit_b, inv_len, partial, unit] + [p[5] for p in order],
        [pltpu.VMEM((vocab, width), b16), pltpu.VMEM((tok, width), b16), pltpu.SemaphoreType.DMA((len(order) + 2,)),
         pltpu.VMEM((tok, vocab), b16), pltpu.VMEM((tok, width), f32)],
        flops=3 * tok * width * vocab, nbytes=2 * vocab * width + 12 * tok * width, room=24 if groups == 4 else 58,
    )
    units = [p[3] for p in unit_sent]

    up, _ = lax.optimization_barrier((up, [p[3] for p in unit_sent[1:3]]))

    grad, = call(
        backward_kernel, [((tok, 4 * hidden), b16)], [VMEM] * 8,
        [up, out_weight, proj, slope, attn, attn_slope, normed, inverse],
        flops=2 * tok * width * hidden, nbytes=20 * tok * width,
    )

    all_tags = [to_group(tags, k) if k else tags for k in range(groups)]
    far = [far_give, to_core(up_give), to_core(grad), far_gated]
    mine, other = call(
        lambda *refs: item_kernel(groups, owners, share, chunks, [p[:3] for p in unit_sent], *refs),
        [((chips * share, width), b16)] * 2, [ANY] * len(units) + [VMEM] * groups + [ANY] * len(near),
        units + all_tags + near,
        [pltpu.VMEM((groups * tok, width), b16), pltpu.VMEM((2 * chips * share, width), b16),
         pltpu.SemaphoreType.DMA((len(units) + 2 * chips,))],
        flops=4 * groups * tok * width * chips * share, nbytes=4 * tok * groups * width, room=16 if groups == 4 else 48,
    )
    far_mine = to_core(other)
    far, mine = lax.optimization_barrier((far, mine))
    half = 5 * hidden // 2
    if groups == 4:
        block = (chips, fine, 5 * hidden)
        split = (chips, fine, half)
        parts = call(
            lambda *refs: weight_kernel(groups, owners, *refs),
            [(block, b16)] + [(split, b16)] * 6, [VMEM] * 8,
            [keep, far[0], up_keep, far[1], grad, far[2], gated, far[3]],
            [pltpu.VMEM((width // 2, 5 * hidden), b16)],
            flops=2 * tok * width * 5 * hidden, nbytes=20 * tok * width, room=14,
        )
        left, right = to_group(parts[5], 1), to_group(parts[6], 2)
        one_left, two_right = to_group(parts[1], 1), to_group(parts[4], 2)
        one_right = (parts[2].astype(f32) + right.astype(f32)).astype(b16)
        two_left = (parts[3].astype(f32) + left.astype(f32)).astype(b16)
        arrived = [one_left, to_group(one_right, 1), to_group(two_left, 2), two_right]
    else:
        def both(x, y):
            return jnp.concatenate([x, y], 0)

        in_part = dot(both(keep, far[0]), both(grad, far[2]), TN)
        out_part = dot(both(up_keep, far[1]), both(gated, far[3]), TN)
        weight = jnp.concatenate([in_part, out_part], 1).astype(b16)
        weight = weight.reshape(chips, groups, fine, 5 * hidden)
        sums = lax.dynamic_index_in_dim(weight, grp, 1, False).astype(f32)
        for k in range(1, groups):
            sums += to_group(lax.dynamic_index_in_dim(weight, grp ^ k, 1, False), k).astype(f32)


    summed = call(
        pair_kernel, [((share, width), b16)] * chips, [VMEM] * 2, [mine, far_mine],
        flops=chips * share * width, nbytes=6 * chips * share * width, room=8,
    )
    come = [to_chip(summed[d], -d) for d in range(1, chips)]
    total = summed[0].astype(f32)
    for x in come:
        total += x.astype(f32)
    total = (total * quarter_inv).astype(b16)
    table_grad, = call(
        lambda *refs: assemble_kernel(groups, [width], *refs), [((vocab_dev, width), f32)], [VMEM] * groups,
        [to_group(total, k) if k else total for k in range(groups)],
        flops=vocab_dev * width, nbytes=6 * vocab_dev * width, room=8,
    )

    if groups == 4:
        base, _ = lax.optimization_barrier((parts[0], come[0]))
        sums = call(
            lambda *refs: sum_kernel(2, *refs), [((fine, 5 * hidden), b16)] * chips, [VMEM] * 5, [base] + arrived,
            flops=chips * fine * 5 * hidden, nbytes=40 * chips * fine * hidden, room=10,
        )
    else:
        sums = [
            lax.dynamic_index_in_dim(sums, (chip + d) % chips, 0, False).astype(b16) for d in range(chips)
        ]
    line = sums[0].astype(f32)
    for d in range(1, chips):
        line += to_chip(sums[d], d).astype(f32)
    line = line.astype(b16)
    lines = [to_group(line, k) if k else line for k in range(groups)]
    if fine % 16 == 0:
        in_grad, out_grad = call(
            lambda *refs: assemble_kernel(groups, [4 * hidden, hidden], *refs),
            [((rows, 4 * hidden), f32), ((rows, hidden), f32)], [VMEM] * groups, lines,
            flops=rows * hidden, nbytes=30 * rows * hidden, room=8,
        )
    else:
        shard = jnp.zeros((rows, 5 * hidden), f32)
        for k in range(groups):
            shard = lax.dynamic_update_slice_in_dim(shard, lines[k].astype(f32), (grp ^ k) * fine, 0)
        in_grad, out_grad = shard[:, : 4 * hidden], shard[:, 4 * hidden :]
    return (layer_out, in_grad, out_grad, table_grad)


def solution(mesh):
    return jax.shard_map(
        body,
        mesh=mesh,
        in_specs=(
            P(("grp", "seq"), None),
            P(("grp", "seq"), None),
            P(("grp", "seq"), None),
            P(("grp", "seq")),
            P(("grp", "seq"), None),
            P(),
            P(),
            P("seq", None),
        ),
        out_specs=(P(("grp", "seq"), None), P("seq", None), P("seq", None), P("seq", None)),
        check_vma=False,
    )
```

```python
import jax
import jax.numpy as jnp
from jax import lax
from jax.experimental import pallas as pl
from jax.experimental.pallas import tpu as pltpu
from jax.sharding import PartitionSpec as P

HEADS = 4
HEAD_DIM = 128
NCAND = 4

epsilon = 1e-05
softmax_warmth = 0.05
EMPTY = 2.0**100

f32, b16, i32 = jnp.float32, jnp.bfloat16, jnp.int32
NN = ((1,), (0,))
NT = ((1,), (1,))
TN = ((0,), (0,))
VMEM = pl.BlockSpec(memory_space=pltpu.VMEM)
SMEM = pl.BlockSpec(memory_space=pltpu.SMEM)
ANY = pl.BlockSpec(memory_space=pl.ANY)


def dot(a, b, dims):
    return lax.dot_general(a, b, (dims, ((), ())), preferred_element_type=f32)


def iota(shape, axis):
    return lax.broadcasted_iota(i32, shape, axis)


def center_scale(values):
    average = jnp.mean(values, -1, keepdims=True)
    centered = values - average
    inverse = lax.rsqrt(jnp.mean(centered * centered, -1, keepdims=True) + epsilon)
    return (centered * inverse, inverse)


def sigmoid(values):
    return 1.0 / (1.0 + jnp.exp(-values))


def split_columns(x, owners, core):
    rows = x.shape[1] // owners
    blocks = [x[:, i * rows : (i + 1) * rows] for i in range(owners)]
    even, odd = jnp.concatenate(blocks[0::2], 1), jnp.concatenate(blocks[1::2], 1)
    first = jnp.broadcast_to(core, even.shape) == 0
    return jnp.where(first, even, odd), jnp.where(first, odd, even)


def call(kernel, out, specs, args, scratch=(), flops=0, nbytes=0, room=14):
    return pl.pallas_call(
        kernel,
        out_shape=[jax.ShapeDtypeStruct(s, t) for s, t in out],
        in_specs=specs,
        out_specs=[VMEM] * len(out),
        scratch_shapes=list(scratch),
        cost_estimate=pl.CostEstimate(flops=flops, bytes_accessed=nbytes, transcendentals=0),
        compiler_params=pltpu.CompilerParams(vmem_limit_bytes=room * 2**20),
    )(*args)


def forward_kernel(
    owners, slot, lengths, dests, events, in_weight, out_weight,
    keep, give, proj, slope, attn, attn_slope, normed_out, inv_out, gated_out, unit, unit_b, inv_len, outgoing,
):
    tok = events.shape[0]
    hidden = out_weight.shape[1]
    scale = HEAD_DIM ** (-0.5)
    core = lax.axis_index("seq") % 2
    x = events[...].astype(f32)
    normed_in = center_scale(x)[0]
    mine, other = split_columns(normed_in, owners, core)
    keep[...] = mine.astype(b16)
    give[...] = other.astype(b16)
    normed_in = normed_in.astype(b16)
    for i in range(4):
        cols = slice(i * hidden, (i + 1) * hidden)
        p = dot(normed_in, in_weight[:, cols], NN)
        sig = sigmoid(p)
        proj[:, cols] = (p * sig).astype(b16)
        slope[:, cols] = (sig * (1.0 + p * (1.0 - sig))).astype(b16)

    pos_c, pos_r = iota((tok, 1), 0), iota((1, tok), 1)
    user_c, user_r = jnp.zeros((tok, 1), i32), jnp.zeros((1, tok), i32)
    target = jnp.zeros((1, tok), i32)
    start = jnp.int32(0)
    for j in range(lengths.shape[1]):
        end = start + lengths[0, j]
        user_c += (pos_c >= end).astype(i32)
        user_r += (pos_r >= end).astype(i32)
        here = (pos_r >= start) & (pos_r < end)
        target = jnp.where(here, dests[0, j] * slot + pos_r - start, target)
        start = end
    mask = (user_c == user_r) & (pos_r <= pos_c)

    outputs = []
    for h in range(HEADS):
        v = proj[:, hidden + h * HEAD_DIM : hidden + (h + 1) * HEAD_DIM]
        q = proj[:, 2 * hidden + h * HEAD_DIM : 2 * hidden + (h + 1) * HEAD_DIM]
        k = proj[:, 3 * hidden + h * HEAD_DIM : 3 * hidden + (h + 1) * HEAD_DIM]
        s = dot(q, k, NT) * scale
        sig = sigmoid(s)
        weight = jnp.where(mask, s * sig, 0.0).astype(b16)
        attn[h] = weight
        attn_slope[h] = jnp.where(mask, sig * (1.0 + s * (1.0 - sig)) * scale, 0.0).astype(b16)
        outputs.append(dot(weight, v, NN))
    normed, inverse = center_scale(jnp.concatenate(outputs, 1))
    normed_out[...] = normed
    inv_out[...] = inverse
    gated = (normed * proj[:, :hidden].astype(f32)).astype(b16)
    gated_out[...] = gated
    result = x + dot(gated, out_weight[...], NT)
    inverse = lax.rsqrt(jnp.sum(result * result, -1, keepdims=True) + epsilon)
    inv_len[...] = inverse
    yn = result * inverse
    unit[...] = yn
    unit_b[...] = yn.astype(b16)
    row = iota((outgoing.shape[0], 1), 0)
    filled = jnp.zeros(row.shape, i32)
    for j in range(lengths.shape[1]):
        at = dests[0, j] * slot
        filled = jnp.where((row >= at) & (row < at + lengths[0, j]), 1, filled)
    placed = dot((row == target).astype(b16), result.astype(b16), NN)
    outgoing[...] = jnp.where(filled == 1, placed, EMPTY).astype(b16)


def owner_ids(owners):
    seq = lax.axis_index("seq")
    chip, core = seq // 2, seq % 2
    chips = owners // 2
    return [2 * ((chip + chips - d) % chips) + (core ^ side) for side in range(2) for d in range(chips)]


def normalise_kernel(share, item_table, own, quarter, quarter_inv):
    grp = lax.axis_index("grp")
    x = item_table[...].astype(f32)
    own[...] = (x * lax.rsqrt(jnp.sum(x * x, -1, keepdims=True) + epsilon)).astype(b16)
    x = item_table[pl.ds(pl.multiple_of(grp * share, share), share)].astype(f32)
    inverse = lax.rsqrt(jnp.sum(x * x, -1, keepdims=True) + epsilon)
    quarter[...] = (x * inverse).astype(b16)
    quarter_inv[...] = inverse


def score_kernel(groups, owners, share, chunks, places, cand, inv_len, unit_hbm, yn_hbm, *refs):
    count = len(places)
    pieces, (tags, up, up_keep, up_give, table, spread, unit_b, unit, sems) = refs[:count], refs[count:]
    chips = owners // 2
    vocab_dev = share * groups
    grp, core = lax.axis_index("grp"), lax.axis_index("seq") % 2
    tok = unit_b.shape[0]
    block = vocab_dev + groups * (chips - 1) * share

    def place(key):
        side, chunk, k = key
        if chunk < 0:
            return side * block, vocab_dev
        before = sum(len(ds) for ds in chunks[:chunk]) * groups * share
        rows = len(chunks[chunk]) * share
        return side * block + vocab_dev + before + k * rows, rows

    load_unit = pltpu.make_async_copy(unit_hbm, unit_b, sems.at[count])
    load_unit.start()
    copies = {}
    for n, (*key, left, wide) in enumerate(places):
        at, rows = place(key)
        copy = pltpu.make_async_copy(pieces[n], table.at[pl.ds(at, rows), pl.ds(left, wide)], sems.at[n])
        copy.start()
        copies.setdefault(tuple(key), []).append(copy)
    load_yn = pltpu.make_async_copy(yn_hbm, unit, sems.at[count + 1])
    load_yn.start()
    ids = owner_ids(owners)
    lane = iota((1, 128), 1)
    owner = jnp.full((1, 128), -1, i32)
    for j in range(owners):
        owner = jnp.where(lane == j, ids[j], owner)
    candidates = cand[...]
    chosen = jnp.full((tok, 128), -1, i32)
    first = jnp.zeros((tok, 128), f32)
    for c in range(NCAND):
        here = candidates[:, c : c + 1] // vocab_dev == owner
        chosen = jnp.where(here, candidates[:, c : c + 1], chosen)
        if c == 0:
            first = here.astype(f32)
    wanted = [jnp.broadcast_to(chosen[:, j : j + 1], (tok, 128)) for j in range(owners)]

    def runs(key):
        side, chunk, k = key
        at, rows = place(key)
        if chunk < 0:
            return at, rows, [(side * chips, 0, vocab_dev, ids[side * chips] * vocab_dev)]
        begin = (grp ^ k) * share
        return at, rows, [
            (side * chips + d, i * share, share, ids[side * chips + d] * vocab_dev + begin)
            for i, d in enumerate(chunks[chunk])
        ]

    def tiles(key):
        at, rows, here = runs(key)
        for j, off, wide, base in here:
            step = min(wide, 128)
            for o in range(0, wide, step):
                hit = wanted[j][:, :step] == base + o + iota((1, step), 1)
                yield j, off + o, step, hit

    load_unit.wait()
    yb = unit_b[...]
    value = [[] for _ in range(owners)]
    for key in copies:
        for copy in copies[key]:
            copy.wait()
        at, rows, _ = runs(key)
        product = dot(yb, table[at : at + rows], NT)
        for j, off, step, hit in tiles(key):
            value[j].append(jnp.where(hit, product[:, off : off + step], 0.0))
    logits = jnp.zeros((tok, 128), f32)
    for j in range(owners):
        total = value[j][0]
        for part in value[j][1:]:
            total = total + part
        logits = jnp.where(lane == j, jnp.sum(total, -1, keepdims=True), logits)
    exponent = jnp.where(chosen >= 0, jnp.exp(logits / softmax_warmth), 0.0)
    coef = (exponent / jnp.sum(exponent, -1, keepdims=True) - first) / softmax_warmth
    tags[:owners] = coef.T[:owners]
    tags[owners:] = chosen.astype(f32).T[:owners]
    amount = [jnp.broadcast_to(coef[:, j : j + 1], (tok, 128)) for j in range(owners)]
    for key in copies:
        at = runs(key)[0]
        for j, off, step, hit in tiles(key):
            spread[:, at + off : at + off + step] = jnp.where(hit, amount[j][:, :step], 0.0).astype(b16)
    pulled = dot(spread[...], table[...], NN)
    load_yn.wait()
    yn = unit[...]
    upstream = (pulled - yn * jnp.sum(yn * pulled, -1, keepdims=True)) * inv_len[...]
    up[...] = upstream.astype(b16)
    mine, other = split_columns(upstream, owners, core)
    up_keep[...] = mine.astype(b16)
    up_give[...] = other.astype(b16)


def backward_kernel(up, out_weight, proj, slope, attn, attn_slope, normed_ref, inverse, grad):
    hidden = out_weight.shape[1]
    normed = normed_ref[...]
    grad_gated = dot(up[...], out_weight[...], NN)
    grad[:, :hidden] = (grad_gated * normed * slope[:, :hidden].astype(f32)).astype(b16)
    grad_normed = grad_gated * proj[:, :hidden].astype(f32)
    grad_attended = inverse[...] * (
        grad_normed
        - jnp.mean(grad_normed, -1, keepdims=True)
        - normed * jnp.mean(grad_normed * normed, -1, keepdims=True)
    )
    grad_attended = grad_attended.astype(b16)
    for h in range(HEADS):
        cv, cq, ck = [slice(i * hidden + h * HEAD_DIM, i * hidden + (h + 1) * HEAD_DIM) for i in (1, 2, 3)]
        part = grad_attended[:, h * HEAD_DIM : (h + 1) * HEAD_DIM]
        grad_attn = dot(part, proj[:, cv], NT)
        grad_score = (grad_attn * attn_slope[h].astype(f32)).astype(b16)
        grad[:, cv] = (dot(attn[h], part, TN) * slope[:, cv].astype(f32)).astype(b16)
        grad[:, cq] = (dot(grad_score, proj[:, ck], NN) * slope[:, cq].astype(f32)).astype(b16)
        grad[:, ck] = (dot(grad_score, proj[:, cq], TN) * slope[:, ck].astype(f32)).astype(b16)


def item_kernel(groups, owners, share, chunks, places, *refs):
    count = len(places)
    units, tags = refs[:count], refs[count : count + groups]
    parts, (keep, give, gathered, near, sems) = refs[count + groups : -5], refs[-5:]
    chips = owners // 2
    vocab_dev = share * groups
    grp = lax.axis_index("grp")
    tok = tags[0].shape[1]
    copies = []
    for n, (k, left, wide) in enumerate(places):
        copies.append(pltpu.make_async_copy(units[n], gathered.at[pl.ds(k * tok, tok), pl.ds(left, wide)], sems.at[n]))
    begin = pl.multiple_of(grp * share, share)
    for n, part in enumerate(parts):
        side, chunk = n // (len(chunks) + 1), n % (len(chunks) + 1) - 1
        for i, d in enumerate([0] if chunk < 0 else chunks[chunk]):
            rows = pl.ds(begin if chunk < 0 else i * share, share)
            at = pl.ds((side * chips + d) * share, share)
            copies.append(pltpu.make_async_copy(part.at[rows], near.at[at], sems.at[len(copies)]))
    for copy in copies:
        copy.start()
    ids = owner_ids(owners)
    amounts = jnp.concatenate([t[:owners] for t in tags], 1)
    chosen = jnp.concatenate([t[owners:] for t in tags], 1).astype(i32)
    for copy in copies:
        copy.wait()
    for side, out in ((0, keep), (1, give)):
        parts = []
        for d in range(chips):
            j = side * chips + d
            hit = ids[j] * vocab_dev + grp * share + iota((share, 1), 0) == chosen[j : j + 1]
            parts.append(jnp.where(hit, amounts[j : j + 1], 0.0).astype(b16))
        summed = dot(jnp.concatenate(parts, 0), gathered[...], NN)
        row = near[side * chips * share : (side + 1) * chips * share].astype(f32)
        out[...] = (summed - row * jnp.sum(row * summed, -1, keepdims=True)).astype(b16)


def weight_kernel(groups, owners, keep, give, up_keep, up_give, grad, far_grad, gated, far_gated, *refs):
    outs, whole = refs[:-1], refs[-1]
    chips = owners // 2
    grp = lax.axis_index("grp")
    wide = grad.shape[1]
    step = gated.shape[1]
    for i in range(0, wide, step):
        cols = slice(i, i + step)
        part = dot(keep[...], grad[:, cols], TN) + dot(give[...], far_grad[:, cols], TN)
        whole[:, cols] = part.astype(b16)
    part = dot(up_keep[...], gated[...], TN) + dot(up_give[...], far_gated[...], TN)
    whole[:, wide:] = part.astype(b16)
    rows = whole.shape[0] // chips
    fine = rows // groups
    half = whole.shape[1] // 2
    base, by_one, by_two, one_right, two_left = outs
    for z in range(chips):
        piece = [whole[pl.ds(pl.multiple_of(z * rows + (grp ^ k) * fine, fine), fine)] for k in range(groups)]
        base[z] = piece[0]
        by_one[0, z], by_one[1, z] = piece[3][:, :half], piece[1][:, :half]
        by_two[0, z], by_two[1, z] = piece[3][:, half:], piece[2][:, half:]
        one_right[z], two_left[z] = piece[1][:, half:], piece[2][:, :half]


def sum_kernel(base, by_one, by_two, one_right, two_left, *outs):
    chips = len(outs)
    chip = lax.axis_index("seq") // 2
    half = base.shape[2] // 2
    for d in range(chips):
        z = lax.rem(chip + d, chips)
        own = base[z].astype(f32)
        left = own[:, :half] + by_one[1, z].astype(f32) + two_left[z].astype(f32)
        right = own[:, half:] + by_two[1, z].astype(f32) + one_right[z].astype(f32)
        outs[d][:, :half] = left.astype(b16)
        outs[d][:, half:] = right.astype(b16)


def pair_kernel(x, y, *outs):
    rows = outs[0].shape[0]
    for d, out in enumerate(outs):
        at = slice(d * rows, (d + 1) * rows)
        out[...] = (x[at].astype(f32) + y[at].astype(f32)).astype(b16)


def assemble_kernel(groups, columns, *refs):
    parts, outs = refs[:groups], refs[groups:]
    grp = lax.axis_index("grp")
    fine = parts[0].shape[0]
    for k in range(groups):
        at = pl.ds(pl.multiple_of((grp ^ k) * fine, fine), fine)
        left = 0
        for out, wide in zip(outs, columns):
            out[at] = parts[k][:, left : left + wide].astype(f32)
            left += wide


def relay_kernel(arrived, out):
    tok, slots = out.shape[0], arrived.shape[0]
    filled = (arrived[:, :128].astype(f32) < EMPTY / 2).astype(b16)
    before = (iota((slots, 1), 0) > iota((1, slots), 1)).astype(b16)
    rank = dot(before, filled, NN)[:, :1].astype(i32)
    rank = jnp.where(filled[:, :1].astype(f32) > 0, rank, -1)
    place = (rank == iota((1, tok), 1)).astype(b16)
    out[...] = dot(place, arrived[...], TN).astype(b16)


def body(events, lengths, destinations, history, negatives, in_weight, out_weight, item_table):
    groups = lax.axis_size("grp")
    owners = lax.axis_size("seq")
    chips = owners // 2
    grp = lax.axis_index("grp")
    seq = lax.axis_index("seq")
    chip, core = seq // 2, seq % 2
    tok = events.shape[0]
    vocab_dev, width = item_table.shape
    hidden = out_weight.shape[1]
    share = vocab_dev // groups
    slot = 3 * tok // (2 * owners)
    rows = width // owners
    fine = rows // groups

    def to_chip(x, d):
        pairs = [(2 * a + b, 2 * ((a + d) % chips) + b) for a in range(chips) for b in range(2)]
        return lax.ppermute(x, "seq", pairs)

    def to_group(x, k):
        return lax.ppermute(x, "grp", [(a, a ^ k) for a in range(groups)])

    def to_core(x):
        return lax.ppermute(x, "seq", [(a, a ^ 1) for a in range(owners)])

    def gather_groups(x):
        wide = x.shape[1]
        if groups != 4:
            return [(k, 0, wide, to_group(x, k) if k else x) for k in range(groups)]
        one, two = to_group(x, 1), to_group(x, 2)
        half = wide // 2
        left, right = to_group(one[:, :half], 2), to_group(two[:, half:], 1)
        return [(0, 0, wide, x), (1, 0, wide, one), (2, 0, wide, two), (3, 0, half, left), (3, half, half, right)]

    own, quarter, quarter_inv = call(
        lambda *refs: normalise_kernel(share, *refs),
        [((vocab_dev, width), b16), ((share, width), b16), ((share, 1), f32)],
        [VMEM], [item_table], flops=8 * vocab_dev * width, nbytes=5 * vocab_dev * width, room=8,
    )
    chunks = [list(range(1, chips))]
    got = [to_chip(quarter, d) for d in chunks[0]]
    far_own = to_core(own)
    outs = [
        ((tok, width // 2), b16), ((tok, width // 2), b16), ((tok, 4 * hidden), b16), ((tok, 4 * hidden), b16),
        ((HEADS, tok, tok), b16), ((HEADS, tok, tok), b16), ((tok, hidden), f32), ((tok, 1), f32),
        ((tok, hidden), b16), ((tok, width), f32), ((tok, width), b16), ((tok, 1), f32),
        ((owners * slot, width), b16),
    ]
    (keep, give, proj, slope, attn, attn_slope, normed, inverse, gated, unit, unit_b, inv_len, outgoing) = call(
        lambda *refs: forward_kernel(owners, slot, *refs), outs, [SMEM, SMEM, VMEM, VMEM, VMEM],
        [lengths, destinations, events, in_weight, out_weight],
        flops=2 * tok * width * 6 * hidden, nbytes=24 * tok * width + 10 * width * hidden, room=28,
    )

    got, far_own, unit_b = lax.optimization_barrier((got, far_own, unit_b))
    others = [jnp.concatenate(got, 0)]
    pieces = [(0, -1, 0, 0, width, own)]
    for j, x in enumerate(others):
        pieces += [(0, j) + p for p in gather_groups(x)]
    pieces = pieces + [(1,) + p[1:5] + (to_core(p[5]) if p[1] >= 0 else far_own,) for p in pieces]
    near = [p[5] for p in pieces if p[2] == 0]
    sent_unit, _ = lax.optimization_barrier((unit_b, [p[5] for p in pieces if p[0] == 0]))
    unit_sent = gather_groups(sent_unit)
    outgoing, _ = lax.optimization_barrier((outgoing, others))

    arrived = lax.all_to_all(
        outgoing.reshape(owners, slot, width), "seq", 0, 0, tiled=True
    ).reshape(owners * slot, width)
    layer_out, = call(
        relay_kernel, [((tok, width), b16)], [VMEM], [arrived],
        flops=3 * tok * tok * width, nbytes=6 * tok * width, room=8,
    )

    candidates = jnp.concatenate([history[:, None], negatives], 1)
    vocab = vocab_dev * owners
    far_give, far_gated = to_core(give), to_core(gated)
    layer_out, score_unit, far_give, far_gated = lax.optimization_barrier((layer_out, unit, far_give, far_gated))
    tags, up, up_keep, up_give = call(
        lambda *refs: score_kernel(groups, owners, share, chunks, [p[:5] for p in pieces], *refs),
        [((2 * owners, tok), f32), ((tok, width), b16), ((tok, width // 2), b16), ((tok, width // 2), b16)],
        [VMEM] * 2 + [ANY] * (len(pieces) + 2), [candidates, inv_len, unit_b, score_unit] + [p[5] for p in pieces],
        [pltpu.VMEM((vocab, width), b16), pltpu.VMEM((tok, vocab), b16), pltpu.VMEM((tok, width), b16),
         pltpu.VMEM((tok, width), f32), pltpu.SemaphoreType.DMA((len(pieces) + 2,))],
        flops=4 * tok * width * vocab, nbytes=2 * vocab * width + 12 * tok * width, room=24 if groups == 4 else 58,
    )
    units = [p[3] for p in unit_sent]

    up, _ = lax.optimization_barrier((up, [p[3] for p in unit_sent[1:3]]))

    grad, = call(
        backward_kernel, [((tok, 4 * hidden), b16)], [VMEM] * 8,
        [up, out_weight, proj, slope, attn, attn_slope, normed, inverse],
        flops=2 * tok * width * hidden, nbytes=20 * tok * width,
    )

    all_tags = [to_group(tags, k) if k else tags for k in range(groups)]
    far = [far_give, to_core(up_give), to_core(grad), far_gated]
    mine, other = call(
        lambda *refs: item_kernel(groups, owners, share, chunks, [p[:3] for p in unit_sent], *refs),
        [((chips * share, width), b16)] * 2, [ANY] * len(units) + [VMEM] * groups + [ANY] * len(near),
        units + all_tags + near,
        [pltpu.VMEM((groups * tok, width), b16), pltpu.VMEM((2 * chips * share, width), b16),
         pltpu.SemaphoreType.DMA((len(units) + 2 * chips,))],
        flops=4 * groups * tok * width * chips * share, nbytes=4 * tok * groups * width, room=16 if groups == 4 else 48,
    )
    far_mine = to_core(other)
    far, mine = lax.optimization_barrier((far, mine))
    half = 5 * hidden // 2
    if groups == 4:
        block = (chips, fine, 5 * hidden)
        split = (chips, fine, half)
        parts = call(
            lambda *refs: weight_kernel(groups, owners, *refs),
            [(block, b16)] + [((2,) + split, b16)] * 2 + [(split, b16)] * 2, [VMEM] * 8,
            [keep, far[0], up_keep, far[1], grad, far[2], gated, far[3]],
            [pltpu.VMEM((width // 2, 5 * hidden), b16)],
            flops=2 * tok * width * 5 * hidden, nbytes=20 * tok * width, room=14,
        )
        by_one, by_two = to_group(parts[1], 1), to_group(parts[2], 2)
        one_right = (parts[3].astype(f32) + by_two[0].astype(f32)).astype(b16)
        two_left = (parts[4].astype(f32) + by_one[0].astype(f32)).astype(b16)
        arrived = [by_one, by_two, to_group(one_right, 1), to_group(two_left, 2)]
    else:
        def both(x, y):
            return jnp.concatenate([x, y], 0)

        in_part = dot(both(keep, far[0]), both(grad, far[2]), TN)
        out_part = dot(both(up_keep, far[1]), both(gated, far[3]), TN)
        weight = jnp.concatenate([in_part, out_part], 1).astype(b16)
        weight = weight.reshape(chips, groups, fine, 5 * hidden)
        sums = lax.dynamic_index_in_dim(weight, grp, 1, False).astype(f32)
        for k in range(1, groups):
            sums += to_group(lax.dynamic_index_in_dim(weight, grp ^ k, 1, False), k).astype(f32)


    summed = call(
        pair_kernel, [((share, width), b16)] * chips, [VMEM] * 2, [mine, far_mine],
        flops=chips * share * width, nbytes=6 * chips * share * width, room=8,
    )
    come = [to_chip(summed[d], -d) for d in range(1, chips)]
    total = summed[0].astype(f32)
    for x in come:
        total += x.astype(f32)
    total = (total * quarter_inv).astype(b16)
    table_grad, = call(
        lambda *refs: assemble_kernel(groups, [width], *refs), [((vocab_dev, width), f32)], [VMEM] * groups,
        [to_group(total, k) if k else total for k in range(groups)],
        flops=vocab_dev * width, nbytes=6 * vocab_dev * width, room=8,
    )

    if groups == 4:
        base, _ = lax.optimization_barrier((parts[0], come[0]))
        sums = call(
            sum_kernel, [((fine, 5 * hidden), b16)] * chips, [VMEM] * 5, [base] + arrived,
            flops=chips * fine * 5 * hidden, nbytes=40 * chips * fine * hidden, room=10,
        )
    else:
        sums = [
            lax.dynamic_index_in_dim(sums, (chip + d) % chips, 0, False).astype(b16) for d in range(chips)
        ]
    line = sums[0].astype(f32)
    for d in range(1, chips):
        line += to_chip(sums[d], d).astype(f32)
    line = line.astype(b16)
    lines = [to_group(line, k) if k else line for k in range(groups)]
    if fine % 16 == 0:
        in_grad, out_grad = call(
            lambda *refs: assemble_kernel(groups, [4 * hidden, hidden], *refs),
            [((rows, 4 * hidden), f32), ((rows, hidden), f32)], [VMEM] * groups, lines,
            flops=rows * hidden, nbytes=30 * rows * hidden, room=8,
        )
    else:
        shard = jnp.zeros((rows, 5 * hidden), f32)
        for k in range(groups):
            shard = lax.dynamic_update_slice_in_dim(shard, lines[k].astype(f32), (grp ^ k) * fine, 0)
        in_grad, out_grad = shard[:, : 4 * hidden], shard[:, 4 * hidden :]
    return (layer_out, in_grad, out_grad, table_grad)


def solution(mesh):
    return jax.shard_map(
        body,
        mesh=mesh,
        in_specs=(
            P(("grp", "seq"), None),
            P(("grp", "seq"), None),
            P(("grp", "seq"), None),
            P(("grp", "seq")),
            P(("grp", "seq"), None),
            P(),
            P(),
            P("seq", None),
        ),
        out_specs=(P(("grp", "seq"), None), P("seq", None), P("seq", None), P("seq", None)),
        check_vma=False,
    )
```

```python
import jax
import jax.numpy as jnp
from jax import lax
from jax.experimental import pallas as pl
from jax.experimental.pallas import tpu as pltpu
from jax.sharding import PartitionSpec as P

HEADS = 4
HEAD_DIM = 128
NCAND = 4

epsilon = 1e-05
softmax_warmth = 0.05
EMPTY = 2.0**100

f32, b16, i32 = jnp.float32, jnp.bfloat16, jnp.int32
NN = ((1,), (0,))
NT = ((1,), (1,))
TN = ((0,), (0,))
VMEM = pl.BlockSpec(memory_space=pltpu.VMEM)
SMEM = pl.BlockSpec(memory_space=pltpu.SMEM)
ANY = pl.BlockSpec(memory_space=pl.ANY)


def dot(a, b, dims):
    return lax.dot_general(a, b, (dims, ((), ())), preferred_element_type=f32)


def iota(shape, axis):
    return lax.broadcasted_iota(i32, shape, axis)


def center_scale(values):
    average = jnp.mean(values, -1, keepdims=True)
    centered = values - average
    inverse = lax.rsqrt(jnp.mean(centered * centered, -1, keepdims=True) + epsilon)
    return (centered * inverse, inverse)


def sigmoid(values):
    return 1.0 / (1.0 + jnp.exp(-values))


def split_columns(x, owners, core):
    rows = x.shape[1] // owners
    blocks = [x[:, i * rows : (i + 1) * rows] for i in range(owners)]
    even, odd = jnp.concatenate(blocks[0::2], 1), jnp.concatenate(blocks[1::2], 1)
    first = jnp.broadcast_to(core, even.shape) == 0
    return jnp.where(first, even, odd), jnp.where(first, odd, even)


def call(kernel, out, specs, args, scratch=(), flops=0, nbytes=0, room=14):
    return pl.pallas_call(
        kernel,
        out_shape=[jax.ShapeDtypeStruct(s, t) for s, t in out],
        in_specs=specs,
        out_specs=[VMEM] * len(out),
        scratch_shapes=list(scratch),
        cost_estimate=pl.CostEstimate(flops=flops, bytes_accessed=nbytes, transcendentals=0),
        compiler_params=pltpu.CompilerParams(vmem_limit_bytes=room * 2**20),
    )(*args)


def forward_kernel(
    owners, slot, lengths, dests, events, in_weight, out_weight,
    keep, give, proj, slope, attn, attn_slope, normed_out, inv_out, gated_out, unit, unit_b, inv_len, outgoing,
):
    tok = events.shape[0]
    hidden = out_weight.shape[1]
    scale = HEAD_DIM ** (-0.5)
    core = lax.axis_index("seq") % 2
    x = events[...].astype(f32)
    normed_in = center_scale(x)[0]
    mine, other = split_columns(normed_in, owners, core)
    keep[...] = mine.astype(b16)
    give[...] = other.astype(b16)
    normed_in = normed_in.astype(b16)
    for i in range(4):
        cols = slice(i * hidden, (i + 1) * hidden)
        p = dot(normed_in, in_weight[:, cols], NN)
        sig = sigmoid(p)
        proj[:, cols] = (p * sig).astype(b16)
        slope[:, cols] = (sig * (1.0 + p * (1.0 - sig))).astype(b16)

    pos_c, pos_r = iota((tok, 1), 0), iota((1, tok), 1)
    user_c, user_r = jnp.zeros((tok, 1), i32), jnp.zeros((1, tok), i32)
    target = jnp.zeros((1, tok), i32)
    start = jnp.int32(0)
    for j in range(lengths.shape[1]):
        end = start + lengths[0, j]
        user_c += (pos_c >= end).astype(i32)
        user_r += (pos_r >= end).astype(i32)
        here = (pos_r >= start) & (pos_r < end)
        target = jnp.where(here, dests[0, j] * slot + pos_r - start, target)
        start = end
    mask = (user_c == user_r) & (pos_r <= pos_c)

    outputs = []
    for h in range(HEADS):
        v = proj[:, hidden + h * HEAD_DIM : hidden + (h + 1) * HEAD_DIM]
        q = proj[:, 2 * hidden + h * HEAD_DIM : 2 * hidden + (h + 1) * HEAD_DIM]
        k = proj[:, 3 * hidden + h * HEAD_DIM : 3 * hidden + (h + 1) * HEAD_DIM]
        s = dot(q, k, NT) * scale
        sig = sigmoid(s)
        weight = jnp.where(mask, s * sig, 0.0).astype(b16)
        attn[h] = weight
        attn_slope[h] = jnp.where(mask, sig * (1.0 + s * (1.0 - sig)) * scale, 0.0).astype(b16)
        outputs.append(dot(weight, v, NN))
    normed, inverse = center_scale(jnp.concatenate(outputs, 1))
    normed_out[...] = normed
    inv_out[...] = inverse
    gated = (normed * proj[:, :hidden].astype(f32)).astype(b16)
    gated_out[...] = gated
    result = x + dot(gated, out_weight[...], NT)
    inverse = lax.rsqrt(jnp.sum(result * result, -1, keepdims=True) + epsilon)
    inv_len[...] = inverse
    yn = result * inverse
    unit[...] = yn
    unit_b[...] = yn.astype(b16)
    row = iota((outgoing.shape[0], 1), 0)
    filled = jnp.zeros(row.shape, i32)
    for j in range(lengths.shape[1]):
        at = dests[0, j] * slot
        filled = jnp.where((row >= at) & (row < at + lengths[0, j]), 1, filled)
    placed = dot((row == target).astype(b16), result.astype(b16), NN)
    outgoing[...] = jnp.where(filled == 1, placed, EMPTY).astype(b16)


def distances(chips):
    order, bit = [0], chips // 2
    while bit:
        order += [x ^ bit for x in order]
        bit //= 2
    return order


def owner_ids(owners):
    seq = lax.axis_index("seq")
    chip, core = seq // 2, seq % 2
    chips = owners // 2
    return [2 * (chip ^ d) + (core ^ side) for side in range(2) for d in distances(chips)]


def normalise_kernel(share, item_table, own, quarter, quarter_inv):
    grp = lax.axis_index("grp")
    x = item_table[...].astype(f32)
    own[...] = (x * lax.rsqrt(jnp.sum(x * x, -1, keepdims=True) + epsilon)).astype(b16)
    x = item_table[pl.ds(pl.multiple_of(grp * share, share), share)].astype(f32)
    inverse = lax.rsqrt(jnp.sum(x * x, -1, keepdims=True) + epsilon)
    quarter[...] = (x * inverse).astype(b16)
    quarter_inv[...] = inverse


def score_kernel(groups, owners, share, chunks, places, cand, inv_len, unit_hbm, yn_hbm, *refs):
    count = len(places)
    pieces, (tags, up, up_keep, up_give, table, spread, unit_b, unit, sems) = refs[:count], refs[count:]
    chips = owners // 2
    vocab_dev = share * groups
    grp, core = lax.axis_index("grp"), lax.axis_index("seq") % 2
    tok = unit_b.shape[0]
    block = vocab_dev + groups * (chips - 1) * share

    def place(key):
        side, chunk, k = key
        if chunk < 0:
            return side * block, vocab_dev
        before = sum(len(ds) for ds in chunks[:chunk]) * groups * share
        rows = len(chunks[chunk]) * share
        return side * block + vocab_dev + before + k * rows, rows

    load_unit = pltpu.make_async_copy(unit_hbm, unit_b, sems.at[count])
    load_unit.start()
    copies = {}
    for n, (*key, left, wide) in enumerate(places):
        at, rows = place(key)
        copy = pltpu.make_async_copy(pieces[n], table.at[pl.ds(at, rows), pl.ds(left, wide)], sems.at[n])
        copy.start()
        copies.setdefault(tuple(key), []).append(copy)
    load_yn = pltpu.make_async_copy(yn_hbm, unit, sems.at[count + 1])
    load_yn.start()
    ids = owner_ids(owners)
    lane = iota((1, 128), 1)
    owner = jnp.full((1, 128), -1, i32)
    for j in range(owners):
        owner = jnp.where(lane == j, ids[j], owner)
    candidates = cand[...]
    chosen = jnp.full((tok, 128), -1, i32)
    first = jnp.zeros((tok, 128), f32)
    for c in range(NCAND):
        here = candidates[:, c : c + 1] // vocab_dev == owner
        chosen = jnp.where(here, candidates[:, c : c + 1], chosen)
        if c == 0:
            first = here.astype(f32)
    wanted = [jnp.broadcast_to(chosen[:, j : j + 1], (tok, 128)) for j in range(owners)]

    def runs(key):
        side, chunk, k = key
        at, rows = place(key)
        if chunk < 0:
            return at, rows, [(side * chips, 0, vocab_dev, ids[side * chips] * vocab_dev)]
        begin = (grp ^ k) * share
        return at, rows, [
            (side * chips + d, i * share, share, ids[side * chips + d] * vocab_dev + begin)
            for i, d in enumerate(chunks[chunk])
        ]

    def tiles(key):
        at, rows, here = runs(key)
        for j, off, wide, base in here:
            step = min(wide, 128)
            for o in range(0, wide, step):
                hit = wanted[j][:, :step] == base + o + iota((1, step), 1)
                yield j, off + o, step, hit

    load_unit.wait()
    yb = unit_b[...]
    value = [[] for _ in range(owners)]
    for key in copies:
        for copy in copies[key]:
            copy.wait()
        at, rows, _ = runs(key)
        product = dot(yb, table[at : at + rows], NT)
        for j, off, step, hit in tiles(key):
            value[j].append(jnp.where(hit, product[:, off : off + step], 0.0))
    logits = jnp.zeros((tok, 128), f32)
    for j in range(owners):
        total = value[j][0]
        for part in value[j][1:]:
            total = total + part
        logits = jnp.where(lane == j, jnp.sum(total, -1, keepdims=True), logits)
    exponent = jnp.where(chosen >= 0, jnp.exp(logits / softmax_warmth), 0.0)
    coef = (exponent / jnp.sum(exponent, -1, keepdims=True) - first) / softmax_warmth
    tags[:owners] = coef.T[:owners]
    tags[owners:] = chosen.astype(f32).T[:owners]
    amount = [jnp.broadcast_to(coef[:, j : j + 1], (tok, 128)) for j in range(owners)]
    for key in copies:
        at = runs(key)[0]
        for j, off, step, hit in tiles(key):
            spread[:, at + off : at + off + step] = jnp.where(hit, amount[j][:, :step], 0.0).astype(b16)
    pulled = dot(spread[...], table[...], NN)
    load_yn.wait()
    yn = unit[...]
    upstream = (pulled - yn * jnp.sum(yn * pulled, -1, keepdims=True)) * inv_len[...]
    up[...] = upstream.astype(b16)
    mine, other = split_columns(upstream, owners, core)
    up_keep[...] = mine.astype(b16)
    up_give[...] = other.astype(b16)


def backward_kernel(up, out_weight, proj, slope, attn, attn_slope, normed_ref, inverse, grad):
    hidden = out_weight.shape[1]
    normed = normed_ref[...]
    grad_gated = dot(up[...], out_weight[...], NN)
    grad[:, :hidden] = (grad_gated * normed * slope[:, :hidden].astype(f32)).astype(b16)
    grad_normed = grad_gated * proj[:, :hidden].astype(f32)
    grad_attended = inverse[...] * (
        grad_normed
        - jnp.mean(grad_normed, -1, keepdims=True)
        - normed * jnp.mean(grad_normed * normed, -1, keepdims=True)
    )
    grad_attended = grad_attended.astype(b16)
    for h in range(HEADS):
        cv, cq, ck = [slice(i * hidden + h * HEAD_DIM, i * hidden + (h + 1) * HEAD_DIM) for i in (1, 2, 3)]
        part = grad_attended[:, h * HEAD_DIM : (h + 1) * HEAD_DIM]
        grad_attn = dot(part, proj[:, cv], NT)
        grad_score = (grad_attn * attn_slope[h].astype(f32)).astype(b16)
        grad[:, cv] = (dot(attn[h], part, TN) * slope[:, cv].astype(f32)).astype(b16)
        grad[:, cq] = (dot(grad_score, proj[:, ck], NN) * slope[:, cq].astype(f32)).astype(b16)
        grad[:, ck] = (dot(grad_score, proj[:, cq], TN) * slope[:, ck].astype(f32)).astype(b16)


def item_kernel(groups, owners, share, chunks, places, *refs):
    count = len(places)
    units, tags = refs[:count], refs[count : count + groups]
    parts, (keep, give, gathered, near, sems) = refs[count + groups : -5], refs[-5:]
    chips = owners // 2
    vocab_dev = share * groups
    grp = lax.axis_index("grp")
    tok = tags[0].shape[1]
    copies = []
    for n, (k, left, wide) in enumerate(places):
        copies.append(pltpu.make_async_copy(units[n], gathered.at[pl.ds(k * tok, tok), pl.ds(left, wide)], sems.at[n]))
    begin = pl.multiple_of(grp * share, share)
    for n, part in enumerate(parts):
        side, chunk = n // (len(chunks) + 1), n % (len(chunks) + 1) - 1
        for i, d in enumerate([0] if chunk < 0 else chunks[chunk]):
            rows = pl.ds(begin if chunk < 0 else i * share, share)
            at = pl.ds((side * chips + d) * share, share)
            copies.append(pltpu.make_async_copy(part.at[rows], near.at[at], sems.at[len(copies)]))
    for copy in copies:
        copy.start()
    ids = owner_ids(owners)
    amounts = jnp.concatenate([t[:owners] for t in tags], 1)
    chosen = jnp.concatenate([t[owners:] for t in tags], 1).astype(i32)
    for copy in copies:
        copy.wait()
    for side, out in ((0, keep), (1, give)):
        parts = []
        for d in range(chips):
            j = side * chips + d
            hit = ids[j] * vocab_dev + grp * share + iota((share, 1), 0) == chosen[j : j + 1]
            parts.append(jnp.where(hit, amounts[j : j + 1], 0.0).astype(b16))
        summed = dot(jnp.concatenate(parts, 0), gathered[...], NN)
        row = near[side * chips * share : (side + 1) * chips * share].astype(f32)
        out[...] = (summed - row * jnp.sum(row * summed, -1, keepdims=True)).astype(b16)


def weight_kernel(groups, owners, keep, give, up_keep, up_give, grad, far_grad, gated, far_gated, *refs):
    outs, whole = refs[:-1], refs[-1]
    chips = owners // 2
    grp = lax.axis_index("grp")
    wide = grad.shape[1]
    step = gated.shape[1]
    for i in range(0, wide, step):
        cols = slice(i, i + step)
        part = dot(keep[...], grad[:, cols], TN) + dot(give[...], far_grad[:, cols], TN)
        whole[:, cols] = part.astype(b16)
    part = dot(up_keep[...], gated[...], TN) + dot(up_give[...], far_gated[...], TN)
    whole[:, wide:] = part.astype(b16)
    rows = whole.shape[0] // chips
    fine = rows // groups
    half = whole.shape[1] // 2
    base, by_one, by_two, one_right, two_left = outs
    for z in range(chips):
        piece = [whole[pl.ds(pl.multiple_of(z * rows + (grp ^ k) * fine, fine), fine)] for k in range(groups)]
        base[z] = piece[0]
        by_one[0, z], by_one[1, z] = piece[3][:, :half], piece[1][:, :half]
        by_two[0, z], by_two[1, z] = piece[3][:, half:], piece[2][:, half:]
        one_right[z], two_left[z] = piece[1][:, half:], piece[2][:, :half]


def sum_kernel(base, by_one, by_two, one_right, two_left, *outs):
    chips = len(outs)
    chip = lax.axis_index("seq") // 2
    half = base.shape[2] // 2
    for d in range(chips):
        z = lax.rem(chip + d, chips)
        own = base[z].astype(f32)
        left = own[:, :half] + by_one[1, z].astype(f32) + two_left[z].astype(f32)
        right = own[:, half:] + by_two[1, z].astype(f32) + one_right[z].astype(f32)
        outs[d][:, :half] = left.astype(b16)
        outs[d][:, half:] = right.astype(b16)


def pair_kernel(x, y, *outs):
    rows = outs[0].shape[0]
    for d, out in enumerate(outs):
        at = slice(d * rows, (d + 1) * rows)
        out[...] = (x[at].astype(f32) + y[at].astype(f32)).astype(b16)


def assemble_kernel(groups, columns, *refs):
    parts, outs = refs[:groups], refs[groups:]
    grp = lax.axis_index("grp")
    fine = parts[0].shape[0]
    for k in range(groups):
        at = pl.ds(pl.multiple_of((grp ^ k) * fine, fine), fine)
        left = 0
        for out, wide in zip(outs, columns):
            out[at] = parts[k][:, left : left + wide].astype(f32)
            left += wide


def relay_kernel(arrived, out):
    tok, slots = out.shape[0], arrived.shape[0]
    filled = (arrived[:, :128].astype(f32) < EMPTY / 2).astype(b16)
    before = (iota((slots, 1), 0) > iota((1, slots), 1)).astype(b16)
    rank = dot(before, filled, NN)[:, :1].astype(i32)
    rank = jnp.where(filled[:, :1].astype(f32) > 0, rank, -1)
    place = (rank == iota((1, tok), 1)).astype(b16)
    out[...] = dot(place, arrived[...], TN).astype(b16)


def body(events, lengths, destinations, history, negatives, in_weight, out_weight, item_table):
    groups = lax.axis_size("grp")
    owners = lax.axis_size("seq")
    chips = owners // 2
    grp = lax.axis_index("grp")
    seq = lax.axis_index("seq")
    chip, core = seq // 2, seq % 2
    tok = events.shape[0]
    vocab_dev, width = item_table.shape
    hidden = out_weight.shape[1]
    share = vocab_dev // groups
    slot = 3 * tok // (2 * owners)
    rows = width // owners
    fine = rows // groups

    def to_chip(x, d):
        pairs = [(2 * a + b, 2 * ((a + d) % chips) + b) for a in range(chips) for b in range(2)]
        return lax.ppermute(x, "seq", pairs)

    def across(x, k):
        pairs = [(2 * a + b, 2 * (a ^ k) + b) for a in range(chips) for b in range(2)]
        return lax.ppermute(x, "seq", pairs)

    def to_group(x, k):
        return lax.ppermute(x, "grp", [(a, a ^ k) for a in range(groups)])

    def to_core(x):
        return lax.ppermute(x, "seq", [(a, a ^ 1) for a in range(owners)])

    def gather_groups(x, near=None):
        wide = x.shape[1]
        if groups != 4:
            return [(k, 0, wide, to_group(x, k) if k else x) for k in range(groups)]
        one, two = near or [to_group(x, k) for k in (1, 2)]
        half = wide // 2
        left, right = to_group(one[:, :half], 2), to_group(two[:, half:], 1)
        return [(0, 0, wide, x), (1, 0, wide, one), (2, 0, wide, two), (3, 0, half, left), (3, half, half, right)]

    own, quarter, quarter_inv = call(
        lambda *refs: normalise_kernel(share, *refs),
        [((vocab_dev, width), b16), ((share, width), b16), ((share, 1), f32)],
        [VMEM], [item_table], flops=8 * vocab_dev * width, nbytes=5 * vocab_dev * width, room=8,
    )
    chunks = [list(range(1, chips))]
    have, bit = {0: quarter}, chips // 2
    while bit:
        have.update({x ^ bit: across(have[x], bit) for x in have})
        bit //= 2
    got = [have[x] for x in distances(chips)[1:]]
    outs = [
        ((tok, width // 2), b16), ((tok, width // 2), b16), ((tok, 4 * hidden), b16), ((tok, 4 * hidden), b16),
        ((HEADS, tok, tok), b16), ((HEADS, tok, tok), b16), ((tok, hidden), f32), ((tok, 1), f32),
        ((tok, hidden), b16), ((tok, width), f32), ((tok, width), b16), ((tok, 1), f32),
        ((owners * slot, width), b16),
    ]
    (keep, give, proj, slope, attn, attn_slope, normed, inverse, gated, unit, unit_b, inv_len, outgoing) = call(
        lambda *refs: forward_kernel(owners, slot, *refs), outs, [SMEM, SMEM, VMEM, VMEM, VMEM],
        [lengths, destinations, events, in_weight, out_weight],
        room=63,
    )

    near_units = [to_group(unit_b, k) for k in (1, 2)]
    got, near_units, own = lax.optimization_barrier((got, near_units, own))
    far_own = to_core(own)
    unit_sent = gather_groups(unit_b, near_units)
    others = [jnp.concatenate(got, 0)]
    pieces = [(0, -1, 0, 0, width, own)]
    for j, x in enumerate(others):
        pieces += [(0, j) + p for p in gather_groups(x)]
    pieces = pieces + [(1,) + p[1:5] + (to_core(p[5]) if p[1] >= 0 else far_own,) for p in pieces]
    near = [p[5] for p in pieces if p[2] == 0]
    outgoing, _ = lax.optimization_barrier((outgoing, others))

    arrived = lax.all_to_all(
        outgoing.reshape(owners, slot, width), "seq", 0, 0, tiled=True
    ).reshape(owners * slot, width)
    layer_out, = call(
        relay_kernel, [((tok, width), b16)], [VMEM], [arrived],
        room=63,
    )

    candidates = jnp.concatenate([history[:, None], negatives], 1)
    vocab = vocab_dev * owners
    far_give, far_gated = to_core(give), to_core(gated)
    units = [p[3] for p in unit_sent]
    layer_out, score_unit, far_give, far_gated, units = lax.optimization_barrier(
        (layer_out, unit, far_give, far_gated, units)
    )
    tags, up, up_keep, up_give = call(
        lambda *refs: score_kernel(groups, owners, share, chunks, [p[:5] for p in pieces], *refs),
        [((2 * owners, tok), f32), ((tok, width), b16), ((tok, width // 2), b16), ((tok, width // 2), b16)],
        [VMEM] * 2 + [ANY] * (len(pieces) + 2), [candidates, inv_len, unit_b, score_unit] + [p[5] for p in pieces],
        [pltpu.VMEM((vocab, width), b16), pltpu.VMEM((tok, vocab), b16), pltpu.VMEM((tok, width), b16),
         pltpu.VMEM((tok, width), f32), pltpu.SemaphoreType.DMA((len(pieces) + 2,))],
        room=63,
    )

    grad, = call(
        backward_kernel, [((tok, 4 * hidden), b16)], [VMEM] * 8,
        [up, out_weight, proj, slope, attn, attn_slope, normed, inverse], room=60,
    )

    all_tags = [to_group(tags, k) if k else tags for k in range(groups)]
    far = [far_give, to_core(up_give), None, far_gated]
    grad, far[1], all_tags = lax.optimization_barrier((grad, far[1], all_tags))
    far[2] = to_core(grad)
    half = 5 * hidden // 2
    if groups == 4:
        block = (chips, fine, 5 * hidden)
        split = (chips, fine, half)
        parts = call(
            lambda *refs: weight_kernel(groups, owners, *refs),
            [(block, b16)] + [((2,) + split, b16)] * 2 + [(split, b16)] * 2, [VMEM] * 8,
            [keep, far[0], up_keep, far[1], grad, far[2], gated, far[3]],
            [pltpu.VMEM((width // 2, 5 * hidden), b16)],
            flops=2 * tok * width * 5 * hidden, nbytes=20 * tok * width, room=60,
        )
        after = parts[0]
        by_one, by_two = to_group(parts[1], 1), to_group(parts[2], 2)
        one_right = (parts[3].astype(f32) + by_two[0].astype(f32)).astype(b16)
        two_left = (parts[4].astype(f32) + by_one[0].astype(f32)).astype(b16)
        arrived = [by_one, by_two, to_group(one_right, 1), to_group(two_left, 2)]
    else:
        def both(x, y):
            return jnp.concatenate([x, y], 0)

        in_part = dot(both(keep, far[0]), both(grad, far[2]), TN)
        out_part = dot(both(up_keep, far[1]), both(gated, far[3]), TN)
        weight = jnp.concatenate([in_part, out_part], 1).astype(b16)
        weight = weight.reshape(chips, groups, fine, 5 * hidden)
        after = weight
        sums = lax.dynamic_index_in_dim(weight, grp, 1, False).astype(f32)
        for k in range(1, groups):
            sums += to_group(lax.dynamic_index_in_dim(weight, grp ^ k, 1, False), k).astype(f32)


    units[0], _ = lax.optimization_barrier((units[0], after))
    mine, other = call(
        lambda *refs: item_kernel(groups, owners, share, chunks, [p[:3] for p in unit_sent], *refs),
        [((chips * share, width), b16)] * 2, [ANY] * len(units) + [VMEM] * groups + [ANY] * len(near),
        units + all_tags + near,
        [pltpu.VMEM((groups * tok, width), b16), pltpu.VMEM((2 * chips * share, width), b16),
         pltpu.SemaphoreType.DMA((len(units) + 2 * chips,))],
        flops=4 * groups * tok * width * chips * share, nbytes=4 * tok * groups * width, room=60,
    )
    far_mine = to_core(other)

    summed = call(
        pair_kernel, [((share, width), b16)] * chips, [VMEM] * 2, [mine, far_mine],
        flops=chips * share * width, nbytes=6 * chips * share * width, room=8,
    )
    come = [across(summed[n], d) for n, d in enumerate(distances(chips)) if d]
    total = summed[0].astype(f32)
    for x in come:
        total += x.astype(f32)
    total = (total * quarter_inv).astype(b16)
    table_grad, = call(
        lambda *refs: assemble_kernel(groups, [width], *refs), [((vocab_dev, width), f32)], [VMEM] * groups,
        [to_group(total, k) if k else total for k in range(groups)],
        flops=vocab_dev * width, nbytes=6 * vocab_dev * width, room=8,
    )

    if groups == 4:
        base = parts[0]
        sums = call(
            sum_kernel, [((fine, 5 * hidden), b16)] * chips, [VMEM] * 5, [base] + arrived,
            flops=chips * fine * 5 * hidden, nbytes=40 * chips * fine * hidden, room=10,
        )
    else:
        sums = [
            lax.dynamic_index_in_dim(sums, (chip + d) % chips, 0, False).astype(b16) for d in range(chips)
        ]
    line = sums[0].astype(f32)
    for d in range(1, chips):
        line += to_chip(sums[d], d).astype(f32)
    line = line.astype(b16)
    lines = [to_group(line, k) if k else line for k in range(groups)]
    if fine % 16 == 0:
        in_grad, out_grad = call(
            lambda *refs: assemble_kernel(groups, [4 * hidden, hidden], *refs),
            [((rows, 4 * hidden), f32), ((rows, hidden), f32)], [VMEM] * groups, lines,
            flops=rows * hidden, nbytes=30 * rows * hidden, room=8,
        )
    else:
        shard = jnp.zeros((rows, 5 * hidden), f32)
        for k in range(groups):
            shard = lax.dynamic_update_slice_in_dim(shard, lines[k].astype(f32), (grp ^ k) * fine, 0)
        in_grad, out_grad = shard[:, : 4 * hidden], shard[:, 4 * hidden :]
    return (layer_out, in_grad, out_grad, table_grad)


def solution(mesh):
    return jax.shard_map(
        body,
        mesh=mesh,
        in_specs=(
            P(("grp", "seq"), None),
            P(("grp", "seq"), None),
            P(("grp", "seq"), None),
            P(("grp", "seq")),
            P(("grp", "seq"), None),
            P(),
            P(),
            P("seq", None),
        ),
        out_specs=(P(("grp", "seq"), None), P("seq", None), P("seq", None), P("seq", None)),
        check_vma=False,
    )
```

```python
import jax
import jax.numpy as jnp
from jax import lax
from jax.experimental import pallas as pl
from jax.experimental.pallas import tpu as pltpu
from jax.sharding import PartitionSpec as P

HEADS = 4
HEAD_DIM = 128
NCAND = 4

epsilon = 1e-05
softmax_warmth = 0.05
EMPTY = 2.0**100

f32, b16, i32 = jnp.float32, jnp.bfloat16, jnp.int32
NN = ((1,), (0,))
NT = ((1,), (1,))
TN = ((0,), (0,))
VMEM = pl.BlockSpec(memory_space=pltpu.VMEM)
SMEM = pl.BlockSpec(memory_space=pltpu.SMEM)
ANY = pl.BlockSpec(memory_space=pl.ANY)


def dot(a, b, dims):
    return lax.dot_general(a, b, (dims, ((), ())), preferred_element_type=f32)


def iota(shape, axis):
    return lax.broadcasted_iota(i32, shape, axis)


def center_scale(values):
    average = jnp.mean(values, -1, keepdims=True)
    centered = values - average
    inverse = lax.rsqrt(jnp.mean(centered * centered, -1, keepdims=True) + epsilon)
    return (centered * inverse, inverse)


def sigmoid(values):
    return 1.0 / (1.0 + jnp.exp(-values))


def split_columns(x, owners, core):
    rows = x.shape[1] // owners
    blocks = [x[:, i * rows : (i + 1) * rows] for i in range(owners)]
    even, odd = jnp.concatenate(blocks[0::2], 1), jnp.concatenate(blocks[1::2], 1)
    first = jnp.broadcast_to(core, even.shape) == 0
    return jnp.where(first, even, odd), jnp.where(first, odd, even)


def call(kernel, out, specs, args, scratch=(), flops=0, nbytes=0, room=14):
    return pl.pallas_call(
        kernel,
        out_shape=[jax.ShapeDtypeStruct(s, t) for s, t in out],
        in_specs=specs,
        out_specs=[VMEM] * len(out),
        scratch_shapes=list(scratch),
        cost_estimate=pl.CostEstimate(flops=flops, bytes_accessed=nbytes, transcendentals=0),
        compiler_params=pltpu.CompilerParams(vmem_limit_bytes=room * 2**20),
    )(*args)


def forward_kernel(
    owners, slot, lengths, dests, events, in_weight, out_weight,
    keep, give, proj, slope, attn, attn_slope, normed_out, inv_out, gated_out, unit, unit_b, inv_len, outgoing,
):
    tok = events.shape[0]
    hidden = out_weight.shape[1]
    scale = HEAD_DIM ** (-0.5)
    core = lax.axis_index("seq") % 2
    x = events[...].astype(f32)
    normed_in = center_scale(x)[0]
    mine, other = split_columns(normed_in, owners, core)
    keep[...] = mine.astype(b16)
    give[...] = other.astype(b16)
    normed_in = normed_in.astype(b16)
    for i in range(4):
        cols = slice(i * hidden, (i + 1) * hidden)
        p = dot(normed_in, in_weight[:, cols], NN)
        sig = sigmoid(p)
        proj[:, cols] = (p * sig).astype(b16)
        slope[:, cols] = (sig * (1.0 + p * (1.0 - sig))).astype(b16)

    pos_c, pos_r = iota((tok, 1), 0), iota((1, tok), 1)
    user_c, user_r = jnp.zeros((tok, 1), i32), jnp.zeros((1, tok), i32)
    target = jnp.zeros((1, tok), i32)
    start = jnp.int32(0)
    for j in range(lengths.shape[1]):
        end = start + lengths[0, j]
        user_c += (pos_c >= end).astype(i32)
        user_r += (pos_r >= end).astype(i32)
        here = (pos_r >= start) & (pos_r < end)
        target = jnp.where(here, dests[0, j] * slot + pos_r - start, target)
        start = end
    mask = (user_c == user_r) & (pos_r <= pos_c)

    outputs = []
    for h in range(HEADS):
        v = proj[:, hidden + h * HEAD_DIM : hidden + (h + 1) * HEAD_DIM]
        q = proj[:, 2 * hidden + h * HEAD_DIM : 2 * hidden + (h + 1) * HEAD_DIM]
        k = proj[:, 3 * hidden + h * HEAD_DIM : 3 * hidden + (h + 1) * HEAD_DIM]
        s = dot(q, k, NT) * scale
        sig = sigmoid(s)
        weight = jnp.where(mask, s * sig, 0.0).astype(b16)
        attn[h] = weight
        attn_slope[h] = jnp.where(mask, sig * (1.0 + s * (1.0 - sig)) * scale, 0.0).astype(b16)
        outputs.append(dot(weight, v, NN))
    normed, inverse = center_scale(jnp.concatenate(outputs, 1))
    normed_out[...] = normed
    inv_out[...] = inverse
    gated = (normed * proj[:, :hidden].astype(f32)).astype(b16)
    gated_out[...] = gated
    result = x + dot(gated, out_weight[...], NT)
    inverse = lax.rsqrt(jnp.sum(result * result, -1, keepdims=True) + epsilon)
    inv_len[...] = inverse
    yn = result * inverse
    unit[...] = yn
    unit_b[...] = yn.astype(b16)
    row = iota((outgoing.shape[0], 1), 0)
    filled = jnp.zeros(row.shape, i32)
    for j in range(lengths.shape[1]):
        at = dests[0, j] * slot
        filled = jnp.where((row >= at) & (row < at + lengths[0, j]), 1, filled)
    placed = dot((row == target).astype(b16), result.astype(b16), NN)
    outgoing[...] = jnp.where(filled == 1, placed, EMPTY).astype(b16)


def distances(chips):
    order, bit = [0], chips // 2
    while bit:
        order += [x ^ bit for x in order]
        bit //= 2
    return order


def owner_ids(owners):
    seq = lax.axis_index("seq")
    chip, core = seq // 2, seq % 2
    chips = owners // 2
    return [2 * (chip ^ d) + (core ^ side) for side in range(2) for d in distances(chips)]


def normalise_kernel(share, item_table, own, quarter, quarter_inv):
    grp = lax.axis_index("grp")
    x = item_table[...].astype(f32)
    own[...] = (x * lax.rsqrt(jnp.sum(x * x, -1, keepdims=True) + epsilon)).astype(b16)
    x = item_table[pl.ds(pl.multiple_of(grp * share, share), share)].astype(f32)
    inverse = lax.rsqrt(jnp.sum(x * x, -1, keepdims=True) + epsilon)
    quarter[...] = (x * inverse).astype(b16)
    quarter_inv[...] = inverse


def score_kernel(groups, owners, share, chunks, places, cand, inv_len, unit_b, unit, *refs):
    count = len(places)
    pieces, (tags, up, up_keep, up_give, pulled) = refs[:count], refs[count:]
    chips = owners // 2
    vocab_dev = share * groups
    grp, core = lax.axis_index("grp"), lax.axis_index("seq") % 2
    tok = unit_b.shape[0]
    parts_of = {}
    for n, (*key, left, wide) in enumerate(places):
        parts_of.setdefault(tuple(key), []).append((slice(left, left + wide), pieces[n]))
    ids = owner_ids(owners)
    lane = iota((1, 128), 1)
    owner = jnp.full((1, 128), -1, i32)
    for j in range(owners):
        owner = jnp.where(lane == j, ids[j], owner)
    candidates = cand[...]
    chosen = jnp.full((tok, 128), -1, i32)
    first = jnp.zeros((tok, 128), f32)
    for c in range(NCAND):
        here = candidates[:, c : c + 1] // vocab_dev == owner
        chosen = jnp.where(here, candidates[:, c : c + 1], chosen)
        if c == 0:
            first = here.astype(f32)
    wanted = [jnp.broadcast_to(chosen[:, j : j + 1], (tok, 128)) for j in range(owners)]

    def runs(key):
        side, chunk, k = key
        if chunk < 0:
            return [(side * chips, 0, vocab_dev, ids[side * chips] * vocab_dev)]
        begin = (grp ^ k) * share
        return [
            (side * chips + d, i * share, share, ids[side * chips + d] * vocab_dev + begin)
            for i, d in enumerate(chunks[chunk])
        ]

    def tiles(key):
        for j, off, wide, base in runs(key):
            step = min(wide, 128)
            for o in range(0, wide, step):
                hit = wanted[j][:, :step] == base + o + iota((1, step), 1)
                yield j, off + o, step, hit

    yb = unit_b[...]
    value = [[] for _ in range(owners)]
    for key, parts in parts_of.items():
        product = sum(dot(yb[:, cols], part[...], NT) for cols, part in parts)
        for j, off, step, hit in tiles(key):
            value[j].append(jnp.where(hit, product[:, off : off + step], 0.0))
    logits = jnp.zeros((tok, 128), f32)
    for j in range(owners):
        total = value[j][0]
        for part in value[j][1:]:
            total = total + part
        logits = jnp.where(lane == j, jnp.sum(total, -1, keepdims=True), logits)
    exponent = jnp.where(chosen >= 0, jnp.exp(logits / softmax_warmth), 0.0)
    coef = (exponent / jnp.sum(exponent, -1, keepdims=True) - first) / softmax_warmth
    tags[:owners] = coef.T[:owners]
    tags[owners:] = chosen.astype(f32).T[:owners]
    amount = [jnp.broadcast_to(coef[:, j : j + 1], (tok, 128)) for j in range(owners)]
    pulled[...] = jnp.zeros(pulled.shape, f32)
    for key, parts in parts_of.items():
        spread = [jnp.where(hit, amount[j][:, :step], 0.0).astype(b16) for j, off, step, hit in tiles(key)]
        spread = jnp.concatenate(spread, 1) if len(spread) > 1 else spread[0]
        for cols, part in parts:
            pulled[:, cols] += dot(spread, part[...], NN)
    yn = unit[...]
    pulled = pulled[...]
    upstream = (pulled - yn * jnp.sum(yn * pulled, -1, keepdims=True)) * inv_len[...]
    up[...] = upstream.astype(b16)
    mine, other = split_columns(upstream, owners, core)
    up_keep[...] = mine.astype(b16)
    up_give[...] = other.astype(b16)


def backward_kernel(up, out_weight, proj, slope, attn, attn_slope, normed_ref, inverse, grad):
    hidden = out_weight.shape[1]
    normed = normed_ref[...]
    grad_gated = dot(up[...], out_weight[...], NN)
    grad[:, :hidden] = (grad_gated * normed * slope[:, :hidden].astype(f32)).astype(b16)
    grad_normed = grad_gated * proj[:, :hidden].astype(f32)
    grad_attended = inverse[...] * (
        grad_normed
        - jnp.mean(grad_normed, -1, keepdims=True)
        - normed * jnp.mean(grad_normed * normed, -1, keepdims=True)
    )
    grad_attended = grad_attended.astype(b16)
    for h in range(HEADS):
        cv, cq, ck = [slice(i * hidden + h * HEAD_DIM, i * hidden + (h + 1) * HEAD_DIM) for i in (1, 2, 3)]
        part = grad_attended[:, h * HEAD_DIM : (h + 1) * HEAD_DIM]
        grad_attn = dot(part, proj[:, cv], NT)
        grad_score = (grad_attn * attn_slope[h].astype(f32)).astype(b16)
        grad[:, cv] = (dot(attn[h], part, TN) * slope[:, cv].astype(f32)).astype(b16)
        grad[:, cq] = (dot(grad_score, proj[:, ck], NN) * slope[:, cq].astype(f32)).astype(b16)
        grad[:, ck] = (dot(grad_score, proj[:, cq], TN) * slope[:, ck].astype(f32)).astype(b16)


def item_kernel(groups, owners, share, chunks, places, *refs):
    count = len(places)
    units, tags = refs[:count], refs[count : count + groups]
    parts, (keep, give, gathered, near, sems) = refs[count + groups : -5], refs[-5:]
    chips = owners // 2
    vocab_dev = share * groups
    grp = lax.axis_index("grp")
    tok = tags[0].shape[1]
    copies = []
    for n, (k, left, wide) in enumerate(places):
        copies.append(pltpu.make_async_copy(units[n], gathered.at[pl.ds(k * tok, tok), pl.ds(left, wide)], sems.at[n]))
    begin = pl.multiple_of(grp * share, share)
    for n, part in enumerate(parts):
        side, chunk = n // (len(chunks) + 1), n % (len(chunks) + 1) - 1
        for i, d in enumerate([0] if chunk < 0 else chunks[chunk]):
            rows = pl.ds(begin if chunk < 0 else i * share, share)
            at = pl.ds((side * chips + d) * share, share)
            copies.append(pltpu.make_async_copy(part.at[rows], near.at[at], sems.at[len(copies)]))
    for copy in copies:
        copy.start()
    ids = owner_ids(owners)
    amounts = jnp.concatenate([t[:owners] for t in tags], 1)
    chosen = jnp.concatenate([t[owners:] for t in tags], 1).astype(i32)
    for copy in copies:
        copy.wait()
    for side, out in ((0, keep), (1, give)):
        parts = []
        for d in range(chips):
            j = side * chips + d
            hit = ids[j] * vocab_dev + grp * share + iota((share, 1), 0) == chosen[j : j + 1]
            parts.append(jnp.where(hit, amounts[j : j + 1], 0.0).astype(b16))
        summed = dot(jnp.concatenate(parts, 0), gathered[...], NN)
        row = near[side * chips * share : (side + 1) * chips * share].astype(f32)
        out[...] = (summed - row * jnp.sum(row * summed, -1, keepdims=True)).astype(b16)


def weight_kernel(groups, owners, keep, give, up_keep, up_give, grad, far_grad, gated, far_gated, *refs):
    outs, whole = refs[:-1], refs[-1]
    chips = owners // 2
    grp = lax.axis_index("grp")
    wide = grad.shape[1]
    step = gated.shape[1]
    for i in range(0, wide, step):
        cols = slice(i, i + step)
        part = dot(keep[...], grad[:, cols], TN) + dot(give[...], far_grad[:, cols], TN)
        whole[:, cols] = part.astype(b16)
    part = dot(up_keep[...], gated[...], TN) + dot(up_give[...], far_gated[...], TN)
    whole[:, wide:] = part.astype(b16)
    rows = whole.shape[0] // chips
    fine = rows // groups
    half = whole.shape[1] // 2
    base, by_one, by_two, one_right, two_left = outs
    for z in range(chips):
        piece = [whole[pl.ds(pl.multiple_of(z * rows + (grp ^ k) * fine, fine), fine)] for k in range(groups)]
        base[z] = piece[0]
        by_one[0, z], by_one[1, z] = piece[3][:, :half], piece[1][:, :half]
        by_two[0, z], by_two[1, z] = piece[3][:, half:], piece[2][:, half:]
        one_right[z], two_left[z] = piece[1][:, half:], piece[2][:, :half]


def corner_kernel(by_one, by_two, one_right, two_left, right_out, left_out):
    right_out[...] = (one_right[...].astype(f32) + by_two[0].astype(f32)).astype(b16)
    left_out[...] = (two_left[...].astype(f32) + by_one[0].astype(f32)).astype(b16)


def sum_kernel(base, by_one, by_two, one_right, two_left, *outs):
    chips, fine, wide = base.shape
    chip = lax.axis_index("seq") // 2
    half = wide // 2
    for n, d in enumerate(distances(chips)):
        z = chip ^ d
        own = base[z].astype(f32)
        left = own[:, :half] + by_one[1, z].astype(f32) + two_left[z].astype(f32)
        right = own[:, half:] + by_two[1, z].astype(f32) + one_right[z].astype(f32)
        out = outs[2 * n // chips]
        at = slice(n % (chips // 2) * fine, (n % (chips // 2) + 1) * fine)
        out[at, :half] = left.astype(b16)
        out[at, half:] = right.astype(b16)


def join_kernel(*refs):
    out, at = refs[-1], 0
    for part in refs[:-1]:
        rows = part.shape[0]
        out[at : at + rows] = part[...]
        at += rows


def columns_kernel(first, x, out):
    out[...] = x[:, first : first + out.shape[1]]


def pair_kernel(x, y, *outs):
    rows = outs[0].shape[0]
    for d, out in enumerate(outs):
        at = slice(d * rows, (d + 1) * rows)
        out[...] = (x[at].astype(f32) + y[at].astype(f32)).astype(b16)


def assemble_kernel(groups, columns, *refs):
    parts, outs = refs[:groups], refs[groups:]
    grp = lax.axis_index("grp")
    fine = parts[0].shape[0]
    for k in range(groups):
        at = pl.ds(pl.multiple_of((grp ^ k) * fine, fine), fine)
        left = 0
        for out, wide in zip(outs, columns):
            out[at] = parts[k][:, left : left + wide].astype(f32)
            left += wide


def relay_kernel(arrived, out):
    tok, slots = out.shape[0], arrived.shape[0]
    filled = (arrived[:, :128].astype(f32) < EMPTY / 2).astype(b16)
    before = (iota((slots, 1), 0) > iota((1, slots), 1)).astype(b16)
    rank = dot(before, filled, NN)[:, :1].astype(i32)
    rank = jnp.where(filled[:, :1].astype(f32) > 0, rank, -1)
    place = (rank == iota((1, tok), 1)).astype(b16)
    out[...] = dot(place, arrived[...], TN).astype(b16)


def body(events, lengths, destinations, history, negatives, in_weight, out_weight, item_table):
    groups = lax.axis_size("grp")
    owners = lax.axis_size("seq")
    chips = owners // 2
    grp = lax.axis_index("grp")
    seq = lax.axis_index("seq")
    chip, core = seq // 2, seq % 2
    tok = events.shape[0]
    vocab_dev, width = item_table.shape
    hidden = out_weight.shape[1]
    share = vocab_dev // groups
    slot = 3 * tok // (2 * owners)
    rows = width // owners
    fine = rows // groups

    def to_chip(x, d):
        pairs = [(2 * a + b, 2 * ((a + d) % chips) + b) for a in range(chips) for b in range(2)]
        return lax.ppermute(x, "seq", pairs)

    def across(x, k):
        pairs = [(2 * a + b, 2 * (a ^ k) + b) for a in range(chips) for b in range(2)]
        return lax.ppermute(x, "seq", pairs)

    def to_group(x, k):
        return lax.ppermute(x, "grp", [(a, a ^ k) for a in range(groups)])

    def to_core(x):
        return lax.ppermute(x, "seq", [(a, a ^ 1) for a in range(owners)])

    def columns(x, first, wide):
        return call(lambda *refs: columns_kernel(first, *refs), [((x.shape[0], wide), b16)], [VMEM], [x], room=8)[0]

    def join(parts):
        rows = sum(x.shape[0] for x in parts)
        return call(join_kernel, [((rows, parts[0].shape[1]), b16)], [VMEM] * len(parts), parts, room=8)[0]

    def reduce_chips(low, high):
        bit = 1
        while True:
            came = across(high, bit)
            bit *= 2
            if bit >= chips:
                return low.astype(f32) + came.astype(f32)
            shape = (low.shape[0] // 2, low.shape[1])
            low, high = call(pair_kernel, [(shape, b16)] * 2, [VMEM] * 2, [low, came], room=8)

    def gather_groups(x, near=None):
        wide = x.shape[1]
        if groups != 4:
            return [(k, 0, wide, to_group(x, k) if k else x) for k in range(groups)]
        one, two = near or [to_group(x, k) for k in (1, 2)]
        half = wide // 2
        left, right = to_group(columns(one, 0, half), 2), to_group(columns(two, half, half), 1)
        return [(0, 0, wide, x), (1, 0, wide, one), (2, 0, wide, two), (3, 0, half, left), (3, half, half, right)]

    own, quarter, quarter_inv = call(
        lambda *refs: normalise_kernel(share, *refs),
        [((vocab_dev, width), b16), ((share, width), b16), ((share, 1), f32)],
        [VMEM], [item_table], flops=8 * vocab_dev * width, nbytes=5 * vocab_dev * width, room=8,
    )
    chunks = [list(range(1, chips))]
    have, bit = {0: quarter}, chips // 2
    while bit:
        have.update({x ^ bit: across(have[x], bit) for x in have})
        bit //= 2
    got = [have[x] for x in distances(chips)[1:]]
    candidates = jnp.concatenate([history[:, None], negatives], 1)
    events, candidates = lax.optimization_barrier((events, candidates))
    outs = [
        ((tok, width // 2), b16), ((tok, width // 2), b16), ((tok, 4 * hidden), b16), ((tok, 4 * hidden), b16),
        ((HEADS, tok, tok), b16), ((HEADS, tok, tok), b16), ((tok, hidden), f32), ((tok, 1), f32),
        ((tok, hidden), b16), ((tok, width), f32), ((tok, width), b16), ((tok, 1), f32),
        ((owners * slot, width), b16),
    ]
    (keep, give, proj, slope, attn, attn_slope, normed, inverse, gated, unit, unit_b, inv_len, outgoing) = call(
        lambda *refs: forward_kernel(owners, slot, *refs), outs, [SMEM, SMEM, VMEM, VMEM, VMEM],
        [lengths, destinations, events, in_weight, out_weight],
        flops=2 * tok * width * 6 * hidden, nbytes=24 * tok * width + 10 * width * hidden, room=28,
    )

    near_units = [to_group(unit_b, k) for k in (1, 2)]
    got, near_units, own = lax.optimization_barrier((got, near_units, own))
    far_own = to_core(own)
    unit_sent = gather_groups(unit_b, near_units)
    others = [join(got)]
    pieces = [(0, -1, 0, 0, width, own)]
    for j, x in enumerate(others):
        pieces += [(0, j) + p for p in gather_groups(x)]
    pieces = pieces + [(1,) + p[1:5] + (to_core(p[5]) if p[1] >= 0 else far_own,) for p in pieces]
    near = [p[5] for p in pieces if p[2] == 0]
    outgoing, _ = lax.optimization_barrier((outgoing, others))

    arrived = lax.all_to_all(
        outgoing.reshape(owners, slot, width), "seq", 0, 0, tiled=True
    ).reshape(owners * slot, width)
    layer_out, = call(
        relay_kernel, [((tok, width), b16)], [VMEM], [arrived],
        room=8,
    )

    vocab = vocab_dev * owners
    far_give, far_gated = to_core(give), to_core(gated)
    units = [p[3] for p in unit_sent]
    layer_out, score_unit, far_give, far_gated, units = lax.optimization_barrier(
        (layer_out, unit, far_give, far_gated, units)
    )
    tags, up, up_keep, up_give = call(
        lambda *refs: score_kernel(groups, owners, share, chunks, [p[:5] for p in pieces], *refs),
        [((2 * owners, tok), f32), ((tok, width), b16), ((tok, width // 2), b16), ((tok, width // 2), b16)],
        [VMEM] * (len(pieces) + 4), [candidates, inv_len, unit_b, score_unit] + [p[5] for p in pieces],
        [pltpu.VMEM((tok, width), f32)],
        flops=4 * tok * width * vocab, nbytes=2 * vocab * width + 12 * tok * width, room=20 if groups == 4 else 40,
    )

    grad, = call(
        backward_kernel, [((tok, 4 * hidden), b16)], [VMEM] * 8,
        [up, out_weight, proj, slope, attn, attn_slope, normed, inverse],
    )

    all_tags = [to_group(tags, k) if k else tags for k in range(groups)]
    far = [far_give, to_core(up_give), None, far_gated]
    grad, far[1], all_tags = lax.optimization_barrier((grad, far[1], all_tags))
    far[2] = to_core(grad)
    half = 5 * hidden // 2
    if groups == 4:
        block = (chips, fine, 5 * hidden)
        split = (chips, fine, half)
        parts = call(
            lambda *refs: weight_kernel(groups, owners, *refs),
            [(block, b16)] + [((2,) + split, b16)] * 2 + [(split, b16)] * 2, [VMEM] * 8,
            [keep, far[0], up_keep, far[1], grad, far[2], gated, far[3]],
            [pltpu.VMEM((width // 2, 5 * hidden), b16)],
            flops=2 * tok * width * 5 * hidden, nbytes=20 * tok * width,
        )
        after = parts[0]
        by_one, by_two = to_group(parts[1], 1), to_group(parts[2], 2)
        corner = (by_one, by_two)
    else:
        def both(x, y):
            return jnp.concatenate([x, y], 0)

        in_part = dot(both(keep, far[0]), both(grad, far[2]), TN)
        out_part = dot(both(up_keep, far[1]), both(gated, far[3]), TN)
        weight = jnp.concatenate([in_part, out_part], 1).astype(b16)
        weight = weight.reshape(chips, groups, fine, 5 * hidden)
        after = weight
        sums = lax.dynamic_index_in_dim(weight, grp, 1, False).astype(f32)
        for k in range(1, groups):
            sums += to_group(lax.dynamic_index_in_dim(weight, grp ^ k, 1, False), k).astype(f32)


    units[0], _ = lax.optimization_barrier((units[0], after))
    mine, other = call(
        lambda *refs: item_kernel(groups, owners, share, chunks, [p[:3] for p in unit_sent], *refs),
        [((chips * share, width), b16)] * 2, [ANY] * len(units) + [VMEM] * groups + [ANY] * len(near),
        units + all_tags + near,
        [pltpu.VMEM((groups * tok, width), b16), pltpu.VMEM((2 * chips * share, width), b16),
         pltpu.SemaphoreType.DMA((len(units) + 2 * chips,))],
        room=16 if groups == 4 else 48,
    )
    far_mine = to_core(other)

    low, high = call(
        pair_kernel, [((chips // 2 * share, width), b16)] * 2, [VMEM] * 2, [mine, far_mine],
        flops=chips * share * width, nbytes=6 * chips * share * width, room=8,
    )
    if groups == 4:
        by_one, by_two, low, high = lax.optimization_barrier(corner + (low, high))
        one_right, two_left = call(
            corner_kernel, [(split, b16)] * 2, [VMEM] * 4, [by_one, by_two, parts[3], parts[4]], room=8,
        )
        arrived = [by_one, by_two, to_group(one_right, 1), to_group(two_left, 2)]
    total = reduce_chips(low, high)
    total = (total * quarter_inv).astype(b16)
    table_grad, = call(
        lambda *refs: assemble_kernel(groups, [width], *refs), [((vocab_dev, width), f32)], [VMEM] * groups,
        [to_group(total, k) if k else total for k in range(groups)],
        flops=vocab_dev * width, nbytes=6 * vocab_dev * width, room=8,
    )

    if groups == 4:
        low, high = call(
            sum_kernel, [((chips // 2 * fine, 5 * hidden), b16)] * 2, [VMEM] * 5, [parts[0]] + arrived,
            flops=chips * fine * 5 * hidden, nbytes=40 * chips * fine * hidden, room=10,
        )
        line = reduce_chips(low, high)
    else:
        blocks = [lax.dynamic_index_in_dim(sums, (chip + d) % chips, 0, False).astype(b16) for d in range(chips)]
        line = blocks[0].astype(f32)
        for d in range(1, chips):
            line += to_chip(blocks[d], d).astype(f32)
    line = line.astype(b16)
    lines = [to_group(line, k) if k else line for k in range(groups)]
    if fine % 16 == 0:
        in_grad, out_grad = call(
            lambda *refs: assemble_kernel(groups, [4 * hidden, hidden], *refs),
            [((rows, 4 * hidden), f32), ((rows, hidden), f32)], [VMEM] * groups, lines,
            flops=rows * hidden, nbytes=30 * rows * hidden, room=8,
        )
    else:
        shard = jnp.zeros((rows, 5 * hidden), f32)
        for k in range(groups):
            shard = lax.dynamic_update_slice_in_dim(shard, lines[k].astype(f32), (grp ^ k) * fine, 0)
        in_grad, out_grad = shard[:, : 4 * hidden], shard[:, 4 * hidden :]
    return (layer_out, in_grad, out_grad, table_grad)


def solution(mesh):
    return jax.shard_map(
        body,
        mesh=mesh,
        in_specs=(
            P(("grp", "seq"), None),
            P(("grp", "seq"), None),
            P(("grp", "seq"), None),
            P(("grp", "seq")),
            P(("grp", "seq"), None),
            P(),
            P(),
            P("seq", None),
        ),
        out_specs=(P(("grp", "seq"), None), P("seq", None), P("seq", None), P("seq", None)),
        check_vma=False,
    )
```

```python
import jax
import jax.numpy as jnp
from jax import lax
from jax.experimental import pallas as pl
from jax.experimental.pallas import tpu as pltpu
from jax.sharding import PartitionSpec as P

HEADS = 4
HEAD_DIM = 128
NCAND = 4

epsilon = 1e-05
softmax_warmth = 0.05
EMPTY = 2.0**100

f32, b16, i32 = jnp.float32, jnp.bfloat16, jnp.int32
NN = ((1,), (0,))
NT = ((1,), (1,))
TN = ((0,), (0,))
VMEM = pl.BlockSpec(memory_space=pltpu.VMEM)
SMEM = pl.BlockSpec(memory_space=pltpu.SMEM)
ANY = pl.BlockSpec(memory_space=pl.ANY)


def dot(a, b, dims):
    return lax.dot_general(a, b, (dims, ((), ())), preferred_element_type=f32)


def iota(shape, axis):
    return lax.broadcasted_iota(i32, shape, axis)


def center_scale(values):
    average = jnp.mean(values, -1, keepdims=True)
    centered = values - average
    inverse = lax.rsqrt(jnp.mean(centered * centered, -1, keepdims=True) + epsilon)
    return (centered * inverse, inverse)


def sigmoid(values):
    return 1.0 / (1.0 + jnp.exp(-values))


def split_columns(x, owners, core):
    rows = x.shape[1] // owners
    blocks = [x[:, i * rows : (i + 1) * rows] for i in range(owners)]
    even, odd = jnp.concatenate(blocks[0::2], 1), jnp.concatenate(blocks[1::2], 1)
    first = jnp.broadcast_to(core, even.shape) == 0
    return jnp.where(first, even, odd), jnp.where(first, odd, even)


def call(kernel, out, specs, args, scratch=(), flops=0, nbytes=0, room=14):
    return pl.pallas_call(
        kernel,
        out_shape=[jax.ShapeDtypeStruct(s, t) for s, t in out],
        in_specs=specs,
        out_specs=[VMEM] * len(out),
        scratch_shapes=list(scratch),
        cost_estimate=pl.CostEstimate(flops=flops, bytes_accessed=nbytes, transcendentals=0),
        compiler_params=pltpu.CompilerParams(vmem_limit_bytes=room * 2**20),
    )(*args)


def forward_kernel(
    owners, slot, lengths, dests, events, in_weight, out_weight, cand, cand_out,
    keep, give, proj, slope, attn, attn_slope, normed_out, inv_out, gated_out, unit, unit_b, inv_len, outgoing,
):
    tok = events.shape[0]
    hidden = out_weight.shape[1]
    scale = HEAD_DIM ** (-0.5)
    core = lax.axis_index("seq") % 2
    cand_out[...] = cand[...]
    x = events[...].astype(f32)
    normed_in = center_scale(x)[0]
    mine, other = split_columns(normed_in, owners, core)
    keep[...] = mine.astype(b16)
    give[...] = other.astype(b16)
    normed_in = normed_in.astype(b16)
    for i in range(4):
        cols = slice(i * hidden, (i + 1) * hidden)
        p = dot(normed_in, in_weight[:, cols], NN)
        sig = sigmoid(p)
        proj[:, cols] = (p * sig).astype(b16)
        slope[:, cols] = (sig * (1.0 + p * (1.0 - sig))).astype(b16)

    pos_c, pos_r = iota((tok, 1), 0), iota((1, tok), 1)
    user_c, user_r = jnp.zeros((tok, 1), i32), jnp.zeros((1, tok), i32)
    target = jnp.zeros((1, tok), i32)
    start = jnp.int32(0)
    for j in range(lengths.shape[1]):
        end = start + lengths[0, j]
        user_c += (pos_c >= end).astype(i32)
        user_r += (pos_r >= end).astype(i32)
        here = (pos_r >= start) & (pos_r < end)
        target = jnp.where(here, dests[0, j] * slot + pos_r - start, target)
        start = end
    mask = (user_c == user_r) & (pos_r <= pos_c)

    outputs = []
    for h in range(HEADS):
        v = proj[:, hidden + h * HEAD_DIM : hidden + (h + 1) * HEAD_DIM]
        q = proj[:, 2 * hidden + h * HEAD_DIM : 2 * hidden + (h + 1) * HEAD_DIM]
        k = proj[:, 3 * hidden + h * HEAD_DIM : 3 * hidden + (h + 1) * HEAD_DIM]
        s = dot(q, k, NT) * scale
        sig = sigmoid(s)
        weight = jnp.where(mask, s * sig, 0.0).astype(b16)
        attn[h] = weight
        attn_slope[h] = jnp.where(mask, sig * (1.0 + s * (1.0 - sig)) * scale, 0.0).astype(b16)
        outputs.append(dot(weight, v, NN))
    normed, inverse = center_scale(jnp.concatenate(outputs, 1))
    normed_out[...] = normed
    inv_out[...] = inverse
    gated = (normed * proj[:, :hidden].astype(f32)).astype(b16)
    gated_out[...] = gated
    result = x + dot(gated, out_weight[...], NT)
    inverse = lax.rsqrt(jnp.sum(result * result, -1, keepdims=True) + epsilon)
    inv_len[...] = inverse
    yn = result * inverse
    unit[...] = yn
    unit_b[...] = yn.astype(b16)
    row = iota((outgoing.shape[0], 1), 0)
    filled = jnp.zeros(row.shape, i32)
    for j in range(lengths.shape[1]):
        at = dests[0, j] * slot
        filled = jnp.where((row >= at) & (row < at + lengths[0, j]), 1, filled)
    placed = dot((row == target).astype(b16), result.astype(b16), NN)
    outgoing[...] = jnp.where(filled == 1, placed, EMPTY).astype(b16)


def distances(chips):
    order, bit = [0], chips // 2
    while bit:
        order += [x ^ bit for x in order]
        bit //= 2
    return order


def owner_ids(owners):
    seq = lax.axis_index("seq")
    chip, core = seq // 2, seq % 2
    chips = owners // 2
    return [2 * (chip ^ d) + (core ^ side) for side in range(2) for d in distances(chips)]


def normalise_kernel(share, item_table, own, quarter, quarter_inv):
    grp = lax.axis_index("grp")
    x = item_table[...].astype(f32)
    own[...] = (x * lax.rsqrt(jnp.sum(x * x, -1, keepdims=True) + epsilon)).astype(b16)
    x = item_table[pl.ds(pl.multiple_of(grp * share, share), share)].astype(f32)
    inverse = lax.rsqrt(jnp.sum(x * x, -1, keepdims=True) + epsilon)
    quarter[...] = (x * inverse).astype(b16)
    quarter_inv[...] = inverse


def score_kernel(groups, owners, share, chunks, places, cand, inv_len, unit_b, unit, *refs):
    count = len(places)
    pieces, (tags, up, up_keep, up_give, pulled) = refs[:count], refs[count:]
    chips = owners // 2
    vocab_dev = share * groups
    grp, core = lax.axis_index("grp"), lax.axis_index("seq") % 2
    tok = unit_b.shape[0]
    parts_of = {}
    for n, (*key, left, wide) in enumerate(places):
        parts_of.setdefault(tuple(key), []).append((slice(left, left + wide), pieces[n]))
    ids = owner_ids(owners)
    lane = iota((1, 128), 1)
    owner = jnp.full((1, 128), -1, i32)
    for j in range(owners):
        owner = jnp.where(lane == j, ids[j], owner)
    candidates = cand[...]
    chosen = jnp.full((tok, 128), -1, i32)
    first = jnp.zeros((tok, 128), f32)
    for c in range(NCAND):
        here = candidates[:, c : c + 1] // vocab_dev == owner
        chosen = jnp.where(here, candidates[:, c : c + 1], chosen)
        if c == 0:
            first = here.astype(f32)
    wanted = [jnp.broadcast_to(chosen[:, j : j + 1], (tok, 128)) for j in range(owners)]

    def runs(key):
        side, chunk, k = key
        if chunk < 0:
            return [(side * chips, 0, vocab_dev, ids[side * chips] * vocab_dev)]
        begin = (grp ^ k) * share
        return [
            (side * chips + d, i * share, share, ids[side * chips + d] * vocab_dev + begin)
            for i, d in enumerate(chunks[chunk])
        ]

    def tiles(key):
        for j, off, wide, base in runs(key):
            step = min(wide, 128)
            for o in range(0, wide, step):
                hit = wanted[j][:, :step] == base + o + iota((1, step), 1)
                yield j, off + o, step, hit

    yb = unit_b[...]
    value = [[] for _ in range(owners)]
    for key, parts in parts_of.items():
        product = sum(dot(yb[:, cols], part[...], NT) for cols, part in parts)
        for j, off, step, hit in tiles(key):
            value[j].append(jnp.where(hit, product[:, off : off + step], 0.0))
    logits = jnp.zeros((tok, 128), f32)
    for j in range(owners):
        total = value[j][0]
        for part in value[j][1:]:
            total = total + part
        logits = jnp.where(lane == j, jnp.sum(total, -1, keepdims=True), logits)
    exponent = jnp.where(chosen >= 0, jnp.exp(logits / softmax_warmth), 0.0)
    coef = (exponent / jnp.sum(exponent, -1, keepdims=True) - first) / softmax_warmth
    tags[:owners] = coef.T[:owners]
    tags[owners:] = chosen.astype(f32).T[:owners]
    amount = [jnp.broadcast_to(coef[:, j : j + 1], (tok, 128)) for j in range(owners)]
    pulled[...] = jnp.zeros(pulled.shape, f32)
    for key, parts in parts_of.items():
        spread = [jnp.where(hit, amount[j][:, :step], 0.0).astype(b16) for j, off, step, hit in tiles(key)]
        spread = jnp.concatenate(spread, 1) if len(spread) > 1 else spread[0]
        for cols, part in parts:
            pulled[:, cols] += dot(spread, part[...], NN)
    yn = unit[...]
    pulled = pulled[...]
    upstream = (pulled - yn * jnp.sum(yn * pulled, -1, keepdims=True)) * inv_len[...]
    up[...] = upstream.astype(b16)
    mine, other = split_columns(upstream, owners, core)
    up_keep[...] = mine.astype(b16)
    up_give[...] = other.astype(b16)


def backward_kernel(up, out_weight, proj, slope, attn, attn_slope, normed_ref, inverse, grad):
    hidden = out_weight.shape[1]
    normed = normed_ref[...]
    grad_gated = dot(up[...], out_weight[...], NN)
    grad[:, :hidden] = (grad_gated * normed * slope[:, :hidden].astype(f32)).astype(b16)
    grad_normed = grad_gated * proj[:, :hidden].astype(f32)
    grad_attended = inverse[...] * (
        grad_normed
        - jnp.mean(grad_normed, -1, keepdims=True)
        - normed * jnp.mean(grad_normed * normed, -1, keepdims=True)
    )
    grad_attended = grad_attended.astype(b16)
    for h in range(HEADS):
        cv, cq, ck = [slice(i * hidden + h * HEAD_DIM, i * hidden + (h + 1) * HEAD_DIM) for i in (1, 2, 3)]
        part = grad_attended[:, h * HEAD_DIM : (h + 1) * HEAD_DIM]
        grad_attn = dot(part, proj[:, cv], NT)
        grad_score = (grad_attn * attn_slope[h].astype(f32)).astype(b16)
        grad[:, cv] = (dot(attn[h], part, TN) * slope[:, cv].astype(f32)).astype(b16)
        grad[:, cq] = (dot(grad_score, proj[:, ck], NN) * slope[:, cq].astype(f32)).astype(b16)
        grad[:, ck] = (dot(grad_score, proj[:, cq], TN) * slope[:, ck].astype(f32)).astype(b16)


def item_kernel(groups, owners, share, chunks, places, *refs):
    count = len(places)
    units, tags = refs[:count], refs[count : count + groups]
    parts, (keep, give, gathered, near, sems) = refs[count + groups : -5], refs[-5:]
    chips = owners // 2
    vocab_dev = share * groups
    grp = lax.axis_index("grp")
    tok = tags[0].shape[1]
    copies = []
    for n, (k, left, wide) in enumerate(places):
        copies.append(pltpu.make_async_copy(units[n], gathered.at[pl.ds(k * tok, tok), pl.ds(left, wide)], sems.at[n]))
    begin = pl.multiple_of(grp * share, share)
    for n, part in enumerate(parts):
        side, chunk = n // (len(chunks) + 1), n % (len(chunks) + 1) - 1
        for i, d in enumerate([0] if chunk < 0 else chunks[chunk]):
            rows = pl.ds(begin if chunk < 0 else i * share, share)
            at = pl.ds((side * chips + d) * share, share)
            copies.append(pltpu.make_async_copy(part.at[rows], near.at[at], sems.at[len(copies)]))
    for copy in copies:
        copy.start()
    ids = owner_ids(owners)
    amounts = jnp.concatenate([t[:owners] for t in tags], 1)
    chosen = jnp.concatenate([t[owners:] for t in tags], 1).astype(i32)
    for copy in copies:
        copy.wait()
    for side, out in ((0, keep), (1, give)):
        parts = []
        for d in range(chips):
            j = side * chips + d
            hit = ids[j] * vocab_dev + grp * share + iota((share, 1), 0) == chosen[j : j + 1]
            parts.append(jnp.where(hit, amounts[j : j + 1], 0.0).astype(b16))
        summed = dot(jnp.concatenate(parts, 0), gathered[...], NN)
        row = near[side * chips * share : (side + 1) * chips * share].astype(f32)
        out[...] = (summed - row * jnp.sum(row * summed, -1, keepdims=True)).astype(b16)


def weight_kernel(groups, owners, keep, give, up_keep, up_give, grad, far_grad, gated, far_gated, *refs):
    outs, whole = refs[:-1], refs[-1]
    chips = owners // 2
    grp = lax.axis_index("grp")
    wide = grad.shape[1]
    step = gated.shape[1]
    for i in range(0, wide, step):
        cols = slice(i, i + step)
        part = dot(keep[...], grad[:, cols], TN) + dot(give[...], far_grad[:, cols], TN)
        whole[:, cols] = part.astype(b16)
    part = dot(up_keep[...], gated[...], TN) + dot(up_give[...], far_gated[...], TN)
    whole[:, wide:] = part.astype(b16)
    rows = whole.shape[0] // chips
    fine = rows // groups
    half = whole.shape[1] // 2
    base, by_one, by_two, one_right, two_left = outs
    for z in range(chips):
        piece = [whole[pl.ds(pl.multiple_of(z * rows + (grp ^ k) * fine, fine), fine)] for k in range(groups)]
        base[z] = piece[0]
        by_one[0, z], by_one[1, z] = piece[3][:, :half], piece[1][:, :half]
        by_two[0, z], by_two[1, z] = piece[3][:, half:], piece[2][:, half:]
        one_right[z], two_left[z] = piece[1][:, half:], piece[2][:, :half]


def corner_kernel(by_one, by_two, one_right, two_left, right_out, left_out):
    right_out[...] = (one_right[...].astype(f32) + by_two[0].astype(f32)).astype(b16)
    left_out[...] = (two_left[...].astype(f32) + by_one[0].astype(f32)).astype(b16)


def sum_kernel(base, by_one, by_two, one_right, two_left, *outs):
    chips, fine, wide = base.shape
    chip = lax.axis_index("seq") // 2
    half = wide // 2
    for n, d in enumerate(distances(chips)):
        z = chip ^ d
        own = base[z].astype(f32)
        left = own[:, :half] + by_one[1, z].astype(f32) + two_left[z].astype(f32)
        right = own[:, half:] + by_two[1, z].astype(f32) + one_right[z].astype(f32)
        out = outs[2 * n // chips]
        at = slice(n % (chips // 2) * fine, (n % (chips // 2) + 1) * fine)
        out[at, :half] = left.astype(b16)
        out[at, half:] = right.astype(b16)


def join_kernel(*refs):
    out, at = refs[-1], 0
    for part in refs[:-1]:
        rows = part.shape[0]
        out[at : at + rows] = part[...]
        at += rows


def columns_kernel(first, x, out):
    out[...] = x[:, first : first + out.shape[1]]


def pair_kernel(x, y, *outs):
    rows = outs[0].shape[0]
    for d, out in enumerate(outs):
        at = slice(d * rows, (d + 1) * rows)
        out[...] = (x[at].astype(f32) + y[at].astype(f32)).astype(b16)


def assemble_kernel(groups, columns, *refs):
    parts, outs = refs[:groups], refs[groups:]
    grp = lax.axis_index("grp")
    fine = parts[0].shape[0]
    for k in range(groups):
        at = pl.ds(pl.multiple_of((grp ^ k) * fine, fine), fine)
        left = 0
        for out, wide in zip(outs, columns):
            out[at] = parts[k][:, left : left + wide].astype(f32)
            left += wide


def relay_kernel(arrived, out):
    tok, slots = out.shape[0], arrived.shape[0]
    filled = (arrived[:, :128].astype(f32) < EMPTY / 2).astype(b16)
    before = (iota((slots, 1), 0) > iota((1, slots), 1)).astype(b16)
    rank = dot(before, filled, NN)[:, :1].astype(i32)
    rank = jnp.where(filled[:, :1].astype(f32) > 0, rank, -1)
    place = (rank == iota((1, tok), 1)).astype(b16)
    out[...] = dot(place, arrived[...], TN).astype(b16)


def body(events, lengths, destinations, history, negatives, in_weight, out_weight, item_table):
    groups = lax.axis_size("grp")
    owners = lax.axis_size("seq")
    chips = owners // 2
    grp = lax.axis_index("grp")
    seq = lax.axis_index("seq")
    chip, core = seq // 2, seq % 2
    tok = events.shape[0]
    vocab_dev, width = item_table.shape
    hidden = out_weight.shape[1]
    share = vocab_dev // groups
    slot = 3 * tok // (2 * owners)
    rows = width // owners
    fine = rows // groups

    def to_chip(x, d):
        pairs = [(2 * a + b, 2 * ((a + d) % chips) + b) for a in range(chips) for b in range(2)]
        return lax.ppermute(x, "seq", pairs)

    def across(x, k):
        pairs = [(2 * a + b, 2 * (a ^ k) + b) for a in range(chips) for b in range(2)]
        return lax.ppermute(x, "seq", pairs)

    def to_group(x, k):
        return lax.ppermute(x, "grp", [(a, a ^ k) for a in range(groups)])

    def to_core(x):
        return lax.ppermute(x, "seq", [(a, a ^ 1) for a in range(owners)])

    def columns(x, first, wide):
        return call(lambda *refs: columns_kernel(first, *refs), [((x.shape[0], wide), b16)], [VMEM], [x], room=8)[0]

    def join(parts):
        rows = sum(x.shape[0] for x in parts)
        return call(join_kernel, [((rows, parts[0].shape[1]), b16)], [VMEM] * len(parts), parts, room=8)[0]

    def fold(low, high):
        bit = 1
        while bit < chips // 2:
            shape = (low.shape[0] // 2, low.shape[1])
            low, high = call(pair_kernel, [(shape, b16)] * 2, [VMEM] * 2, [low, across(high, bit)], room=8)
            bit *= 2
        return low, high

    def finish(low, high):
        return low.astype(f32) + across(high, chips // 2).astype(f32)

    def gather_groups(x, near=None):
        wide = x.shape[1]
        if groups != 4:
            return [(k, 0, wide, to_group(x, k) if k else x) for k in range(groups)]
        one, two = near or [to_group(x, k) for k in (1, 2)]
        half = wide // 2
        left, right = to_group(columns(one, 0, half), 2), to_group(columns(two, half, half), 1)
        return [(0, 0, wide, x), (1, 0, wide, one), (2, 0, wide, two), (3, 0, half, left), (3, half, half, right)]

    own, quarter, quarter_inv = call(
        lambda *refs: normalise_kernel(share, *refs),
        [((vocab_dev, width), b16), ((share, width), b16), ((share, 1), f32)],
        [VMEM], [item_table], flops=8 * vocab_dev * width, nbytes=5 * vocab_dev * width, room=8,
    )
    chunks = [list(range(1, chips))]
    have, bit = {0: quarter}, chips // 2
    while bit:
        have.update({x ^ bit: across(have[x], bit) for x in have})
        bit //= 2
    got = [have[x] for x in distances(chips)[1:]]
    candidates = jnp.concatenate([history[:, None], negatives], 1)
    events, candidates, _ = lax.optimization_barrier((events, candidates, [have[x] for x in have if x and not x & (x - 1)]))
    outs = [
        ((tok, NCAND), i32), ((tok, width // 2), b16), ((tok, width // 2), b16), ((tok, 4 * hidden), b16), ((tok, 4 * hidden), b16),
        ((HEADS, tok, tok), b16), ((HEADS, tok, tok), b16), ((tok, hidden), f32), ((tok, 1), f32),
        ((tok, hidden), b16), ((tok, width), f32), ((tok, width), b16), ((tok, 1), f32),
        ((owners * slot, width), b16),
    ]
    (candidates, keep, give, proj, slope, attn, attn_slope, normed, inverse, gated, unit, unit_b, inv_len, outgoing) = call(
        lambda *refs: forward_kernel(owners, slot, *refs), outs, [SMEM, SMEM, VMEM, VMEM, VMEM, VMEM],
        [lengths, destinations, events, in_weight, out_weight, candidates],
        flops=2 * tok * width * 6 * hidden, nbytes=24 * tok * width + 10 * width * hidden, room=28,
    )

    near_units = [to_group(unit_b, k) for k in (1, 2)]
    got, near_units, own = lax.optimization_barrier((got, near_units, own))
    far_own = to_core(own)
    unit_sent = gather_groups(unit_b, near_units)
    others = [join(got)]
    pieces = [(0, -1, 0, 0, width, own)]
    for j, x in enumerate(others):
        pieces += [(0, j) + p for p in gather_groups(x)]
    pieces = pieces + [(1,) + p[1:5] + (to_core(p[5]) if p[1] >= 0 else far_own,) for p in pieces]
    near = [p[5] for p in pieces if p[2] == 0]
    outgoing, _ = lax.optimization_barrier((outgoing, others))

    arrived = lax.all_to_all(
        outgoing.reshape(owners, slot, width), "seq", 0, 0, tiled=True
    ).reshape(owners * slot, width)
    layer_out, = call(
        relay_kernel, [((tok, width), b16)], [VMEM], [arrived],
        room=8,
    )

    vocab = vocab_dev * owners
    far_give, far_gated = to_core(give), to_core(gated)
    units = [p[3] for p in unit_sent]
    layer_out, score_unit, far_give, far_gated, units = lax.optimization_barrier(
        (layer_out, unit, far_give, far_gated, units)
    )
    tags, up, up_keep, up_give = call(
        lambda *refs: score_kernel(groups, owners, share, chunks, [p[:5] for p in pieces], *refs),
        [((2 * owners, tok), f32), ((tok, width), b16), ((tok, width // 2), b16), ((tok, width // 2), b16)],
        [VMEM] * (len(pieces) + 4), [candidates, inv_len, unit_b, score_unit] + [p[5] for p in pieces],
        [pltpu.VMEM((tok, width), f32)],
        flops=4 * tok * width * vocab, nbytes=2 * vocab * width + 12 * tok * width, room=20 if groups == 4 else 40,
    )

    grad, = call(
        backward_kernel, [((tok, 4 * hidden), b16)], [VMEM] * 8,
        [up, out_weight, proj, slope, attn, attn_slope, normed, inverse],
    )

    all_tags = [to_group(tags, k) if k else tags for k in range(groups)]
    far = [far_give, to_core(up_give), None, far_gated]
    grad, far[1], all_tags = lax.optimization_barrier((grad, far[1], all_tags))
    far[2] = to_core(grad)
    mine, other = call(
        lambda *refs: item_kernel(groups, owners, share, chunks, [p[:3] for p in unit_sent], *refs),
        [((chips * share, width), b16)] * 2, [ANY] * len(units) + [VMEM] * groups + [ANY] * len(near),
        units + all_tags + near,
        [pltpu.VMEM((groups * tok, width), b16), pltpu.VMEM((2 * chips * share, width), b16),
         pltpu.SemaphoreType.DMA((len(units) + 2 * chips,))],
        room=16 if groups == 4 else 48,
    )
    far_mine = to_core(other)
    far, mine = lax.optimization_barrier((far, mine))
    half = 5 * hidden // 2
    if groups == 4:
        block = (chips, fine, 5 * hidden)
        split = (chips, fine, half)
        parts = call(
            lambda *refs: weight_kernel(groups, owners, *refs),
            [(block, b16)] + [((2,) + split, b16)] * 2 + [(split, b16)] * 2, [VMEM] * 8,
            [keep, far[0], up_keep, far[1], grad, far[2], gated, far[3]],
            [pltpu.VMEM((width // 2, 5 * hidden), b16)],
            flops=2 * tok * width * 5 * hidden, nbytes=20 * tok * width,
        )
        by_one, by_two = to_group(parts[1], 1), to_group(parts[2], 2)
        corner = (by_one, by_two)
    else:
        def both(x, y):
            return jnp.concatenate([x, y], 0)

        in_part = dot(both(keep, far[0]), both(grad, far[2]), TN)
        out_part = dot(both(up_keep, far[1]), both(gated, far[3]), TN)
        weight = jnp.concatenate([in_part, out_part], 1).astype(b16)
        weight = weight.reshape(chips, groups, fine, 5 * hidden)
        sums = lax.dynamic_index_in_dim(weight, grp, 1, False).astype(f32)
        for k in range(1, groups):
            sums += to_group(lax.dynamic_index_in_dim(weight, grp ^ k, 1, False), k).astype(f32)


    low, high = call(
        pair_kernel, [((chips // 2 * share, width), b16)] * 2, [VMEM] * 2, [mine, far_mine],
        flops=chips * share * width, nbytes=6 * chips * share * width, room=8,
    )
    low, high = fold(low, high)
    if groups == 4:
        by_one, by_two, low, high = lax.optimization_barrier(corner + (low, high))
        one_right, two_left = call(
            corner_kernel, [(split, b16)] * 2, [VMEM] * 4, [by_one, by_two, parts[3], parts[4]], room=8,
        )
        arrived = [by_one, by_two, to_group(one_right, 1), to_group(two_left, 2)]
    total = finish(low, high)
    total = (total * quarter_inv).astype(b16)
    table_grad, = call(
        lambda *refs: assemble_kernel(groups, [width], *refs), [((vocab_dev, width), f32)], [VMEM] * groups,
        [to_group(total, k) if k else total for k in range(groups)],
        flops=vocab_dev * width, nbytes=6 * vocab_dev * width, room=8,
    )

    if groups == 4:
        base, _ = lax.optimization_barrier((parts[0], total))
        low, high = call(
            sum_kernel, [((chips // 2 * fine, 5 * hidden), b16)] * 2, [VMEM] * 5, [base] + arrived,
            flops=chips * fine * 5 * hidden, nbytes=40 * chips * fine * hidden, room=10,
        )
        line = finish(*fold(low, high))
    else:
        blocks = [lax.dynamic_index_in_dim(sums, (chip + d) % chips, 0, False).astype(b16) for d in range(chips)]
        line = blocks[0].astype(f32)
        for d in range(1, chips):
            line += to_chip(blocks[d], d).astype(f32)
    line = line.astype(b16)
    lines = [to_group(line, k) if k else line for k in range(groups)]
    if fine % 16 == 0:
        in_grad, out_grad = call(
            lambda *refs: assemble_kernel(groups, [4 * hidden, hidden], *refs),
            [((rows, 4 * hidden), f32), ((rows, hidden), f32)], [VMEM] * groups, lines,
            flops=rows * hidden, nbytes=30 * rows * hidden, room=8,
        )
    else:
        shard = jnp.zeros((rows, 5 * hidden), f32)
        for k in range(groups):
            shard = lax.dynamic_update_slice_in_dim(shard, lines[k].astype(f32), (grp ^ k) * fine, 0)
        in_grad, out_grad = shard[:, : 4 * hidden], shard[:, 4 * hidden :]
    return (layer_out, in_grad, out_grad, table_grad)


def solution(mesh):
    return jax.shard_map(
        body,
        mesh=mesh,
        in_specs=(
            P(("grp", "seq"), None),
            P(("grp", "seq"), None),
            P(("grp", "seq"), None),
            P(("grp", "seq")),
            P(("grp", "seq"), None),
            P(),
            P(),
            P("seq", None),
        ),
        out_specs=(P(("grp", "seq"), None), P("seq", None), P("seq", None), P("seq", None)),
        check_vma=False,
    )
```

```python
import jax
import jax.numpy as jnp
from jax import lax
from jax.experimental import pallas as pl
from jax.experimental.pallas import tpu as pltpu
from jax.sharding import PartitionSpec as P

HEADS = 4
HEAD_DIM = 128
NCAND = 4

epsilon = 1e-05
softmax_warmth = 0.05
EMPTY = 2.0**100

f32, b16, i32 = jnp.float32, jnp.bfloat16, jnp.int32
NN = ((1,), (0,))
NT = ((1,), (1,))
TN = ((0,), (0,))
VMEM = pl.BlockSpec(memory_space=pltpu.VMEM)
SMEM = pl.BlockSpec(memory_space=pltpu.SMEM)
ANY = pl.BlockSpec(memory_space=pl.ANY)


def dot(a, b, dims):
    return lax.dot_general(a, b, (dims, ((), ())), preferred_element_type=f32)


def iota(shape, axis):
    return lax.broadcasted_iota(i32, shape, axis)


def center_scale(values):
    average = jnp.mean(values, -1, keepdims=True)
    centered = values - average
    inverse = lax.rsqrt(jnp.mean(centered * centered, -1, keepdims=True) + epsilon)
    return (centered * inverse, inverse)


def sigmoid(values):
    return 1.0 / (1.0 + jnp.exp(-values))


def split_columns(x, owners, core):
    rows = x.shape[1] // owners
    blocks = [x[:, i * rows : (i + 1) * rows] for i in range(owners)]
    even, odd = jnp.concatenate(blocks[0::2], 1), jnp.concatenate(blocks[1::2], 1)
    first = jnp.broadcast_to(core, even.shape) == 0
    return jnp.where(first, even, odd), jnp.where(first, odd, even)


def call(kernel, out, specs, args, scratch=(), flops=0, nbytes=0, room=14):
    return pl.pallas_call(
        kernel,
        out_shape=[jax.ShapeDtypeStruct(s, t) for s, t in out],
        in_specs=specs,
        out_specs=[VMEM] * len(out),
        scratch_shapes=list(scratch),
        cost_estimate=pl.CostEstimate(flops=flops, bytes_accessed=nbytes, transcendentals=0),
        compiler_params=pltpu.CompilerParams(vmem_limit_bytes=room * 2**20),
    )(*args)


def forward_kernel(
    owners, slot, lengths, dests, events, in_weight, out_weight,
    keep, give, proj, slope, attn, attn_slope, normed_out, inv_out, gated_out, unit, unit_b, inv_len, outgoing,
):
    tok = events.shape[0]
    hidden = out_weight.shape[1]
    scale = HEAD_DIM ** (-0.5)
    core = lax.axis_index("seq") % 2
    x = events[...].astype(f32)
    normed_in = center_scale(x)[0]
    mine, other = split_columns(normed_in, owners, core)
    keep[...] = mine.astype(b16)
    give[...] = other.astype(b16)
    normed_in = normed_in.astype(b16)
    for i in range(4):
        cols = slice(i * hidden, (i + 1) * hidden)
        p = dot(normed_in, in_weight[:, cols], NN)
        sig = sigmoid(p)
        proj[:, cols] = (p * sig).astype(b16)
        slope[:, cols] = (sig * (1.0 + p * (1.0 - sig))).astype(b16)

    pos_c, pos_r = iota((tok, 1), 0), iota((1, tok), 1)
    user_c, user_r = jnp.zeros((tok, 1), i32), jnp.zeros((1, tok), i32)
    target = jnp.zeros((1, tok), i32)
    start = jnp.int32(0)
    for j in range(lengths.shape[1]):
        end = start + lengths[0, j]
        user_c += (pos_c >= end).astype(i32)
        user_r += (pos_r >= end).astype(i32)
        here = (pos_r >= start) & (pos_r < end)
        target = jnp.where(here, dests[0, j] * slot + pos_r - start, target)
        start = end
    mask = (user_c == user_r) & (pos_r <= pos_c)

    outputs = []
    for h in range(HEADS):
        v = proj[:, hidden + h * HEAD_DIM : hidden + (h + 1) * HEAD_DIM]
        q = proj[:, 2 * hidden + h * HEAD_DIM : 2 * hidden + (h + 1) * HEAD_DIM]
        k = proj[:, 3 * hidden + h * HEAD_DIM : 3 * hidden + (h + 1) * HEAD_DIM]
        s = dot(q, k, NT) * scale
        sig = sigmoid(s)
        weight = jnp.where(mask, s * sig, 0.0).astype(b16)
        attn[h] = weight
        attn_slope[h] = jnp.where(mask, sig * (1.0 + s * (1.0 - sig)) * scale, 0.0).astype(b16)
        outputs.append(dot(weight, v, NN))
    normed, inverse = center_scale(jnp.concatenate(outputs, 1))
    normed_out[...] = normed
    inv_out[...] = inverse
    gated = (normed * proj[:, :hidden].astype(f32)).astype(b16)
    gated_out[...] = gated
    result = x + dot(gated, out_weight[...], NT)
    inverse = lax.rsqrt(jnp.sum(result * result, -1, keepdims=True) + epsilon)
    inv_len[...] = inverse
    yn = result * inverse
    unit[...] = yn
    unit_b[...] = yn.astype(b16)
    row = iota((outgoing.shape[0], 1), 0)
    filled = jnp.zeros(row.shape, i32)
    for j in range(lengths.shape[1]):
        at = dests[0, j] * slot
        filled = jnp.where((row >= at) & (row < at + lengths[0, j]), 1, filled)
    placed = dot((row == target).astype(b16), result.astype(b16), NN)
    outgoing[...] = jnp.where(filled == 1, placed, EMPTY).astype(b16)


def distances(chips):
    order, bit = [0], chips // 2
    while bit:
        order += [x ^ bit for x in order]
        bit //= 2
    return order


def owner_ids(owners):
    seq = lax.axis_index("seq")
    chip, core = seq // 2, seq % 2
    chips = owners // 2
    return [2 * (chip ^ d) + (core ^ side) for side in range(2) for d in distances(chips)]


def normalise_kernel(share, item_table, own, quarter, quarter_inv):
    grp = lax.axis_index("grp")
    x = item_table[...].astype(f32)
    own[...] = (x * lax.rsqrt(jnp.sum(x * x, -1, keepdims=True) + epsilon)).astype(b16)
    x = item_table[pl.ds(pl.multiple_of(grp * share, share), share)].astype(f32)
    inverse = lax.rsqrt(jnp.sum(x * x, -1, keepdims=True) + epsilon)
    quarter[...] = (x * inverse).astype(b16)
    quarter_inv[...] = inverse


def backward(up, inverse, out_weight, proj, slope, attn, attn_slope, normed_ref, grad):
    hidden = out_weight.shape[1]
    normed = normed_ref[...]
    grad_gated = dot(up, out_weight[...], NN)
    grad[:, :hidden] = (grad_gated * normed * slope[:, :hidden].astype(f32)).astype(b16)
    grad_normed = grad_gated * proj[:, :hidden].astype(f32)
    grad_attended = inverse[...] * (
        grad_normed
        - jnp.mean(grad_normed, -1, keepdims=True)
        - normed * jnp.mean(grad_normed * normed, -1, keepdims=True)
    )
    grad_attended = grad_attended.astype(b16)
    for h in range(HEADS):
        cv, cq, ck = [slice(i * hidden + h * HEAD_DIM, i * hidden + (h + 1) * HEAD_DIM) for i in (1, 2, 3)]
        part = grad_attended[:, h * HEAD_DIM : (h + 1) * HEAD_DIM]
        grad_attn = dot(part, proj[:, cv], NT)
        grad_score = (grad_attn * attn_slope[h].astype(f32)).astype(b16)
        grad[:, cv] = (dot(attn[h], part, TN) * slope[:, cv].astype(f32)).astype(b16)
        grad[:, cq] = (dot(grad_score, proj[:, ck], NN) * slope[:, cq].astype(f32)).astype(b16)
        grad[:, ck] = (dot(grad_score, proj[:, cq], TN) * slope[:, ck].astype(f32)).astype(b16)


def score_kernel(groups, owners, share, chunks, places, cand, inv_len, inverse, unit_hbm, yn_hbm, *refs):
    count = len(places)
    pieces, saved_hbm, refs = refs[:count], refs[count : count + 6], refs[count + 6 :]
    tags, up_keep, up_give, grad, table, spread, unit_b, unit, *saved, sems = refs
    chips = owners // 2
    vocab_dev = share * groups
    grp, core = lax.axis_index("grp"), lax.axis_index("seq") % 2
    tok = unit_b.shape[0]
    block = vocab_dev + groups * (chips - 1) * share

    def place(key):
        side, chunk, k = key
        if chunk < 0:
            return side * block, vocab_dev
        before = sum(len(ds) for ds in chunks[:chunk]) * groups * share
        rows = len(chunks[chunk]) * share
        return side * block + vocab_dev + before + k * rows, rows

    load_unit = pltpu.make_async_copy(unit_hbm, unit_b, sems.at[count])
    load_unit.start()
    copies = {}
    for n, (*key, left, wide) in enumerate(places):
        at, rows = place(key)
        copy = pltpu.make_async_copy(pieces[n], table.at[pl.ds(at, rows), pl.ds(left, wide)], sems.at[n])
        copy.start()
        copies.setdefault(tuple(key), []).append(copy)
    load_yn = pltpu.make_async_copy(yn_hbm, unit, sems.at[count + 1])
    load_yn.start()
    load_saved = [
        pltpu.make_async_copy(x, y, sems.at[count + 2 + n]) for n, (x, y) in enumerate(zip(saved_hbm, saved))
    ]
    for copy in load_saved:
        copy.start()
    ids = owner_ids(owners)
    lane = iota((1, 128), 1)
    owner = jnp.full((1, 128), -1, i32)
    for j in range(owners):
        owner = jnp.where(lane == j, ids[j], owner)
    candidates = cand[...]
    chosen = jnp.full((tok, 128), -1, i32)
    first = jnp.zeros((tok, 128), f32)
    for c in range(NCAND):
        here = candidates[:, c : c + 1] // vocab_dev == owner
        chosen = jnp.where(here, candidates[:, c : c + 1], chosen)
        if c == 0:
            first = here.astype(f32)
    wanted = [jnp.broadcast_to(chosen[:, j : j + 1], (tok, 128)) for j in range(owners)]

    def runs(key):
        side, chunk, k = key
        at, rows = place(key)
        if chunk < 0:
            return at, rows, [(side * chips, 0, vocab_dev, ids[side * chips] * vocab_dev)]
        begin = (grp ^ k) * share
        return at, rows, [
            (side * chips + d, i * share, share, ids[side * chips + d] * vocab_dev + begin)
            for i, d in enumerate(chunks[chunk])
        ]

    def tiles(key):
        at, rows, here = runs(key)
        for j, off, wide, base in here:
            step = min(wide, 128)
            for o in range(0, wide, step):
                hit = wanted[j][:, :step] == base + o + iota((1, step), 1)
                yield j, off + o, step, hit

    load_unit.wait()
    yb = unit_b[...]
    value = [[] for _ in range(owners)]
    for key in copies:
        for copy in copies[key]:
            copy.wait()
        at, rows, _ = runs(key)
        product = dot(yb, table[at : at + rows], NT)
        for j, off, step, hit in tiles(key):
            value[j].append(jnp.where(hit, product[:, off : off + step], 0.0))
    logits = jnp.zeros((tok, 128), f32)
    for j in range(owners):
        total = value[j][0]
        for part in value[j][1:]:
            total = total + part
        logits = jnp.where(lane == j, jnp.sum(total, -1, keepdims=True), logits)
    exponent = jnp.where(chosen >= 0, jnp.exp(logits / softmax_warmth), 0.0)
    coef = (exponent / jnp.sum(exponent, -1, keepdims=True) - first) / softmax_warmth
    tags[:owners] = coef.T[:owners]
    tags[owners:] = chosen.astype(f32).T[:owners]
    amount = [jnp.broadcast_to(coef[:, j : j + 1], (tok, 128)) for j in range(owners)]
    for key in copies:
        at = runs(key)[0]
        for j, off, step, hit in tiles(key):
            spread[:, at + off : at + off + step] = jnp.where(hit, amount[j][:, :step], 0.0).astype(b16)
    pulled = dot(spread[...], table[...], NN)
    load_yn.wait()
    yn = unit[...]
    upstream = (pulled - yn * jnp.sum(yn * pulled, -1, keepdims=True)) * inv_len[...]
    mine, other = split_columns(upstream, owners, core)
    up_keep[...] = mine.astype(b16)
    up_give[...] = other.astype(b16)
    for copy in load_saved:
        copy.wait()
    backward(upstream.astype(b16), inverse, *saved, grad)


def item_kernel(groups, owners, share, chunks, places, *refs):
    count = len(places)
    units, tags = refs[:count], refs[count : count + groups]
    parts, (keep, give, gathered, near, sems) = refs[count + groups : -5], refs[-5:]
    chips = owners // 2
    vocab_dev = share * groups
    grp = lax.axis_index("grp")
    tok = tags[0].shape[1]
    copies = []
    for n, (k, left, wide) in enumerate(places):
        copies.append(pltpu.make_async_copy(units[n], gathered.at[pl.ds(k * tok, tok), pl.ds(left, wide)], sems.at[n]))
    begin = pl.multiple_of(grp * share, share)
    for n, part in enumerate(parts):
        side, chunk = n // (len(chunks) + 1), n % (len(chunks) + 1) - 1
        for i, d in enumerate([0] if chunk < 0 else chunks[chunk]):
            rows = pl.ds(begin if chunk < 0 else i * share, share)
            at = pl.ds((side * chips + d) * share, share)
            copies.append(pltpu.make_async_copy(part.at[rows], near.at[at], sems.at[len(copies)]))
    for copy in copies:
        copy.start()
    ids = owner_ids(owners)
    amounts = jnp.concatenate([t[:owners] for t in tags], 1)
    chosen = jnp.concatenate([t[owners:] for t in tags], 1).astype(i32)
    for copy in copies:
        copy.wait()
    for side, out in ((0, keep), (1, give)):
        parts = []
        for d in range(chips):
            j = side * chips + d
            hit = ids[j] * vocab_dev + grp * share + iota((share, 1), 0) == chosen[j : j + 1]
            parts.append(jnp.where(hit, amounts[j : j + 1], 0.0).astype(b16))
        summed = dot(jnp.concatenate(parts, 0), gathered[...], NN)
        row = near[side * chips * share : (side + 1) * chips * share].astype(f32)
        out[...] = (summed - row * jnp.sum(row * summed, -1, keepdims=True)).astype(b16)


def weight_kernel(groups, owners, keep, give, up_keep, up_give, grad, far_grad, gated, far_gated, *refs):
    outs, whole = refs[:-1], refs[-1]
    chips = owners // 2
    grp = lax.axis_index("grp")
    wide = grad.shape[1]
    step = gated.shape[1]
    for i in range(0, wide, step):
        cols = slice(i, i + step)
        part = dot(keep[...], grad[:, cols], TN) + dot(give[...], far_grad[:, cols], TN)
        whole[:, cols] = part.astype(b16)
    part = dot(up_keep[...], gated[...], TN) + dot(up_give[...], far_gated[...], TN)
    whole[:, wide:] = part.astype(b16)
    rows = whole.shape[0] // chips
    fine = rows // groups
    half = whole.shape[1] // 2
    base, by_one, by_two, one_right, two_left = outs
    for z in range(chips):
        piece = [whole[pl.ds(pl.multiple_of(z * rows + (grp ^ k) * fine, fine), fine)] for k in range(groups)]
        base[z] = piece[0]
        by_one[0, z], by_one[1, z] = piece[3][:, :half], piece[1][:, :half]
        by_two[0, z], by_two[1, z] = piece[3][:, half:], piece[2][:, half:]
        one_right[z], two_left[z] = piece[1][:, half:], piece[2][:, :half]


def corner_kernel(by_one, by_two, one_right, two_left, right_out, left_out):
    right_out[...] = (one_right[...].astype(f32) + by_two[0].astype(f32)).astype(b16)
    left_out[...] = (two_left[...].astype(f32) + by_one[0].astype(f32)).astype(b16)


def sum_kernel(base, by_one, by_two, one_right, two_left, *outs):
    chips, fine, wide = base.shape
    chip = lax.axis_index("seq") // 2
    half = wide // 2
    for n, d in enumerate(distances(chips)):
        z = chip ^ d
        own = base[z].astype(f32)
        left = own[:, :half] + by_one[1, z].astype(f32) + two_left[z].astype(f32)
        right = own[:, half:] + by_two[1, z].astype(f32) + one_right[z].astype(f32)
        out = outs[2 * n // chips]
        at = slice(n % (chips // 2) * fine, (n % (chips // 2) + 1) * fine)
        out[at, :half] = left.astype(b16)
        out[at, half:] = right.astype(b16)


def pair_kernel(x, y, *outs):
    rows = outs[0].shape[0]
    for d, out in enumerate(outs):
        at = slice(d * rows, (d + 1) * rows)
        out[...] = (x[at].astype(f32) + y[at].astype(f32)).astype(b16)


def assemble_kernel(groups, columns, *refs):
    parts, outs = refs[:groups], refs[groups:]
    grp = lax.axis_index("grp")
    fine = parts[0].shape[0]
    for k in range(groups):
        at = pl.ds(pl.multiple_of((grp ^ k) * fine, fine), fine)
        left = 0
        for out, wide in zip(outs, columns):
            out[at] = parts[k][:, left : left + wide].astype(f32)
            left += wide


def relay_kernel(arrived, out):
    tok, slots = out.shape[0], arrived.shape[0]
    filled = (arrived[:, :128].astype(f32) < EMPTY / 2).astype(b16)
    before = (iota((slots, 1), 0) > iota((1, slots), 1)).astype(b16)
    rank = dot(before, filled, NN)[:, :1].astype(i32)
    rank = jnp.where(filled[:, :1].astype(f32) > 0, rank, -1)
    place = (rank == iota((1, tok), 1)).astype(b16)
    out[...] = dot(place, arrived[...], TN).astype(b16)


def body(events, lengths, destinations, history, negatives, in_weight, out_weight, item_table):
    groups = lax.axis_size("grp")
    owners = lax.axis_size("seq")
    chips = owners // 2
    grp = lax.axis_index("grp")
    seq = lax.axis_index("seq")
    chip, core = seq // 2, seq % 2
    tok = events.shape[0]
    vocab_dev, width = item_table.shape
    hidden = out_weight.shape[1]
    share = vocab_dev // groups
    slot = 3 * tok // (2 * owners)
    rows = width // owners
    fine = rows // groups

    def to_chip(x, d):
        pairs = [(2 * a + b, 2 * ((a + d) % chips) + b) for a in range(chips) for b in range(2)]
        return lax.ppermute(x, "seq", pairs)

    def across(x, k):
        pairs = [(2 * a + b, 2 * (a ^ k) + b) for a in range(chips) for b in range(2)]
        return lax.ppermute(x, "seq", pairs)

    def to_group(x, k):
        return lax.ppermute(x, "grp", [(a, a ^ k) for a in range(groups)])

    def to_core(x):
        return lax.ppermute(x, "seq", [(a, a ^ 1) for a in range(owners)])

    def fold(low, high):
        bit = 1
        while bit < chips // 2:
            shape = (low.shape[0] // 2, low.shape[1])
            low, high = call(pair_kernel, [(shape, b16)] * 2, [VMEM] * 2, [low, across(high, bit)], room=8)
            bit *= 2
        return low, high

    def finish(low, high):
        return low.astype(f32) + across(high, chips // 2).astype(f32)

    def gather_groups(x, near=None):
        wide = x.shape[1]
        if groups != 4:
            return [(k, 0, wide, to_group(x, k) if k else x) for k in range(groups)]
        one, two = near or [to_group(x, k) for k in (1, 2)]
        half = wide // 2
        left, right = to_group(one[:, :half], 2), to_group(two[:, half:], 1)
        return [(0, 0, wide, x), (1, 0, wide, one), (2, 0, wide, two), (3, 0, half, left), (3, half, half, right)]

    own, quarter, quarter_inv = call(
        lambda *refs: normalise_kernel(share, *refs),
        [((vocab_dev, width), b16), ((share, width), b16), ((share, 1), f32)],
        [VMEM], [item_table], flops=8 * vocab_dev * width, nbytes=5 * vocab_dev * width, room=8,
    )
    chunks = [list(range(1, chips))]
    have, bit = {0: quarter}, chips // 2
    while bit:
        have.update({x ^ bit: across(have[x], bit) for x in have})
        bit //= 2
    got = [have[x] for x in distances(chips)[1:]]
    candidates = jnp.concatenate([history[:, None], negatives], 1)
    outs = [
        ((tok, width // 2), b16), ((tok, width // 2), b16), ((tok, 4 * hidden), b16), ((tok, 4 * hidden), b16),
        ((HEADS, tok, tok), b16), ((HEADS, tok, tok), b16), ((tok, hidden), f32), ((tok, 1), f32),
        ((tok, hidden), b16), ((tok, width), f32), ((tok, width), b16), ((tok, 1), f32),
        ((owners * slot, width), b16),
    ]
    (keep, give, proj, slope, attn, attn_slope, normed, inverse, gated, unit, unit_b, inv_len, outgoing) = call(
        lambda *refs: forward_kernel(owners, slot, *refs), outs, [SMEM, SMEM, VMEM, VMEM, VMEM],
        [lengths, destinations, events, in_weight, out_weight],
        room=63,
    )

    near_units = [to_group(unit_b, k) for k in (1, 2)]
    got, near_units, own = lax.optimization_barrier((got, near_units, own))
    far_own = to_core(own)
    unit_sent = gather_groups(unit_b, near_units)
    others = [jnp.concatenate(got, 0)]
    pieces = [(0, -1, 0, 0, width, own)]
    for j, x in enumerate(others):
        pieces += [(0, j) + p for p in gather_groups(x)]
    pieces = pieces + [(1,) + p[1:5] + (to_core(p[5]) if p[1] >= 0 else far_own,) for p in pieces]
    near = [p[5] for p in pieces if p[2] == 0]
    outgoing, _ = lax.optimization_barrier((outgoing, others))

    arrived = lax.all_to_all(
        outgoing.reshape(owners, slot, width), "seq", 0, 0, tiled=True
    ).reshape(owners * slot, width)
    layer_out, = call(
        relay_kernel, [((tok, width), b16)], [VMEM], [arrived],
        room=63,
    )

    vocab = vocab_dev * owners
    far_give, far_gated = to_core(give), to_core(gated)
    units = [p[3] for p in unit_sent]
    layer_out, score_unit, far_give, far_gated, units = lax.optimization_barrier(
        (layer_out, unit, far_give, far_gated, units)
    )
    saved = [out_weight, proj, slope, attn, attn_slope, normed]
    tags, up_keep, up_give, grad = call(
        lambda *refs: score_kernel(groups, owners, share, chunks, [p[:5] for p in pieces], *refs),
        [((2 * owners, tok), f32), ((tok, width // 2), b16), ((tok, width // 2), b16), ((tok, 4 * hidden), b16)],
        [VMEM] * 3 + [ANY] * (len(pieces) + 8),
        [candidates, inv_len, inverse, unit_b, score_unit] + [p[5] for p in pieces] + saved,
        [pltpu.VMEM((vocab, width), b16), pltpu.VMEM((tok, vocab), b16), pltpu.VMEM((tok, width), b16),
         pltpu.VMEM((tok, width), f32)] + [pltpu.VMEM(x.shape, x.dtype) for x in saved]
        + [pltpu.SemaphoreType.DMA((len(pieces) + 8,))],
        room=63,
    )

    all_tags = [to_group(tags, k) if k else tags for k in range(groups)]
    far = [far_give, to_core(up_give), None, far_gated]
    grad, far[1], all_tags = lax.optimization_barrier((grad, far[1], all_tags))
    far[2] = to_core(grad)
    mine, other = call(
        lambda *refs: item_kernel(groups, owners, share, chunks, [p[:3] for p in unit_sent], *refs),
        [((chips * share, width), b16)] * 2, [ANY] * len(units) + [VMEM] * groups + [ANY] * len(near),
        units + all_tags + near,
        [pltpu.VMEM((groups * tok, width), b16), pltpu.VMEM((2 * chips * share, width), b16),
         pltpu.SemaphoreType.DMA((len(units) + 2 * chips,))],
        room=63,
    )
    far_mine = to_core(other)
    far, mine = lax.optimization_barrier((far, mine))
    half = 5 * hidden // 2
    if groups == 4:
        block = (chips, fine, 5 * hidden)
        split = (chips, fine, half)
        parts = call(
            lambda *refs: weight_kernel(groups, owners, *refs),
            [(block, b16)] + [((2,) + split, b16)] * 2 + [(split, b16)] * 2, [VMEM] * 8,
            [keep, far[0], up_keep, far[1], grad, far[2], gated, far[3]],
            [pltpu.VMEM((width // 2, 5 * hidden), b16)],
            flops=2 * tok * width * 5 * hidden, nbytes=20 * tok * width, room=60,
        )
        by_one, by_two = to_group(parts[1], 1), to_group(parts[2], 2)
        corner = (by_one, by_two)
    else:
        def both(x, y):
            return jnp.concatenate([x, y], 0)

        in_part = dot(both(keep, far[0]), both(grad, far[2]), TN)
        out_part = dot(both(up_keep, far[1]), both(gated, far[3]), TN)
        weight = jnp.concatenate([in_part, out_part], 1).astype(b16)
        weight = weight.reshape(chips, groups, fine, 5 * hidden)
        sums = lax.dynamic_index_in_dim(weight, grp, 1, False).astype(f32)
        for k in range(1, groups):
            sums += to_group(lax.dynamic_index_in_dim(weight, grp ^ k, 1, False), k).astype(f32)


    low, high = call(
        pair_kernel, [((chips // 2 * share, width), b16)] * 2, [VMEM] * 2, [mine, far_mine],
        flops=chips * share * width, nbytes=6 * chips * share * width, room=8,
    )
    low, high = fold(low, high)
    if groups == 4:
        by_one, by_two, low, high = lax.optimization_barrier(corner + (low, high))
        one_right, two_left = call(
            corner_kernel, [(split, b16)] * 2, [VMEM] * 4, [by_one, by_two, parts[3], parts[4]], room=8,
        )
        arrived = [by_one, by_two, to_group(one_right, 1), to_group(two_left, 2)]
    total = finish(low, high)
    total = (total * quarter_inv).astype(b16)
    table_grad, = call(
        lambda *refs: assemble_kernel(groups, [width], *refs), [((vocab_dev, width), f32)], [VMEM] * groups,
        [to_group(total, k) if k else total for k in range(groups)],
        flops=vocab_dev * width, nbytes=6 * vocab_dev * width, room=8,
    )

    if groups == 4:
        base, _ = lax.optimization_barrier((parts[0], total))
        low, high = call(
            sum_kernel, [((chips // 2 * fine, 5 * hidden), b16)] * 2, [VMEM] * 5, [base] + arrived,
            flops=chips * fine * 5 * hidden, nbytes=40 * chips * fine * hidden, room=10,
        )
        line = finish(*fold(low, high))
    else:
        blocks = [lax.dynamic_index_in_dim(sums, (chip + d) % chips, 0, False).astype(b16) for d in range(chips)]
        line = blocks[0].astype(f32)
        for d in range(1, chips):
            line += to_chip(blocks[d], d).astype(f32)
    line = line.astype(b16)
    lines = [to_group(line, k) if k else line for k in range(groups)]
    if fine % 16 == 0:
        in_grad, out_grad = call(
            lambda *refs: assemble_kernel(groups, [4 * hidden, hidden], *refs),
            [((rows, 4 * hidden), f32), ((rows, hidden), f32)], [VMEM] * groups, lines,
            flops=rows * hidden, nbytes=30 * rows * hidden, room=8,
        )
    else:
        shard = jnp.zeros((rows, 5 * hidden), f32)
        for k in range(groups):
            shard = lax.dynamic_update_slice_in_dim(shard, lines[k].astype(f32), (grp ^ k) * fine, 0)
        in_grad, out_grad = shard[:, : 4 * hidden], shard[:, 4 * hidden :]
    return (layer_out, in_grad, out_grad, table_grad)


def solution(mesh):
    return jax.shard_map(
        body,
        mesh=mesh,
        in_specs=(
            P(("grp", "seq"), None),
            P(("grp", "seq"), None),
            P(("grp", "seq"), None),
            P(("grp", "seq")),
            P(("grp", "seq"), None),
            P(),
            P(),
            P("seq", None),
        ),
        out_specs=(P(("grp", "seq"), None), P("seq", None), P("seq", None), P("seq", None)),
        check_vma=False,
    )
```

```python
import jax
import jax.numpy as jnp
from jax import lax
from jax.experimental import pallas as pl
from jax.experimental.pallas import tpu as pltpu
from jax.sharding import PartitionSpec as P

HEADS = 4
HEAD_DIM = 128
NCAND = 4

epsilon = 1e-05
softmax_warmth = 0.05
EMPTY = 2.0**100

f32, b16, i32 = jnp.float32, jnp.bfloat16, jnp.int32
NN = ((1,), (0,))
NT = ((1,), (1,))
TN = ((0,), (0,))
VMEM = pl.BlockSpec(memory_space=pltpu.VMEM)
SMEM = pl.BlockSpec(memory_space=pltpu.SMEM)
ANY = pl.BlockSpec(memory_space=pl.ANY)


def dot(a, b, dims):
    return lax.dot_general(a, b, (dims, ((), ())), preferred_element_type=f32)


def iota(shape, axis):
    return lax.broadcasted_iota(i32, shape, axis)


def center_scale(values):
    average = jnp.mean(values, -1, keepdims=True)
    centered = values - average
    inverse = lax.rsqrt(jnp.mean(centered * centered, -1, keepdims=True) + epsilon)
    return (centered * inverse, inverse)


def sigmoid(values):
    return 1.0 / (1.0 + jnp.exp(-values))


def split_columns(x, owners, core):
    rows = x.shape[1] // owners
    blocks = [x[:, i * rows : (i + 1) * rows] for i in range(owners)]
    even, odd = jnp.concatenate(blocks[0::2], 1), jnp.concatenate(blocks[1::2], 1)
    first = jnp.broadcast_to(core, even.shape) == 0
    return jnp.where(first, even, odd), jnp.where(first, odd, even)


def call(kernel, out, specs, args, scratch=(), flops=0, nbytes=0, room=14):
    return pl.pallas_call(
        kernel,
        out_shape=[jax.ShapeDtypeStruct(s, t) for s, t in out],
        in_specs=specs,
        out_specs=[VMEM] * len(out),
        scratch_shapes=list(scratch),
        cost_estimate=pl.CostEstimate(flops=flops, bytes_accessed=nbytes, transcendentals=0),
        compiler_params=pltpu.CompilerParams(vmem_limit_bytes=room * 2**20),
    )(*args)


def forward_kernel(
    owners, slot, lengths, dests, events, in_weight, out_weight,
    keep, give, proj, slope, attn, attn_slope, normed_out, inv_out, gated_out, unit, unit_b, inv_len, outgoing,
):
    tok = events.shape[0]
    hidden = out_weight.shape[1]
    scale = HEAD_DIM ** (-0.5)
    core = lax.axis_index("seq") % 2
    x = events[...].astype(f32)
    normed_in = center_scale(x)[0]
    mine, other = split_columns(normed_in, owners, core)
    keep[...] = mine.astype(b16)
    give[...] = other.astype(b16)
    normed_in = normed_in.astype(b16)
    for i in range(4):
        cols = slice(i * hidden, (i + 1) * hidden)
        p = dot(normed_in, in_weight[:, cols], NN)
        sig = sigmoid(p)
        proj[:, cols] = (p * sig).astype(b16)
        slope[:, cols] = (sig * (1.0 + p * (1.0 - sig))).astype(b16)

    pos_c, pos_r = iota((tok, 1), 0), iota((1, tok), 1)
    user_c, user_r = jnp.zeros((tok, 1), i32), jnp.zeros((1, tok), i32)
    target = jnp.zeros((1, tok), i32)
    start = jnp.int32(0)
    for j in range(lengths.shape[1]):
        end = start + lengths[0, j]
        user_c += (pos_c >= end).astype(i32)
        user_r += (pos_r >= end).astype(i32)
        here = (pos_r >= start) & (pos_r < end)
        target = jnp.where(here, dests[0, j] * slot + pos_r - start, target)
        start = end
    mask = (user_c == user_r) & (pos_r <= pos_c)

    outputs = []
    for h in range(HEADS):
        v = proj[:, hidden + h * HEAD_DIM : hidden + (h + 1) * HEAD_DIM]
        q = proj[:, 2 * hidden + h * HEAD_DIM : 2 * hidden + (h + 1) * HEAD_DIM]
        k = proj[:, 3 * hidden + h * HEAD_DIM : 3 * hidden + (h + 1) * HEAD_DIM]
        s = dot(q, k, NT) * scale
        sig = sigmoid(s)
        weight = jnp.where(mask, s * sig, 0.0).astype(b16)
        attn[h] = weight
        attn_slope[h] = jnp.where(mask, sig * (1.0 + s * (1.0 - sig)) * scale, 0.0).astype(b16)
        outputs.append(dot(weight, v, NN))
    normed, inverse = center_scale(jnp.concatenate(outputs, 1))
    normed_out[...] = normed
    inv_out[...] = inverse
    gated = (normed * proj[:, :hidden].astype(f32)).astype(b16)
    gated_out[...] = gated
    result = x + dot(gated, out_weight[...], NT)
    inverse = lax.rsqrt(jnp.sum(result * result, -1, keepdims=True) + epsilon)
    inv_len[...] = inverse
    yn = result * inverse
    unit[...] = yn
    unit_b[...] = yn.astype(b16)
    row = iota((outgoing.shape[0], 1), 0)
    filled = jnp.zeros(row.shape, i32)
    for j in range(lengths.shape[1]):
        at = dests[0, j] * slot
        filled = jnp.where((row >= at) & (row < at + lengths[0, j]), 1, filled)
    placed = dot((row == target).astype(b16), result.astype(b16), NN)
    outgoing[...] = jnp.where(filled == 1, placed, EMPTY).astype(b16)


def distances(chips):
    order, bit = [0], chips // 2
    while bit:
        order += [x ^ bit for x in order]
        bit //= 2
    return order


def owner_ids(owners):
    seq = lax.axis_index("seq")
    chip, core = seq // 2, seq % 2
    chips = owners // 2
    return [2 * (chip ^ d) + (core ^ side) for side in range(2) for d in distances(chips)]


def normalise_kernel(share, item_table, own, quarter, quarter_inv):
    grp = lax.axis_index("grp")
    x = item_table[...].astype(f32)
    own[...] = (x * lax.rsqrt(jnp.sum(x * x, -1, keepdims=True) + epsilon)).astype(b16)
    x = item_table[pl.ds(pl.multiple_of(grp * share, share), share)].astype(f32)
    inverse = lax.rsqrt(jnp.sum(x * x, -1, keepdims=True) + epsilon)
    quarter[...] = (x * inverse).astype(b16)
    quarter_inv[...] = inverse


def backward(up, inverse, out_weight, proj, slope, attn, attn_slope, normed_ref, grad):
    hidden = out_weight.shape[1]
    normed = normed_ref[...]
    grad_gated = dot(up, out_weight[...], NN)
    grad[:, :hidden] = (grad_gated * normed * slope[:, :hidden].astype(f32)).astype(b16)
    grad_normed = grad_gated * proj[:, :hidden].astype(f32)
    grad_attended = inverse[...] * (
        grad_normed
        - jnp.mean(grad_normed, -1, keepdims=True)
        - normed * jnp.mean(grad_normed * normed, -1, keepdims=True)
    )
    grad_attended = grad_attended.astype(b16)
    for h in range(HEADS):
        cv, cq, ck = [slice(i * hidden + h * HEAD_DIM, i * hidden + (h + 1) * HEAD_DIM) for i in (1, 2, 3)]
        part = grad_attended[:, h * HEAD_DIM : (h + 1) * HEAD_DIM]
        grad_attn = dot(part, proj[:, cv], NT)
        grad_score = (grad_attn * attn_slope[h].astype(f32)).astype(b16)
        grad[:, cv] = (dot(attn[h], part, TN) * slope[:, cv].astype(f32)).astype(b16)
        grad[:, cq] = (dot(grad_score, proj[:, ck], NN) * slope[:, cq].astype(f32)).astype(b16)
        grad[:, ck] = (dot(grad_score, proj[:, cq], TN) * slope[:, ck].astype(f32)).astype(b16)


def score_kernel(groups, owners, share, chunks, places, cand, inv_len, inverse, unit_hbm, yn_hbm, *refs):
    count = len(places)
    pieces, saved_hbm, refs = refs[:count], refs[count : count + 6], refs[count + 6 :]
    tags, up_keep, up_give, grad, table, spread, unit_b, unit, *saved, sems = refs
    chips = owners // 2
    vocab_dev = share * groups
    grp, core = lax.axis_index("grp"), lax.axis_index("seq") % 2
    tok = unit_b.shape[0]
    block = vocab_dev + groups * (chips - 1) * share

    def place(key):
        side, chunk, k = key
        if chunk < 0:
            return side * block, vocab_dev
        before = sum(len(ds) for ds in chunks[:chunk]) * groups * share
        rows = len(chunks[chunk]) * share
        return side * block + vocab_dev + before + k * rows, rows

    load_unit = pltpu.make_async_copy(unit_hbm, unit_b, sems.at[count])
    load_unit.start()
    copies = {}
    for n, (*key, left, wide) in enumerate(places):
        at, rows = place(key)
        copy = pltpu.make_async_copy(pieces[n], table.at[pl.ds(at, rows), pl.ds(left, wide)], sems.at[n])
        copy.start()
        copies.setdefault(tuple(key), []).append(copy)
    load_yn = pltpu.make_async_copy(yn_hbm, unit, sems.at[count + 1])
    load_yn.start()
    load_saved = [
        pltpu.make_async_copy(x, y, sems.at[count + 2 + n]) for n, (x, y) in enumerate(zip(saved_hbm, saved))
    ]
    for copy in load_saved:
        copy.start()
    ids = owner_ids(owners)
    lane = iota((1, 128), 1)
    owner = jnp.full((1, 128), -1, i32)
    for j in range(owners):
        owner = jnp.where(lane == j, ids[j], owner)
    candidates = cand[...]
    chosen = jnp.full((tok, 128), -1, i32)
    first = jnp.zeros((tok, 128), f32)
    for c in range(NCAND):
        here = candidates[:, c : c + 1] // vocab_dev == owner
        chosen = jnp.where(here, candidates[:, c : c + 1], chosen)
        if c == 0:
            first = here.astype(f32)
    wanted = [jnp.broadcast_to(chosen[:, j : j + 1], (tok, 128)) for j in range(owners)]

    def runs(key):
        side, chunk, k = key
        at, rows = place(key)
        if chunk < 0:
            return at, rows, [(side * chips, 0, vocab_dev, ids[side * chips] * vocab_dev)]
        begin = (grp ^ k) * share
        return at, rows, [
            (side * chips + d, i * share, share, ids[side * chips + d] * vocab_dev + begin)
            for i, d in enumerate(chunks[chunk])
        ]

    def tiles(key):
        at, rows, here = runs(key)
        for j, off, wide, base in here:
            step = min(wide, 128)
            for o in range(0, wide, step):
                hit = wanted[j][:, :step] == base + o + iota((1, step), 1)
                yield j, off + o, step, hit

    load_unit.wait()
    yb = unit_b[...]
    value = [[] for _ in range(owners)]
    for key in copies:
        for copy in copies[key]:
            copy.wait()
        at, rows, _ = runs(key)
        product = dot(yb, table[at : at + rows], NT)
        for j, off, step, hit in tiles(key):
            value[j].append(jnp.where(hit, product[:, off : off + step], 0.0))
    logits = jnp.zeros((tok, 128), f32)
    for j in range(owners):
        total = value[j][0]
        for part in value[j][1:]:
            total = total + part
        logits = jnp.where(lane == j, jnp.sum(total, -1, keepdims=True), logits)
    exponent = jnp.where(chosen >= 0, jnp.exp(logits / softmax_warmth), 0.0)
    coef = (exponent / jnp.sum(exponent, -1, keepdims=True) - first) / softmax_warmth
    tags[:owners] = coef.T[:owners]
    tags[owners:] = chosen.astype(f32).T[:owners]
    amount = [jnp.broadcast_to(coef[:, j : j + 1], (tok, 128)) for j in range(owners)]
    for key in copies:
        at = runs(key)[0]
        for j, off, step, hit in tiles(key):
            spread[:, at + off : at + off + step] = jnp.where(hit, amount[j][:, :step], 0.0).astype(b16)
    pulled = dot(spread[...], table[...], NN)
    load_yn.wait()
    yn = unit[...]
    upstream = (pulled - yn * jnp.sum(yn * pulled, -1, keepdims=True)) * inv_len[...]
    mine, other = split_columns(upstream, owners, core)
    up_keep[...] = mine.astype(b16)
    up_give[...] = other.astype(b16)
    for copy in load_saved:
        copy.wait()
    backward(upstream.astype(b16), inverse, *saved, grad)


def item_kernel(groups, owners, share, chunks, places, *refs):
    count = len(places)
    units, tags = refs[:count], refs[count : count + groups]
    parts, (keep, give, gathered, near, sems) = refs[count + groups : -5], refs[-5:]
    chips = owners // 2
    vocab_dev = share * groups
    grp = lax.axis_index("grp")
    tok = tags[0].shape[1]
    copies = []
    for n, (k, left, wide) in enumerate(places):
        copies.append(pltpu.make_async_copy(units[n], gathered.at[pl.ds(k * tok, tok), pl.ds(left, wide)], sems.at[n]))
    begin = pl.multiple_of(grp * share, share)
    for n, part in enumerate(parts):
        side, chunk = n // (len(chunks) + 1), n % (len(chunks) + 1) - 1
        for i, d in enumerate([0] if chunk < 0 else chunks[chunk]):
            rows = pl.ds(begin if chunk < 0 else i * share, share)
            at = pl.ds((side * chips + d) * share, share)
            copies.append(pltpu.make_async_copy(part.at[rows], near.at[at], sems.at[len(copies)]))
    for copy in copies:
        copy.start()
    ids = owner_ids(owners)
    amounts = jnp.concatenate([t[:owners] for t in tags], 1)
    chosen = jnp.concatenate([t[owners:] for t in tags], 1).astype(i32)
    for copy in copies[:count]:
        copy.wait()
    for side, out in ((0, keep), (1, give)):
        parts = []
        for d in range(chips):
            j = side * chips + d
            hit = ids[j] * vocab_dev + grp * share + iota((share, 1), 0) == chosen[j : j + 1]
            parts.append(jnp.where(hit, amounts[j : j + 1], 0.0).astype(b16))
        summed = dot(jnp.concatenate(parts, 0), gathered[...], NN)
        for copy in copies[count + side * chips : count + (side + 1) * chips]:
            copy.wait()
        row = near[side * chips * share : (side + 1) * chips * share].astype(f32)
        out[...] = (summed - row * jnp.sum(row * summed, -1, keepdims=True)).astype(b16)


def weight_kernel(groups, owners, *refs):
    given, outs, loaded, (own, whole, sems) = refs[:8], refs[8:13], refs[13:21], refs[21:]
    copies = [pltpu.make_async_copy(x, y, sems.at[n]) for n, (x, y) in enumerate(zip(given, loaded))]
    for copy in copies:
        copy.start()
    keep, grad, up_keep, gated, up_give, far_gated, give, far_grad = loaded
    chips = owners // 2
    grp = lax.axis_index("grp")
    wide = grad.shape[1]
    step = gated.shape[1]
    for copy in copies[:2]:
        copy.wait()
    for i in range(0, wide, step):
        own[:, i : i + step] = dot(keep[...], grad[:, i : i + step], TN)
    for copy in copies[2:6]:
        copy.wait()
    part = dot(up_keep[...], gated[...], TN) + dot(up_give[...], far_gated[...], TN)
    whole[:, wide:] = part.astype(b16)
    for copy in copies[6:]:
        copy.wait()
    for i in range(0, wide, step):
        cols = slice(i, i + step)
        whole[:, cols] = (own[:, cols] + dot(give[...], far_grad[:, cols], TN)).astype(b16)
    rows = whole.shape[0] // chips
    fine = rows // groups
    half = whole.shape[1] // 2
    base, by_one, by_two, one_right, two_left = outs
    for z in range(chips):
        piece = [whole[pl.ds(pl.multiple_of(z * rows + (grp ^ k) * fine, fine), fine)] for k in range(groups)]
        base[z] = piece[0]
        by_one[0, z], by_one[1, z] = piece[3][:, :half], piece[1][:, :half]
        by_two[0, z], by_two[1, z] = piece[3][:, half:], piece[2][:, half:]
        one_right[z], two_left[z] = piece[1][:, half:], piece[2][:, :half]


def corner_kernel(by_one, by_two, one_right, two_left, right_out, left_out):
    right_out[...] = (one_right[...].astype(f32) + by_two[0].astype(f32)).astype(b16)
    left_out[...] = (two_left[...].astype(f32) + by_one[0].astype(f32)).astype(b16)


def sum_kernel(base, by_one, by_two, one_right, two_left, *outs):
    chips, fine, wide = base.shape
    chip = lax.axis_index("seq") // 2
    half = wide // 2
    for n, d in enumerate(distances(chips)):
        z = chip ^ d
        own = base[z].astype(f32)
        left = own[:, :half] + by_one[1, z].astype(f32) + two_left[z].astype(f32)
        right = own[:, half:] + by_two[1, z].astype(f32) + one_right[z].astype(f32)
        out = outs[2 * n // chips]
        at = slice(n % (chips // 2) * fine, (n % (chips // 2) + 1) * fine)
        out[at, :half] = left.astype(b16)
        out[at, half:] = right.astype(b16)


def pair_kernel(x, y, *outs):
    rows = outs[0].shape[0]
    for d, out in enumerate(outs):
        at = slice(d * rows, (d + 1) * rows)
        out[...] = (x[at].astype(f32) + y[at].astype(f32)).astype(b16)


def assemble_kernel(groups, columns, *refs):
    parts, outs = refs[:groups], refs[groups:]
    grp = lax.axis_index("grp")
    fine = parts[0].shape[0]
    for k in range(groups):
        at = pl.ds(pl.multiple_of((grp ^ k) * fine, fine), fine)
        left = 0
        for out, wide in zip(outs, columns):
            out[at] = parts[k][:, left : left + wide].astype(f32)
            left += wide


def relay_kernel(arrived, out):
    tok, slots = out.shape[0], arrived.shape[0]
    filled = (arrived[:, :128].astype(f32) < EMPTY / 2).astype(b16)
    before = (iota((slots, 1), 0) > iota((1, slots), 1)).astype(b16)
    rank = dot(before, filled, NN)[:, :1].astype(i32)
    rank = jnp.where(filled[:, :1].astype(f32) > 0, rank, -1)
    place = (rank == iota((1, tok), 1)).astype(b16)
    out[...] = dot(place, arrived[...], TN).astype(b16)


def body(events, lengths, destinations, history, negatives, in_weight, out_weight, item_table):
    groups = lax.axis_size("grp")
    owners = lax.axis_size("seq")
    chips = owners // 2
    grp = lax.axis_index("grp")
    seq = lax.axis_index("seq")
    chip, core = seq // 2, seq % 2
    tok = events.shape[0]
    vocab_dev, width = item_table.shape
    hidden = out_weight.shape[1]
    share = vocab_dev // groups
    slot = 3 * tok // (2 * owners)
    rows = width // owners
    fine = rows // groups

    def to_chip(x, d):
        pairs = [(2 * a + b, 2 * ((a + d) % chips) + b) for a in range(chips) for b in range(2)]
        return lax.ppermute(x, "seq", pairs)

    def across(x, k):
        pairs = [(2 * a + b, 2 * (a ^ k) + b) for a in range(chips) for b in range(2)]
        return lax.ppermute(x, "seq", pairs)

    def to_group(x, k):
        return lax.ppermute(x, "grp", [(a, a ^ k) for a in range(groups)])

    def to_core(x):
        return lax.ppermute(x, "seq", [(a, a ^ 1) for a in range(owners)])

    def fold(low, high, gate=()):
        bit = 1
        while bit < chips // 2:
            shape = (low.shape[0] // 2, low.shape[1])
            came, _ = lax.optimization_barrier((across(high, bit), gate))
            low, high = call(pair_kernel, [(shape, b16)] * 2, [VMEM] * 2, [low, came], room=8)
            bit *= 2
        return low, high

    def finish(low, high):
        return low.astype(f32) + across(high, chips // 2).astype(f32)

    def gather_groups(x, near=None):
        wide = x.shape[1]
        if groups != 4:
            return [(k, 0, wide, to_group(x, k) if k else x) for k in range(groups)]
        one, two = near or [to_group(x, k) for k in (1, 2)]
        half = wide // 2
        left, right = to_group(one[:, :half], 2), to_group(two[:, half:], 1)
        return [(0, 0, wide, x), (1, 0, wide, one), (2, 0, wide, two), (3, 0, half, left), (3, half, half, right)]

    own, quarter, quarter_inv = call(
        lambda *refs: normalise_kernel(share, *refs),
        [((vocab_dev, width), b16), ((share, width), b16), ((share, 1), f32)],
        [VMEM], [item_table], flops=8 * vocab_dev * width, nbytes=5 * vocab_dev * width, room=8,
    )
    chunks = [list(range(1, chips))]
    have, bit = {0: quarter}, chips // 2
    while bit:
        have.update({x ^ bit: across(have[x], bit) for x in have})
        bit //= 2
    got = [have[x] for x in distances(chips)[1:]]
    outs = [
        ((tok, width // 2), b16), ((tok, width // 2), b16), ((tok, 4 * hidden), b16), ((tok, 4 * hidden), b16),
        ((HEADS, tok, tok), b16), ((HEADS, tok, tok), b16), ((tok, hidden), f32), ((tok, 1), f32),
        ((tok, hidden), b16), ((tok, width), f32), ((tok, width), b16), ((tok, 1), f32),
        ((owners * slot, width), b16),
    ]
    (keep, give, proj, slope, attn, attn_slope, normed, inverse, gated, unit, unit_b, inv_len, outgoing) = call(
        lambda *refs: forward_kernel(owners, slot, *refs), outs, [SMEM, SMEM, VMEM, VMEM, VMEM],
        [lengths, destinations, events, in_weight, out_weight],
        room=63,
    )

    near_units = [to_group(unit_b, k) for k in (1, 2)]
    candidates = jnp.concatenate([history[:, None], negatives], 1)
    got, near_units, own, candidates = lax.optimization_barrier((got, near_units, own, candidates))
    far_own = to_core(own)
    unit_sent = gather_groups(unit_b, near_units)
    others = [jnp.concatenate(got, 0)]
    pieces = [(0, -1, 0, 0, width, own)]
    for j, x in enumerate(others):
        pieces += [(0, j) + p for p in gather_groups(x)]
    pieces = pieces + [(1,) + p[1:5] + (to_core(p[5]) if p[1] >= 0 else far_own,) for p in pieces]
    near = [p[5] for p in pieces if p[2] == 0]
    outgoing, _ = lax.optimization_barrier((outgoing, others))

    arrived = lax.all_to_all(
        outgoing.reshape(owners, slot, width), "seq", 0, 0, tiled=True
    ).reshape(owners * slot, width)
    vocab = vocab_dev * owners
    far_give, far_gated = to_core(give), to_core(gated)
    units = [p[3] for p in unit_sent]
    layer_out, = call(relay_kernel, [((tok, width), b16)], [VMEM], [arrived], room=63)
    layer_out, score_unit, far_give, far_gated, units = lax.optimization_barrier(
        (layer_out, unit, far_give, far_gated, units)
    )
    saved = [out_weight, proj, slope, attn, attn_slope, normed]
    tags, up_keep, up_give, grad = call(
        lambda *refs: score_kernel(groups, owners, share, chunks, [p[:5] for p in pieces], *refs),
        [((2 * owners, tok), f32), ((tok, width // 2), b16), ((tok, width // 2), b16), ((tok, 4 * hidden), b16)],
        [VMEM] * 3 + [ANY] * (len(pieces) + 8),
        [candidates, inv_len, inverse, unit_b, score_unit] + [p[5] for p in pieces] + saved,
        [pltpu.VMEM((vocab, width), b16), pltpu.VMEM((tok, vocab), b16), pltpu.VMEM((tok, width), b16),
         pltpu.VMEM((tok, width), f32)] + [pltpu.VMEM(x.shape, x.dtype) for x in saved]
        + [pltpu.SemaphoreType.DMA((len(pieces) + 8,))],
        room=63,
    )

    all_tags = [to_group(tags, k) if k else tags for k in range(groups)]
    far = [far_give, to_core(up_give), None, far_gated]
    grad, far[1], all_tags = lax.optimization_barrier((grad, far[1], all_tags))
    far[2] = to_core(grad)
    mine, other = call(
        lambda *refs: item_kernel(groups, owners, share, chunks, [p[:3] for p in unit_sent], *refs),
        [((chips * share, width), b16)] * 2, [ANY] * len(units) + [VMEM] * groups + [ANY] * len(near),
        units + all_tags + near,
        [pltpu.VMEM((groups * tok, width), b16), pltpu.VMEM((2 * chips * share, width), b16),
         pltpu.SemaphoreType.DMA((len(units) + 2 * chips,))],
        room=63,
    )
    far_mine = to_core(other)
    far, mine = lax.optimization_barrier((far, mine))
    half = 5 * hidden // 2
    if groups == 4:
        block = (chips, fine, 5 * hidden)
        split = (chips, fine, half)
        parts = call(
            lambda *refs: weight_kernel(groups, owners, *refs),
            [(block, b16)] + [((2,) + split, b16)] * 2 + [(split, b16)] * 2, [ANY] * 8,
            [keep, grad, up_keep, gated, far[1], far[3], far[0], far[2]],
            [pltpu.VMEM(x.shape, b16) for x in (keep, grad, up_keep, gated, up_keep, gated, keep, grad)]
            + [pltpu.VMEM((width // 2, 4 * hidden), f32), pltpu.VMEM((width // 2, 5 * hidden), b16),
               pltpu.SemaphoreType.DMA((8,))],
            flops=2 * tok * width * 5 * hidden, nbytes=20 * tok * width, room=60,
        )
        by_one, by_two = to_group(parts[1], 1), to_group(parts[2], 2)
        corner = (by_one, by_two)
    else:
        def both(x, y):
            return jnp.concatenate([x, y], 0)

        in_part = dot(both(keep, far[0]), both(grad, far[2]), TN)
        out_part = dot(both(up_keep, far[1]), both(gated, far[3]), TN)
        weight = jnp.concatenate([in_part, out_part], 1).astype(b16)
        weight = weight.reshape(chips, groups, fine, 5 * hidden)
        sums = lax.dynamic_index_in_dim(weight, grp, 1, False).astype(f32)
        for k in range(1, groups):
            sums += to_group(lax.dynamic_index_in_dim(weight, grp ^ k, 1, False), k).astype(f32)


    low, high = call(
        pair_kernel, [((chips // 2 * share, width), b16)] * 2, [VMEM] * 2, [mine, far_mine],
        flops=chips * share * width, nbytes=6 * chips * share * width, room=8,
    )
    low, high = fold(low, high)
    if groups == 4:
        by_one, by_two, low, high = lax.optimization_barrier(corner + (low, high))
        one_right, two_left = call(
            corner_kernel, [(split, b16)] * 2, [VMEM] * 4, [by_one, by_two, parts[3], parts[4]], room=8,
        )
        arrived = [by_one, by_two, to_group(one_right, 1), to_group(two_left, 2)]
    total = finish(low, high)
    total = (total * quarter_inv).astype(b16)
    totals = [to_group(total, k) if k else total for k in range(groups)]
    table_grad, = call(
        lambda *refs: assemble_kernel(groups, [width], *refs), [((vocab_dev, width), f32)], [VMEM] * groups, totals,
        flops=vocab_dev * width, nbytes=6 * vocab_dev * width, room=8,
    )

    if groups == 4:
        base, _ = lax.optimization_barrier((parts[0], total))
        low, high = call(
            sum_kernel, [((chips // 2 * fine, 5 * hidden), b16)] * 2, [VMEM] * 5, [base] + arrived,
            flops=chips * fine * 5 * hidden, nbytes=40 * chips * fine * hidden, room=10,
        )
        line = finish(*fold(low, high, totals))
    else:
        blocks = [lax.dynamic_index_in_dim(sums, (chip + d) % chips, 0, False).astype(b16) for d in range(chips)]
        line = blocks[0].astype(f32)
        for d in range(1, chips):
            line += to_chip(blocks[d], d).astype(f32)
    line = line.astype(b16)
    lines = [to_group(line, k) if k else line for k in range(groups)]
    if fine % 16 == 0:
        in_grad, out_grad = call(
            lambda *refs: assemble_kernel(groups, [4 * hidden, hidden], *refs),
            [((rows, 4 * hidden), f32), ((rows, hidden), f32)], [VMEM] * groups, lines,
            flops=rows * hidden, nbytes=30 * rows * hidden, room=8,
        )
    else:
        shard = jnp.zeros((rows, 5 * hidden), f32)
        for k in range(groups):
            shard = lax.dynamic_update_slice_in_dim(shard, lines[k].astype(f32), (grp ^ k) * fine, 0)
        in_grad, out_grad = shard[:, : 4 * hidden], shard[:, 4 * hidden :]
    return (layer_out, in_grad, out_grad, table_grad)


def solution(mesh):
    return jax.shard_map(
        body,
        mesh=mesh,
        in_specs=(
            P(("grp", "seq"), None),
            P(("grp", "seq"), None),
            P(("grp", "seq"), None),
            P(("grp", "seq")),
            P(("grp", "seq"), None),
            P(),
            P(),
            P("seq", None),
        ),
        out_specs=(P(("grp", "seq"), None), P("seq", None), P("seq", None), P("seq", None)),
        check_vma=False,
    )
```

```python
import jax
import jax.numpy as jnp
from jax import lax
from jax.experimental import pallas as pl
from jax.experimental.pallas import tpu as pltpu
from jax.sharding import PartitionSpec as P

HEADS = 4
HEAD_DIM = 128
NCAND = 4

epsilon = 1e-05
softmax_warmth = 0.05
EMPTY = 2.0**100

f32, b16, i32 = jnp.float32, jnp.bfloat16, jnp.int32
NN = ((1,), (0,))
NT = ((1,), (1,))
TN = ((0,), (0,))
VMEM = pl.BlockSpec(memory_space=pltpu.VMEM)
SMEM = pl.BlockSpec(memory_space=pltpu.SMEM)
ANY = pl.BlockSpec(memory_space=pl.ANY)


def dot(a, b, dims):
    return lax.dot_general(a, b, (dims, ((), ())), preferred_element_type=f32)


def iota(shape, axis):
    return lax.broadcasted_iota(i32, shape, axis)


def center_scale(values):
    average = jnp.mean(values, -1, keepdims=True)
    centered = values - average
    inverse = lax.rsqrt(jnp.mean(centered * centered, -1, keepdims=True) + epsilon)
    return (centered * inverse, inverse)


def sigmoid(values):
    return 1.0 / (1.0 + jnp.exp(-values))


def split_columns(x, owners, core):
    rows = x.shape[1] // owners
    blocks = [x[:, i * rows : (i + 1) * rows] for i in range(owners)]
    even, odd = jnp.concatenate(blocks[0::2], 1), jnp.concatenate(blocks[1::2], 1)
    first = jnp.broadcast_to(core, even.shape) == 0
    return jnp.where(first, even, odd), jnp.where(first, odd, even)


def call(kernel, out, specs, args, scratch=(), flops=0, nbytes=0, room=14):
    return pl.pallas_call(
        kernel,
        out_shape=[jax.ShapeDtypeStruct(s, t) for s, t in out],
        in_specs=specs,
        out_specs=[VMEM] * len(out),
        scratch_shapes=list(scratch),
        cost_estimate=pl.CostEstimate(flops=flops, bytes_accessed=nbytes, transcendentals=0),
        compiler_params=pltpu.CompilerParams(vmem_limit_bytes=room * 2**20),
    )(*args)


def forward_kernel(
    owners, slot, lengths, dests, events, in_weight, out_weight,
    keep, give, proj, slope, attn, attn_slope, normed_out, inv_out, gated_out, unit, unit_b, inv_len, outgoing,
):
    tok = events.shape[0]
    hidden = out_weight.shape[1]
    scale = HEAD_DIM ** (-0.5)
    core = lax.axis_index("seq") % 2
    x = events[...].astype(f32)
    normed_in = center_scale(x)[0]
    mine, other = split_columns(normed_in, owners, core)
    keep[...] = mine.astype(b16)
    give[...] = other.astype(b16)
    normed_in = normed_in.astype(b16)
    for i in range(4):
        cols = slice(i * hidden, (i + 1) * hidden)
        p = dot(normed_in, in_weight[:, cols], NN)
        sig = sigmoid(p)
        proj[:, cols] = (p * sig).astype(b16)
        slope[:, cols] = (sig * (1.0 + p * (1.0 - sig))).astype(b16)

    pos_c, pos_r = iota((tok, 1), 0), iota((1, tok), 1)
    user_c, user_r = jnp.zeros((tok, 1), i32), jnp.zeros((1, tok), i32)
    target = jnp.zeros((1, tok), i32)
    start = jnp.int32(0)
    for j in range(lengths.shape[1]):
        end = start + lengths[0, j]
        user_c += (pos_c >= end).astype(i32)
        user_r += (pos_r >= end).astype(i32)
        here = (pos_r >= start) & (pos_r < end)
        target = jnp.where(here, dests[0, j] * slot + pos_r - start, target)
        start = end
    mask = (user_c == user_r) & (pos_r <= pos_c)

    outputs = []
    for h in range(HEADS):
        v = proj[:, hidden + h * HEAD_DIM : hidden + (h + 1) * HEAD_DIM]
        q = proj[:, 2 * hidden + h * HEAD_DIM : 2 * hidden + (h + 1) * HEAD_DIM]
        k = proj[:, 3 * hidden + h * HEAD_DIM : 3 * hidden + (h + 1) * HEAD_DIM]
        s = dot(q, k, NT) * scale
        sig = sigmoid(s)
        weight = jnp.where(mask, s * sig, 0.0).astype(b16)
        attn[h] = weight
        attn_slope[h] = jnp.where(mask, sig * (1.0 + s * (1.0 - sig)) * scale, 0.0).astype(b16)
        outputs.append(dot(weight, v, NN))
    normed, inverse = center_scale(jnp.concatenate(outputs, 1))
    normed_out[...] = normed
    inv_out[...] = inverse
    gated = (normed * proj[:, :hidden].astype(f32)).astype(b16)
    gated_out[...] = gated
    result = x + dot(gated, out_weight[...], NT)
    inverse = lax.rsqrt(jnp.sum(result * result, -1, keepdims=True) + epsilon)
    inv_len[...] = inverse
    yn = result * inverse
    unit[...] = yn
    unit_b[...] = yn.astype(b16)
    row = iota((outgoing.shape[0], 1), 0)
    filled = jnp.zeros(row.shape, i32)
    for j in range(lengths.shape[1]):
        at = dests[0, j] * slot
        filled = jnp.where((row >= at) & (row < at + lengths[0, j]), 1, filled)
    placed = dot((row == target).astype(b16), result.astype(b16), NN)
    outgoing[...] = jnp.where(filled == 1, placed, EMPTY).astype(b16)


def distances(chips):
    order, bit = [0], chips // 2
    while bit:
        order += [x ^ bit for x in order]
        bit //= 2
    return order


def owner_ids(owners):
    seq = lax.axis_index("seq")
    chip, core = seq // 2, seq % 2
    chips = owners // 2
    return [2 * (chip ^ d) + (core ^ side) for side in range(2) for d in distances(chips)]


def normalise_kernel(share, item_table, own, quarter, quarter_inv):
    grp = lax.axis_index("grp")
    x = item_table[...].astype(f32)
    own[...] = (x * lax.rsqrt(jnp.sum(x * x, -1, keepdims=True) + epsilon)).astype(b16)
    x = item_table[pl.ds(pl.multiple_of(grp * share, share), share)].astype(f32)
    inverse = lax.rsqrt(jnp.sum(x * x, -1, keepdims=True) + epsilon)
    quarter[...] = (x * inverse).astype(b16)
    quarter_inv[...] = inverse


def backward(up, inverse, out_weight, proj, slope, attn, attn_slope, normed_ref, grad):
    hidden = out_weight.shape[1]
    normed = normed_ref[...]
    grad_gated = dot(up, out_weight[...], NN)
    grad[:, :hidden] = (grad_gated * normed * slope[:, :hidden].astype(f32)).astype(b16)
    grad_normed = grad_gated * proj[:, :hidden].astype(f32)
    grad_attended = inverse[...] * (
        grad_normed
        - jnp.mean(grad_normed, -1, keepdims=True)
        - normed * jnp.mean(grad_normed * normed, -1, keepdims=True)
    )
    grad_attended = grad_attended.astype(b16)
    for h in range(HEADS):
        cv, cq, ck = [slice(i * hidden + h * HEAD_DIM, i * hidden + (h + 1) * HEAD_DIM) for i in (1, 2, 3)]
        part = grad_attended[:, h * HEAD_DIM : (h + 1) * HEAD_DIM]
        grad_attn = dot(part, proj[:, cv], NT)
        grad_score = (grad_attn * attn_slope[h].astype(f32)).astype(b16)
        grad[:, cv] = (dot(attn[h], part, TN) * slope[:, cv].astype(f32)).astype(b16)
        grad[:, cq] = (dot(grad_score, proj[:, ck], NN) * slope[:, cq].astype(f32)).astype(b16)
        grad[:, ck] = (dot(grad_score, proj[:, cq], TN) * slope[:, ck].astype(f32)).astype(b16)


def score_kernel(groups, owners, share, chunks, places, cand, inv_len, inverse, unit_hbm, yn_hbm, *refs):
    count = len(places)
    pieces, saved_hbm, refs = refs[:count], refs[count : count + 6], refs[count + 6 :]
    tags, up_keep, up_give, grad, table, spread, unit_b, unit, *saved, sems = refs
    chips = owners // 2
    vocab_dev = share * groups
    grp, core = lax.axis_index("grp"), lax.axis_index("seq") % 2
    tok = unit_b.shape[0]
    block = vocab_dev + groups * (chips - 1) * share

    def place(key):
        side, chunk, k = key
        if chunk < 0:
            return side * block, vocab_dev
        before = sum(len(ds) for ds in chunks[:chunk]) * groups * share
        rows = len(chunks[chunk]) * share
        return side * block + vocab_dev + before + k * rows, rows

    load_unit = pltpu.make_async_copy(unit_hbm, unit_b, sems.at[count])
    load_unit.start()
    copies = {}
    for n, (*key, left, wide) in enumerate(places):
        at, rows = place(key)
        copy = pltpu.make_async_copy(pieces[n], table.at[pl.ds(at, rows), pl.ds(left, wide)], sems.at[n])
        copy.start()
        copies.setdefault(tuple(key), []).append(copy)
    load_yn = pltpu.make_async_copy(yn_hbm, unit, sems.at[count + 1])
    load_yn.start()
    load_saved = [
        pltpu.make_async_copy(x, y, sems.at[count + 2 + n]) for n, (x, y) in enumerate(zip(saved_hbm, saved))
    ]
    for copy in load_saved:
        copy.start()
    ids = owner_ids(owners)
    lane = iota((1, 128), 1)
    owner = jnp.full((1, 128), -1, i32)
    for j in range(owners):
        owner = jnp.where(lane == j, ids[j], owner)
    candidates = cand[...]
    chosen = jnp.full((tok, 128), -1, i32)
    first = jnp.zeros((tok, 128), f32)
    for c in range(NCAND):
        here = candidates[:, c : c + 1] // vocab_dev == owner
        chosen = jnp.where(here, candidates[:, c : c + 1], chosen)
        if c == 0:
            first = here.astype(f32)
    wanted = [jnp.broadcast_to(chosen[:, j : j + 1], (tok, 128)) for j in range(owners)]

    def runs(key):
        side, chunk, k = key
        at, rows = place(key)
        if chunk < 0:
            return at, rows, [(side * chips, 0, vocab_dev, ids[side * chips] * vocab_dev)]
        begin = (grp ^ k) * share
        return at, rows, [
            (side * chips + d, i * share, share, ids[side * chips + d] * vocab_dev + begin)
            for i, d in enumerate(chunks[chunk])
        ]

    def tiles(key):
        at, rows, here = runs(key)
        for j, off, wide, base in here:
            step = min(wide, 128)
            for o in range(0, wide, step):
                hit = wanted[j][:, :step] == base + o + iota((1, step), 1)
                yield j, off + o, step, hit

    load_unit.wait()
    yb = unit_b[...]
    value = [[] for _ in range(owners)]
    for key in copies:
        for copy in copies[key]:
            copy.wait()
        at, rows, _ = runs(key)
        product = dot(yb, table[at : at + rows], NT)
        for j, off, step, hit in tiles(key):
            value[j].append(jnp.where(hit, product[:, off : off + step], 0.0))
    logits = jnp.zeros((tok, 128), f32)
    for j in range(owners):
        total = value[j][0]
        for part in value[j][1:]:
            total = total + part
        logits = jnp.where(lane == j, jnp.sum(total, -1, keepdims=True), logits)
    exponent = jnp.where(chosen >= 0, jnp.exp(logits / softmax_warmth), 0.0)
    coef = (exponent / jnp.sum(exponent, -1, keepdims=True) - first) / softmax_warmth
    tags[:owners] = coef.T[:owners]
    tags[owners:] = chosen.astype(f32).T[:owners]
    amount = [jnp.broadcast_to(coef[:, j : j + 1], (tok, 128)) for j in range(owners)]
    for key in copies:
        at = runs(key)[0]
        for j, off, step, hit in tiles(key):
            spread[:, at + off : at + off + step] = jnp.where(hit, amount[j][:, :step], 0.0).astype(b16)
    pulled = dot(spread[...], table[...], NN)
    load_yn.wait()
    yn = unit[...]
    upstream = (pulled - yn * jnp.sum(yn * pulled, -1, keepdims=True)) * inv_len[...]
    mine, other = split_columns(upstream, owners, core)
    up_keep[...] = mine.astype(b16)
    up_give[...] = other.astype(b16)
    for copy in load_saved:
        copy.wait()
    backward(upstream.astype(b16), inverse, *saved, grad)


def item_kernel(groups, owners, share, chunks, places, *refs):
    count = len(places)
    units, tags = refs[:count], refs[count : count + groups]
    parts, (keep, give, gathered, near, sems) = refs[count + groups : -5], refs[-5:]
    chips = owners // 2
    vocab_dev = share * groups
    grp = lax.axis_index("grp")
    tok = tags[0].shape[1]
    copies = []
    for n, (k, left, wide) in enumerate(places):
        copies.append(pltpu.make_async_copy(units[n], gathered.at[pl.ds(k * tok, tok), pl.ds(left, wide)], sems.at[n]))
    begin = pl.multiple_of(grp * share, share)
    for n, part in enumerate(parts):
        side, chunk = n // (len(chunks) + 1), n % (len(chunks) + 1) - 1
        for i, d in enumerate([0] if chunk < 0 else chunks[chunk]):
            rows = pl.ds(begin if chunk < 0 else i * share, share)
            at = pl.ds((side * chips + d) * share, share)
            copies.append(pltpu.make_async_copy(part.at[rows], near.at[at], sems.at[len(copies)]))
    for copy in copies:
        copy.start()
    ids = owner_ids(owners)
    amounts = jnp.concatenate([t[:owners] for t in tags], 1)
    chosen = jnp.concatenate([t[owners:] for t in tags], 1).astype(i32)
    for copy in copies[:count]:
        copy.wait()
    for side, out in ((0, keep), (1, give)):
        parts = []
        for d in range(chips):
            j = side * chips + d
            hit = ids[j] * vocab_dev + grp * share + iota((share, 1), 0) == chosen[j : j + 1]
            parts.append(jnp.where(hit, amounts[j : j + 1], 0.0).astype(b16))
        summed = dot(jnp.concatenate(parts, 0), gathered[...], NN)
        for copy in copies[count + side * chips : count + (side + 1) * chips]:
            copy.wait()
        row = near[side * chips * share : (side + 1) * chips * share].astype(f32)
        out[...] = (summed - row * jnp.sum(row * summed, -1, keepdims=True)).astype(b16)


def weight_kernel(groups, owners, *refs):
    given, outs, loaded, (own, whole, sems) = refs[:8], refs[8:13], refs[13:21], refs[21:]
    copies = [pltpu.make_async_copy(x, y, sems.at[n]) for n, (x, y) in enumerate(zip(given, loaded))]
    for copy in copies:
        copy.start()
    keep, grad, up_keep, gated, up_give, far_gated, give, far_grad = loaded
    chips = owners // 2
    grp = lax.axis_index("grp")
    wide = grad.shape[1]
    step = gated.shape[1]
    for copy in copies[:2]:
        copy.wait()
    for i in range(0, wide, step):
        own[:, i : i + step] = dot(keep[...], grad[:, i : i + step], TN)
    for copy in copies[2:6]:
        copy.wait()
    part = dot(up_keep[...], gated[...], TN) + dot(up_give[...], far_gated[...], TN)
    whole[:, wide:] = part.astype(b16)
    for copy in copies[6:]:
        copy.wait()
    for i in range(0, wide, step):
        cols = slice(i, i + step)
        whole[:, cols] = (own[:, cols] + dot(give[...], far_grad[:, cols], TN)).astype(b16)
    rows = whole.shape[0] // chips
    fine = rows // groups
    half = whole.shape[1] // 2
    base, by_one, by_two, one_right, two_left = outs
    for z in range(chips):
        piece = [whole[pl.ds(pl.multiple_of(z * rows + (grp ^ k) * fine, fine), fine)] for k in range(groups)]
        base[z] = piece[0]
        by_one[0, z], by_one[1, z] = piece[3][:, :half], piece[1][:, :half]
        by_two[0, z], by_two[1, z] = piece[3][:, half:], piece[2][:, half:]
        one_right[z], two_left[z] = piece[1][:, half:], piece[2][:, :half]


def corner_kernel(by_one, by_two, one_right, two_left, right_out, left_out):
    right_out[...] = (one_right[...].astype(f32) + by_two[0].astype(f32)).astype(b16)
    left_out[...] = (two_left[...].astype(f32) + by_one[0].astype(f32)).astype(b16)


def sum_kernel(base, by_one, by_two, one_right, two_left, *outs):
    chips, fine, wide = base.shape
    chip = lax.axis_index("seq") // 2
    half = wide // 2
    for n, d in enumerate(distances(chips)):
        z = chip ^ d
        own = base[z].astype(f32)
        left = own[:, :half] + by_one[1, z].astype(f32) + two_left[z].astype(f32)
        right = own[:, half:] + by_two[1, z].astype(f32) + one_right[z].astype(f32)
        out = outs[2 * n // chips]
        at = slice(n % (chips // 2) * fine, (n % (chips // 2) + 1) * fine)
        out[at, :half] = left.astype(b16)
        out[at, half:] = right.astype(b16)


def pair_kernel(x, y, *outs):
    rows = outs[0].shape[0]
    for d, out in enumerate(outs):
        at = slice(d * rows, (d + 1) * rows)
        out[...] = (x[at].astype(f32) + y[at].astype(f32)).astype(b16)


def assemble_kernel(groups, columns, *refs):
    parts, outs = refs[:groups], refs[groups:]
    grp = lax.axis_index("grp")
    fine = parts[0].shape[0]
    for k in range(groups):
        at = pl.ds(pl.multiple_of((grp ^ k) * fine, fine), fine)
        left = 0
        for out, wide in zip(outs, columns):
            out[at] = parts[k][:, left : left + wide].astype(f32)
            left += wide


def relay_kernel(arrived, out):
    tok, slots = out.shape[0], arrived.shape[0]
    filled = (arrived[:, :128].astype(f32) < EMPTY / 2).astype(b16)
    before = (iota((slots, 1), 0) > iota((1, slots), 1)).astype(b16)
    rank = dot(before, filled, NN)[:, :1].astype(i32)
    rank = jnp.where(filled[:, :1].astype(f32) > 0, rank, -1)
    place = (rank == iota((1, tok), 1)).astype(b16)
    out[...] = dot(place, arrived[...], TN).astype(b16)


def body(events, lengths, destinations, history, negatives, in_weight, out_weight, item_table):
    groups = lax.axis_size("grp")
    owners = lax.axis_size("seq")
    chips = owners // 2
    grp = lax.axis_index("grp")
    seq = lax.axis_index("seq")
    chip, core = seq // 2, seq % 2
    tok = events.shape[0]
    vocab_dev, width = item_table.shape
    hidden = out_weight.shape[1]
    share = vocab_dev // groups
    slot = 3 * tok // (2 * owners)
    rows = width // owners
    fine = rows // groups

    def to_chip(x, d):
        pairs = [(2 * a + b, 2 * ((a + d) % chips) + b) for a in range(chips) for b in range(2)]
        return lax.ppermute(x, "seq", pairs)

    def across(x, k):
        pairs = [(2 * a + b, 2 * (a ^ k) + b) for a in range(chips) for b in range(2)]
        return lax.ppermute(x, "seq", pairs)

    def to_group(x, k):
        return lax.ppermute(x, "grp", [(a, a ^ k) for a in range(groups)])

    def to_core(x):
        return lax.ppermute(x, "seq", [(a, a ^ 1) for a in range(owners)])

    def fold(low, high, gate=()):
        bit = 1
        while bit < chips // 2:
            shape = (low.shape[0] // 2, low.shape[1])
            came, _ = lax.optimization_barrier((across(high, bit), gate))
            low, high = call(pair_kernel, [(shape, b16)] * 2, [VMEM] * 2, [low, came], room=8)
            bit *= 2
        return low, high

    def finish(low, high):
        return low.astype(f32) + across(high, chips // 2).astype(f32)

    def gather_groups(x, near=None):
        wide = x.shape[1]
        if groups != 4:
            return [(k, 0, wide, to_group(x, k) if k else x) for k in range(groups)]
        one, two = near or [to_group(x, k) for k in (1, 2)]
        half = wide // 2
        left, right = to_group(one[:, :half], 2), to_group(two[:, half:], 1)
        return [(0, 0, wide, x), (1, 0, wide, one), (2, 0, wide, two), (3, 0, half, left), (3, half, half, right)]

    own, quarter, quarter_inv = call(
        lambda *refs: normalise_kernel(share, *refs),
        [((vocab_dev, width), b16), ((share, width), b16), ((share, 1), f32)],
        [VMEM], [item_table], flops=8 * vocab_dev * width, nbytes=5 * vocab_dev * width, room=8,
    )
    chunks = [list(range(1, chips))]
    have, bit = {0: quarter}, chips // 2
    while bit:
        have.update({x ^ bit: across(have[x], bit) for x in have})
        bit //= 2
    got = [have[x] for x in distances(chips)[1:]]
    outs = [
        ((tok, width // 2), b16), ((tok, width // 2), b16), ((tok, 4 * hidden), b16), ((tok, 4 * hidden), b16),
        ((HEADS, tok, tok), b16), ((HEADS, tok, tok), b16), ((tok, hidden), f32), ((tok, 1), f32),
        ((tok, hidden), b16), ((tok, width), f32), ((tok, width), b16), ((tok, 1), f32),
        ((owners * slot, width), b16),
    ]
    (keep, give, proj, slope, attn, attn_slope, normed, inverse, gated, unit, unit_b, inv_len, outgoing) = call(
        lambda *refs: forward_kernel(owners, slot, *refs), outs, [SMEM, SMEM, VMEM, VMEM, VMEM],
        [lengths, destinations, events, in_weight, out_weight],
        room=63,
    )

    near_units = [to_group(unit_b, k) for k in (1, 2)]
    candidates = jnp.concatenate([history[:, None], negatives], 1)
    got, near_units, own, candidates = lax.optimization_barrier((got, near_units, own, candidates))
    far_own = to_core(own)
    unit_sent = gather_groups(unit_b, near_units)
    others = [jnp.concatenate(got, 0)]
    pieces = [(0, -1, 0, 0, width, own)]
    for j, x in enumerate(others):
        pieces += [(0, j) + p for p in gather_groups(x)]
    pieces = pieces + [(1,) + p[1:5] + (to_core(p[5]) if p[1] >= 0 else far_own,) for p in pieces]
    near = [p[5] for p in pieces if p[2] == 0]
    outgoing, _ = lax.optimization_barrier((outgoing, others))

    arrived = lax.all_to_all(
        outgoing.reshape(owners, slot, width), "seq", 0, 0, tiled=True
    ).reshape(owners * slot, width)
    vocab = vocab_dev * owners
    far_give, far_gated = to_core(give), to_core(gated)
    units = [p[3] for p in unit_sent]
    layer_out, = call(relay_kernel, [((tok, width), b16)], [VMEM], [arrived], room=63)
    layer_out, score_unit, far_give, far_gated, units = lax.optimization_barrier(
        (layer_out, unit, far_give, far_gated, units)
    )
    saved = [out_weight, proj, slope, attn, attn_slope, normed]
    tags, up_keep, up_give, grad = call(
        lambda *refs: score_kernel(groups, owners, share, chunks, [p[:5] for p in pieces], *refs),
        [((2 * owners, tok), f32), ((tok, width // 2), b16), ((tok, width // 2), b16), ((tok, 4 * hidden), b16)],
        [VMEM] * 3 + [ANY] * (len(pieces) + 8),
        [candidates, inv_len, inverse, unit_b, score_unit] + [p[5] for p in pieces] + saved,
        [pltpu.VMEM((vocab, width), b16), pltpu.VMEM((tok, vocab), b16), pltpu.VMEM((tok, width), b16),
         pltpu.VMEM((tok, width), f32)] + [pltpu.VMEM(x.shape, x.dtype) for x in saved]
        + [pltpu.SemaphoreType.DMA((len(pieces) + 8,))],
        room=63,
    )

    all_tags = [to_group(tags, k) if k else tags for k in range(groups)]
    far = [far_give, to_core(up_give), to_core(grad), far_gated]
    far[1], all_tags = lax.optimization_barrier((far[1], all_tags))
    mine, other = call(
        lambda *refs: item_kernel(groups, owners, share, chunks, [p[:3] for p in unit_sent], *refs),
        [((chips * share, width), b16)] * 2, [ANY] * len(units) + [VMEM] * groups + [ANY] * len(near),
        units + all_tags + near,
        [pltpu.VMEM((groups * tok, width), b16), pltpu.VMEM((2 * chips * share, width), b16),
         pltpu.SemaphoreType.DMA((len(units) + 2 * chips,))],
        room=63,
    )
    far_mine = to_core(other)
    far, mine = lax.optimization_barrier((far, mine))
    half = 5 * hidden // 2
    if groups == 4:
        block = (chips, fine, 5 * hidden)
        split = (chips, fine, half)
        parts = call(
            lambda *refs: weight_kernel(groups, owners, *refs),
            [(block, b16)] + [((2,) + split, b16)] * 2 + [(split, b16)] * 2, [ANY] * 8,
            [keep, grad, up_keep, gated, far[1], far[3], far[0], far[2]],
            [pltpu.VMEM(x.shape, b16) for x in (keep, grad, up_keep, gated, up_keep, gated, keep, grad)]
            + [pltpu.VMEM((width // 2, 4 * hidden), f32), pltpu.VMEM((width // 2, 5 * hidden), b16),
               pltpu.SemaphoreType.DMA((8,))],
            flops=2 * tok * width * 5 * hidden, nbytes=20 * tok * width, room=60,
        )
        by_one, by_two = to_group(parts[1], 1), to_group(parts[2], 2)
        corner = (by_one, by_two)
    else:
        def both(x, y):
            return jnp.concatenate([x, y], 0)

        in_part = dot(both(keep, far[0]), both(grad, far[2]), TN)
        out_part = dot(both(up_keep, far[1]), both(gated, far[3]), TN)
        weight = jnp.concatenate([in_part, out_part], 1).astype(b16)
        weight = weight.reshape(chips, groups, fine, 5 * hidden)
        sums = lax.dynamic_index_in_dim(weight, grp, 1, False).astype(f32)
        for k in range(1, groups):
            sums += to_group(lax.dynamic_index_in_dim(weight, grp ^ k, 1, False), k).astype(f32)


    low, high = call(
        pair_kernel, [((chips // 2 * share, width), b16)] * 2, [VMEM] * 2, [mine, far_mine],
        flops=chips * share * width, nbytes=6 * chips * share * width, room=8,
    )
    low, high = fold(low, high)
    if groups == 4:
        by_one, by_two, low, high = lax.optimization_barrier(corner + (low, high))
        one_right, two_left = call(
            corner_kernel, [(split, b16)] * 2, [VMEM] * 4, [by_one, by_two, parts[3], parts[4]], room=8,
        )
        arrived = [by_one, by_two, to_group(one_right, 1), to_group(two_left, 2)]
    total = finish(low, high)
    total = (total * quarter_inv).astype(b16)
    totals = [to_group(total, k) if k else total for k in range(groups)]
    table_grad, = call(
        lambda *refs: assemble_kernel(groups, [width], *refs), [((vocab_dev, width), f32)], [VMEM] * groups, totals,
        flops=vocab_dev * width, nbytes=6 * vocab_dev * width, room=8,
    )

    if groups == 4:
        base, _ = lax.optimization_barrier((parts[0], total))
        low, high = call(
            sum_kernel, [((chips // 2 * fine, 5 * hidden), b16)] * 2, [VMEM] * 5, [base] + arrived,
            flops=chips * fine * 5 * hidden, nbytes=40 * chips * fine * hidden, room=10,
        )
        line = finish(*fold(low, high, totals[1]))
    else:
        blocks = [lax.dynamic_index_in_dim(sums, (chip + d) % chips, 0, False).astype(b16) for d in range(chips)]
        line = blocks[0].astype(f32)
        for d in range(1, chips):
            line += to_chip(blocks[d], d).astype(f32)
    line = line.astype(b16)
    lines = [to_group(line, k) if k else line for k in range(groups)]
    if fine % 16 == 0:
        in_grad, out_grad = call(
            lambda *refs: assemble_kernel(groups, [4 * hidden, hidden], *refs),
            [((rows, 4 * hidden), f32), ((rows, hidden), f32)], [VMEM] * groups, lines,
            flops=rows * hidden, nbytes=30 * rows * hidden, room=8,
        )
    else:
        shard = jnp.zeros((rows, 5 * hidden), f32)
        for k in range(groups):
            shard = lax.dynamic_update_slice_in_dim(shard, lines[k].astype(f32), (grp ^ k) * fine, 0)
        in_grad, out_grad = shard[:, : 4 * hidden], shard[:, 4 * hidden :]
    return (layer_out, in_grad, out_grad, table_grad)


def solution(mesh):
    return jax.shard_map(
        body,
        mesh=mesh,
        in_specs=(
            P(("grp", "seq"), None),
            P(("grp", "seq"), None),
            P(("grp", "seq"), None),
            P(("grp", "seq")),
            P(("grp", "seq"), None),
            P(),
            P(),
            P("seq", None),
        ),
        out_specs=(P(("grp", "seq"), None), P("seq", None), P("seq", None), P("seq", None)),
        check_vma=False,
    )
```

```python
import jax
import jax.numpy as jnp
from jax import lax
from jax.experimental import pallas as pl
from jax.experimental.pallas import tpu as pltpu
from jax.sharding import PartitionSpec as P

HEADS = 4
HEAD_DIM = 128
NCAND = 4

epsilon = 1e-05
softmax_warmth = 0.05
EMPTY = 2.0**100

f32, b16, i32 = jnp.float32, jnp.bfloat16, jnp.int32
NN = ((1,), (0,))
NT = ((1,), (1,))
TN = ((0,), (0,))
VMEM = pl.BlockSpec(memory_space=pltpu.VMEM)
SMEM = pl.BlockSpec(memory_space=pltpu.SMEM)
ANY = pl.BlockSpec(memory_space=pl.ANY)


def dot(a, b, dims):
    return lax.dot_general(a, b, (dims, ((), ())), preferred_element_type=f32)


def iota(shape, axis):
    return lax.broadcasted_iota(i32, shape, axis)


def center_scale(values):
    average = jnp.mean(values, -1, keepdims=True)
    centered = values - average
    inverse = lax.rsqrt(jnp.mean(centered * centered, -1, keepdims=True) + epsilon)
    return (centered * inverse, inverse)


def sigmoid(values):
    return 1.0 / (1.0 + jnp.exp(-values))


def split_columns(x, owners, core):
    rows = x.shape[1] // owners
    blocks = [x[:, i * rows : (i + 1) * rows] for i in range(owners)]
    even, odd = jnp.concatenate(blocks[0::2], 1), jnp.concatenate(blocks[1::2], 1)
    first = jnp.broadcast_to(core, even.shape) == 0
    return jnp.where(first, even, odd), jnp.where(first, odd, even)


def call(kernel, out, specs, args, scratch=(), flops=0, nbytes=0, room=14):
    return pl.pallas_call(
        kernel,
        out_shape=[jax.ShapeDtypeStruct(s, t) for s, t in out],
        in_specs=specs,
        out_specs=[VMEM] * len(out),
        scratch_shapes=list(scratch),
        cost_estimate=pl.CostEstimate(flops=flops, bytes_accessed=nbytes, transcendentals=0),
        compiler_params=pltpu.CompilerParams(vmem_limit_bytes=room * 2**20),
    )(*args)


def forward_kernel(
    owners, slot, lengths, dests, events, in_weight, out_weight,
    keep, give, proj, slope, attn, attn_slope, normed_out, inv_out, gated_out, unit, unit_b, inv_len, outgoing,
):
    tok = events.shape[0]
    hidden = out_weight.shape[1]
    scale = HEAD_DIM ** (-0.5)
    core = lax.axis_index("seq") % 2
    x = events[...].astype(f32)
    normed_in = center_scale(x)[0]
    mine, other = split_columns(normed_in, owners, core)
    keep[...] = mine.astype(b16)
    give[...] = other.astype(b16)
    normed_in = normed_in.astype(b16)
    for i in range(4):
        cols = slice(i * hidden, (i + 1) * hidden)
        p = dot(normed_in, in_weight[:, cols], NN)
        sig = sigmoid(p)
        proj[:, cols] = (p * sig).astype(b16)
        slope[:, cols] = (sig * (1.0 + p * (1.0 - sig))).astype(b16)

    pos_c, pos_r = iota((tok, 1), 0), iota((1, tok), 1)
    user_c, user_r = jnp.zeros((tok, 1), i32), jnp.zeros((1, tok), i32)
    target = jnp.zeros((1, tok), i32)
    start = jnp.int32(0)
    for j in range(lengths.shape[1]):
        end = start + lengths[0, j]
        user_c += (pos_c >= end).astype(i32)
        user_r += (pos_r >= end).astype(i32)
        here = (pos_r >= start) & (pos_r < end)
        target = jnp.where(here, dests[0, j] * slot + pos_r - start, target)
        start = end
    mask = (user_c == user_r) & (pos_r <= pos_c)

    outputs = []
    for h in range(HEADS):
        v = proj[:, hidden + h * HEAD_DIM : hidden + (h + 1) * HEAD_DIM]
        q = proj[:, 2 * hidden + h * HEAD_DIM : 2 * hidden + (h + 1) * HEAD_DIM]
        k = proj[:, 3 * hidden + h * HEAD_DIM : 3 * hidden + (h + 1) * HEAD_DIM]
        s = dot(q, k, NT) * scale
        sig = sigmoid(s)
        weight = jnp.where(mask, s * sig, 0.0).astype(b16)
        attn[h] = weight
        attn_slope[h] = jnp.where(mask, sig * (1.0 + s * (1.0 - sig)) * scale, 0.0).astype(b16)
        outputs.append(dot(weight, v, NN))
    normed, inverse = center_scale(jnp.concatenate(outputs, 1))
    normed_out[...] = normed
    inv_out[...] = inverse
    gated = (normed * proj[:, :hidden].astype(f32)).astype(b16)
    gated_out[...] = gated
    result = x + dot(gated, out_weight[...], NT)
    inverse = lax.rsqrt(jnp.sum(result * result, -1, keepdims=True) + epsilon)
    inv_len[...] = inverse
    yn = result * inverse
    unit[...] = yn
    unit_b[...] = yn.astype(b16)
    row = iota((outgoing.shape[0], 1), 0)
    filled = jnp.zeros(row.shape, i32)
    for j in range(lengths.shape[1]):
        at = dests[0, j] * slot
        filled = jnp.where((row >= at) & (row < at + lengths[0, j]), 1, filled)
    placed = dot((row == target).astype(b16), result.astype(b16), NN)
    outgoing[...] = jnp.where(filled == 1, placed, EMPTY).astype(b16)


def distances(chips):
    order, bit = [0], chips // 2
    while bit:
        order += [x ^ bit for x in order]
        bit //= 2
    return order


def owner_ids(owners):
    seq = lax.axis_index("seq")
    chip, core = seq // 2, seq % 2
    chips = owners // 2
    return [2 * (chip ^ d) + (core ^ side) for side in range(2) for d in distances(chips)]


def normalise_kernel(share, item_table, own, quarter, quarter_inv):
    grp = lax.axis_index("grp")
    x = item_table[...].astype(f32)
    own[...] = (x * lax.rsqrt(jnp.sum(x * x, -1, keepdims=True) + epsilon)).astype(b16)
    x = item_table[pl.ds(pl.multiple_of(grp * share, share), share)].astype(f32)
    inverse = lax.rsqrt(jnp.sum(x * x, -1, keepdims=True) + epsilon)
    quarter[...] = (x * inverse).astype(b16)
    quarter_inv[...] = inverse


def backward(up, inverse, out_weight, proj, slope, attn, attn_slope, normed_ref, grad):
    hidden = out_weight.shape[1]
    normed = normed_ref[...]
    grad_gated = dot(up, out_weight[...], NN)
    grad[:, :hidden] = (grad_gated * normed * slope[:, :hidden].astype(f32)).astype(b16)
    grad_normed = grad_gated * proj[:, :hidden].astype(f32)
    grad_attended = inverse[...] * (
        grad_normed
        - jnp.mean(grad_normed, -1, keepdims=True)
        - normed * jnp.mean(grad_normed * normed, -1, keepdims=True)
    )
    grad_attended = grad_attended.astype(b16)
    for h in range(HEADS):
        cv, cq, ck = [slice(i * hidden + h * HEAD_DIM, i * hidden + (h + 1) * HEAD_DIM) for i in (1, 2, 3)]
        part = grad_attended[:, h * HEAD_DIM : (h + 1) * HEAD_DIM]
        grad_attn = dot(part, proj[:, cv], NT)
        grad_score = (grad_attn * attn_slope[h].astype(f32)).astype(b16)
        grad[:, cv] = (dot(attn[h], part, TN) * slope[:, cv].astype(f32)).astype(b16)
        grad[:, cq] = (dot(grad_score, proj[:, ck], NN) * slope[:, cq].astype(f32)).astype(b16)
        grad[:, ck] = (dot(grad_score, proj[:, cq], TN) * slope[:, ck].astype(f32)).astype(b16)


def score_kernel(groups, owners, share, chunks, places, cand, inv_len, inverse, unit_hbm, yn_hbm, *refs):
    count = len(places)
    pieces, saved_hbm, refs = refs[:count], refs[count : count + 6], refs[count + 6 :]
    tags, up_keep, up_give, grad, table, spread, unit_b, unit, *saved, sems = refs
    chips = owners // 2
    vocab_dev = share * groups
    grp, core = lax.axis_index("grp"), lax.axis_index("seq") % 2
    tok = unit_b.shape[0]
    block = vocab_dev + groups * (chips - 1) * share

    def place(key):
        side, chunk, k = key
        if chunk < 0:
            return side * block, vocab_dev
        before = sum(len(ds) for ds in chunks[:chunk]) * groups * share
        rows = len(chunks[chunk]) * share
        return side * block + vocab_dev + before + k * rows, rows

    load_unit = pltpu.make_async_copy(unit_hbm, unit_b, sems.at[count])
    load_unit.start()
    copies = {}
    for n, (*key, left, wide) in enumerate(places):
        at, rows = place(key)
        copy = pltpu.make_async_copy(pieces[n], table.at[pl.ds(at, rows), pl.ds(left, wide)], sems.at[n])
        copy.start()
        copies.setdefault(tuple(key), []).append(copy)
    load_yn = pltpu.make_async_copy(yn_hbm, unit, sems.at[count + 1])
    load_yn.start()
    load_saved = [
        pltpu.make_async_copy(x, y, sems.at[count + 2 + n]) for n, (x, y) in enumerate(zip(saved_hbm, saved))
    ]
    for copy in load_saved:
        copy.start()
    ids = owner_ids(owners)
    lane = iota((1, 128), 1)
    owner = jnp.full((1, 128), -1, i32)
    for j in range(owners):
        owner = jnp.where(lane == j, ids[j], owner)
    candidates = cand[...]
    chosen = jnp.full((tok, 128), -1, i32)
    first = jnp.zeros((tok, 128), f32)
    for c in range(NCAND):
        here = candidates[:, c : c + 1] // vocab_dev == owner
        chosen = jnp.where(here, candidates[:, c : c + 1], chosen)
        if c == 0:
            first = here.astype(f32)
    wanted = [jnp.broadcast_to(chosen[:, j : j + 1], (tok, 128)) for j in range(owners)]

    def runs(key):
        side, chunk, k = key
        at, rows = place(key)
        if chunk < 0:
            return at, rows, [(side * chips, 0, vocab_dev, ids[side * chips] * vocab_dev)]
        begin = (grp ^ k) * share
        return at, rows, [
            (side * chips + d, i * share, share, ids[side * chips + d] * vocab_dev + begin)
            for i, d in enumerate(chunks[chunk])
        ]

    def tiles(key):
        at, rows, here = runs(key)
        for j, off, wide, base in here:
            step = min(wide, 128)
            for o in range(0, wide, step):
                hit = wanted[j][:, :step] == base + o + iota((1, step), 1)
                yield j, off + o, step, hit

    load_unit.wait()
    yb = unit_b[...]
    value = [[] for _ in range(owners)]
    for key in copies:
        for copy in copies[key]:
            copy.wait()
        at, rows, _ = runs(key)
        product = dot(yb, table[at : at + rows], NT)
        for j, off, step, hit in tiles(key):
            value[j].append(jnp.where(hit, product[:, off : off + step], 0.0))
    logits = jnp.zeros((tok, 128), f32)
    for j in range(owners):
        total = value[j][0]
        for part in value[j][1:]:
            total = total + part
        logits = jnp.where(lane == j, jnp.sum(total, -1, keepdims=True), logits)
    exponent = jnp.where(chosen >= 0, jnp.exp(logits / softmax_warmth), 0.0)
    coef = (exponent / jnp.sum(exponent, -1, keepdims=True) - first) / softmax_warmth
    tags[:owners] = coef.T[:owners]
    tags[owners:] = chosen.astype(f32).T[:owners]
    amount = [jnp.broadcast_to(coef[:, j : j + 1], (tok, 128)) for j in range(owners)]
    for key in copies:
        at = runs(key)[0]
        for j, off, step, hit in tiles(key):
            spread[:, at + off : at + off + step] = jnp.where(hit, amount[j][:, :step], 0.0).astype(b16)
    pulled = dot(spread[...], table[...], NN)
    load_yn.wait()
    yn = unit[...]
    upstream = (pulled - yn * jnp.sum(yn * pulled, -1, keepdims=True)) * inv_len[...]
    mine, other = split_columns(upstream, owners, core)
    up_keep[...] = mine.astype(b16)
    up_give[...] = other.astype(b16)
    for copy in load_saved:
        copy.wait()
    backward(upstream.astype(b16), inverse, *saved, grad)


def item_kernel(groups, owners, share, chunks, places, *refs):
    count = len(places)
    units, tags = refs[:count], refs[count : count + groups]
    parts, (keep, give, gathered, near, sems) = refs[count + groups : -5], refs[-5:]
    chips = owners // 2
    vocab_dev = share * groups
    grp = lax.axis_index("grp")
    tok = tags[0].shape[1]
    copies = []
    for n, (k, left, wide) in enumerate(places):
        copies.append(pltpu.make_async_copy(units[n], gathered.at[pl.ds(k * tok, tok), pl.ds(left, wide)], sems.at[n]))
    begin = pl.multiple_of(grp * share, share)
    for n, part in enumerate(parts):
        side, chunk = n // (len(chunks) + 1), n % (len(chunks) + 1) - 1
        for i, d in enumerate([0] if chunk < 0 else chunks[chunk]):
            rows = pl.ds(begin if chunk < 0 else i * share, share)
            at = pl.ds((side * chips + d) * share, share)
            copies.append(pltpu.make_async_copy(part.at[rows], near.at[at], sems.at[len(copies)]))
    for copy in copies:
        copy.start()
    ids = owner_ids(owners)
    amounts = jnp.concatenate([t[:owners] for t in tags], 1)
    chosen = jnp.concatenate([t[owners:] for t in tags], 1).astype(i32)
    for copy in copies[:count]:
        copy.wait()
    for side, out in ((0, keep), (1, give)):
        parts = []
        for d in range(chips):
            j = side * chips + d
            hit = ids[j] * vocab_dev + grp * share + iota((share, 1), 0) == chosen[j : j + 1]
            parts.append(jnp.where(hit, amounts[j : j + 1], 0.0).astype(b16))
        summed = dot(jnp.concatenate(parts, 0), gathered[...], NN)
        for copy in copies[count + side * chips : count + (side + 1) * chips]:
            copy.wait()
        row = near[side * chips * share : (side + 1) * chips * share].astype(f32)
        out[...] = (summed - row * jnp.sum(row * summed, -1, keepdims=True)).astype(b16)


def weight_kernel(groups, owners, *refs):
    given, outs, loaded, (own, whole, sems) = refs[:8], refs[8:15], refs[15:23], refs[23:]
    copies = [pltpu.make_async_copy(x, y, sems.at[n]) for n, (x, y) in enumerate(zip(given, loaded))]
    for copy in copies:
        copy.start()
    keep, grad, up_keep, gated, up_give, far_gated, give, far_grad = loaded
    chips = owners // 2
    grp = lax.axis_index("grp")
    wide = grad.shape[1]
    step = gated.shape[1]
    for copy in copies[:2]:
        copy.wait()
    for i in range(0, wide, step):
        own[:, i : i + step] = dot(keep[...], grad[:, i : i + step], TN)
    for copy in copies[2:6]:
        copy.wait()
    part = dot(up_keep[...], gated[...], TN) + dot(up_give[...], far_gated[...], TN)
    whole[:, wide:] = part.astype(b16)
    for copy in copies[6:]:
        copy.wait()
    for i in range(0, wide, step):
        cols = slice(i, i + step)
        whole[:, cols] = (own[:, cols] + dot(give[...], far_grad[:, cols], TN)).astype(b16)
    rows = whole.shape[0] // chips
    fine = rows // groups
    half = whole.shape[1] // 2
    base = outs[0]
    for z in range(chips):
        for k in range(groups):
            piece = whole[pl.ds(pl.multiple_of(z * rows + (grp ^ k) * fine, fine), fine)]
            if k == 0:
                base[z] = piece
            else:
                outs[2 * k - 1][z] = piece[:, :half]
                outs[2 * k][z] = piece[:, half:]


def corner_kernel(left, right, one_right, two_left, right_out, left_out):
    right_out[...] = (one_right[...].astype(f32) + right[...].astype(f32)).astype(b16)
    left_out[...] = (two_left[...].astype(f32) + left[...].astype(f32)).astype(b16)


def sum_kernel(base, one_left, one_right, two_left, two_right, *outs):
    chips, fine, wide = base.shape
    chip = lax.axis_index("seq") // 2
    half = wide // 2
    for n, d in enumerate(distances(chips)):
        z = chip ^ d
        own = base[z].astype(f32)
        left = own[:, :half] + one_left[z].astype(f32) + two_left[z].astype(f32)
        right = own[:, half:] + two_right[z].astype(f32) + one_right[z].astype(f32)
        out = outs[2 * n // chips]
        at = slice(n % (chips // 2) * fine, (n % (chips // 2) + 1) * fine)
        out[at, :half] = left.astype(b16)
        out[at, half:] = right.astype(b16)


def pair_kernel(x, y, *outs):
    rows = outs[0].shape[0]
    for d, out in enumerate(outs):
        at = slice(d * rows, (d + 1) * rows)
        out[...] = (x[at].astype(f32) + y[at].astype(f32)).astype(b16)


def assemble_kernel(groups, columns, *refs):
    parts, outs = refs[:groups], refs[groups:]
    grp = lax.axis_index("grp")
    fine = parts[0].shape[0]
    for k in range(groups):
        at = pl.ds(pl.multiple_of((grp ^ k) * fine, fine), fine)
        left = 0
        for out, wide in zip(outs, columns):
            out[at] = parts[k][:, left : left + wide].astype(f32)
            left += wide


def relay_kernel(arrived, out):
    tok, slots = out.shape[0], arrived.shape[0]
    filled = (arrived[:, :128].astype(f32) < EMPTY / 2).astype(b16)
    before = (iota((slots, 1), 0) > iota((1, slots), 1)).astype(b16)
    rank = dot(before, filled, NN)[:, :1].astype(i32)
    rank = jnp.where(filled[:, :1].astype(f32) > 0, rank, -1)
    place = (rank == iota((1, tok), 1)).astype(b16)
    out[...] = dot(place, arrived[...], TN).astype(b16)


def body(events, lengths, destinations, history, negatives, in_weight, out_weight, item_table):
    groups = lax.axis_size("grp")
    owners = lax.axis_size("seq")
    chips = owners // 2
    grp = lax.axis_index("grp")
    seq = lax.axis_index("seq")
    chip, core = seq // 2, seq % 2
    tok = events.shape[0]
    vocab_dev, width = item_table.shape
    hidden = out_weight.shape[1]
    share = vocab_dev // groups
    slot = 3 * tok // (2 * owners)
    rows = width // owners
    fine = rows // groups

    def to_chip(x, d):
        pairs = [(2 * a + b, 2 * ((a + d) % chips) + b) for a in range(chips) for b in range(2)]
        return lax.ppermute(x, "seq", pairs)

    def across(x, k):
        pairs = [(2 * a + b, 2 * (a ^ k) + b) for a in range(chips) for b in range(2)]
        return lax.ppermute(x, "seq", pairs)

    def to_group(x, k):
        return lax.ppermute(x, "grp", [(a, a ^ k) for a in range(groups)])

    def to_core(x):
        return lax.ppermute(x, "seq", [(a, a ^ 1) for a in range(owners)])

    def fold(low, high, gate=()):
        bit = 1
        while bit < chips // 2:
            shape = (low.shape[0] // 2, low.shape[1])
            came, _ = lax.optimization_barrier((across(high, bit), gate))
            low, high = call(pair_kernel, [(shape, b16)] * 2, [VMEM] * 2, [low, came], room=8)
            bit *= 2
        return low, high

    def finish(low, high):
        return low.astype(f32) + across(high, chips // 2).astype(f32)

    def gather_groups(x, near=None):
        wide = x.shape[1]
        if groups != 4:
            return [(k, 0, wide, to_group(x, k) if k else x) for k in range(groups)]
        one, two = near or [to_group(x, k) for k in (1, 2)]
        half = wide // 2
        left, right = to_group(one[:, :half], 2), to_group(two[:, half:], 1)
        return [(0, 0, wide, x), (1, 0, wide, one), (2, 0, wide, two), (3, 0, half, left), (3, half, half, right)]

    own, quarter, quarter_inv = call(
        lambda *refs: normalise_kernel(share, *refs),
        [((vocab_dev, width), b16), ((share, width), b16), ((share, 1), f32)],
        [VMEM], [item_table], flops=8 * vocab_dev * width, nbytes=5 * vocab_dev * width, room=8,
    )
    chunks = [list(range(1, chips))]
    have, bit = {0: quarter}, chips // 2
    while bit:
        have.update({x ^ bit: across(have[x], bit) for x in have})
        bit //= 2
    got = [have[x] for x in distances(chips)[1:]]
    outs = [
        ((tok, width // 2), b16), ((tok, width // 2), b16), ((tok, 4 * hidden), b16), ((tok, 4 * hidden), b16),
        ((HEADS, tok, tok), b16), ((HEADS, tok, tok), b16), ((tok, hidden), f32), ((tok, 1), f32),
        ((tok, hidden), b16), ((tok, width), f32), ((tok, width), b16), ((tok, 1), f32),
        ((owners * slot, width), b16),
    ]
    (keep, give, proj, slope, attn, attn_slope, normed, inverse, gated, unit, unit_b, inv_len, outgoing) = call(
        lambda *refs: forward_kernel(owners, slot, *refs), outs, [SMEM, SMEM, VMEM, VMEM, VMEM],
        [lengths, destinations, events, in_weight, out_weight],
        room=63,
    )

    near_units = [to_group(unit_b, k) for k in (1, 2)]
    candidates = jnp.concatenate([history[:, None], negatives], 1)
    got, near_units, own, candidates = lax.optimization_barrier((got, near_units, own, candidates))
    far_own = to_core(own)
    unit_sent = gather_groups(unit_b, near_units)
    others = [jnp.concatenate(got, 0)]
    pieces = [(0, -1, 0, 0, width, own)]
    for j, x in enumerate(others):
        pieces += [(0, j) + p for p in gather_groups(x)]
    pieces = pieces + [(1,) + p[1:5] + (to_core(p[5]) if p[1] >= 0 else far_own,) for p in pieces]
    near = [p[5] for p in pieces if p[2] == 0]
    outgoing, _ = lax.optimization_barrier((outgoing, others))

    arrived = lax.all_to_all(
        outgoing.reshape(owners, slot, width), "seq", 0, 0, tiled=True
    ).reshape(owners * slot, width)
    vocab = vocab_dev * owners
    far_give, far_gated = to_core(give), to_core(gated)
    units = [p[3] for p in unit_sent]
    layer_out, = call(relay_kernel, [((tok, width), b16)], [VMEM], [arrived], room=63)
    layer_out, score_unit, far_give, far_gated, units = lax.optimization_barrier(
        (layer_out, unit, far_give, far_gated, units)
    )
    saved = [out_weight, proj, slope, attn, attn_slope, normed]
    tags, up_keep, up_give, grad = call(
        lambda *refs: score_kernel(groups, owners, share, chunks, [p[:5] for p in pieces], *refs),
        [((2 * owners, tok), f32), ((tok, width // 2), b16), ((tok, width // 2), b16), ((tok, 4 * hidden), b16)],
        [VMEM] * 3 + [ANY] * (len(pieces) + 8),
        [candidates, inv_len, inverse, unit_b, score_unit] + [p[5] for p in pieces] + saved,
        [pltpu.VMEM((vocab, width), b16), pltpu.VMEM((tok, vocab), b16), pltpu.VMEM((tok, width), b16),
         pltpu.VMEM((tok, width), f32)] + [pltpu.VMEM(x.shape, x.dtype) for x in saved]
        + [pltpu.SemaphoreType.DMA((len(pieces) + 8,))],
        room=63,
    )

    all_tags = [to_group(tags, k) if k else tags for k in range(groups)]
    far = [far_give, to_core(up_give), to_core(grad), far_gated]
    far, all_tags = lax.optimization_barrier((far, all_tags))
    half = 5 * hidden // 2
    if groups == 4:
        block = (chips, fine, 5 * hidden)
        split = (chips, fine, half)
        parts = call(
            lambda *refs: weight_kernel(groups, owners, *refs),
            [(block, b16)] + [(split, b16)] * 6, [ANY] * 8,
            [keep, grad, up_keep, gated, far[1], far[3], far[0], far[2]],
            [pltpu.VMEM(x.shape, b16) for x in (keep, grad, up_keep, gated, up_keep, gated, keep, grad)]
            + [pltpu.VMEM((width // 2, 4 * hidden), f32), pltpu.VMEM((width // 2, 5 * hidden), b16),
               pltpu.SemaphoreType.DMA((8,))],
            flops=2 * tok * width * 5 * hidden, nbytes=20 * tok * width, room=60,
        )
        left, right = to_group(parts[5], 1), to_group(parts[6], 2)
        one_left, two_right = to_group(parts[1], 1), to_group(parts[4], 2)
        one_right, two_left = call(
            corner_kernel, [(split, b16)] * 2, [VMEM] * 4, [left, right, parts[2], parts[3]], room=8,
        )
        arrived = [one_left, to_group(one_right, 1), to_group(two_left, 2), two_right]
        after = one_right
    else:
        def both(x, y):
            return jnp.concatenate([x, y], 0)

        in_part = dot(both(keep, far[0]), both(grad, far[2]), TN)
        out_part = dot(both(up_keep, far[1]), both(gated, far[3]), TN)
        weight = jnp.concatenate([in_part, out_part], 1).astype(b16)
        weight = weight.reshape(chips, groups, fine, 5 * hidden)
        after = weight
        sums = lax.dynamic_index_in_dim(weight, grp, 1, False).astype(f32)
        for k in range(1, groups):
            sums += to_group(lax.dynamic_index_in_dim(weight, grp ^ k, 1, False), k).astype(f32)


    units[0], _ = lax.optimization_barrier((units[0], after))
    mine, other = call(
        lambda *refs: item_kernel(groups, owners, share, chunks, [p[:3] for p in unit_sent], *refs),
        [((chips * share, width), b16)] * 2, [ANY] * len(units) + [VMEM] * groups + [ANY] * len(near),
        units + all_tags + near,
        [pltpu.VMEM((groups * tok, width), b16), pltpu.VMEM((2 * chips * share, width), b16),
         pltpu.SemaphoreType.DMA((len(units) + 2 * chips,))],
        room=63,
    )
    far_mine = to_core(other)

    low, high = call(
        pair_kernel, [((chips // 2 * share, width), b16)] * 2, [VMEM] * 2, [mine, far_mine],
        flops=chips * share * width, nbytes=6 * chips * share * width, room=8,
    )
    low, high = fold(low, high)
    total = finish(low, high)
    total = (total * quarter_inv).astype(b16)
    totals = [to_group(total, k) if k else total for k in range(groups)]
    table_grad, = call(
        lambda *refs: assemble_kernel(groups, [width], *refs), [((vocab_dev, width), f32)], [VMEM] * groups, totals,
        flops=vocab_dev * width, nbytes=6 * vocab_dev * width, room=8,
    )

    if groups == 4:
        base = parts[0]
        low, high = call(
            sum_kernel, [((chips // 2 * fine, 5 * hidden), b16)] * 2, [VMEM] * 5, [base] + arrived,
            flops=chips * fine * 5 * hidden, nbytes=40 * chips * fine * hidden, room=10,
        )
        line = finish(*fold(low, high))
    else:
        blocks = [lax.dynamic_index_in_dim(sums, (chip + d) % chips, 0, False).astype(b16) for d in range(chips)]
        line = blocks[0].astype(f32)
        for d in range(1, chips):
            line += to_chip(blocks[d], d).astype(f32)
    line = line.astype(b16)
    lines = [to_group(line, k) if k else line for k in range(groups)]
    if fine % 16 == 0:
        in_grad, out_grad = call(
            lambda *refs: assemble_kernel(groups, [4 * hidden, hidden], *refs),
            [((rows, 4 * hidden), f32), ((rows, hidden), f32)], [VMEM] * groups, lines,
            flops=rows * hidden, nbytes=30 * rows * hidden, room=8,
        )
    else:
        shard = jnp.zeros((rows, 5 * hidden), f32)
        for k in range(groups):
            shard = lax.dynamic_update_slice_in_dim(shard, lines[k].astype(f32), (grp ^ k) * fine, 0)
        in_grad, out_grad = shard[:, : 4 * hidden], shard[:, 4 * hidden :]
    return (layer_out, in_grad, out_grad, table_grad)


def solution(mesh):
    return jax.shard_map(
        body,
        mesh=mesh,
        in_specs=(
            P(("grp", "seq"), None),
            P(("grp", "seq"), None),
            P(("grp", "seq"), None),
            P(("grp", "seq")),
            P(("grp", "seq"), None),
            P(),
            P(),
            P("seq", None),
        ),
        out_specs=(P(("grp", "seq"), None), P("seq", None), P("seq", None), P("seq", None)),
        check_vma=False,
    )
```

```python
import jax
import jax.numpy as jnp
from jax import lax
from jax.experimental import pallas as pl
from jax.experimental.pallas import tpu as pltpu
from jax.sharding import PartitionSpec as P

HEADS = 4
HEAD_DIM = 128
NCAND = 4

epsilon = 1e-05
softmax_warmth = 0.05
EMPTY = 2.0**100

f32, b16, i32 = jnp.float32, jnp.bfloat16, jnp.int32
NN = ((1,), (0,))
NT = ((1,), (1,))
TN = ((0,), (0,))
VMEM = pl.BlockSpec(memory_space=pltpu.VMEM)
SMEM = pl.BlockSpec(memory_space=pltpu.SMEM)
ANY = pl.BlockSpec(memory_space=pl.ANY)


def dot(a, b, dims):
    return lax.dot_general(a, b, (dims, ((), ())), preferred_element_type=f32)


def iota(shape, axis):
    return lax.broadcasted_iota(i32, shape, axis)


def center_scale(values):
    average = jnp.mean(values, -1, keepdims=True)
    centered = values - average
    inverse = lax.rsqrt(jnp.mean(centered * centered, -1, keepdims=True) + epsilon)
    return (centered * inverse, inverse)


def sigmoid(values):
    return 1.0 / (1.0 + jnp.exp(-values))


def split_columns(x, owners, core):
    rows = x.shape[1] // owners
    blocks = [x[:, i * rows : (i + 1) * rows] for i in range(owners)]
    even, odd = jnp.concatenate(blocks[0::2], 1), jnp.concatenate(blocks[1::2], 1)
    first = jnp.broadcast_to(core, even.shape) == 0
    return jnp.where(first, even, odd), jnp.where(first, odd, even)


def call(kernel, out, specs, args, scratch=(), flops=0, nbytes=0, room=14):
    return pl.pallas_call(
        kernel,
        out_shape=[jax.ShapeDtypeStruct(s, t) for s, t in out],
        in_specs=specs,
        out_specs=[VMEM] * len(out),
        scratch_shapes=list(scratch),
        cost_estimate=pl.CostEstimate(flops=flops, bytes_accessed=nbytes, transcendentals=0),
        compiler_params=pltpu.CompilerParams(vmem_limit_bytes=room * 2**20),
    )(*args)


def forward_kernel(
    owners, slot, lengths, dests, events, in_weight, out_weight,
    keep, give, proj, slope, attn, attn_slope, normed_out, inv_out, gated_out, unit, unit_b, inv_len, outgoing,
):
    tok = events.shape[0]
    hidden = out_weight.shape[1]
    scale = HEAD_DIM ** (-0.5)
    core = lax.axis_index("seq") % 2
    x = events[...].astype(f32)
    normed_in = center_scale(x)[0]
    mine, other = split_columns(normed_in, owners, core)
    keep[...] = mine.astype(b16)
    give[...] = other.astype(b16)
    normed_in = normed_in.astype(b16)
    for i in range(4):
        cols = slice(i * hidden, (i + 1) * hidden)
        p = dot(normed_in, in_weight[:, cols], NN)
        sig = sigmoid(p)
        proj[:, cols] = (p * sig).astype(b16)
        slope[:, cols] = (sig * (1.0 + p * (1.0 - sig))).astype(b16)

    pos_c, pos_r = iota((tok, 1), 0), iota((1, tok), 1)
    user_c, user_r = jnp.zeros((tok, 1), i32), jnp.zeros((1, tok), i32)
    target = jnp.zeros((1, tok), i32)
    start = jnp.int32(0)
    for j in range(lengths.shape[1]):
        end = start + lengths[0, j]
        user_c += (pos_c >= end).astype(i32)
        user_r += (pos_r >= end).astype(i32)
        here = (pos_r >= start) & (pos_r < end)
        target = jnp.where(here, dests[0, j] * slot + pos_r - start, target)
        start = end
    mask = (user_c == user_r) & (pos_r <= pos_c)

    outputs = []
    for h in range(HEADS):
        v = proj[:, hidden + h * HEAD_DIM : hidden + (h + 1) * HEAD_DIM]
        q = proj[:, 2 * hidden + h * HEAD_DIM : 2 * hidden + (h + 1) * HEAD_DIM]
        k = proj[:, 3 * hidden + h * HEAD_DIM : 3 * hidden + (h + 1) * HEAD_DIM]
        s = dot(q, k, NT) * scale
        sig = sigmoid(s)
        weight = jnp.where(mask, s * sig, 0.0).astype(b16)
        attn[h] = weight
        attn_slope[h] = jnp.where(mask, sig * (1.0 + s * (1.0 - sig)) * scale, 0.0).astype(b16)
        outputs.append(dot(weight, v, NN))
    normed, inverse = center_scale(jnp.concatenate(outputs, 1))
    normed_out[...] = normed
    inv_out[...] = inverse
    gated = (normed * proj[:, :hidden].astype(f32)).astype(b16)
    gated_out[...] = gated
    result = x + dot(gated, out_weight[...], NT)
    inverse = lax.rsqrt(jnp.sum(result * result, -1, keepdims=True) + epsilon)
    inv_len[...] = inverse
    yn = result * inverse
    unit[...] = yn
    unit_b[...] = yn.astype(b16)
    row = iota((outgoing.shape[0], 1), 0)
    filled = jnp.zeros(row.shape, i32)
    for j in range(lengths.shape[1]):
        at = dests[0, j] * slot
        filled = jnp.where((row >= at) & (row < at + lengths[0, j]), 1, filled)
    placed = dot((row == target).astype(b16), result.astype(b16), NN)
    outgoing[...] = jnp.where(filled == 1, placed, EMPTY).astype(b16)


def distances(chips):
    order, bit = [0], chips // 2
    while bit:
        order += [x ^ bit for x in order]
        bit //= 2
    return order


def owner_ids(owners):
    seq = lax.axis_index("seq")
    chip, core = seq // 2, seq % 2
    chips = owners // 2
    return [2 * (chip ^ d) + (core ^ side) for side in range(2) for d in distances(chips)]


def normalise_kernel(share, item_table, own, quarter, quarter_inv):
    grp = lax.axis_index("grp")
    x = item_table[...].astype(f32)
    own[...] = (x * lax.rsqrt(jnp.sum(x * x, -1, keepdims=True) + epsilon)).astype(b16)
    x = item_table[pl.ds(pl.multiple_of(grp * share, share), share)].astype(f32)
    inverse = lax.rsqrt(jnp.sum(x * x, -1, keepdims=True) + epsilon)
    quarter[...] = (x * inverse).astype(b16)
    quarter_inv[...] = inverse


def backward(up, inverse, out_weight, proj, slope, attn, attn_slope, normed_ref, grad):
    hidden = out_weight.shape[1]
    normed = normed_ref[...]
    grad_gated = dot(up, out_weight[...], NN)
    grad[:, :hidden] = (grad_gated * normed * slope[:, :hidden].astype(f32)).astype(b16)
    grad_normed = grad_gated * proj[:, :hidden].astype(f32)
    grad_attended = inverse[...] * (
        grad_normed
        - jnp.mean(grad_normed, -1, keepdims=True)
        - normed * jnp.mean(grad_normed * normed, -1, keepdims=True)
    )
    grad_attended = grad_attended.astype(b16)
    for h in range(HEADS):
        cv, cq, ck = [slice(i * hidden + h * HEAD_DIM, i * hidden + (h + 1) * HEAD_DIM) for i in (1, 2, 3)]
        part = grad_attended[:, h * HEAD_DIM : (h + 1) * HEAD_DIM]
        grad_attn = dot(part, proj[:, cv], NT)
        grad_score = (grad_attn * attn_slope[h].astype(f32)).astype(b16)
        grad[:, cv] = (dot(attn[h], part, TN) * slope[:, cv].astype(f32)).astype(b16)
        grad[:, cq] = (dot(grad_score, proj[:, ck], NN) * slope[:, cq].astype(f32)).astype(b16)
        grad[:, ck] = (dot(grad_score, proj[:, cq], TN) * slope[:, ck].astype(f32)).astype(b16)


def score_kernel(groups, owners, share, chunks, places, cand, inv_len, inverse, unit_hbm, yn_hbm, *refs):
    count = len(places)
    pieces, saved_hbm, refs = refs[:count], refs[count : count + 6], refs[count + 6 :]
    tags, up_keep, up_give, grad, table, spread, unit_b, unit, *saved, sems = refs
    chips = owners // 2
    vocab_dev = share * groups
    grp, core = lax.axis_index("grp"), lax.axis_index("seq") % 2
    tok = unit_b.shape[0]
    block = vocab_dev + groups * (chips - 1) * share

    def place(key):
        side, chunk, k = key
        if chunk < 0:
            return side * block, vocab_dev
        before = sum(len(ds) for ds in chunks[:chunk]) * groups * share
        rows = len(chunks[chunk]) * share
        return side * block + vocab_dev + before + k * rows, rows

    load_unit = pltpu.make_async_copy(unit_hbm, unit_b, sems.at[count])
    load_unit.start()
    copies = {}
    for n, (*key, left, wide) in enumerate(places):
        at, rows = place(key)
        copy = pltpu.make_async_copy(pieces[n], table.at[pl.ds(at, rows), pl.ds(left, wide)], sems.at[n])
        copy.start()
        copies.setdefault(tuple(key), []).append(copy)
    load_yn = pltpu.make_async_copy(yn_hbm, unit, sems.at[count + 1])
    load_yn.start()
    load_saved = [
        pltpu.make_async_copy(x, y, sems.at[count + 2 + n]) for n, (x, y) in enumerate(zip(saved_hbm, saved))
    ]
    for copy in load_saved:
        copy.start()
    ids = owner_ids(owners)
    lane = iota((1, 128), 1)
    owner = jnp.full((1, 128), -1, i32)
    for j in range(owners):
        owner = jnp.where(lane == j, ids[j], owner)
    candidates = cand[...]
    chosen = jnp.full((tok, 128), -1, i32)
    first = jnp.zeros((tok, 128), f32)
    for c in range(NCAND):
        here = candidates[:, c : c + 1] // vocab_dev == owner
        chosen = jnp.where(here, candidates[:, c : c + 1], chosen)
        if c == 0:
            first = here.astype(f32)
    wanted = [jnp.broadcast_to(chosen[:, j : j + 1], (tok, 128)) for j in range(owners)]

    def runs(key):
        side, chunk, k = key
        at, rows = place(key)
        if chunk < 0:
            return at, rows, [(side * chips, 0, vocab_dev, ids[side * chips] * vocab_dev)]
        begin = (grp ^ k) * share
        return at, rows, [
            (side * chips + d, i * share, share, ids[side * chips + d] * vocab_dev + begin)
            for i, d in enumerate(chunks[chunk])
        ]

    def tiles(key):
        at, rows, here = runs(key)
        for j, off, wide, base in here:
            step = min(wide, 128)
            for o in range(0, wide, step):
                hit = wanted[j][:, :step] == base + o + iota((1, step), 1)
                yield j, off + o, step, hit

    load_unit.wait()
    yb = unit_b[...]
    value = [[] for _ in range(owners)]
    for key in copies:
        for copy in copies[key]:
            copy.wait()
        at, rows, _ = runs(key)
        product = dot(yb, table[at : at + rows], NT)
        for j, off, step, hit in tiles(key):
            value[j].append(jnp.where(hit, product[:, off : off + step], 0.0))
    logits = jnp.zeros((tok, 128), f32)
    for j in range(owners):
        total = value[j][0]
        for part in value[j][1:]:
            total = total + part
        logits = jnp.where(lane == j, jnp.sum(total, -1, keepdims=True), logits)
    exponent = jnp.where(chosen >= 0, jnp.exp(logits / softmax_warmth), 0.0)
    coef = (exponent / jnp.sum(exponent, -1, keepdims=True) - first) / softmax_warmth
    tags[:owners] = coef.T[:owners]
    tags[owners:] = chosen.astype(f32).T[:owners]
    amount = [jnp.broadcast_to(coef[:, j : j + 1], (tok, 128)) for j in range(owners)]
    for key in copies:
        at = runs(key)[0]
        for j, off, step, hit in tiles(key):
            spread[:, at + off : at + off + step] = jnp.where(hit, amount[j][:, :step], 0.0).astype(b16)
    pulled = dot(spread[...], table[...], NN)
    load_yn.wait()
    yn = unit[...]
    upstream = (pulled - yn * jnp.sum(yn * pulled, -1, keepdims=True)) * inv_len[...]
    mine, other = split_columns(upstream, owners, core)
    up_keep[...] = mine.astype(b16)
    up_give[...] = other.astype(b16)
    for copy in load_saved:
        copy.wait()
    backward(upstream.astype(b16), inverse, *saved, grad)


def item_kernel(groups, owners, share, chunks, places, *refs):
    count = len(places)
    units, tags = refs[:count], refs[count : count + groups]
    parts, (keep, give, gathered, near, sems) = refs[count + groups : -5], refs[-5:]
    chips = owners // 2
    vocab_dev = share * groups
    grp = lax.axis_index("grp")
    tok = tags[0].shape[1]
    copies = []
    for n, (k, left, wide) in enumerate(places):
        copies.append(pltpu.make_async_copy(units[n], gathered.at[pl.ds(k * tok, tok), pl.ds(left, wide)], sems.at[n]))
    begin = pl.multiple_of(grp * share, share)
    for n, part in enumerate(parts):
        side, chunk = n // (len(chunks) + 1), n % (len(chunks) + 1) - 1
        for i, d in enumerate([0] if chunk < 0 else chunks[chunk]):
            rows = pl.ds(begin if chunk < 0 else i * share, share)
            at = pl.ds((side * chips + d) * share, share)
            copies.append(pltpu.make_async_copy(part.at[rows], near.at[at], sems.at[len(copies)]))
    for copy in copies:
        copy.start()
    ids = owner_ids(owners)
    amounts = jnp.concatenate([t[:owners] for t in tags], 1)
    chosen = jnp.concatenate([t[owners:] for t in tags], 1).astype(i32)
    for copy in copies[:count]:
        copy.wait()
    for side, out in ((0, keep), (1, give)):
        parts = []
        for d in range(chips):
            j = side * chips + d
            hit = ids[j] * vocab_dev + grp * share + iota((share, 1), 0) == chosen[j : j + 1]
            parts.append(jnp.where(hit, amounts[j : j + 1], 0.0).astype(b16))
        summed = dot(jnp.concatenate(parts, 0), gathered[...], NN)
        for copy in copies[count + side * chips : count + (side + 1) * chips]:
            copy.wait()
        row = near[side * chips * share : (side + 1) * chips * share].astype(f32)
        out[...] = (summed - row * jnp.sum(row * summed, -1, keepdims=True)).astype(b16)


def weight_kernel(groups, owners, *refs):
    given, outs, loaded, (own, whole, sems) = refs[:8], refs[8:13], refs[13:21], refs[21:]
    copies = [pltpu.make_async_copy(x, y, sems.at[n]) for n, (x, y) in enumerate(zip(given, loaded))]
    for copy in copies:
        copy.start()
    keep, grad, up_keep, gated, up_give, far_gated, give, far_grad = loaded
    chips = owners // 2
    grp = lax.axis_index("grp")
    wide = grad.shape[1]
    step = gated.shape[1]
    for copy in copies[:2]:
        copy.wait()
    for i in range(0, wide, step):
        own[:, i : i + step] = dot(keep[...], grad[:, i : i + step], TN)
    for copy in copies[2:6]:
        copy.wait()
    part = dot(up_keep[...], gated[...], TN) + dot(up_give[...], far_gated[...], TN)
    whole[:, wide:] = part.astype(b16)
    for copy in copies[6:]:
        copy.wait()
    for i in range(0, wide, step):
        cols = slice(i, i + step)
        whole[:, cols] = (own[:, cols] + dot(give[...], far_grad[:, cols], TN)).astype(b16)
    rows = whole.shape[0] // chips
    fine = rows // groups
    half = whole.shape[1] // 2
    base, by_one, by_two, one_right, two_left = outs
    for z in range(chips):
        piece = [whole[pl.ds(pl.multiple_of(z * rows + (grp ^ k) * fine, fine), fine)] for k in range(groups)]
        base[z] = piece[0]
        by_one[0, z], by_one[1, z] = piece[3][:, :half], piece[1][:, :half]
        by_two[0, z], by_two[1, z] = piece[3][:, half:], piece[2][:, half:]
        one_right[z], two_left[z] = piece[1][:, half:], piece[2][:, :half]


def corner_kernel(by_one, by_two, one_right, two_left, right_out, left_out):
    right_out[...] = (one_right[...].astype(f32) + by_two[0].astype(f32)).astype(b16)
    left_out[...] = (two_left[...].astype(f32) + by_one[0].astype(f32)).astype(b16)


def sum_kernel(base, by_one, by_two, one_right, two_left, *outs):
    chips, fine, wide = base.shape
    chip = lax.axis_index("seq") // 2
    half = wide // 2
    for n, d in enumerate(distances(chips)):
        z = chip ^ d
        own = base[z].astype(f32)
        left = own[:, :half] + by_one[1, z].astype(f32) + two_left[z].astype(f32)
        right = own[:, half:] + by_two[1, z].astype(f32) + one_right[z].astype(f32)
        out = outs[2 * n // chips]
        at = slice(n % (chips // 2) * fine, (n % (chips // 2) + 1) * fine)
        out[at, :half] = left.astype(b16)
        out[at, half:] = right.astype(b16)


def pair_kernel(x, y, *outs):
    rows = outs[0].shape[0]
    for d, out in enumerate(outs):
        at = slice(d * rows, (d + 1) * rows)
        out[...] = (x[at].astype(f32) + y[at].astype(f32)).astype(b16)


def assemble_kernel(groups, columns, *refs):
    parts, outs = refs[:groups], refs[groups:]
    grp = lax.axis_index("grp")
    fine = parts[0].shape[0]
    for k in range(groups):
        at = pl.ds(pl.multiple_of((grp ^ k) * fine, fine), fine)
        left = 0
        for out, wide in zip(outs, columns):
            out[at] = parts[k][:, left : left + wide].astype(f32)
            left += wide


def relay_kernel(arrived, out):
    tok, slots = out.shape[0], arrived.shape[0]
    filled = (arrived[:, :128].astype(f32) < EMPTY / 2).astype(b16)
    before = (iota((slots, 1), 0) > iota((1, slots), 1)).astype(b16)
    rank = dot(before, filled, NN)[:, :1].astype(i32)
    rank = jnp.where(filled[:, :1].astype(f32) > 0, rank, -1)
    place = (rank == iota((1, tok), 1)).astype(b16)
    out[...] = dot(place, arrived[...], TN).astype(b16)


def body(events, lengths, destinations, history, negatives, in_weight, out_weight, item_table):
    groups = lax.axis_size("grp")
    owners = lax.axis_size("seq")
    chips = owners // 2
    grp = lax.axis_index("grp")
    seq = lax.axis_index("seq")
    chip, core = seq // 2, seq % 2
    tok = events.shape[0]
    vocab_dev, width = item_table.shape
    hidden = out_weight.shape[1]
    share = vocab_dev // groups
    slot = 3 * tok // (2 * owners)
    rows = width // owners
    fine = rows // groups

    def to_chip(x, d):
        pairs = [(2 * a + b, 2 * ((a + d) % chips) + b) for a in range(chips) for b in range(2)]
        return lax.ppermute(x, "seq", pairs)

    def across(x, k):
        pairs = [(2 * a + b, 2 * (a ^ k) + b) for a in range(chips) for b in range(2)]
        return lax.ppermute(x, "seq", pairs)

    def to_group(x, k):
        return lax.ppermute(x, "grp", [(a, a ^ k) for a in range(groups)])

    def to_core(x):
        return lax.ppermute(x, "seq", [(a, a ^ 1) for a in range(owners)])

    def fold(low, high, gate=()):
        bit = 1
        while bit < chips // 2:
            shape = (low.shape[0] // 2, low.shape[1])
            came, _ = lax.optimization_barrier((across(high, bit), gate))
            low, high = call(pair_kernel, [(shape, b16)] * 2, [VMEM] * 2, [low, came], room=8)
            bit *= 2
        return low, high

    def finish(low, high):
        return low.astype(f32) + across(high, chips // 2).astype(f32)

    def gather_groups(x, near=None):
        wide = x.shape[1]
        if groups != 4:
            return [(k, 0, wide, to_group(x, k) if k else x) for k in range(groups)]
        one, two = near or [to_group(x, k) for k in (1, 2)]
        half = wide // 2
        left, right = to_group(one[:, :half], 2), to_group(two[:, half:], 1)
        return [(0, 0, wide, x), (1, 0, wide, one), (2, 0, wide, two), (3, 0, half, left), (3, half, half, right)]

    own, quarter, quarter_inv = call(
        lambda *refs: normalise_kernel(share, *refs),
        [((vocab_dev, width), b16), ((share, width), b16), ((share, 1), f32)],
        [VMEM], [item_table], flops=8 * vocab_dev * width, nbytes=5 * vocab_dev * width, room=8,
    )
    chunks = [list(range(1, chips))]
    have, bit = {0: quarter}, chips // 2
    while bit:
        have.update({x ^ bit: across(have[x], bit) for x in have})
        bit //= 2
    got = [have[x] for x in distances(chips)[1:]]
    outs = [
        ((tok, width // 2), b16), ((tok, width // 2), b16), ((tok, 4 * hidden), b16), ((tok, 4 * hidden), b16),
        ((HEADS, tok, tok), b16), ((HEADS, tok, tok), b16), ((tok, hidden), f32), ((tok, 1), f32),
        ((tok, hidden), b16), ((tok, width), f32), ((tok, width), b16), ((tok, 1), f32),
        ((owners * slot, width), b16),
    ]
    (keep, give, proj, slope, attn, attn_slope, normed, inverse, gated, unit, unit_b, inv_len, outgoing) = call(
        lambda *refs: forward_kernel(owners, slot, *refs), outs, [SMEM, SMEM, VMEM, VMEM, VMEM],
        [lengths, destinations, events, in_weight, out_weight],
        room=63,
    )

    near_units = [to_group(unit_b, k) for k in (1, 2)]
    candidates = jnp.concatenate([history[:, None], negatives], 1)
    got, near_units, candidates = lax.optimization_barrier((got, near_units, candidates))
    unit_sent = gather_groups(unit_b, near_units)
    others = [jnp.concatenate(got, 0)]
    pieces = [(0, -1, 0, 0, width, own)]
    for j, x in enumerate(others):
        pieces += [(0, j) + p for p in gather_groups(x)]
    later, _ = lax.optimization_barrier((own, [p[5] for p in pieces[1:4]]))
    far_own = to_core(later)
    pieces = pieces + [(1,) + p[1:5] + (to_core(p[5]) if p[1] >= 0 else far_own,) for p in pieces]
    near = [p[5] for p in pieces if p[2] == 0]
    outgoing, _ = lax.optimization_barrier((outgoing, others))

    arrived = lax.all_to_all(
        outgoing.reshape(owners, slot, width), "seq", 0, 0, tiled=True
    ).reshape(owners * slot, width)
    vocab = vocab_dev * owners
    far_give, far_gated = to_core(give), to_core(gated)
    units = [p[3] for p in unit_sent]
    layer_out, = call(relay_kernel, [((tok, width), b16)], [VMEM], [arrived], room=63)
    layer_out, score_unit, far_give, far_gated, units = lax.optimization_barrier(
        (layer_out, unit, far_give, far_gated, units)
    )
    saved = [out_weight, proj, slope, attn, attn_slope, normed]
    tags, up_keep, up_give, grad = call(
        lambda *refs: score_kernel(groups, owners, share, chunks, [p[:5] for p in pieces], *refs),
        [((2 * owners, tok), f32), ((tok, width // 2), b16), ((tok, width // 2), b16), ((tok, 4 * hidden), b16)],
        [VMEM] * 3 + [ANY] * (len(pieces) + 8),
        [candidates, inv_len, inverse, unit_b, score_unit] + [p[5] for p in pieces] + saved,
        [pltpu.VMEM((vocab, width), b16), pltpu.VMEM((tok, vocab), b16), pltpu.VMEM((tok, width), b16),
         pltpu.VMEM((tok, width), f32)] + [pltpu.VMEM(x.shape, x.dtype) for x in saved]
        + [pltpu.SemaphoreType.DMA((len(pieces) + 8,))],
        room=63,
    )

    all_tags = [to_group(tags, k) if k else tags for k in range(groups)]
    far = [far_give, to_core(up_give), to_core(grad), far_gated]
    far[1], all_tags = lax.optimization_barrier((far[1], all_tags))
    mine, other = call(
        lambda *refs: item_kernel(groups, owners, share, chunks, [p[:3] for p in unit_sent], *refs),
        [((chips * share, width), b16)] * 2, [ANY] * len(units) + [VMEM] * groups + [ANY] * len(near),
        units + all_tags + near,
        [pltpu.VMEM((groups * tok, width), b16), pltpu.VMEM((2 * chips * share, width), b16),
         pltpu.SemaphoreType.DMA((len(units) + 2 * chips,))],
        room=63,
    )
    far_mine = to_core(other)
    far, mine = lax.optimization_barrier((far, mine))
    half = 5 * hidden // 2
    if groups == 4:
        block = (chips, fine, 5 * hidden)
        split = (chips, fine, half)
        parts = call(
            lambda *refs: weight_kernel(groups, owners, *refs),
            [(block, b16)] + [((2,) + split, b16)] * 2 + [(split, b16)] * 2, [ANY] * 8,
            [keep, grad, up_keep, gated, far[1], far[3], far[0], far[2]],
            [pltpu.VMEM(x.shape, b16) for x in (keep, grad, up_keep, gated, up_keep, gated, keep, grad)]
            + [pltpu.VMEM((width // 2, 4 * hidden), f32), pltpu.VMEM((width // 2, 5 * hidden), b16),
               pltpu.SemaphoreType.DMA((8,))],
            flops=2 * tok * width * 5 * hidden, nbytes=20 * tok * width, room=60,
        )
        by_one, by_two = to_group(parts[1], 1), to_group(parts[2], 2)
        corner = (by_one, by_two)
    else:
        def both(x, y):
            return jnp.concatenate([x, y], 0)

        in_part = dot(both(keep, far[0]), both(grad, far[2]), TN)
        out_part = dot(both(up_keep, far[1]), both(gated, far[3]), TN)
        weight = jnp.concatenate([in_part, out_part], 1).astype(b16)
        weight = weight.reshape(chips, groups, fine, 5 * hidden)
        sums = lax.dynamic_index_in_dim(weight, grp, 1, False).astype(f32)
        for k in range(1, groups):
            sums += to_group(lax.dynamic_index_in_dim(weight, grp ^ k, 1, False), k).astype(f32)


    low, high = call(
        pair_kernel, [((chips // 2 * share, width), b16)] * 2, [VMEM] * 2, [mine, far_mine],
        flops=chips * share * width, nbytes=6 * chips * share * width, room=8,
    )
    low, high = fold(low, high)
    if groups == 4:
        by_one, by_two, low, high = lax.optimization_barrier(corner + (low, high))
        one_right, two_left = call(
            corner_kernel, [(split, b16)] * 2, [VMEM] * 4, [by_one, by_two, parts[3], parts[4]], room=8,
        )
        arrived = [by_one, by_two, to_group(one_right, 1), to_group(two_left, 2)]
    total = finish(low, high)
    total = (total * quarter_inv).astype(b16)
    totals = [to_group(total, k) if k else total for k in range(groups)]
    table_grad, = call(
        lambda *refs: assemble_kernel(groups, [width], *refs), [((vocab_dev, width), f32)], [VMEM] * groups, totals,
        flops=vocab_dev * width, nbytes=6 * vocab_dev * width, room=8,
    )

    if groups == 4:
        base, _ = lax.optimization_barrier((parts[0], total))
        low, high = call(
            sum_kernel, [((chips // 2 * fine, 5 * hidden), b16)] * 2, [VMEM] * 5, [base] + arrived,
            flops=chips * fine * 5 * hidden, nbytes=40 * chips * fine * hidden, room=10,
        )
        line = finish(*fold(low, high, totals[1]))
    else:
        blocks = [lax.dynamic_index_in_dim(sums, (chip + d) % chips, 0, False).astype(b16) for d in range(chips)]
        line = blocks[0].astype(f32)
        for d in range(1, chips):
            line += to_chip(blocks[d], d).astype(f32)
    line = line.astype(b16)
    lines = [to_group(line, k) if k else line for k in range(groups)]
    if fine % 16 == 0:
        in_grad, out_grad = call(
            lambda *refs: assemble_kernel(groups, [4 * hidden, hidden], *refs),
            [((rows, 4 * hidden), f32), ((rows, hidden), f32)], [VMEM] * groups, lines,
            flops=rows * hidden, nbytes=30 * rows * hidden, room=8,
        )
    else:
        shard = jnp.zeros((rows, 5 * hidden), f32)
        for k in range(groups):
            shard = lax.dynamic_update_slice_in_dim(shard, lines[k].astype(f32), (grp ^ k) * fine, 0)
        in_grad, out_grad = shard[:, : 4 * hidden], shard[:, 4 * hidden :]
    return (layer_out, in_grad, out_grad, table_grad)


def solution(mesh):
    return jax.shard_map(
        body,
        mesh=mesh,
        in_specs=(
            P(("grp", "seq"), None),
            P(("grp", "seq"), None),
            P(("grp", "seq"), None),
            P(("grp", "seq")),
            P(("grp", "seq"), None),
            P(),
            P(),
            P("seq", None),
        ),
        out_specs=(P(("grp", "seq"), None), P("seq", None), P("seq", None), P("seq", None)),
        check_vma=False,
    )
```

```python
import jax
import jax.numpy as jnp
from jax import lax
from jax.experimental import pallas as pl
from jax.experimental.pallas import tpu as pltpu
from jax.sharding import PartitionSpec as P

HEADS = 4
HEAD_DIM = 128
NCAND = 4

epsilon = 1e-05
softmax_warmth = 0.05
EMPTY = 2.0**100

f32, b16, i32 = jnp.float32, jnp.bfloat16, jnp.int32
NN = ((1,), (0,))
NT = ((1,), (1,))
TN = ((0,), (0,))
VMEM = pl.BlockSpec(memory_space=pltpu.VMEM)
SMEM = pl.BlockSpec(memory_space=pltpu.SMEM)
ANY = pl.BlockSpec(memory_space=pl.ANY)


def dot(a, b, dims):
    return lax.dot_general(a, b, (dims, ((), ())), preferred_element_type=f32)


def iota(shape, axis):
    return lax.broadcasted_iota(i32, shape, axis)


def center_scale(values):
    average = jnp.mean(values, -1, keepdims=True)
    centered = values - average
    inverse = lax.rsqrt(jnp.mean(centered * centered, -1, keepdims=True) + epsilon)
    return (centered * inverse, inverse)


def sigmoid(values):
    return 1.0 / (1.0 + jnp.exp(-values))


def split_columns(x, owners, core):
    rows = x.shape[1] // owners
    blocks = [x[:, i * rows : (i + 1) * rows] for i in range(owners)]
    even, odd = jnp.concatenate(blocks[0::2], 1), jnp.concatenate(blocks[1::2], 1)
    first = jnp.broadcast_to(core, even.shape) == 0
    return jnp.where(first, even, odd), jnp.where(first, odd, even)


def call(kernel, out, specs, args, scratch=(), flops=0, nbytes=0, room=14):
    return pl.pallas_call(
        kernel,
        out_shape=[jax.ShapeDtypeStruct(s, t) for s, t in out],
        in_specs=specs,
        out_specs=[VMEM] * len(out),
        scratch_shapes=list(scratch),
        cost_estimate=pl.CostEstimate(flops=flops, bytes_accessed=nbytes, transcendentals=0),
        compiler_params=pltpu.CompilerParams(vmem_limit_bytes=room * 2**20),
    )(*args)


def forward_kernel(
    owners, slot, lengths, dests, events, in_weight, out_weight,
    keep, give, proj, slope, attn, attn_slope, normed_out, inv_out, gated_out, unit_b, inv_len, outgoing,
):
    tok = events.shape[0]
    hidden = out_weight.shape[1]
    scale = HEAD_DIM ** (-0.5)
    core = lax.axis_index("seq") % 2
    x = events[...].astype(f32)
    normed_in = center_scale(x)[0]
    mine, other = split_columns(normed_in, owners, core)
    keep[...] = mine.astype(b16)
    give[...] = other.astype(b16)
    normed_in = normed_in.astype(b16)
    for i in range(4):
        cols = slice(i * hidden, (i + 1) * hidden)
        p = dot(normed_in, in_weight[:, cols], NN)
        sig = sigmoid(p)
        proj[:, cols] = (p * sig).astype(b16)
        slope[:, cols] = (sig * (1.0 + p * (1.0 - sig))).astype(b16)

    pos_c, pos_r = iota((tok, 1), 0), iota((1, tok), 1)
    user_c, user_r = jnp.zeros((tok, 1), i32), jnp.zeros((1, tok), i32)
    target = jnp.zeros((1, tok), i32)
    start = jnp.int32(0)
    for j in range(lengths.shape[1]):
        end = start + lengths[0, j]
        user_c += (pos_c >= end).astype(i32)
        user_r += (pos_r >= end).astype(i32)
        here = (pos_r >= start) & (pos_r < end)
        target = jnp.where(here, dests[0, j] * slot + pos_r - start, target)
        start = end
    mask = (user_c == user_r) & (pos_r <= pos_c)

    outputs = []
    for h in range(HEADS):
        v = proj[:, hidden + h * HEAD_DIM : hidden + (h + 1) * HEAD_DIM]
        q = proj[:, 2 * hidden + h * HEAD_DIM : 2 * hidden + (h + 1) * HEAD_DIM]
        k = proj[:, 3 * hidden + h * HEAD_DIM : 3 * hidden + (h + 1) * HEAD_DIM]
        s = dot(q, k, NT) * scale
        sig = sigmoid(s)
        weight = jnp.where(mask, s * sig, 0.0).astype(b16)
        attn[h] = weight
        attn_slope[h] = jnp.where(mask, sig * (1.0 + s * (1.0 - sig)) * scale, 0.0).astype(b16)
        outputs.append(dot(weight, v, NN))
    normed, inverse = center_scale(jnp.concatenate(outputs, 1))
    normed_out[...] = normed.astype(b16)
    inv_out[...] = inverse
    gated = (normed * proj[:, :hidden].astype(f32)).astype(b16)
    gated_out[...] = gated
    result = x + dot(gated, out_weight[...], NT)
    inverse = lax.rsqrt(jnp.sum(result * result, -1, keepdims=True) + epsilon)
    inv_len[...] = inverse
    yn = result * inverse
    unit_b[...] = yn.astype(b16)
    row = iota((outgoing.shape[0], 1), 0)
    filled = jnp.zeros(row.shape, i32)
    for j in range(lengths.shape[1]):
        at = dests[0, j] * slot
        filled = jnp.where((row >= at) & (row < at + lengths[0, j]), 1, filled)
    placed = dot((row == target).astype(b16), result.astype(b16), NN)
    outgoing[...] = jnp.where(filled == 1, placed, EMPTY).astype(b16)


def distances(chips):
    order, bit = [0], chips // 2
    while bit:
        order += [x ^ bit for x in order]
        bit //= 2
    return order


def owner_ids(owners):
    seq = lax.axis_index("seq")
    chip, core = seq // 2, seq % 2
    chips = owners // 2
    return [2 * (chip ^ d) + (core ^ side) for side in range(2) for d in distances(chips)]


def normalise_kernel(share, item_table, own, quarter, quarter_inv):
    grp = lax.axis_index("grp")
    x = item_table[...].astype(f32)
    own[...] = (x * lax.rsqrt(jnp.sum(x * x, -1, keepdims=True) + epsilon)).astype(b16)
    x = item_table[pl.ds(pl.multiple_of(grp * share, share), share)].astype(f32)
    inverse = lax.rsqrt(jnp.sum(x * x, -1, keepdims=True) + epsilon)
    quarter[...] = (x * inverse).astype(b16)
    quarter_inv[...] = inverse


def backward(up, inverse, out_weight, proj, slope, attn, attn_slope, normed_ref, grad):
    hidden = out_weight.shape[1]
    normed = normed_ref[...].astype(f32)
    grad_gated = dot(up, out_weight[...], NN)
    grad[:, :hidden] = (grad_gated * normed * slope[:, :hidden].astype(f32)).astype(b16)
    grad_normed = grad_gated * proj[:, :hidden].astype(f32)
    grad_attended = inverse[...] * (
        grad_normed
        - jnp.mean(grad_normed, -1, keepdims=True)
        - normed * jnp.mean(grad_normed * normed, -1, keepdims=True)
    )
    grad_attended = grad_attended.astype(b16)
    for h in range(HEADS):
        cv, cq, ck = [slice(i * hidden + h * HEAD_DIM, i * hidden + (h + 1) * HEAD_DIM) for i in (1, 2, 3)]
        part = grad_attended[:, h * HEAD_DIM : (h + 1) * HEAD_DIM]
        grad_attn = dot(part, proj[:, cv], NT)
        grad_score = (grad_attn * attn_slope[h].astype(f32)).astype(b16)
        grad[:, cv] = (dot(attn[h], part, TN) * slope[:, cv].astype(f32)).astype(b16)
        grad[:, cq] = (dot(grad_score, proj[:, ck], NN) * slope[:, cq].astype(f32)).astype(b16)
        grad[:, ck] = (dot(grad_score, proj[:, cq], TN) * slope[:, ck].astype(f32)).astype(b16)


def score_kernel(groups, owners, share, chunks, places, cand, inv_len, inverse, unit_hbm, *refs):
    count = len(places)
    pieces, saved_hbm, refs = refs[:count], refs[count : count + 6], refs[count + 6 :]
    tags, up_keep, up_give, grad, table, spread, unit_b, *saved, sems = refs
    chips = owners // 2
    vocab_dev = share * groups
    grp, core = lax.axis_index("grp"), lax.axis_index("seq") % 2
    tok = unit_b.shape[0]
    block = vocab_dev + groups * (chips - 1) * share

    def place(key):
        side, chunk, k = key
        if chunk < 0:
            return side * block, vocab_dev
        before = sum(len(ds) for ds in chunks[:chunk]) * groups * share
        rows = len(chunks[chunk]) * share
        return side * block + vocab_dev + before + k * rows, rows

    load_unit = pltpu.make_async_copy(unit_hbm, unit_b, sems.at[count])
    load_unit.start()
    copies = {}
    for n, (*key, left, wide) in enumerate(places):
        at, rows = place(key)
        copy = pltpu.make_async_copy(pieces[n], table.at[pl.ds(at, rows), pl.ds(left, wide)], sems.at[n])
        copy.start()
        copies.setdefault(tuple(key), []).append(copy)
    load_saved = [
        pltpu.make_async_copy(x, y, sems.at[count + 2 + n]) for n, (x, y) in enumerate(zip(saved_hbm, saved))
    ]
    for copy in load_saved:
        copy.start()
    ids = owner_ids(owners)
    lane = iota((1, 128), 1)
    owner = jnp.full((1, 128), -1, i32)
    for j in range(owners):
        owner = jnp.where(lane == j, ids[j], owner)
    candidates = cand[...]
    chosen = jnp.full((tok, 128), -1, i32)
    first = jnp.zeros((tok, 128), f32)
    for c in range(NCAND):
        here = candidates[:, c : c + 1] // vocab_dev == owner
        chosen = jnp.where(here, candidates[:, c : c + 1], chosen)
        if c == 0:
            first = here.astype(f32)
    wanted = [jnp.broadcast_to(chosen[:, j : j + 1], (tok, 128)) for j in range(owners)]

    def runs(key):
        side, chunk, k = key
        at, rows = place(key)
        if chunk < 0:
            return at, rows, [(side * chips, 0, vocab_dev, ids[side * chips] * vocab_dev)]
        begin = (grp ^ k) * share
        return at, rows, [
            (side * chips + d, i * share, share, ids[side * chips + d] * vocab_dev + begin)
            for i, d in enumerate(chunks[chunk])
        ]

    def tiles(key):
        at, rows, here = runs(key)
        for j, off, wide, base in here:
            step = min(wide, 128)
            for o in range(0, wide, step):
                hit = wanted[j][:, :step] == base + o + iota((1, step), 1)
                yield j, off + o, step, hit

    load_unit.wait()
    yb = unit_b[...]
    value = [[] for _ in range(owners)]
    for key in copies:
        for copy in copies[key]:
            copy.wait()
        at, rows, _ = runs(key)
        product = dot(yb, table[at : at + rows], NT)
        for j, off, step, hit in tiles(key):
            value[j].append(jnp.where(hit, product[:, off : off + step], 0.0))
    logits = jnp.zeros((tok, 128), f32)
    for j in range(owners):
        total = value[j][0]
        for part in value[j][1:]:
            total = total + part
        logits = jnp.where(lane == j, jnp.sum(total, -1, keepdims=True), logits)
    exponent = jnp.where(chosen >= 0, jnp.exp(logits / softmax_warmth), 0.0)
    coef = (exponent / jnp.sum(exponent, -1, keepdims=True) - first) / softmax_warmth
    tags[:owners] = coef.T[:owners]
    tags[owners:] = chosen.astype(f32).T[:owners]
    amount = [jnp.broadcast_to(coef[:, j : j + 1], (tok, 128)) for j in range(owners)]
    for key in copies:
        at = runs(key)[0]
        for j, off, step, hit in tiles(key):
            spread[:, at + off : at + off + step] = jnp.where(hit, amount[j][:, :step], 0.0).astype(b16)
    pulled = dot(spread[...], table[...], NN)
    yn = yb.astype(f32)
    upstream = (pulled - yn * jnp.sum(yn * pulled, -1, keepdims=True)) * inv_len[...]
    mine, other = split_columns(upstream, owners, core)
    up_keep[...] = mine.astype(b16)
    up_give[...] = other.astype(b16)
    for copy in load_saved:
        copy.wait()
    backward(upstream.astype(b16), inverse, *saved, grad)


def item_kernel(groups, owners, share, chunks, places, *refs):
    count = len(places)
    units, tags = refs[:count], refs[count : count + groups]
    parts, (keep, give, gathered, near, sems) = refs[count + groups : -5], refs[-5:]
    chips = owners // 2
    vocab_dev = share * groups
    grp = lax.axis_index("grp")
    tok = tags[0].shape[1]
    copies = []
    for n, (k, left, wide) in enumerate(places):
        copies.append(pltpu.make_async_copy(units[n], gathered.at[pl.ds(k * tok, tok), pl.ds(left, wide)], sems.at[n]))
    begin = pl.multiple_of(grp * share, share)
    for n, part in enumerate(parts):
        side, chunk = n // (len(chunks) + 1), n % (len(chunks) + 1) - 1
        for i, d in enumerate([0] if chunk < 0 else chunks[chunk]):
            rows = pl.ds(begin if chunk < 0 else i * share, share)
            at = pl.ds((side * chips + d) * share, share)
            copies.append(pltpu.make_async_copy(part.at[rows], near.at[at], sems.at[len(copies)]))
    for copy in copies:
        copy.start()
    ids = owner_ids(owners)
    amounts = jnp.concatenate([t[:owners] for t in tags], 1)
    chosen = jnp.concatenate([t[owners:] for t in tags], 1).astype(i32)
    for copy in copies[:count]:
        copy.wait()
    for side, out in ((0, keep), (1, give)):
        parts = []
        for d in range(chips):
            j = side * chips + d
            hit = ids[j] * vocab_dev + grp * share + iota((share, 1), 0) == chosen[j : j + 1]
            parts.append(jnp.where(hit, amounts[j : j + 1], 0.0).astype(b16))
        summed = dot(jnp.concatenate(parts, 0), gathered[...], NN)
        for copy in copies[count + side * chips : count + (side + 1) * chips]:
            copy.wait()
        row = near[side * chips * share : (side + 1) * chips * share].astype(f32)
        out[...] = (summed - row * jnp.sum(row * summed, -1, keepdims=True)).astype(b16)


def weight_kernel(groups, owners, *refs):
    given, outs, loaded, (own, whole, sems) = refs[:8], refs[8:13], refs[13:21], refs[21:]
    copies = [pltpu.make_async_copy(x, y, sems.at[n]) for n, (x, y) in enumerate(zip(given, loaded))]
    for copy in copies:
        copy.start()
    keep, grad, up_keep, gated, up_give, far_gated, give, far_grad = loaded
    chips = owners // 2
    grp = lax.axis_index("grp")
    wide = grad.shape[1]
    step = gated.shape[1]
    for copy in copies[:2]:
        copy.wait()
    for i in range(0, wide, step):
        own[:, i : i + step] = dot(keep[...], grad[:, i : i + step], TN)
    for copy in copies[2:6]:
        copy.wait()
    part = dot(up_keep[...], gated[...], TN) + dot(up_give[...], far_gated[...], TN)
    whole[:, wide:] = part.astype(b16)
    for copy in copies[6:]:
        copy.wait()
    for i in range(0, wide, step):
        cols = slice(i, i + step)
        whole[:, cols] = (own[:, cols] + dot(give[...], far_grad[:, cols], TN)).astype(b16)
    rows = whole.shape[0] // chips
    fine = rows // groups
    half = whole.shape[1] // 2
    base, by_one, by_two, one_right, two_left = outs
    for z in range(chips):
        piece = [whole[pl.ds(pl.multiple_of(z * rows + (grp ^ k) * fine, fine), fine)] for k in range(groups)]
        base[z] = piece[0]
        by_one[0, z], by_one[1, z] = piece[3][:, :half], piece[1][:, :half]
        by_two[0, z], by_two[1, z] = piece[3][:, half:], piece[2][:, half:]
        one_right[z], two_left[z] = piece[1][:, half:], piece[2][:, :half]


def corner_kernel(by_one, by_two, one_right, two_left, right_out, left_out):
    right_out[...] = (one_right[...].astype(f32) + by_two[0].astype(f32)).astype(b16)
    left_out[...] = (two_left[...].astype(f32) + by_one[0].astype(f32)).astype(b16)


def sum_kernel(base, by_one, by_two, one_right, two_left, *outs):
    chips, fine, wide = base.shape
    chip = lax.axis_index("seq") // 2
    half = wide // 2
    for n, d in enumerate(distances(chips)):
        z = chip ^ d
        own = base[z].astype(f32)
        left = own[:, :half] + by_one[1, z].astype(f32) + two_left[z].astype(f32)
        right = own[:, half:] + by_two[1, z].astype(f32) + one_right[z].astype(f32)
        out = outs[2 * n // chips]
        at = slice(n % (chips // 2) * fine, (n % (chips // 2) + 1) * fine)
        out[at, :half] = left.astype(b16)
        out[at, half:] = right.astype(b16)


def pair_kernel(x, y, *outs):
    rows = outs[0].shape[0]
    for d, out in enumerate(outs):
        at = slice(d * rows, (d + 1) * rows)
        out[...] = (x[at].astype(f32) + y[at].astype(f32)).astype(b16)


def assemble_kernel(groups, columns, *refs):
    parts, outs = refs[:groups], refs[groups:]
    grp = lax.axis_index("grp")
    fine = parts[0].shape[0]
    for k in range(groups):
        at = pl.ds(pl.multiple_of((grp ^ k) * fine, fine), fine)
        left = 0
        for out, wide in zip(outs, columns):
            out[at] = parts[k][:, left : left + wide].astype(f32)
            left += wide


def relay_kernel(arrived, out):
    tok, slots = out.shape[0], arrived.shape[0]
    filled = (arrived[:, :128].astype(f32) < EMPTY / 2).astype(b16)
    before = (iota((slots, 1), 0) > iota((1, slots), 1)).astype(b16)
    rank = dot(before, filled, NN)[:, :1].astype(i32)
    rank = jnp.where(filled[:, :1].astype(f32) > 0, rank, -1)
    place = (rank == iota((1, tok), 1)).astype(b16)
    out[...] = dot(place, arrived[...], TN).astype(b16)


def body(events, lengths, destinations, history, negatives, in_weight, out_weight, item_table):
    groups = lax.axis_size("grp")
    owners = lax.axis_size("seq")
    chips = owners // 2
    grp = lax.axis_index("grp")
    seq = lax.axis_index("seq")
    chip, core = seq // 2, seq % 2
    tok = events.shape[0]
    vocab_dev, width = item_table.shape
    hidden = out_weight.shape[1]
    share = vocab_dev // groups
    slot = 3 * tok // (2 * owners)
    rows = width // owners
    fine = rows // groups

    def to_chip(x, d):
        pairs = [(2 * a + b, 2 * ((a + d) % chips) + b) for a in range(chips) for b in range(2)]
        return lax.ppermute(x, "seq", pairs)

    def across(x, k):
        pairs = [(2 * a + b, 2 * (a ^ k) + b) for a in range(chips) for b in range(2)]
        return lax.ppermute(x, "seq", pairs)

    def to_group(x, k):
        return lax.ppermute(x, "grp", [(a, a ^ k) for a in range(groups)])

    def to_core(x):
        return lax.ppermute(x, "seq", [(a, a ^ 1) for a in range(owners)])

    def fold(low, high, gate=()):
        bit = 1
        while bit < chips // 2:
            shape = (low.shape[0] // 2, low.shape[1])
            came, _ = lax.optimization_barrier((across(high, bit), gate))
            low, high = call(pair_kernel, [(shape, b16)] * 2, [VMEM] * 2, [low, came], room=8)
            bit *= 2
        return low, high

    def finish(low, high):
        return low.astype(f32) + across(high, chips // 2).astype(f32)

    def gather_groups(x, near=None):
        wide = x.shape[1]
        if groups != 4:
            return [(k, 0, wide, to_group(x, k) if k else x) for k in range(groups)]
        one, two = near or [to_group(x, k) for k in (1, 2)]
        half = wide // 2
        left, right = to_group(one[:, :half], 2), to_group(two[:, half:], 1)
        return [(0, 0, wide, x), (1, 0, wide, one), (2, 0, wide, two), (3, 0, half, left), (3, half, half, right)]

    own, quarter, quarter_inv = call(
        lambda *refs: normalise_kernel(share, *refs),
        [((vocab_dev, width), b16), ((share, width), b16), ((share, 1), f32)],
        [VMEM], [item_table], flops=8 * vocab_dev * width, nbytes=5 * vocab_dev * width, room=8,
    )
    chunks = [list(range(1, chips))]
    have, bit = {0: quarter}, chips // 2
    while bit:
        have.update({x ^ bit: across(have[x], bit) for x in have})
        bit //= 2
    got = [have[x] for x in distances(chips)[1:]]
    outs = [
        ((tok, width // 2), b16), ((tok, width // 2), b16), ((tok, 4 * hidden), b16), ((tok, 4 * hidden), b16),
        ((HEADS, tok, tok), b16), ((HEADS, tok, tok), b16), ((tok, hidden), b16), ((tok, 1), f32),
        ((tok, hidden), b16), ((tok, width), b16), ((tok, 1), f32),
        ((owners * slot, width), b16),
    ]
    (keep, give, proj, slope, attn, attn_slope, normed, inverse, gated, unit_b, inv_len, outgoing) = call(
        lambda *refs: forward_kernel(owners, slot, *refs), outs, [SMEM, SMEM, VMEM, VMEM, VMEM],
        [lengths, destinations, events, in_weight, out_weight],
        room=63,
    )

    near_units = [to_group(unit_b, k) for k in (1, 2)]
    candidates = jnp.concatenate([history[:, None], negatives], 1)
    got, near_units, candidates = lax.optimization_barrier((got, near_units, candidates))
    unit_sent = gather_groups(unit_b, near_units)
    others = [jnp.concatenate(got, 0)]
    pieces = [(0, -1, 0, 0, width, own)]
    for j, x in enumerate(others):
        pieces += [(0, j) + p for p in gather_groups(x)]
    later, _ = lax.optimization_barrier((own, [p[5] for p in pieces[1:4]]))
    far_own = to_core(later)
    pieces = pieces + [(1,) + p[1:5] + (to_core(p[5]) if p[1] >= 0 else far_own,) for p in pieces]
    near = [p[5] for p in pieces if p[2] == 0]
    outgoing, _ = lax.optimization_barrier((outgoing, others))

    arrived = lax.all_to_all(
        outgoing.reshape(owners, slot, width), "seq", 0, 0, tiled=True
    ).reshape(owners * slot, width)
    vocab = vocab_dev * owners
    far_give, far_gated = to_core(give), to_core(gated)
    units = [p[3] for p in unit_sent]
    layer_out, = call(relay_kernel, [((tok, width), b16)], [VMEM], [arrived], room=63)
    layer_out, inv_len, far_give, far_gated, units = lax.optimization_barrier(
        (layer_out, inv_len, far_give, far_gated, units)
    )
    saved = [out_weight, proj, slope, attn, attn_slope, normed]
    tags, up_keep, up_give, grad = call(
        lambda *refs: score_kernel(groups, owners, share, chunks, [p[:5] for p in pieces], *refs),
        [((2 * owners, tok), f32), ((tok, width // 2), b16), ((tok, width // 2), b16), ((tok, 4 * hidden), b16)],
        [VMEM] * 3 + [ANY] * (len(pieces) + 7),
        [candidates, inv_len, inverse, unit_b] + [p[5] for p in pieces] + saved,
        [pltpu.VMEM((vocab, width), b16), pltpu.VMEM((tok, vocab), b16), pltpu.VMEM((tok, width), b16),
        ] + [pltpu.VMEM(x.shape, x.dtype) for x in saved]
        + [pltpu.SemaphoreType.DMA((len(pieces) + 8,))],
        room=63,
    )

    all_tags = [to_group(tags, k) if k else tags for k in range(groups)]
    far = [far_give, to_core(up_give), to_core(grad), far_gated]
    far[1], all_tags = lax.optimization_barrier((far[1], all_tags))
    mine, other = call(
        lambda *refs: item_kernel(groups, owners, share, chunks, [p[:3] for p in unit_sent], *refs),
        [((chips * share, width), b16)] * 2, [ANY] * len(units) + [VMEM] * groups + [ANY] * len(near),
        units + all_tags + near,
        [pltpu.VMEM((groups * tok, width), b16), pltpu.VMEM((2 * chips * share, width), b16),
         pltpu.SemaphoreType.DMA((len(units) + 2 * chips,))],
        room=63,
    )
    far_mine = to_core(other)
    far, mine = lax.optimization_barrier((far, mine))
    half = 5 * hidden // 2
    if groups == 4:
        block = (chips, fine, 5 * hidden)
        split = (chips, fine, half)
        parts = call(
            lambda *refs: weight_kernel(groups, owners, *refs),
            [(block, b16)] + [((2,) + split, b16)] * 2 + [(split, b16)] * 2, [ANY] * 8,
            [keep, grad, up_keep, gated, far[1], far[3], far[0], far[2]],
            [pltpu.VMEM(x.shape, b16) for x in (keep, grad, up_keep, gated, up_keep, gated, keep, grad)]
            + [pltpu.VMEM((width // 2, 4 * hidden), f32), pltpu.VMEM((width // 2, 5 * hidden), b16),
               pltpu.SemaphoreType.DMA((8,))],
            flops=2 * tok * width * 5 * hidden, nbytes=20 * tok * width, room=60,
        )
        by_one, by_two = to_group(parts[1], 1), to_group(parts[2], 2)
        corner = (by_one, by_two)
    else:
        def both(x, y):
            return jnp.concatenate([x, y], 0)

        in_part = dot(both(keep, far[0]), both(grad, far[2]), TN)
        out_part = dot(both(up_keep, far[1]), both(gated, far[3]), TN)
        weight = jnp.concatenate([in_part, out_part], 1).astype(b16)
        weight = weight.reshape(chips, groups, fine, 5 * hidden)
        sums = lax.dynamic_index_in_dim(weight, grp, 1, False).astype(f32)
        for k in range(1, groups):
            sums += to_group(lax.dynamic_index_in_dim(weight, grp ^ k, 1, False), k).astype(f32)


    low, high = call(
        pair_kernel, [((chips // 2 * share, width), b16)] * 2, [VMEM] * 2, [mine, far_mine],
        flops=chips * share * width, nbytes=6 * chips * share * width, room=8,
    )
    low, high = fold(low, high)
    if groups == 4:
        by_one, by_two, low, high = lax.optimization_barrier(corner + (low, high))
        one_right, two_left = call(
            corner_kernel, [(split, b16)] * 2, [VMEM] * 4, [by_one, by_two, parts[3], parts[4]], room=8,
        )
        arrived = [by_one, by_two, to_group(one_right, 1), to_group(two_left, 2)]
    total = finish(low, high)
    total = (total * quarter_inv).astype(b16)
    totals = [to_group(total, k) if k else total for k in range(groups)]
    table_grad, = call(
        lambda *refs: assemble_kernel(groups, [width], *refs), [((vocab_dev, width), f32)], [VMEM] * groups, totals,
        flops=vocab_dev * width, nbytes=6 * vocab_dev * width, room=8,
    )

    if groups == 4:
        base, _ = lax.optimization_barrier((parts[0], total))
        low, high = call(
            sum_kernel, [((chips // 2 * fine, 5 * hidden), b16)] * 2, [VMEM] * 5, [base] + arrived,
            flops=chips * fine * 5 * hidden, nbytes=40 * chips * fine * hidden, room=10,
        )
        line = finish(*fold(low, high, totals[1]))
    else:
        blocks = [lax.dynamic_index_in_dim(sums, (chip + d) % chips, 0, False).astype(b16) for d in range(chips)]
        line = blocks[0].astype(f32)
        for d in range(1, chips):
            line += to_chip(blocks[d], d).astype(f32)
    line = line.astype(b16)
    lines = [to_group(line, k) if k else line for k in range(groups)]
    if fine % 16 == 0:
        in_grad, out_grad = call(
            lambda *refs: assemble_kernel(groups, [4 * hidden, hidden], *refs),
            [((rows, 4 * hidden), f32), ((rows, hidden), f32)], [VMEM] * groups, lines,
            flops=rows * hidden, nbytes=30 * rows * hidden, room=8,
        )
    else:
        shard = jnp.zeros((rows, 5 * hidden), f32)
        for k in range(groups):
            shard = lax.dynamic_update_slice_in_dim(shard, lines[k].astype(f32), (grp ^ k) * fine, 0)
        in_grad, out_grad = shard[:, : 4 * hidden], shard[:, 4 * hidden :]
    return (layer_out, in_grad, out_grad, table_grad)


def solution(mesh):
    return jax.shard_map(
        body,
        mesh=mesh,
        in_specs=(
            P(("grp", "seq"), None),
            P(("grp", "seq"), None),
            P(("grp", "seq"), None),
            P(("grp", "seq")),
            P(("grp", "seq"), None),
            P(),
            P(),
            P("seq", None),
        ),
        out_specs=(P(("grp", "seq"), None), P("seq", None), P("seq", None), P("seq", None)),
        check_vma=False,
    )
```
